32 devices in a mesh: dp: 16 (over z, y, core), seq: 2 (over x).
Axes of the slice: x: 2, y: 2, z: 4, core: 2. Of those that a mesh axis runs over, the one named last changes fastest.
Arguments:
- inputs: bfloat16 [16, 2048, 512], P('dp', 'seq'), may hold values from -6 to 6
- cotangent: bfloat16 [16, 2048, 512], P('dp', 'seq'), may hold values from -6 to 6
- mixer_gain: float32 [512], replicated, may hold values from 0.5 to 1.5
- mixer_bias: float32 [512], replicated, may hold values from -1.75 to 1.75
- query_weight: bfloat16 [512, 512], replicated, may hold values from -0.25 to 0.25
- key_weight: bfloat16 [512, 512], replicated, may hold values from -0.25 to 0.25
- value_weight: bfloat16 [512, 512], replicated, may hold values from -0.25 to 0.25
- gate_weight: bfloat16 [512, 8], replicated, may hold values from -0.25 to 0.25
- gate_bias: float32 [8], replicated, may hold values from 3 to 9
- output_weight: bfloat16 [512, 512], replicated, may hold values from -0.5 to 0.5
- projections: float32 [8, 64, 128], replicated, may hold values from -6 to 6
- start_state: float32 [8, 256, 64], replicated, may hold values from -1.75 to 1.75
- start_norm: float32 [8, 256], replicated, may hold values from -1.75 to 1.75
- feed_gain: float32 [512], replicated, may hold values from 0.5 to 1.5
- feed_bias: float32 [512], replicated, may hold values from -1.75 to 1.75
- up_weight: bfloat16 [512, 2048], P(None, 'seq'), may hold values from -0.25 to 0.25
- up_bias: bfloat16 [2048], P('seq'), may hold values from -3 to 3
- down_weight: bfloat16 [512, 2048], P(None, 'seq'), may hold values from -0.1875 to 0.1875
- down_bias: float32 [512], replicated, may hold values from -1.75 to 1.75
Outputs:
- block_output: bfloat16 [16, 2048, 512], P('dp', 'seq')
- input_grad: float32 [16, 2048, 512], P('dp', 'seq')
- mixer_gain_grad: float32 [512], replicated
- mixer_bias_grad: float32 [512], replicated
- query_weight_grad: float32 [512, 512], replicated
- key_weight_grad: float32 [512, 512], replicated
- value_weight_grad: float32 [512, 512], replicated
- gate_weight_grad: float32 [512, 8], replicated
- gate_bias_grad: float32 [8], replicated
- output_weight_grad: float32 [512, 512], replicated
- start_state_grad: float32 [8, 256, 64], replicated
- start_norm_grad: float32 [8, 256], replicated
- feed_gain_grad: float32 [512], replicated
- feed_bias_grad: float32 [512], replicated
- up_weight_grad: float32 [512, 2048], P(None, 'seq')
- up_bias_grad: float32 [2048], P('seq')
- down_weight_grad: float32 [512, 2048], P(None, 'seq')
- down_bias_grad: float32 [512], replicated
The draws below stay inside these ranges and needn't reach their ends.
All inputs are finite; a program needn't handle non-finite values.
Results may differ from the reference program's by a relative error of at most 0.02.
Values may be sent and summed in bfloat16 or wider, within the bound.
A program may use at most 256 MiB of HBM per device.

```python
import math
import jax
import jax.numpy as jnp
from jax import lax

D = 512
HEADS = 8
HD = 64
FEAT = 128
FF = 2048
GROUP = 32
LEN = 2048
ROWS = 16


def draw_gate_bias(key, part):
    key = jax.random.fold_in(key, 7)
    drawn = jax.random.uniform(key, (HEADS,), jnp.float32, 3.0, 9.0)
    return drawn


def shard_levels(rng, shape, shards, least, top_value):
    loudness = 1.0
    for dim, shards_of in shards:
        draws = jax.random.uniform(jax.random.fold_in(jax.random.fold_in(rng, 6), dim), (shards_of,), jnp.float32, least / len(shards), top_value / len(shards))
        loudness = loudness * jnp.repeat(jnp.exp(draws), shape[dim] // shards_of).reshape((-1,) + (1,) * (len(shape) - 1 - dim))
    return loudness


def gaussian(key, shape, scale, reach, split=(), held_as=jnp.bfloat16):
    array = jax.random.normal(key, shape, jnp.float32) * scale
    if len(split) > 0:
        array = shard_levels(key, shape, split, -0.22, 0.18) * array
    return jnp.clip(array, min=-reach, max=reach).astype(held_as)


def setup_inputs(seed: int = 0) -> dict:
    arg_keys = jax.random.split(jax.random.key(seed), 20)
    return {
        "inputs": gaussian(arg_keys[0], (ROWS, LEN, D), 1.0, 6.0, ((0, 16), (1, 2))),
        "cotangent": gaussian(arg_keys[1], (ROWS, LEN, D), 1.0, 6.0, ((0, 16), (1, 2))),
        "mixer_gain": jnp.clip(1.0 + 0.1 * jax.random.normal(arg_keys[2], (D,), jnp.float32), 0.5, 1.5),
        "mixer_bias": gaussian(arg_keys[3], (D,), 0.3, 1.75, (), jnp.float32),
        "query_weight": gaussian(arg_keys[4], (D, D), D ** -0.5, 0.25),
        "key_weight": gaussian(arg_keys[5], (D, D), D ** -0.5, 0.25),
        "value_weight": gaussian(arg_keys[6], (D, D), D ** -0.5, 0.25),
        "gate_weight": gaussian(arg_keys[7], (D, HEADS), D ** -0.5, 0.25),
        "gate_bias": draw_gate_bias(jax.random.fold_in(arg_keys[19], 71), 0),
        "output_weight": gaussian(arg_keys[9], (D, D), (D // 4) ** -0.5, 0.5),
        "projections": gaussian(arg_keys[10], (HEADS, HD, FEAT), 1.0, 6.0, (), jnp.float32),
        "start_state": gaussian(arg_keys[11], (HEADS, 2 * FEAT, HD), 0.3, 1.75, (), jnp.float32),
        "start_norm": gaussian(arg_keys[12], (HEADS, 2 * FEAT), 0.3, 1.75, (), jnp.float32),
        "feed_gain": jnp.clip(1.0 + 0.1 * jax.random.normal(arg_keys[13], (D,), jnp.float32), 0.5, 1.5),
        "feed_bias": gaussian(arg_keys[14], (D,), 0.3, 1.75, (), jnp.float32),
        "up_weight": gaussian(arg_keys[15], (D, FF), D ** -0.5, 0.25, ((1, 2),)),
        "up_bias": gaussian(arg_keys[16], (FF,), 0.5, 3.0, ((0, 2),)),
        "down_weight": gaussian(arg_keys[17], (D, FF), (FF // 2) ** -0.5, 0.1875, ((1, 2),)),
        "down_bias": gaussian(arg_keys[18], (D,), 0.3, 1.75, (), jnp.float32),
    }


EPS_NORM = 1e-05
EPS_UNIT = 1e-06
GUARD = 0.0625
HIGH = lax.Precision.HIGHEST

@jax.custom_vjp
def low(v):
    return lax.optimization_barrier(v.astype(jnp.bfloat16)).astype(jnp.float32)

@jax.custom_vjp
def low_back(v):
    return v

def low_keep(v):
    return (low(v), None)

def low_pass(kept, grad):
    return (grad,)

def back_keep(v):
    return (v, None)

def back_low(kept, grad):
    return (low(grad),)
low.defvjp(low_keep, low_pass)
low_back.defvjp(back_keep, back_low)

def round_both(values_in):
    return low_back(low(values_in))

def product(left, right):
    return jnp.dot(left, right, precision=HIGH, preferred_element_type=jnp.float32)

def layer_norm(values_in, gain_row, bias_row):
    centred = values_in - lax.optimization_barrier(jnp.mean(values_in, axis=-1, keepdims=True))
    scaling = lax.rsqrt(lax.optimization_barrier(jnp.mean(centred * centred, axis=-1, keepdims=True)) + EPS_NORM)
    return centred * scaling * gain_row + bias_row

def unit_features(vectors, projections):
    unit_rows = vectors * lax.rsqrt(lax.optimization_barrier(jnp.sum(vectors * vectors, axis=-1, keepdims=True)) + EPS_UNIT)
    angles = jnp.einsum('lhd,hdf->lhf', unit_rows, projections, precision=HIGH)
    return jnp.concatenate([jnp.sin(angles), jnp.cos(angles)], axis=-1) / math.sqrt(projections.shape[2])

def group_step(carried, block):
    state_now, norm_now = carried
    query_feats, key_feats, value_rows, logit_rows = block
    decay_log = jnp.cumsum(jax.nn.log_sigmoid(logit_rows), axis=0)
    inflow = jax.nn.sigmoid(-logit_rows)
    width_here = logit_rows.shape[0]
    causal = (jnp.arange(width_here)[:, None] >= jnp.arange(width_here)[None, :])[:, :, None]
    log_gap = jnp.where(causal, decay_log[:, None, :] - decay_log[None, :, :], 0.0)
    pair_weights = jnp.where(causal, jnp.exp(log_gap), 0.0) * inflow[None, :, :]
    scores = round_both(jnp.einsum('thf,shf->tsh', query_feats, key_feats, precision=HIGH) * pair_weights)
    inner_sum = jnp.einsum('tsh,shd->thd', scores, value_rows, precision=HIGH)
    lifted = query_feats * jnp.exp(decay_log)[:, :, None]
    numerator = inner_sum + jnp.einsum('thf,hfd->thd', lifted, state_now, precision=HIGH)
    denominator = lax.optimization_barrier(jnp.sum(scores, axis=1)) + jnp.einsum('thf,hf->th', lifted, norm_now, precision=HIGH)
    mixed_rows = numerator * lax.rsqrt(denominator * denominator + GUARD)[:, :, None]
    to_end = jnp.exp(decay_log[-1:, :] - decay_log) * inflow
    weighted = round_both(key_feats * to_end[:, :, None])
    total_decay = jnp.exp(decay_log[-1])
    next_state = total_decay[:, None, None] * state_now + jnp.einsum('shf,shd->hfd', weighted, value_rows, precision=HIGH)
    next_norm = total_decay[:, None] * norm_now + lax.optimization_barrier(jnp.sum(weighted, axis=0))
    return ((next_state, next_norm), mixed_rows)

def forward(params, sequence, projections):
    mixer_gain, mixer_bias, query_weight, key_weight, value_weight, gate_weight, gate_bias, output_weight, start_state, start_norm, feed_gain, feed_bias, up_weight, up_bias, down_weight, down_bias = params
    length = sequence.shape[0]
    mixer_low = low(layer_norm(sequence, mixer_gain, mixer_bias))
    query_vectors = low_back(product(mixer_low, query_weight)).reshape(length, HEADS, HD)
    key_vectors = low_back(product(mixer_low, key_weight)).reshape(length, HEADS, HD)
    value_vectors = round_both(low_back(product(mixer_low, value_weight))).reshape(length, HEADS, HD)
    logit_rows = low_back(product(mixer_low, gate_weight) + gate_bias)
    query_feats = round_both(unit_features(query_vectors, projections))
    key_feats = round_both(unit_features(key_vectors, projections))
    blocks = length // GROUP
    scanned = (query_feats.reshape(blocks, GROUP, HEADS, 2 * FEAT), key_feats.reshape(blocks, GROUP, HEADS, 2 * FEAT), value_vectors.reshape(blocks, GROUP, HEADS, HD), logit_rows.reshape(blocks, GROUP, HEADS))
    final_states, mixed_rows = lax.scan(jax.checkpoint(group_step), (start_state, start_norm), scanned)
    mixed_low = low(mixed_rows.reshape(length, D))
    middle = sequence + low_back(product(mixed_low, output_weight))
    feed_low = low(layer_norm(middle, feed_gain, feed_bias))
    hidden_pre = low_back(product(feed_low, up_weight) + up_bias)
    hidden_low = low(jax.nn.gelu(hidden_pre, approximate=False))
    return middle + low_back(product(hidden_low, down_weight.T) + down_bias)

def reference(inputs, cotangent, mixer_gain, mixer_bias, query_weight, key_weight, value_weight, gate_weight, gate_bias, output_weight, projections, start_state, start_norm, feed_gain, feed_bias, up_weight, up_bias, down_weight, down_bias):
    params = tuple((item.astype(jnp.float32) for item in (mixer_gain, mixer_bias, query_weight, key_weight, value_weight, gate_weight, gate_bias, output_weight, start_state, start_norm, feed_gain, feed_bias, up_weight, up_bias, down_weight, down_bias)))
    fixed_projections = projections.astype(jnp.float32)

    def one_row(totals, row_pair):
        sequence, row_cot = row_pair
        result, pullback = jax.vjp(lambda par, seq_in: forward(par, seq_in, fixed_projections), params, sequence.astype(jnp.float32))
        param_grads, sequence_grad = pullback(row_cot.astype(jnp.float32))
        totals = jax.tree.map(jnp.add, totals, param_grads)
        return (totals, (result.astype(jnp.bfloat16), sequence_grad))
    zeros_start = jax.tree.map(jnp.zeros_like, params)
    totals, (outputs, input_grads) = lax.scan(one_row, zeros_start, (inputs, cotangent))
    g_mixer_gain, g_mixer_bias, g_query, g_key, g_value, g_gate, g_gate_bias, g_output, g_state, g_norm, g_feed_gain, g_feed_bias, g_up, g_up_bias, g_down, g_down_bias = totals
    return (outputs, input_grads, g_mixer_gain, g_mixer_bias, g_query, g_key, g_value, g_gate, g_gate_bias, g_output, g_state, g_norm, g_feed_gain, g_feed_bias, g_up, g_up_bias, g_down, g_down_bias)
```

```python
from functools import partial
import math

import jax
import jax.numpy as jnp
from jax import lax
from jax.experimental import pallas as pl
from jax.experimental.pallas import tpu as pltpu
from jax.sharding import PartitionSpec as P

F32 = jnp.float32
BF16 = jnp.bfloat16
EPS_NORM = 1e-05
EPS_UNIT = 1e-06
GUARD = 0.0625
HIGH = lax.Precision.HIGHEST
VMEM = 56 * 1024 * 1024

C = 128
T = 256
HB = 512
LANES = 128
PAY = 80

SIN = (3.14158202, -5.16714278, 2.54189892, -0.55463591)
COS = (0.99999995, -4.93479286, 4.05841191, -1.33188012, 0.21969671)
ERF = (0.319381530, -0.356563782, 1.781477937, -1.821255978, 1.330274429)
ERF_P = 0.2316419
INV_SQRT_2PI = 0.3989422804014327


def nn(a, b):
    return lax.dot_general(a, b, (((1,), (0,)), ((), ())), preferred_element_type=F32)


def nt(a, b):
    return lax.dot_general(a, b, (((1,), (1,)), ((), ())), preferred_element_type=F32)


def tn(a, b):
    return lax.dot_general(a, b, (((0,), (0,)), ((), ())), preferred_element_type=F32)


def exact(a, b):
    return lax.dot_general(
        a, b, (((1,), (0,)), ((), ())), precision=HIGH, preferred_element_type=F32
    )


def iota(shape, dim):
    return lax.broadcasted_iota(jnp.int32, shape, dim)


def log_sigmoid(x):
    return jnp.minimum(x, 0.0) - jnp.log(1.0 + jnp.exp(-jnp.abs(x)))


def normalize(x):
    centred = x - jnp.mean(x, axis=-1, keepdims=True)
    scale = lax.rsqrt(jnp.mean(centred * centred, axis=-1, keepdims=True) + EPS_NORM)
    return centred * scale, scale


def normalize_back(grad, gain, xhat, scale):
    inner = grad * gain
    mean_inner = jnp.mean(inner, axis=-1, keepdims=True)
    mean_both = jnp.mean(inner * xhat, axis=-1, keepdims=True)
    return scale * (inner - mean_inner - xhat * mean_both)


def fold_rows(x):
    return jnp.sum(x.reshape(x.shape[0] // 8, 8, x.shape[1]), axis=0)


def block_ones():
    return jnp.where(
        iota((LANES, LANES), 0) // 64 == iota((LANES, LANES), 1) // 64, 1.0, 0.0
    ).astype(BF16)


def head_sums(x):
    high = x.astype(BF16)
    rest = (x - high.astype(F32)).astype(BF16)
    ones = block_ones()
    return nn(jnp.concatenate([high, rest], axis=1), jnp.concatenate([ones, ones], axis=0))


def lower_half(shape):
    return iota(shape, 1) < 64


def mine(h, lower):
    return lower if h % 2 == 0 else jnp.logical_not(lower)


def column(block, index, rows, width):
    return jnp.broadcast_to(block[:, index : index + 1], (rows, width))


def sin_cos(turns, scale):
    r = turns - jnp.floor(turns + 0.5)
    r2 = r * r
    s = (((SIN[3] * r2 + SIN[2]) * r2 + SIN[1]) * r2 + SIN[0]) * r
    k = 2.0 * scale
    c = (((k * COS[4] * r2 + k * COS[3]) * r2 + k * COS[2]) * r2 + k * COS[1]) * r2 + k * COS[0]
    return s * c, scale - (k * s) * s


def grow_state(payload, h):
    state = payload[h, 0:64, :]
    norm = jnp.broadcast_to(payload[h, 64:65, :].astype(F32), (64, state.shape[1]))
    state = state.astype(F32)
    return jnp.concatenate([state, norm] if h % 2 == 0 else [norm, state], axis=0)


def shrink_state(state, h):
    if h % 2 == 0:
        return state[0:PAY].astype(BF16)
    return jnp.concatenate([state[64:128], state[0 : PAY - 64]], axis=0).astype(BF16)


def features_kernel(
    heads,
    x_ref,
    gain_ref,
    bias_ref,
    wq_ref,
    wk_ref,
    wv_ref,
    wg_ref,
    wgt_ref,
    gb_ref,
    gbt_ref,
    pcat_ref,
    start_ref,
    ml_ref,
    uq_ref,
    uk_ref,
    rq_ref,
    rk_ref,
    qf_ref,
    kf_ref,
    v_ref,
    gcol_ref,
    grow_ref,
    before_ref,
    final_ref,
    total_ref,
    state,
    carry,
):
    step = pl.program_id(0)

    @pl.when(step == 0)
    def _():
        state[...] = start_ref[...]
        carry[...] = jnp.zeros_like(carry)

    xhat, _ = normalize(x_ref[...].astype(F32))
    ml = (xhat * gain_ref[...] + bias_ref[...]).astype(BF16)
    ml_ref[...] = ml
    q = nn(ml, wq_ref[...])
    k = nn(ml, wk_ref[...])
    v = nn(ml, wv_ref[...])
    v_ref[...] = v.astype(BF16)
    logit = nn(ml, wg_ref[...]) + gb_ref[...]
    keep = log_sigmoid(logit)
    gain_in = keep - logit
    tri = jnp.where(iota((C, C), 0) >= iota((C, C), 1), 1.0, 0.0)
    decay = exact(tri, keep)
    total = decay[C - 1 : C, :]
    group = iota((C, LANES), 1) // 8
    everywhere = carry[...] + decay
    coef = total - decay + gain_in
    packed = jnp.where(group == 0, decay, coef)
    packed = jnp.where(group == 2, everywhere, packed)
    packed = jnp.where(group == 3, jax.nn.sigmoid(logit), packed)
    packed = jnp.where(group == 4, gain_in - decay, packed)
    packed = jnp.where(group == 5, jax.nn.sigmoid(-logit), packed)
    packed = jnp.where(group == 6, jnp.broadcast_to(carry[...], (C, LANES)), packed)
    packed = jnp.where(group == 7, jnp.broadcast_to(total, (C, LANES)), packed)
    gcol_ref[...] = packed
    carry[...] = carry[...] + total
    total_ref[...] = jnp.broadcast_to(carry[...], total_ref.shape)
    logit_row = nt(wgt_ref[...], ml) + gbt_ref[...][:, 0:1]
    keep_row = log_sigmoid(logit_row)
    upper = jnp.where(iota((C, C), 0) <= iota((C, C), 1), 1.0, 0.0)
    decay_row = exact(keep_row, upper)
    grow_ref[...] = jnp.concatenate([keep_row - logit_row - decay_row, decay_row], axis=0)

    lower = lower_half((C, LANES))
    ftr_scale = 1.0 / math.sqrt(LANES)
    for p in range(heads // 2):
        lanes = slice(LANES * p, LANES * (p + 1))
        both = jnp.concatenate([q[:, lanes], k[:, lanes]], axis=0)
        scale = lax.rsqrt(head_sums(both * both) + EPS_UNIT)
        unit = both * scale
        high = unit.astype(BF16)
        rest = (unit - high.astype(F32)).astype(BF16)
        uq_ref[:, lanes] = high[:C]
        uk_ref[:, lanes] = high[C:]
        rq_ref[:, lanes] = scale[:C]
        rk_ref[:, lanes] = scale[C:]
        turns = nn(jnp.concatenate([high, rest, high], axis=1), pcat_ref[p])
        s, c = sin_cos(turns, ftr_scale)
        s = s.astype(BF16)
        c = c.astype(BF16)
        for j in range(2):
            h = 2 * p + j
            half = slice(LANES * j, LANES * (j + 1))
            feats = jnp.concatenate([s[:, half], c[:, half]], axis=1)
            qf_ref[:, 256 * h : 256 * (h + 1)] = feats[:C]
            kf = feats[C:]
            kf_ref[:, 256 * h : 256 * (h + 1)] = kf
            values = jnp.where(mine(h, lower), v[:, lanes], 1.0)
            weighted = (values * jnp.exp(column(coef, h, C, LANES))).astype(BF16)
            now = state[h]
            before_ref[0, h] = now.astype(BF16)
            state[h] = jnp.exp(total[:, h : h + 1]) * now + tn(weighted, kf)

    @pl.when(step == pl.num_programs(0) - 1)
    def _():
        for h in range(heads):
            final_ref[h] = shrink_state(state[h], h)


def inner_kernel(heads, qf_ref, kf_ref, v_ref, gcol_ref, grow_ref, before_ref, n_ref):
    causal = iota((C, C), 0) >= iota((C, C), 1)
    lower = lower_half((C, LANES))
    gcol = gcol_ref[...]
    for h in range(heads):
        qf = qf_ref[:, 256 * h : 256 * (h + 1)]
        kf = kf_ref[:, 256 * h : 256 * (h + 1)]
        p = h // 2
        v = v_ref[:, LANES * p : LANES * (p + 1)].astype(F32)
        values = jnp.where(mine(h, lower), v, 1.0).astype(BF16)
        decay = column(gcol, h, C, LANES)
        pairs = jnp.where(causal, jnp.exp(decay + grow_ref[h : h + 1, :]), 0.0)
        weights = (nt(qf, kf) * pairs).astype(BF16)
        n_ref[:, LANES * h : LANES * (h + 1)] = nn(weights, values) + jnp.exp(decay) * nt(
            qf, before_ref[0, h]
        )


def feed_kernel(
    heads,
    shards,
    x_ref,
    dout_ref,
    qf_ref,
    n_ref,
    gcol_ref,
    entry_ref,
    wo_ref,
    gain_ref,
    bias_ref,
    up_ref,
    upb_ref,
    down_ref,
    downb_ref,
    out_ref,
    mg_ref,
    fl_ref,
    hl_ref,
    pre_ref,
    mix_ref,
    br_ref,
    a_ref,
    final_ref,
    sums_ref,
    upbg_ref,
    adj,
    entry,
):
    step = pl.program_id(0)
    rows = x_ref.shape[0]

    @pl.when(step == 0)
    def _():
        adj[...] = jnp.zeros_like(adj)
        sums_ref[...] = jnp.zeros_like(sums_ref)
        upbg_ref[...] = jnp.zeros_like(upbg_ref)
        for h in range(heads):
            entry[h] = grow_state(entry_ref, h).astype(BF16)

    lower = lower_half((rows, LANES))
    gcol = gcol_ref[...]
    parts = []
    for p in range(heads // 2):
        both = []
        for h in (2 * p, 2 * p + 1):
            far = nt(qf_ref[:, 256 * h : 256 * (h + 1)], entry[h])
            far = far * jnp.exp(column(gcol, 16 + h, rows, LANES))
            both.append(n_ref[:, LANES * h : LANES * (h + 1)] + far)
        num = jnp.where(lower, both[0], both[1])
        den = pltpu.roll(jnp.where(lower, both[1], both[0]), 64, 1)
        inv = lax.rsqrt(den * den + GUARD)
        parts.append((num, den, inv))
    mixed = jnp.concatenate([num * inv for num, den, inv in parts], axis=1).astype(BF16)
    mix_ref[...] = mixed
    middle = x_ref[...].astype(F32) + nn(mixed, wo_ref[...])
    xhat, scale = normalize(middle)
    gain = gain_ref[...]
    feed_low = (xhat * gain + bias_ref[...]).astype(BF16)
    fl_ref[...] = feed_low
    dout_low = dout_ref[...]
    dout = dout_low.astype(F32)
    out = middle + downb_ref[...]
    feed_grad = jnp.zeros_like(middle)
    width = up_ref.shape[2]
    block = min(HB, width)
    for s in range(shards):
        for b in range(width // block):
            cols = slice(block * b, block * (b + 1))
            place = slice(width * s + block * b, width * s + block * (b + 1))
            up = up_ref[s, :, cols]
            down = down_ref[s, :, cols]
            pre = nn(feed_low, up) + upb_ref[:, place]
            t = 1.0 / (1.0 + ERF_P * jnp.abs(pre))
            bell = INV_SQRT_2PI * jnp.exp(-0.5 * pre * pre)
            tail = ((((ERF[4] * t + ERF[3]) * t + ERF[2]) * t + ERF[1]) * t + ERF[0]) * t * bell
            phi = jnp.where(pre >= 0.0, 1.0 - tail, tail)
            hidden = (pre * phi).astype(BF16)
            hl_ref[:, place] = hidden
            out = out + nt(hidden, down)
            pre_grad = nn(dout_low, down) * (phi + pre * bell)
            pre_low = pre_grad.astype(BF16)
            pre_ref[:, place] = pre_low
            upbg_ref[:, place] += fold_rows(pre_low.astype(F32))
            feed_grad = feed_grad + nt(pre_low, up)
    out_ref[...] = out.astype(BF16)
    sums_ref[0:8, :] += fold_rows(feed_grad * xhat)
    sums_ref[8:16, :] += fold_rows(feed_grad)
    sums_ref[16:24, :] += fold_rows(dout)
    middle_grad = dout + normalize_back(feed_grad, gain, xhat, scale)
    mg_ref[...] = middle_grad
    branch = middle_grad.astype(BF16)
    br_ref[...] = branch
    mixed_grad = nt(branch, wo_ref[...])
    for p in range(heads // 2):
        num, den, inv = parts[p]
        mg = mixed_grad[:, LANES * p : LANES * (p + 1)]
        a = mg * inv
        b = head_sums(mg * num) * den * (inv * inv * inv) * (-1.0 / 64)
        b = pltpu.roll(b, 64, 1)
        for h in (2 * p, 2 * p + 1):
            a_low = jnp.where(mine(h, lower), a, b)
            a_ref[:, LANES * h : LANES * (h + 1)] = a_low.astype(BF16)
            lifted = (a_low * jnp.exp(column(gcol, 16 + h, rows, LANES))).astype(BF16)
            adj[h] += tn(lifted, qf_ref[:, 256 * h : 256 * (h + 1)])

    @pl.when(step == pl.num_programs(0) - 1)
    def _():
        for h in range(heads):
            final_ref[h] = shrink_state(adj[h], h)


def back_kernel(
    heads,
    x_ref,
    mg_ref,
    ml_ref,
    uq_ref,
    uk_ref,
    rq_ref,
    rk_ref,
    qf_ref,
    kf_ref,
    v_ref,
    a_ref,
    gcol_ref,
    grow_ref,
    before_ref,
    entry_ref,
    after_ref,
    gain_ref,
    wq_ref,
    wk_ref,
    wv_ref,
    wgt_ref,
    pcat_ref,
    dx_ref,
    dwq_ref,
    dwk_ref,
    dwv_ref,
    dwg_ref,
    adj_ref,
    sums_ref,
):
    step = pl.program_id(0)

    @pl.when(step == 0)
    def _():
        for h in range(heads):
            adj_ref[h] = grow_state(after_ref, h)
        for ref in (dwq_ref, dwk_ref, dwv_ref, dwg_ref, sums_ref):
            ref[...] = jnp.zeros_like(ref)

    row = iota((C, C), 0)
    col = iota((C, C), 1)
    causal = row >= col
    strict = row > col
    from_here = jnp.where(row <= col, 1.0, 0.0).astype(BF16)
    until_here = jnp.where(strict, 1.0, 0.0).astype(BF16)
    both_sums = jnp.concatenate([from_here, until_here], axis=1)
    lower = lower_half((C, LANES))
    gcol = gcol_ref[...]
    grads = {"q": [], "k": [], "v": []}
    logit_parts = []
    for p in range(heads // 2):
        lanes = slice(LANES * p, LANES * (p + 1))
        angle_q, angle_k, dvs = [], [], []
        v_pair = v_ref[:, lanes].astype(F32)
        for h in (2 * p, 2 * p + 1):
            qf = qf_ref[:, 256 * h : 256 * (h + 1)]
            kf = kf_ref[:, 256 * h : 256 * (h + 1)]
            values = jnp.where(mine(h, lower), v_pair, 1.0)
            values_low = values.astype(BF16)
            a_low = a_ref[:, LANES * h : LANES * (h + 1)]
            a = a_low.astype(F32)
            decay = column(gcol, h, C, LANES)
            lift = jnp.exp(decay)
            coef = jnp.exp(column(gcol, 8 + h, C, LANES))
            carried = jnp.exp(gcol[0:1, 48 + h : 49 + h])
            total = jnp.exp(gcol[0:1, 56 + h : 57 + h])
            entry = grow_state(entry_ref, h)
            before = before_ref[0, h].astype(F32) + carried * entry
            before_low = before.astype(BF16)
            adj = adj_ref[h]
            adj_low = adj.astype(BF16)
            pairs = jnp.where(causal, jnp.exp(decay + grow_ref[h : h + 1, :]), 0.0)
            raw = nt(qf, kf)
            weights = (raw * pairs).astype(BF16)
            dweights = nt(a_low, values_low).astype(BF16).astype(F32)
            draw = dweights * pairs
            draw_low = draw.astype(BF16)
            both = (raw * draw).astype(BF16)
            a_lift = (a * lift).astype(BF16)
            v_coef = (values * coef).astype(BF16)
            dq = nn(
                jnp.concatenate([draw_low, a_lift], axis=1),
                jnp.concatenate([kf, before_low], axis=0),
            )
            dk = tn(draw_low, qf) + nn(v_coef, adj_low)
            dv_far = coef * nt(kf, adj_low)
            dv = tn(weights, a_low) + dv_far
            n_far = lift * nt(qf, before_low)
            near = jnp.concatenate([a * n_far, values * dv_far], axis=0).astype(BF16)
            through = jnp.sum(total * adj * before, axis=0, keepdims=True)
            through = through[:, :LANES] + through[:, LANES:]
            flow = nn(both_sums, near) + jnp.where(strict, nn(from_here, both), 0.0) + through
            stay = column(gcol, 24 + h, C, LANES)
            leave = column(gcol, 40 + h, C, LANES)
            logit_parts.append((leave * flow - stay * (values * dv)).astype(BF16))
            adj_ref[h] = total * adj + tn(a_lift, qf)
            for feats, grad, angle in ((qf, dq, angle_q), (kf, dk, angle_k)):
                f = feats.astype(F32)
                angle.append(grad[:, :LANES] * f[:, LANES:] - grad[:, LANES:] * f[:, :LANES])
            dvs.append(dv)
        proj = pcat_ref[p, 0:LANES, :]
        for name, angle, u_ref, r_ref in (
            ("q", angle_q, uq_ref, rq_ref),
            ("k", angle_k, uk_ref, rk_ref),
        ):
            du = nt(jnp.concatenate(angle, axis=1).astype(BF16), proj)
            u = u_ref[:, lanes].astype(F32)
            along = nn((u * du).astype(BF16), block_ones())
            grads[name].append((2.0 * math.pi) * r_ref[:, lanes] * (du - u * along))
        grads["v"].append(jnp.where(lower, dvs[0], dvs[1]))
    dq, dk, dv = (jnp.concatenate(grads[name], axis=1).astype(BF16) for name in "qkv")
    select = jnp.where(
        iota((LANES * heads, LANES), 0) // LANES == iota((LANES * heads, LANES), 1), 1.0, 0.0
    ).astype(BF16)
    dlogit = nn(jnp.concatenate(logit_parts, axis=1), select).astype(BF16)
    ml = ml_ref[...]
    dwq_ref[...] += tn(ml, dq)
    dwk_ref[...] += tn(ml, dk)
    dwv_ref[...] += tn(ml, dv)
    dwg_ref[...] += tn(ml, dlogit)
    mixer_grad = (
        nt(dq, wq_ref[...])
        + nt(dk, wk_ref[...])
        + nt(dv, wv_ref[...])
        + nn(dlogit, wgt_ref[...])
    )
    xhat, scale = normalize(x_ref[...].astype(F32))
    sums_ref[0:8, :] += fold_rows(mixer_grad * xhat)
    sums_ref[8:16, :] += fold_rows(mixer_grad)
    sums_ref[16:24, 0:LANES] += fold_rows(dlogit.astype(F32))
    dx_ref[...] = mg_ref[...] + normalize_back(mixer_grad, gain_ref[...], xhat, scale)


def whole(shape):
    zeros = (0,) * len(shape)
    return pl.BlockSpec(shape, lambda i: zeros)


def call(kernel, steps, ins, outs, scratch, name):
    in_specs = [
        whole(array.shape) if block is None else pl.BlockSpec(block, index)
        for array, block, index in ins
    ]
    out_specs = [
        whole(shape) if block is None else pl.BlockSpec(block, index)
        for shape, dtype, block, index in outs
    ]
    return pl.pallas_call(
        kernel,
        grid=(steps,),
        in_specs=in_specs,
        out_specs=out_specs,
        out_shape=[jax.ShapeDtypeStruct(shape, dtype) for shape, dtype, _, _ in outs],
        scratch_shapes=scratch,
        compiler_params=pltpu.CompilerParams(
            dimension_semantics=("arbitrary",), vmem_limit_bytes=VMEM
        ),
        name=name,
    )(*[array for array, _, _ in ins])


def carry_over(payload, logs, forward):
    n, index = lax.axis_size("seq"), lax.axis_index("seq")
    if n == 2:
        return lax.ppermute(payload, "seq", [(0, 1)] if forward else [(1, 0)])
    everything = lax.all_gather(payload, "seq")
    every_log = lax.all_gather(logs, "seq")
    total = jnp.zeros(payload.shape, F32)
    for k in range(n) if forward else reversed(range(n)):
        ahead = (k < index) if forward else (k > index)
        new = jnp.exp(every_log[k])[:, None, None] * total + everything[k].astype(F32)
        total = jnp.where(ahead, new, total)
    return total.astype(BF16)


def local(
    inputs,
    cotangent,
    mixer_gain,
    mixer_bias,
    query_weight,
    key_weight,
    value_weight,
    gate_weight,
    gate_bias,
    output_weight,
    projections,
    start_state,
    start_norm,
    feed_gain,
    feed_bias,
    up_weight,
    up_bias,
    down_weight,
    down_bias,
):
    _, tokens, width = inputs.shape
    heads, size, feats = projections.shape
    chunks = tokens // C
    tile = min(T, tokens)
    tiles = tokens // tile
    shards = lax.axis_size("seq")
    first = lax.axis_index("seq") == 0
    x = inputs.reshape(tokens, width)
    dout = cotangent.reshape(tokens, width)

    every_up = lax.all_gather(up_weight, "seq")
    every_down = lax.all_gather(down_weight, "seq")
    every_upb = lax.all_gather(up_bias.astype(F32), "seq").reshape(1, -1)
    hidden = every_upb.shape[1]

    turns = projections * (1.0 / (2.0 * math.pi))
    high = lax.reduce_precision(turns, 8, 7)
    rest = turns - high
    zeros = jnp.zeros_like(turns)

    def pair_blocks(part):
        left = jnp.concatenate([part[0::2], zeros[0::2]], axis=2)
        right = jnp.concatenate([zeros[0::2], part[1::2]], axis=2)
        return jnp.concatenate([left, right], axis=1)

    pcat = jnp.concatenate(
        [pair_blocks(high), pair_blocks(high), pair_blocks(rest)], axis=1
    ).astype(BF16)
    wg = jnp.tile(gate_weight, (1, LANES // heads))
    wgt = gate_weight.T
    gb = jnp.tile(gate_bias, LANES // heads)[None]
    gbt = jnp.broadcast_to(gate_bias[:, None], (heads, LANES))
    start_rows = start_state.transpose(0, 2, 1)
    norm_rows = jnp.broadcast_to(start_norm[:, None, :], start_rows.shape)
    even = (jnp.arange(heads) % 2 == 0)[:, None, None]
    start = jnp.concatenate(
        [jnp.where(even, start_rows, norm_rows), jnp.where(even, norm_rows, start_rows)], axis=1
    )
    start = jnp.where(first, start, 0.0)

    def rows(n, block_rows=C):
        return (block_rows, n), lambda i: (i, 0)

    def out_rows(n, dtype, block_rows=C):
        return ((tokens, n), dtype) + rows(n, block_rows)

    def const(array):
        return (array if array.ndim > 1 else array[None], None, None)

    def keep(shape, dtype):
        return (shape, dtype, None, None)

    wide = heads * LANES
    wider = heads * 2 * feats
    ml, uq, uk, rq, rk, qf, kf, v, gcol, grow, before, final, total = call(
        partial(features_kernel, heads),
        chunks,
        [
            (x,) + rows(width),
            const(mixer_gain),
            const(mixer_bias),
            const(query_weight),
            const(key_weight),
            const(value_weight),
            const(wg),
            const(wgt),
            const(gb),
            const(gbt),
            const(pcat),
            const(start),
        ],
        [
            out_rows(width, BF16),
            out_rows(width, BF16),
            out_rows(width, BF16),
            out_rows(width, F32),
            out_rows(width, F32),
            out_rows(wider, BF16),
            out_rows(wider, BF16),
            out_rows(width, BF16),
            out_rows(LANES, F32),
            ((2 * heads, tokens), F32, (2 * heads, C), lambda i: (0, i)),
            (
                (chunks, heads, LANES, 2 * feats),
                BF16,
                (1, heads, LANES, 2 * feats),
                lambda i: (i, 0, 0, 0),
            ),
            keep((heads, PAY, 2 * feats), BF16),
            keep((8, LANES), F32),
        ],
        [pltpu.VMEM((heads, LANES, 2 * feats), F32), pltpu.VMEM((1, LANES), F32)],
        "features",
    )
    logs = total[0, :heads]
    entry = carry_over(final, logs, True)
    state_block = (1, heads, LANES, 2 * feats)
    (num,) = call(
        partial(inner_kernel, heads),
        chunks,
        [
            (qf,) + rows(wider),
            (kf,) + rows(wider),
            (v,) + rows(width),
            (gcol,) + rows(LANES),
            (grow, (2 * heads, C), lambda i: (0, i)),
            (before, state_block, lambda i: (i, 0, 0, 0)),
        ],
        [out_rows(wide, F32)],
        [],
        "inner",
    )
    out, mg, fl, hl, pre, mix, br, a, adj_final, feed_sums, upbg = call(
        partial(feed_kernel, heads, shards),
        tiles,
        [
            (x,) + rows(width, tile),
            (dout,) + rows(width, tile),
            (qf,) + rows(wider, tile),
            (num,) + rows(wide, tile),
            (gcol,) + rows(LANES, tile),
            const(entry),
            const(output_weight),
            const(feed_gain),
            const(feed_bias),
            const(every_up),
            const(every_upb),
            const(every_down),
            const(down_bias),
        ],
        [
            out_rows(width, BF16, tile),
            out_rows(width, F32, tile),
            out_rows(width, BF16, tile),
            out_rows(hidden, BF16, tile),
            out_rows(hidden, BF16, tile),
            out_rows(width, BF16, tile),
            out_rows(width, BF16, tile),
            out_rows(wide, BF16, tile),
            keep((heads, PAY, 2 * feats), BF16),
            keep((24, width), F32),
            keep((8, hidden), F32),
        ],
        [
            pltpu.VMEM((heads, LANES, 2 * feats), F32),
            pltpu.VMEM((heads, LANES, 2 * feats), BF16),
        ],
        "feed",
    )
    after = carry_over(adj_final, logs, False)
    down_grad = tn(dout, hl).astype(BF16)
    up_grad = tn(fl, pre).astype(BF16)
    output_grad = tn(mix, br).astype(BF16)

    def back_rows(n):
        return (C, n), lambda i: (chunks - 1 - i, 0)

    dx, dwq, dwk, dwv, dwg, adj, mixer_sums = call(
        partial(back_kernel, heads),
        chunks,
        [
            (x,) + back_rows(width),
            (mg,) + back_rows(width),
            (ml,) + back_rows(width),
            (uq,) + back_rows(width),
            (uk,) + back_rows(width),
            (rq,) + back_rows(width),
            (rk,) + back_rows(width),
            (qf,) + back_rows(wider),
            (kf,) + back_rows(wider),
            (v,) + back_rows(width),
            (a,) + back_rows(wide),
            (gcol,) + back_rows(LANES),
            (grow, (2 * heads, C), lambda i: (0, chunks - 1 - i)),
            (before, state_block, lambda i: (chunks - 1 - i, 0, 0, 0)),
            const(entry),
            const(after),
            const(mixer_gain),
            const(query_weight),
            const(key_weight),
            const(value_weight),
            const(jnp.pad(wgt, ((0, LANES - heads), (0, 0)))),
            const(pcat),
        ],
        [
            ((tokens, width), F32) + back_rows(width),
            keep((width, width), F32),
            keep((width, width), F32),
            keep((width, width), F32),
            keep((width, LANES), F32),
            keep((heads, LANES, 2 * feats), F32),
            keep((24, width), F32),
        ],
        [],
        "back",
    )
    adj = jnp.where(first, adj, 0.0)
    state_grad = jnp.where(even, adj[:, :64], adj[:, 64:])
    norm_grad = jnp.sum(jnp.where(even, adj[:, 64:], adj[:, :64]), axis=1)

    up_half = lax.psum_scatter(
        jnp.stack([up_grad, down_grad]), "seq", scatter_dimension=2, tiled=True
    )
    upb_half = lax.psum_scatter(jnp.sum(upbg, axis=0), "seq", scatter_dimension=0, tiled=True)
    sum_up_down, sum_upb = lax.psum((up_half, upb_half), "dp")
    sum_up, sum_down = (part.astype(F32) for part in sum_up_down)
    wide_sums = lax.psum(
        (
            dwq.astype(BF16),
            dwk.astype(BF16),
            dwv.astype(BF16),
            output_grad,
            state_grad.astype(BF16),
        ),
        ("dp", "seq"),
    )
    sum_q, sum_k, sum_v, sum_o, sum_state = (part.astype(F32) for part in wide_sums)
    feed_three = jnp.sum(feed_sums.reshape(3, 8, width), axis=1)
    mixer_three = jnp.sum(mixer_sums.reshape(3, 8, width), axis=1)
    sum_g, sum_norm, sum_feed, sum_mixer = lax.psum(
        (dwg[:, :heads], norm_grad, feed_three, mixer_three), ("dp", "seq")
    )
    return (
        out.reshape(inputs.shape),
        dx.reshape(inputs.shape),
        sum_mixer[0],
        sum_mixer[1],
        sum_q,
        sum_k,
        sum_v,
        sum_g,
        sum_mixer[2, :heads],
        sum_o,
        sum_state.transpose(0, 2, 1),
        sum_norm,
        sum_feed[0],
        sum_feed[1],
        sum_up,
        sum_upb,
        sum_down,
        sum_feed[2],
    )


def solution(mesh):
    tokens = P("dp", "seq", None)
    columns = P(None, "seq")
    return jax.shard_map(
        local,
        mesh=mesh,
        in_specs=(tokens, tokens) + (P(),) * 13 + (columns, P("seq"), columns, P()),
        out_specs=(tokens, tokens) + (P(),) * 12 + (columns, P("seq"), columns, P()),
        check_vma=False,
    )
```

```python
from functools import partial
import math

import jax
import jax.numpy as jnp
from jax import lax
from jax.experimental import pallas as pl
from jax.experimental.pallas import tpu as pltpu
from jax.sharding import PartitionSpec as P

F32 = jnp.float32
BF16 = jnp.bfloat16
EPS_NORM = 1e-05
EPS_UNIT = 1e-06
GUARD = 0.0625
MESH = pl.DeviceIdType.MESH
HIGH = lax.Precision.HIGHEST
VMEM = 56 * 1024 * 1024

C = 128
T = 256
HB = 512
LANES = 128
PAY = 80

SIN = (3.14158202, -5.16714278, 2.54189892, -0.55463591)
COS = (0.99999995, -4.93479286, 4.05841191, -1.33188012, 0.21969671)
ERF = (0.319381530, -0.356563782, 1.781477937, -1.821255978, 1.330274429)
ERF_P = 0.2316419
INV_SQRT_2PI = 0.3989422804014327


def nn(a, b):
    return lax.dot_general(a, b, (((1,), (0,)), ((), ())), preferred_element_type=F32)


def nt(a, b):
    return lax.dot_general(a, b, (((1,), (1,)), ((), ())), preferred_element_type=F32)


def tn(a, b):
    return lax.dot_general(a, b, (((0,), (0,)), ((), ())), preferred_element_type=F32)


def exact(a, b):
    return lax.dot_general(
        a, b, (((1,), (0,)), ((), ())), precision=HIGH, preferred_element_type=F32
    )


def iota(shape, dim):
    return lax.broadcasted_iota(jnp.int32, shape, dim)


def log_sigmoid(x):
    return jnp.minimum(x, 0.0) - jnp.log(1.0 + jnp.exp(-jnp.abs(x)))


def normalize(x):
    centred = x - jnp.mean(x, axis=-1, keepdims=True)
    scale = lax.rsqrt(jnp.mean(centred * centred, axis=-1, keepdims=True) + EPS_NORM)
    return centred * scale, scale


def normalize_back(grad, gain, xhat, scale):
    inner = grad * gain
    mean_inner = jnp.mean(inner, axis=-1, keepdims=True)
    mean_both = jnp.mean(inner * xhat, axis=-1, keepdims=True)
    return scale * (inner - mean_inner - xhat * mean_both)


def fold_rows(x):
    return jnp.sum(x.reshape(x.shape[0] // 8, 8, x.shape[1]), axis=0)


def block_ones():
    return jnp.where(
        iota((LANES, LANES), 0) // 64 == iota((LANES, LANES), 1) // 64, 1.0, 0.0
    ).astype(BF16)


def head_sums(x):
    high = x.astype(BF16)
    rest = (x - high.astype(F32)).astype(BF16)
    ones = block_ones()
    return nn(jnp.concatenate([high, rest], axis=1), jnp.concatenate([ones, ones], axis=0))


def lower_half(shape):
    return iota(shape, 1) < 64


def mine(h, lower):
    return lower if h % 2 == 0 else jnp.logical_not(lower)


def column(block, index, rows, width):
    return jnp.broadcast_to(block[:, index : index + 1], (rows, width))


def sin_cos(turns, scale):
    r = turns - jnp.floor(turns + 0.5)
    r2 = r * r
    s = (((SIN[3] * r2 + SIN[2]) * r2 + SIN[1]) * r2 + SIN[0]) * r
    k = 2.0 * scale
    c = (((k * COS[4] * r2 + k * COS[3]) * r2 + k * COS[2]) * r2 + k * COS[1]) * r2 + k * COS[0]
    return s * c, scale - (k * s) * s


def grow_state(payload, h):
    state = payload[h, 0:64, :]
    norm = jnp.broadcast_to(payload[h, 64:65, :].astype(F32), (64, state.shape[1]))
    state = state.astype(F32)
    return jnp.concatenate([state, norm] if h % 2 == 0 else [norm, state], axis=0)


def shrink_state(state, h):
    if h % 2 == 0:
        return state[0:PAY].astype(BF16)
    return jnp.concatenate([state[64:128], state[0 : PAY - 64]], axis=0).astype(BF16)


def features_kernel(
    heads,
    x_ref,
    gain_ref,
    bias_ref,
    wq_ref,
    wk_ref,
    wv_ref,
    wg_ref,
    wgt_ref,
    gb_ref,
    gbt_ref,
    pcat_ref,
    start_ref,
    ml_ref,
    uq_ref,
    uk_ref,
    rq_ref,
    rk_ref,
    qf_ref,
    kf_ref,
    v_ref,
    gcol_ref,
    grow_ref,
    before_ref,
    final_ref,
    total_ref,
    state,
    carry,
):
    step = pl.program_id(0)

    @pl.when(step == 0)
    def _():
        state[...] = start_ref[...]
        carry[...] = jnp.zeros_like(carry)

    xhat, _ = normalize(x_ref[...].astype(F32))
    ml = (xhat * gain_ref[...] + bias_ref[...]).astype(BF16)
    ml_ref[...] = ml
    q = nn(ml, wq_ref[...])
    k = nn(ml, wk_ref[...])
    v = nn(ml, wv_ref[...])
    v_ref[...] = v.astype(BF16)
    logit = nn(ml, wg_ref[...]) + gb_ref[...]
    keep = log_sigmoid(logit)
    gain_in = keep - logit
    tri = jnp.where(iota((C, C), 0) >= iota((C, C), 1), 1.0, 0.0)
    decay = exact(tri, keep)
    total = decay[C - 1 : C, :]
    group = iota((C, LANES), 1) // 8
    everywhere = carry[...] + decay
    coef = total - decay + gain_in
    packed = jnp.where(group == 0, decay, coef)
    packed = jnp.where(group == 2, everywhere, packed)
    packed = jnp.where(group == 3, jax.nn.sigmoid(logit), packed)
    packed = jnp.where(group == 4, gain_in - decay, packed)
    packed = jnp.where(group == 5, jax.nn.sigmoid(-logit), packed)
    packed = jnp.where(group == 6, jnp.broadcast_to(carry[...], (C, LANES)), packed)
    packed = jnp.where(group == 7, jnp.broadcast_to(total, (C, LANES)), packed)
    gcol_ref[...] = packed
    carry[...] = carry[...] + total
    total_ref[...] = jnp.broadcast_to(carry[...], total_ref.shape)
    logit_row = nt(wgt_ref[...], ml) + gbt_ref[...][:, 0:1]
    keep_row = log_sigmoid(logit_row)
    upper = jnp.where(iota((C, C), 0) <= iota((C, C), 1), 1.0, 0.0)
    decay_row = exact(keep_row, upper)
    grow_ref[...] = jnp.concatenate([keep_row - logit_row - decay_row, decay_row], axis=0)

    lower = lower_half((C, LANES))
    ftr_scale = 1.0 / math.sqrt(LANES)
    for p in range(heads // 2):
        lanes = slice(LANES * p, LANES * (p + 1))
        both = jnp.concatenate([q[:, lanes], k[:, lanes]], axis=0)
        scale = lax.rsqrt(head_sums(both * both) + EPS_UNIT)
        unit = both * scale
        high = unit.astype(BF16)
        rest = (unit - high.astype(F32)).astype(BF16)
        uq_ref[:, lanes] = high[:C]
        uk_ref[:, lanes] = high[C:]
        rq_ref[:, lanes] = scale[:C]
        rk_ref[:, lanes] = scale[C:]
        turns = nn(jnp.concatenate([high, rest, high], axis=1), pcat_ref[p])
        s, c = sin_cos(turns, ftr_scale)
        s = s.astype(BF16)
        c = c.astype(BF16)
        for j in range(2):
            h = 2 * p + j
            half = slice(LANES * j, LANES * (j + 1))
            feats = jnp.concatenate([s[:, half], c[:, half]], axis=1)
            qf_ref[:, 256 * h : 256 * (h + 1)] = feats[:C]
            kf = feats[C:]
            kf_ref[:, 256 * h : 256 * (h + 1)] = kf
            values = jnp.where(mine(h, lower), v[:, lanes], 1.0)
            weighted = (values * jnp.exp(column(coef, h, C, LANES))).astype(BF16)
            now = state[h]
            before_ref[0, h] = now.astype(BF16)
            state[h] = jnp.exp(total[:, h : h + 1]) * now + tn(weighted, kf)

    @pl.when(step == pl.num_programs(0) - 1)
    def _():
        for h in range(heads):
            final_ref[h] = shrink_state(state[h], h)


def inner_kernel(heads, qf_ref, kf_ref, v_ref, gcol_ref, grow_ref, before_ref, n_ref):
    causal = iota((C, C), 0) >= iota((C, C), 1)
    lower = lower_half((C, LANES))
    gcol = gcol_ref[...]
    for h in range(heads):
        qf = qf_ref[:, 256 * h : 256 * (h + 1)]
        kf = kf_ref[:, 256 * h : 256 * (h + 1)]
        p = h // 2
        v = v_ref[:, LANES * p : LANES * (p + 1)].astype(F32)
        values = jnp.where(mine(h, lower), v, 1.0).astype(BF16)
        decay = column(gcol, h, C, LANES)
        pairs = jnp.where(causal, jnp.exp(decay + grow_ref[h : h + 1, :]), 0.0)
        weights = (nt(qf, kf) * pairs).astype(BF16)
        n_ref[:, LANES * h : LANES * (h + 1)] = nn(weights, values) + jnp.exp(decay) * nt(
            qf, before_ref[0, h]
        )


def feed_kernel(
    heads,
    shards,
    x_ref,
    dout_ref,
    qf_ref,
    n_ref,
    gcol_ref,
    entry_ref,
    wo_ref,
    gain_ref,
    bias_ref,
    up_ref,
    upb_ref,
    down_ref,
    downb_ref,
    out_ref,
    mg_ref,
    fl_ref,
    hl_ref,
    pre_ref,
    mix_ref,
    br_ref,
    a_ref,
    final_ref,
    sums_ref,
    upbg_ref,
    adj,
    entry,
):
    step = pl.program_id(0)
    rows = x_ref.shape[0]

    @pl.when(step == 0)
    def _():
        adj[...] = jnp.zeros_like(adj)
        sums_ref[...] = jnp.zeros_like(sums_ref)
        upbg_ref[...] = jnp.zeros_like(upbg_ref)
        for h in range(heads):
            entry[h] = grow_state(entry_ref, h).astype(BF16)

    lower = lower_half((rows, LANES))
    gcol = gcol_ref[...]
    parts = []
    for p in range(heads // 2):
        both = []
        for h in (2 * p, 2 * p + 1):
            far = nt(qf_ref[:, 256 * h : 256 * (h + 1)], entry[h])
            far = far * jnp.exp(column(gcol, 16 + h, rows, LANES))
            both.append(n_ref[:, LANES * h : LANES * (h + 1)] + far)
        num = jnp.where(lower, both[0], both[1])
        den = pltpu.roll(jnp.where(lower, both[1], both[0]), 64, 1)
        inv = lax.rsqrt(den * den + GUARD)
        parts.append((num, den, inv))
    mixed = jnp.concatenate([num * inv for num, den, inv in parts], axis=1).astype(BF16)
    mix_ref[...] = mixed
    middle = x_ref[...].astype(F32) + nn(mixed, wo_ref[...])
    xhat, scale = normalize(middle)
    gain = gain_ref[...]
    feed_low = (xhat * gain + bias_ref[...]).astype(BF16)
    fl_ref[...] = feed_low
    dout_low = dout_ref[...]
    dout = dout_low.astype(F32)
    out = middle + downb_ref[...]
    feed_grad = jnp.zeros_like(middle)
    width = up_ref.shape[2]
    block = min(HB, width)
    for s in range(shards):
        for b in range(width // block):
            cols = slice(block * b, block * (b + 1))
            place = slice(width * s + block * b, width * s + block * (b + 1))
            up = up_ref[s, :, cols]
            down = down_ref[s, :, cols]
            pre = nn(feed_low, up) + upb_ref[:, place]
            t = 1.0 / (1.0 + ERF_P * jnp.abs(pre))
            bell = INV_SQRT_2PI * jnp.exp(-0.5 * pre * pre)
            tail = ((((ERF[4] * t + ERF[3]) * t + ERF[2]) * t + ERF[1]) * t + ERF[0]) * t * bell
            phi = jnp.where(pre >= 0.0, 1.0 - tail, tail)
            hidden = (pre * phi).astype(BF16)
            hl_ref[:, place] = hidden
            out = out + nt(hidden, down)
            pre_grad = nn(dout_low, down) * (phi + pre * bell)
            pre_low = pre_grad.astype(BF16)
            pre_ref[:, place] = pre_low
            upbg_ref[:, place] += fold_rows(pre_low.astype(F32))
            feed_grad = feed_grad + nt(pre_low, up)
    out_ref[...] = out.astype(BF16)
    sums_ref[0:8, :] += fold_rows(feed_grad * xhat)
    sums_ref[8:16, :] += fold_rows(feed_grad)
    sums_ref[16:24, :] += fold_rows(dout)
    middle_grad = dout + normalize_back(feed_grad, gain, xhat, scale)
    mg_ref[...] = middle_grad
    branch = middle_grad.astype(BF16)
    br_ref[...] = branch
    mixed_grad = nt(branch, wo_ref[...])
    for p in range(heads // 2):
        num, den, inv = parts[p]
        mg = mixed_grad[:, LANES * p : LANES * (p + 1)]
        a = mg * inv
        b = head_sums(mg * num) * den * (inv * inv * inv) * (-1.0 / 64)
        b = pltpu.roll(b, 64, 1)
        for h in (2 * p, 2 * p + 1):
            a_low = jnp.where(mine(h, lower), a, b)
            a_ref[:, LANES * h : LANES * (h + 1)] = a_low.astype(BF16)
            lifted = (a_low * jnp.exp(column(gcol, 16 + h, rows, LANES))).astype(BF16)
            adj[h] += tn(lifted, qf_ref[:, 256 * h : 256 * (h + 1)])

    @pl.when(step == pl.num_programs(0) - 1)
    def _():
        for h in range(heads):
            final_ref[h] = shrink_state(adj[h], h)


def back_kernel(
    heads,
    x_ref,
    mg_ref,
    ml_ref,
    uq_ref,
    uk_ref,
    rq_ref,
    rk_ref,
    qf_ref,
    kf_ref,
    v_ref,
    a_ref,
    gcol_ref,
    grow_ref,
    before_ref,
    entry_ref,
    after_ref,
    gain_ref,
    wq_ref,
    wk_ref,
    wv_ref,
    wgt_ref,
    pcat_ref,
    dx_ref,
    dwq_ref,
    dwk_ref,
    dwv_ref,
    dwg_ref,
    adj_ref,
    sums_ref,
):
    step = pl.program_id(0)

    @pl.when(step == 0)
    def _():
        for h in range(heads):
            adj_ref[h] = grow_state(after_ref, h)
        for ref in (dwq_ref, dwk_ref, dwv_ref, dwg_ref, sums_ref):
            ref[...] = jnp.zeros_like(ref)

    row = iota((C, C), 0)
    col = iota((C, C), 1)
    causal = row >= col
    strict = row > col
    from_here = jnp.where(row <= col, 1.0, 0.0).astype(BF16)
    until_here = jnp.where(strict, 1.0, 0.0).astype(BF16)
    both_sums = jnp.concatenate([from_here, until_here], axis=1)
    lower = lower_half((C, LANES))
    gcol = gcol_ref[...]
    grads = {"q": [], "k": [], "v": []}
    logit_parts = []
    for p in range(heads // 2):
        lanes = slice(LANES * p, LANES * (p + 1))
        angle_q, angle_k, dvs = [], [], []
        v_pair = v_ref[:, lanes].astype(F32)
        for h in (2 * p, 2 * p + 1):
            qf = qf_ref[:, 256 * h : 256 * (h + 1)]
            kf = kf_ref[:, 256 * h : 256 * (h + 1)]
            values = jnp.where(mine(h, lower), v_pair, 1.0)
            values_low = values.astype(BF16)
            a_low = a_ref[:, LANES * h : LANES * (h + 1)]
            a = a_low.astype(F32)
            decay = column(gcol, h, C, LANES)
            lift = jnp.exp(decay)
            coef = jnp.exp(column(gcol, 8 + h, C, LANES))
            carried = jnp.exp(gcol[0:1, 48 + h : 49 + h])
            total = jnp.exp(gcol[0:1, 56 + h : 57 + h])
            entry = grow_state(entry_ref, h)
            before = before_ref[0, h].astype(F32) + carried * entry
            before_low = before.astype(BF16)
            adj = adj_ref[h]
            adj_low = adj.astype(BF16)
            pairs = jnp.where(causal, jnp.exp(decay + grow_ref[h : h + 1, :]), 0.0)
            raw = nt(qf, kf)
            weights = (raw * pairs).astype(BF16)
            dweights = nt(a_low, values_low).astype(BF16).astype(F32)
            draw = dweights * pairs
            draw_low = draw.astype(BF16)
            both = (raw * draw).astype(BF16)
            a_lift = (a * lift).astype(BF16)
            v_coef = (values * coef).astype(BF16)
            dq = nn(
                jnp.concatenate([draw_low, a_lift], axis=1),
                jnp.concatenate([kf, before_low], axis=0),
            )
            dk = tn(draw_low, qf) + nn(v_coef, adj_low)
            dv_far = coef * nt(kf, adj_low)
            dv = tn(weights, a_low) + dv_far
            n_far = lift * nt(qf, before_low)
            near = jnp.concatenate([a * n_far, values * dv_far], axis=0).astype(BF16)
            through = jnp.sum(total * adj * before, axis=0, keepdims=True)
            through = through[:, :LANES] + through[:, LANES:]
            flow = nn(both_sums, near) + jnp.where(strict, nn(from_here, both), 0.0) + through
            stay = column(gcol, 24 + h, C, LANES)
            leave = column(gcol, 40 + h, C, LANES)
            logit_parts.append((leave * flow - stay * (values * dv)).astype(BF16))
            adj_ref[h] = total * adj + tn(a_lift, qf)
            for feats, grad, angle in ((qf, dq, angle_q), (kf, dk, angle_k)):
                f = feats.astype(F32)
                angle.append(grad[:, :LANES] * f[:, LANES:] - grad[:, LANES:] * f[:, :LANES])
            dvs.append(dv)
        proj = pcat_ref[p, 0:LANES, :]
        for name, angle, u_ref, r_ref in (
            ("q", angle_q, uq_ref, rq_ref),
            ("k", angle_k, uk_ref, rk_ref),
        ):
            du = nt(jnp.concatenate(angle, axis=1).astype(BF16), proj)
            u = u_ref[:, lanes].astype(F32)
            along = nn((u * du).astype(BF16), block_ones())
            grads[name].append((2.0 * math.pi) * r_ref[:, lanes] * (du - u * along))
        grads["v"].append(jnp.where(lower, dvs[0], dvs[1]))
    dq, dk, dv = (jnp.concatenate(grads[name], axis=1).astype(BF16) for name in "qkv")
    select = jnp.where(
        iota((LANES * heads, LANES), 0) // LANES == iota((LANES * heads, LANES), 1), 1.0, 0.0
    ).astype(BF16)
    dlogit = nn(jnp.concatenate(logit_parts, axis=1), select).astype(BF16)
    ml = ml_ref[...]
    dwq_ref[...] += tn(ml, dq)
    dwk_ref[...] += tn(ml, dk)
    dwv_ref[...] += tn(ml, dv)
    dwg_ref[...] += tn(ml, dlogit)
    mixer_grad = (
        nt(dq, wq_ref[...])
        + nt(dk, wk_ref[...])
        + nt(dv, wv_ref[...])
        + nn(dlogit, wgt_ref[...])
    )
    xhat, scale = normalize(x_ref[...].astype(F32))
    sums_ref[0:8, :] += fold_rows(mixer_grad * xhat)
    sums_ref[8:16, :] += fold_rows(mixer_grad)
    sums_ref[16:24, 0:LANES] += fold_rows(dlogit.astype(F32))
    dx_ref[...] = mg_ref[...] + normalize_back(mixer_grad, gain_ref[...], xhat, scale)


def whole(shape):
    zeros = (0,) * len(shape)
    return pl.BlockSpec(shape, lambda i: zeros)


def call(kernel, steps, ins, outs, scratch, name):
    in_specs = [
        whole(array.shape) if block is None else pl.BlockSpec(block, index)
        for array, block, index in ins
    ]
    out_specs = [
        whole(shape) if block is None else pl.BlockSpec(block, index)
        for shape, dtype, block, index in outs
    ]
    return pl.pallas_call(
        kernel,
        grid=(steps,),
        in_specs=in_specs,
        out_specs=out_specs,
        out_shape=[jax.ShapeDtypeStruct(shape, dtype) for shape, dtype, _, _ in outs],
        scratch_shapes=scratch,
        compiler_params=pltpu.CompilerParams(
            dimension_semantics=("arbitrary",), vmem_limit_bytes=VMEM
        ),
        name=name,
    )(*[array for array, _, _ in ins])


def carry_over(payload, logs, forward):
    n, index = lax.axis_size("seq"), lax.axis_index("seq")
    if n == 2:
        return lax.ppermute(payload, "seq", [(0, 1)] if forward else [(1, 0)])
    everything = lax.all_gather(payload, "seq")
    every_log = lax.all_gather(logs, "seq")
    total = jnp.zeros(payload.shape, F32)
    for k in range(n) if forward else reversed(range(n)):
        ahead = (k < index) if forward else (k > index)
        new = jnp.exp(every_log[k])[:, None, None] * total + everything[k].astype(F32)
        total = jnp.where(ahead, new, total)
    return total.astype(BF16)


def local(
    inputs,
    cotangent,
    mixer_gain,
    mixer_bias,
    query_weight,
    key_weight,
    value_weight,
    gate_weight,
    gate_bias,
    output_weight,
    projections,
    start_state,
    start_norm,
    feed_gain,
    feed_bias,
    up_weight,
    up_bias,
    down_weight,
    down_bias,
):
    _, tokens, width = inputs.shape
    heads, size, feats = projections.shape
    chunks = tokens // C
    tile = min(T, tokens)
    tiles = tokens // tile
    shards = lax.axis_size("seq")
    first = lax.axis_index("seq") == 0
    x = inputs.reshape(tokens, width)
    dout = cotangent.reshape(tokens, width)

    every_up = lax.all_gather(up_weight, "seq")
    every_down = lax.all_gather(down_weight, "seq")
    every_upb = lax.all_gather(up_bias.astype(F32), "seq").reshape(1, -1)
    hidden = every_upb.shape[1]

    turns = projections * (1.0 / (2.0 * math.pi))
    high = lax.reduce_precision(turns, 8, 7)
    rest = turns - high
    zeros = jnp.zeros_like(turns)

    def pair_blocks(part):
        left = jnp.concatenate([part[0::2], zeros[0::2]], axis=2)
        right = jnp.concatenate([zeros[0::2], part[1::2]], axis=2)
        return jnp.concatenate([left, right], axis=1)

    pcat = jnp.concatenate(
        [pair_blocks(high), pair_blocks(high), pair_blocks(rest)], axis=1
    ).astype(BF16)
    wg = jnp.tile(gate_weight, (1, LANES // heads))
    wgt = gate_weight.T
    gb = jnp.tile(gate_bias, LANES // heads)[None]
    gbt = jnp.broadcast_to(gate_bias[:, None], (heads, LANES))
    start_rows = start_state.transpose(0, 2, 1)
    norm_rows = jnp.broadcast_to(start_norm[:, None, :], start_rows.shape)
    even = (jnp.arange(heads) % 2 == 0)[:, None, None]
    start = jnp.concatenate(
        [jnp.where(even, start_rows, norm_rows), jnp.where(even, norm_rows, start_rows)], axis=1
    )
    start = jnp.where(first, start, 0.0)

    def rows(n, block_rows=C):
        return (block_rows, n), lambda i: (i, 0)

    def out_rows(n, dtype, block_rows=C):
        return ((tokens, n), dtype) + rows(n, block_rows)

    def const(array):
        return (array if array.ndim > 1 else array[None], None, None)

    def keep(shape, dtype):
        return (shape, dtype, None, None)

    wide = heads * LANES
    wider = heads * 2 * feats
    ml, uq, uk, rq, rk, qf, kf, v, gcol, grow, before, final, total = call(
        partial(features_kernel, heads),
        chunks,
        [
            (x,) + rows(width),
            const(mixer_gain),
            const(mixer_bias),
            const(query_weight),
            const(key_weight),
            const(value_weight),
            const(wg),
            const(wgt),
            const(gb),
            const(gbt),
            const(pcat),
            const(start),
        ],
        [
            out_rows(width, BF16),
            out_rows(width, BF16),
            out_rows(width, BF16),
            out_rows(width, F32),
            out_rows(width, F32),
            out_rows(wider, BF16),
            out_rows(wider, BF16),
            out_rows(width, BF16),
            out_rows(LANES, F32),
            ((2 * heads, tokens), F32, (2 * heads, C), lambda i: (0, i)),
            (
                (chunks, heads, LANES, 2 * feats),
                BF16,
                (1, heads, LANES, 2 * feats),
                lambda i: (i, 0, 0, 0),
            ),
            keep((heads, PAY, 2 * feats), BF16),
            keep((8, LANES), F32),
        ],
        [pltpu.VMEM((heads, LANES, 2 * feats), F32), pltpu.VMEM((1, LANES), F32)],
        "features",
    )
    logs = total[0, :heads]
    entry = carry_over(final, logs, True)
    state_block = (1, heads, LANES, 2 * feats)
    (num,) = call(
        partial(inner_kernel, heads),
        chunks,
        [
            (qf,) + rows(wider),
            (kf,) + rows(wider),
            (v,) + rows(width),
            (gcol,) + rows(LANES),
            (grow, (2 * heads, C), lambda i: (0, i)),
            (before, state_block, lambda i: (i, 0, 0, 0)),
        ],
        [out_rows(wide, F32)],
        [],
        "inner",
    )
    out, mg, fl, hl, pre, mix, br, a, adj_final, feed_sums, upbg = call(
        partial(feed_kernel, heads, shards),
        tiles,
        [
            (x,) + rows(width, tile),
            (dout,) + rows(width, tile),
            (qf,) + rows(wider, tile),
            (num,) + rows(wide, tile),
            (gcol,) + rows(LANES, tile),
            const(entry),
            const(output_weight),
            const(feed_gain),
            const(feed_bias),
            const(every_up),
            const(every_upb),
            const(every_down),
            const(down_bias),
        ],
        [
            out_rows(width, BF16, tile),
            out_rows(width, F32, tile),
            out_rows(width, BF16, tile),
            out_rows(hidden, BF16, tile),
            out_rows(hidden, BF16, tile),
            out_rows(width, BF16, tile),
            out_rows(width, BF16, tile),
            out_rows(wide, BF16, tile),
            keep((heads, PAY, 2 * feats), BF16),
            keep((24, width), F32),
            keep((8, hidden), F32),
        ],
        [
            pltpu.VMEM((heads, LANES, 2 * feats), F32),
            pltpu.VMEM((heads, LANES, 2 * feats), BF16),
        ],
        "feed",
    )
    after = carry_over(adj_final, logs, False)
    down_grad = tn(dout, hl).astype(BF16)
    up_grad = tn(fl, pre).astype(BF16)
    output_grad = tn(mix, br).astype(BF16)

    def back_rows(n):
        return (C, n), lambda i: (chunks - 1 - i, 0)

    dx, dwq, dwk, dwv, dwg, adj, mixer_sums = call(
        partial(back_kernel, heads),
        chunks,
        [
            (x,) + back_rows(width),
            (mg,) + back_rows(width),
            (ml,) + back_rows(width),
            (uq,) + back_rows(width),
            (uk,) + back_rows(width),
            (rq,) + back_rows(width),
            (rk,) + back_rows(width),
            (qf,) + back_rows(wider),
            (kf,) + back_rows(wider),
            (v,) + back_rows(width),
            (a,) + back_rows(wide),
            (gcol,) + back_rows(LANES),
            (grow, (2 * heads, C), lambda i: (0, chunks - 1 - i)),
            (before, state_block, lambda i: (chunks - 1 - i, 0, 0, 0)),
            const(entry),
            const(after),
            const(mixer_gain),
            const(query_weight),
            const(key_weight),
            const(value_weight),
            const(jnp.pad(wgt, ((0, LANES - heads), (0, 0)))),
            const(pcat),
        ],
        [
            ((tokens, width), F32) + back_rows(width),
            keep((width, width), F32),
            keep((width, width), F32),
            keep((width, width), F32),
            keep((width, LANES), F32),
            keep((heads, LANES, 2 * feats), F32),
            keep((24, width), F32),
        ],
        [],
        "back",
    )
    adj = jnp.where(first, adj, 0.0)
    state_grad = jnp.where(even, adj[:, :64], adj[:, 64:])
    norm_grad = jnp.sum(jnp.where(even, adj[:, 64:], adj[:, :64]), axis=1)

    feed_three = jnp.sum(feed_sums.reshape(3, 8, width), axis=1)
    mixer_three = jnp.sum(mixer_sums.reshape(3, 8, width), axis=1)
    upb_grad = jnp.sum(upbg, axis=0)
    weight_grads = (dwq.astype(BF16), dwk.astype(BF16), dwv.astype(BF16), output_grad)
    small = (dwg[:, :heads].T, norm_grad, feed_three, mixer_three)
    if (lax.axis_size("dp"), lax.axis_size("seq")) == (16, 2):
        half = hidden // 2
        up_down = jnp.concatenate(
            [up_grad[:, :half], up_grad[:, half:], down_grad[:, :half], down_grad[:, half:]]
        )
        flat = jnp.concatenate([part.reshape(-1) for part in small + (upb_grad,)])
        flat = jnp.pad(flat, (0, 256 * LANES - flat.shape[0])).reshape(256, LANES)
        state_rows = state_grad.astype(BF16).reshape(heads * 64, 2 * feats)
        sum_up_down, sum_q, sum_k, sum_v, sum_o, sum_state, flat = sum_devices(
            (up_down,) + weight_grads + (state_rows, flat),
            ("half", "all", "all", "all", "all", "all", "all"),
            (4, 1, 1, 1, 1, 1, 1),
        )
        sum_up, sum_down = sum_up_down[:width], sum_up_down[width:]
        flat = flat.reshape(-1)
        sums, at = [], 0
        for part in small + (upb_grad,):
            sums.append(flat[at : at + part.size].reshape(part.shape))
            at += part.size
        sum_g, sum_norm, sum_feed, sum_mixer, sum_upb = sums
        sum_upb = jnp.where(first, sum_upb[:half], sum_upb[half:])
        sum_state = sum_state.reshape(heads, 64, 2 * feats)
    else:
        halves = lax.psum_scatter(
            jnp.stack([up_grad, down_grad]), "seq", scatter_dimension=2, tiled=True
        )
        upb_half = lax.psum_scatter(upb_grad, "seq", scatter_dimension=0, tiled=True)
        (sum_up, sum_down), sum_upb = lax.psum((halves, upb_half), "dp")
        sum_q, sum_k, sum_v, sum_o, sum_state = lax.psum(
            weight_grads + (state_grad.astype(BF16),), ("dp", "seq")
        )
        sum_g, sum_norm, sum_feed, sum_mixer = lax.psum(small, ("dp", "seq"))
    return (
        out.reshape(inputs.shape),
        dx.reshape(inputs.shape),
        sum_mixer[0],
        sum_mixer[1],
        sum_q.astype(F32),
        sum_k.astype(F32),
        sum_v.astype(F32),
        sum_g.T,
        sum_mixer[2, :heads],
        sum_o.astype(F32),
        sum_state.astype(F32).transpose(0, 2, 1),
        sum_norm,
        sum_feed[0],
        sum_feed[1],
        sum_up.astype(F32),
        sum_upb,
        sum_down.astype(F32),
        sum_feed[2],
    )


class Links:
    def __init__(self):
        self.dp, self.seq = lax.axis_index("dp"), lax.axis_index("seq")
        core, y, z = self.dp % 2, (self.dp // 2) % 2, self.dp // 4
        self.y = y
        self.at = {"core": core, "x": self.seq, "y": y, "z": z, "plane": self.seq * 2 + y}

    size = {"core": 2, "x": 2, "y": 2, "z": 4, "plane": 4}

    def partner(self, group, step):
        dp, seq = self.dp, self.seq
        if group == "core":
            return (dp + 1 - 2 * self.at["core"], seq)
        if group == "x":
            return (dp, 1 - seq)
        if group == "y":
            return (dp + 2 - 4 * self.y, seq)
        target = (self.at[group] + step) % 4
        if group == "z":
            return (dp % 4 + 4 * target, seq)
        return (dp + 2 * (target % 2 - self.y), target // 2)

    def greet(self, groups):
        barrier = pltpu.get_barrier_semaphore()
        count = 0
        for group in groups:
            for step in range(1, self.size[group]):
                pl.semaphore_signal(
                    barrier, inc=1, device_id=self.partner(group, step), device_id_type=MESH
                )
                count += 1
        pl.semaphore_wait(barrier, count)


class Plan:
    def __init__(self, rows, lanes, dtype, scatter, gather):
        self.scatter, self.gather, self.lanes, self.dtype = scatter, gather, lanes, dtype
        self.rows = rows
        self.stages = len(scatter) + len(gather)

    def scratch(self):
        shapes = []
        rows = self.rows
        for i, group in enumerate(self.scatter):
            n = Links.size[group]
            rows //= n
            shapes.append(pltpu.VMEM((n - 1, rows, self.lanes), self.dtype))
            if i < len(self.scatter) - 1:
                shapes.append(pltpu.VMEM((rows, self.lanes), self.dtype))
        for group in self.scatter + self.gather:
            n = Links.size[group]
            shapes.append(pltpu.SemaphoreType.DMA((n - 1,)))
            shapes.append(pltpu.SemaphoreType.DMA((n - 1,)))
        return shapes


class Stream:
    def __init__(self, plan, links, source, out, scratch):
        self.plan, self.links, self.source, self.out = plan, links, source, out
        scratch = list(scratch)
        self.landing, self.parts = [], [source]
        for i in range(len(plan.scatter)):
            self.landing.append(scratch.pop(0))
            if i < len(plan.scatter) - 1:
                self.parts.append(scratch.pop(0))
        self.sems = [(scratch.pop(0), scratch.pop(0)) for _ in range(plan.stages)]
        self.places = {}
        rows, start = out.shape[0], 0
        for group in plan.scatter:
            if group in plan.gather:
                rows //= Links.size[group]
                self.places[group] = (start, rows)
                start = start + links.at[group] * rows
        self.final = (start, rows)

    def copies(self, stage, sending):
        plan, links = self.plan, self.links
        scattering = stage < len(plan.scatter)
        group = (plan.scatter + plan.gather)[stage]
        n, me = Links.size[group], links.at[group]
        sends, recvs = self.sems[stage]
        made = []
        for step in range(1, n):
            if scattering:
                landing = self.landing[stage]
                rows = landing.shape[1]
                target = (me + step) % n
                source = self.parts[stage].at[pl.ds(pl.multiple_of(target * rows, 8), rows)]
                arrives = lands = landing.at[step - 1]
            else:
                start, rows = self.places[group]
                mine_at = pl.multiple_of(start + me * rows, 8)
                theirs_at = pl.multiple_of(start + ((me + n - step) % n) * rows, 8)
                source = lands = self.out.at[pl.ds(mine_at, rows)]
                arrives = self.out.at[pl.ds(theirs_at, rows)]
            device = links.partner(group, step)

            def copy(src, dst):
                return pltpu.make_async_remote_copy(
                    src_ref=src,
                    dst_ref=dst,
                    send_sem=sends.at[step - 1],
                    recv_sem=recvs.at[step - 1],
                    device_id=device,
                    device_id_type=MESH,
                )

            made.append(copy(source, lands) if sending else copy(arrives, arrives))
        return made

    def start(self, stage):
        for copy in self.copies(stage, True):
            copy.start()

    def finish(self, stage):
        for copy in self.copies(stage, False):
            copy.wait_recv()
        if stage >= len(self.plan.scatter):
            return
        group = self.plan.scatter[stage]
        landing = self.landing[stage]
        arrivals, rows, _ = landing.shape
        own = pl.multiple_of(self.links.at[group] * rows, 8)
        total = self.parts[stage][pl.ds(own, rows), :].astype(F32)
        for step in range(arrivals):
            total = total + landing[step].astype(F32)
        total = total.astype(landing.dtype)
        if stage + 1 < len(self.plan.scatter):
            self.parts[stage + 1][...] = total
        else:
            start, rows = self.final
            self.out[pl.ds(pl.multiple_of(start, 8), rows), :] = total

    def drain(self):
        for stage in range(self.plan.stages):
            for copy in self.copies(stage, True):
                copy.wait_send()


def run_streams(streams):
    stages = max(stream.plan.stages for stream in streams)
    for tick in range(stages + len(streams)):
        for i, stream in enumerate(streams):
            stage = tick - i
            if 0 < stage <= stream.plan.stages:
                stream.finish(stage - 1)
            if 0 <= stage < stream.plan.stages:
                stream.start(stage)
    for stream in streams:
        stream.drain()


UP_PLAN = (("core", "x", "y", "z"), ("z", "y", "core"))
ALL_PLAN = (("core", "plane", "z"), ("z", "plane", "core"))


def sum_kernel(plans, splits, n_in, *refs):
    sources, outs, scratch = refs[:n_in], refs[n_in : 2 * n_in], list(refs[2 * n_in :])
    links = Links()
    links.greet(("core", "plane", "z"))
    streams = []
    for source, out, plan, split in zip(sources, outs, plans, splits):
        for part in range(split):
            own = [scratch.pop(0) for _ in plan.scratch()]
            lanes = pl.ds(part * plan.lanes, plan.lanes)
            streams.append(Stream(plan, links, source.at[:, lanes], out.at[:, lanes], own))
    run_streams(streams)


def sum_devices(arrays, kinds, splits):
    plans, shapes, scratch = [], [], []
    for array, kind, split in zip(arrays, kinds, splits):
        rows, lanes = array.shape
        scatter, gather = UP_PLAN if kind == "half" else ALL_PLAN
        plan = Plan(rows, lanes // split, array.dtype, scatter, gather)
        plans.append(plan)
        for _ in range(split):
            scratch.extend(plan.scratch())
        out_rows = rows // 2 if kind == "half" else rows
        shapes.append(jax.ShapeDtypeStruct((out_rows, lanes), array.dtype))
    return pl.pallas_call(
        partial(sum_kernel, plans, splits, len(arrays)),
        in_specs=[pl.BlockSpec(memory_space=pltpu.VMEM)] * len(arrays),
        out_specs=[pl.BlockSpec(memory_space=pltpu.VMEM)] * len(arrays),
        out_shape=shapes,
        scratch_shapes=scratch,
        compiler_params=pltpu.CompilerParams(
            collective_id=1, has_side_effects=True, vmem_limit_bytes=VMEM
        ),
        name="sums",
    )(*arrays)


def solution(mesh):
    tokens = P("dp", "seq", None)
    columns = P(None, "seq")
    return jax.shard_map(
        local,
        mesh=mesh,
        in_specs=(tokens, tokens) + (P(),) * 13 + (columns, P("seq"), columns, P()),
        out_specs=(tokens, tokens) + (P(),) * 12 + (columns, P("seq"), columns, P()),
        check_vma=False,
    )
```

```python
from functools import partial
import math

import jax
import jax.numpy as jnp
from jax import lax
from jax.experimental import pallas as pl
from jax.experimental.pallas import tpu as pltpu
from jax.sharding import PartitionSpec as P

F32 = jnp.float32
BF16 = jnp.bfloat16
EPS_NORM = 1e-05
EPS_UNIT = 1e-06
GUARD = 0.0625
MESH = pl.DeviceIdType.MESH
HIGH = lax.Precision.HIGHEST
VMEM = 56 * 1024 * 1024

C = 128
T = 256
HB = 512
GROUP_HEADS = 4
LANES = 128
PAY = 80

SIN = (3.14158202, -5.16714278, 2.54189892, -0.55463591)
COS = (0.99999995, -4.93479286, 4.05841191, -1.33188012, 0.21969671)
ERF = (0.319381530, -0.356563782, 1.781477937, -1.821255978, 1.330274429)
ERF_P = 0.2316419
INV_SQRT_2PI = 0.3989422804014327


def nn(a, b):
    return lax.dot_general(a, b, (((1,), (0,)), ((), ())), preferred_element_type=F32)


def nt(a, b):
    return lax.dot_general(a, b, (((1,), (1,)), ((), ())), preferred_element_type=F32)


def tn(a, b):
    return lax.dot_general(a, b, (((0,), (0,)), ((), ())), preferred_element_type=F32)


def exact(a, b):
    return lax.dot_general(
        a, b, (((1,), (0,)), ((), ())), precision=HIGH, preferred_element_type=F32
    )


def iota(shape, dim):
    return lax.broadcasted_iota(jnp.int32, shape, dim)


def log_sigmoid(x):
    return jnp.minimum(x, 0.0) - jnp.log(1.0 + jnp.exp(-jnp.abs(x)))


def normalize(x):
    centred = x - jnp.mean(x, axis=-1, keepdims=True)
    scale = lax.rsqrt(jnp.mean(centred * centred, axis=-1, keepdims=True) + EPS_NORM)
    return centred * scale, scale


def normalize_back(grad, gain, xhat, scale):
    inner = grad * gain
    mean_inner = jnp.mean(inner, axis=-1, keepdims=True)
    mean_both = jnp.mean(inner * xhat, axis=-1, keepdims=True)
    return scale * (inner - mean_inner - xhat * mean_both)


def fold_rows(x):
    return jnp.sum(x.reshape(x.shape[0] // 8, 8, x.shape[1]), axis=0)


def block_ones():
    return jnp.where(
        iota((LANES, LANES), 0) // 64 == iota((LANES, LANES), 1) // 64, 1.0, 0.0
    ).astype(BF16)


def head_sums(x):
    high = x.astype(BF16)
    rest = (x - high.astype(F32)).astype(BF16)
    ones = block_ones()
    return nn(jnp.concatenate([high, rest], axis=1), jnp.concatenate([ones, ones], axis=0))


def lower_half(shape):
    return iota(shape, 1) < 64


def mine(h, lower):
    return lower if h % 2 == 0 else jnp.logical_not(lower)


def column(block, index, rows, width):
    return jnp.broadcast_to(block[:, index : index + 1], (rows, width))


def sin_cos(turns, scale):
    r = turns - jnp.floor(turns + 0.5)
    r2 = r * r
    s = (((SIN[3] * r2 + SIN[2]) * r2 + SIN[1]) * r2 + SIN[0]) * r
    k = 2.0 * scale
    c = (((k * COS[4] * r2 + k * COS[3]) * r2 + k * COS[2]) * r2 + k * COS[1]) * r2 + k * COS[0]
    return s * c, scale - (k * s) * s


def grow_state(payload, h):
    state = payload[h, 0:64, :]
    norm = jnp.broadcast_to(payload[h, 64:65, :].astype(F32), (64, state.shape[1]))
    state = state.astype(F32)
    return jnp.concatenate([state, norm] if h % 2 == 0 else [norm, state], axis=0)


def shrink_state(state, h):
    if h % 2 == 0:
        return state[0:PAY].astype(BF16)
    return jnp.concatenate([state[64:128], state[0 : PAY - 64]], axis=0).astype(BF16)


def features_kernel(
    heads,
    x_ref,
    gain_ref,
    bias_ref,
    wq_ref,
    wk_ref,
    wv_ref,
    wg_ref,
    wgt_ref,
    gb_ref,
    gbt_ref,
    pcat_ref,
    start_ref,
    ml_ref,
    uq_ref,
    uk_ref,
    rq_ref,
    rk_ref,
    qf_ref,
    kf_ref,
    v_ref,
    gcol_ref,
    grow_ref,
    before_ref,
    final_ref,
    total_ref,
    state,
    carry,
):
    step = pl.program_id(0)

    @pl.when(step == 0)
    def _():
        state[...] = start_ref[...]
        carry[...] = jnp.zeros_like(carry)

    xhat, _ = normalize(x_ref[...].astype(F32))
    ml = (xhat * gain_ref[...] + bias_ref[...]).astype(BF16)
    ml_ref[...] = ml
    q = nn(ml, wq_ref[...])
    k = nn(ml, wk_ref[...])
    v = nn(ml, wv_ref[...])
    v_ref[...] = v.astype(BF16)
    logit = nn(ml, wg_ref[...]) + gb_ref[...]
    keep = log_sigmoid(logit)
    gain_in = keep - logit
    tri = jnp.where(iota((C, C), 0) >= iota((C, C), 1), 1.0, 0.0)
    decay = exact(tri, keep)
    total = decay[C - 1 : C, :]
    group = iota((C, LANES), 1) // 8
    everywhere = carry[...] + decay
    coef = total - decay + gain_in
    packed = jnp.where(group == 0, decay, coef)
    packed = jnp.where(group == 2, everywhere, packed)
    packed = jnp.where(group == 3, jax.nn.sigmoid(logit), packed)
    packed = jnp.where(group == 4, gain_in - decay, packed)
    packed = jnp.where(group == 5, jax.nn.sigmoid(-logit), packed)
    packed = jnp.where(group == 6, jnp.broadcast_to(carry[...], (C, LANES)), packed)
    packed = jnp.where(group == 7, jnp.broadcast_to(total, (C, LANES)), packed)
    gcol_ref[...] = packed
    carry[...] = carry[...] + total
    total_ref[...] = jnp.broadcast_to(carry[...], total_ref.shape)
    logit_row = nt(wgt_ref[...], ml) + gbt_ref[...][:, 0:1]
    keep_row = log_sigmoid(logit_row)
    upper = jnp.where(iota((C, C), 0) <= iota((C, C), 1), 1.0, 0.0)
    decay_row = exact(keep_row, upper)
    grow_ref[...] = jnp.concatenate(
        [
            keep_row - logit_row - decay_row,
            decay_row,
            jax.nn.sigmoid(logit_row),
            jax.nn.sigmoid(-logit_row),
        ],
        axis=0,
    )

    lower = lower_half((C, LANES))
    ftr_scale = 1.0 / math.sqrt(LANES)
    for p in range(heads // 2):
        lanes = slice(LANES * p, LANES * (p + 1))
        both = jnp.concatenate([q[:, lanes], k[:, lanes]], axis=0)
        scale = lax.rsqrt(head_sums(both * both) + EPS_UNIT)
        unit = both * scale
        high = unit.astype(BF16)
        rest = (unit - high.astype(F32)).astype(BF16)
        uq_ref[:, lanes] = high[:C]
        uk_ref[:, lanes] = high[C:]
        rq_ref[:, lanes] = scale[:C]
        rk_ref[:, lanes] = scale[C:]
        turns = nn(jnp.concatenate([high, rest, high], axis=1), pcat_ref[p])
        s, c = sin_cos(turns, ftr_scale)
        s = s.astype(BF16)
        c = c.astype(BF16)
        for j in range(2):
            h = 2 * p + j
            half = slice(LANES * j, LANES * (j + 1))
            feats = jnp.concatenate([s[:, half], c[:, half]], axis=1)
            qf_ref[:, 256 * h : 256 * (h + 1)] = feats[:C]
            kf = feats[C:]
            kf_ref[:, 256 * h : 256 * (h + 1)] = kf
            values = jnp.where(mine(h, lower), v[:, lanes], 1.0)
            weighted = (values * jnp.exp(column(coef, h, C, LANES))).astype(BF16)
            now = state[h]
            before_ref[0, h] = now.astype(BF16)
            state[h] = jnp.exp(total[:, h : h + 1]) * now + tn(weighted, kf)

    @pl.when(step == pl.num_programs(0) - 1)
    def _():
        for h in range(heads):
            final_ref[h] = shrink_state(state[h], h)


def inner_kernel(heads, qf_ref, kf_ref, v_ref, gcol_ref, grow_ref, before_ref, n_ref):
    causal = iota((C, C), 0) >= iota((C, C), 1)
    lower = lower_half((C, LANES))
    gcol = gcol_ref[...]
    for h in range(heads):
        qf = qf_ref[:, 256 * h : 256 * (h + 1)]
        kf = kf_ref[:, 256 * h : 256 * (h + 1)]
        p = h // 2
        v = v_ref[:, LANES * p : LANES * (p + 1)].astype(F32)
        values = jnp.where(mine(h, lower), v, 1.0).astype(BF16)
        decay = column(gcol, h, C, LANES)
        pairs = jnp.where(causal, jnp.exp(decay + grow_ref[h : h + 1, :]), 0.0)
        weights = (nt(qf, kf) * pairs).astype(BF16)
        n_ref[:, LANES * h : LANES * (h + 1)] = nn(weights, values) + jnp.exp(decay) * nt(
            qf, before_ref[0, h]
        )


def feed_kernel(
    heads,
    shards,
    x_ref,
    dout_ref,
    qf_ref,
    n_ref,
    gcol_ref,
    entry_ref,
    wo_ref,
    gain_ref,
    bias_ref,
    up_ref,
    upb_ref,
    down_ref,
    downb_ref,
    out_ref,
    mg_ref,
    fl_ref,
    hl_ref,
    pre_ref,
    mix_ref,
    br_ref,
    a_ref,
    final_ref,
    sums_ref,
    upbg_ref,
    adj,
    entry,
):
    step = pl.program_id(0)
    rows = x_ref.shape[0]

    @pl.when(step == 0)
    def _():
        adj[...] = jnp.zeros_like(adj)
        sums_ref[...] = jnp.zeros_like(sums_ref)
        upbg_ref[...] = jnp.zeros_like(upbg_ref)
        for h in range(heads):
            entry[h] = grow_state(entry_ref, h).astype(BF16)

    lower = lower_half((rows, LANES))
    gcol = gcol_ref[...]
    parts = []
    for p in range(heads // 2):
        both = []
        for h in (2 * p, 2 * p + 1):
            far = nt(qf_ref[:, 256 * h : 256 * (h + 1)], entry[h])
            far = far * jnp.exp(column(gcol, 16 + h, rows, LANES))
            both.append(n_ref[:, LANES * h : LANES * (h + 1)] + far)
        num = jnp.where(lower, both[0], both[1])
        den = pltpu.roll(jnp.where(lower, both[1], both[0]), 64, 1)
        inv = lax.rsqrt(den * den + GUARD)
        parts.append((num, den, inv))
    mixed = jnp.concatenate([num * inv for num, den, inv in parts], axis=1).astype(BF16)
    mix_ref[...] = mixed
    middle = x_ref[...].astype(F32) + nn(mixed, wo_ref[...])
    xhat, scale = normalize(middle)
    gain = gain_ref[...]
    feed_low = (xhat * gain + bias_ref[...]).astype(BF16)
    fl_ref[...] = feed_low
    dout_low = dout_ref[...]
    dout = dout_low.astype(F32)
    out = middle + downb_ref[...]
    feed_grad = jnp.zeros_like(middle)
    width = up_ref.shape[2]
    block = min(HB, width)
    for s in range(shards):
        for b in range(width // block):
            cols = slice(block * b, block * (b + 1))
            place = slice(width * s + block * b, width * s + block * (b + 1))
            up = up_ref[s, :, cols]
            down = down_ref[s, :, cols]
            pre = nn(feed_low, up) + upb_ref[:, place]
            t = 1.0 / (1.0 + ERF_P * jnp.abs(pre))
            bell = INV_SQRT_2PI * jnp.exp(-0.5 * pre * pre)
            tail = ((((ERF[4] * t + ERF[3]) * t + ERF[2]) * t + ERF[1]) * t + ERF[0]) * t * bell
            phi = jnp.where(pre >= 0.0, 1.0 - tail, tail)
            hidden = (pre * phi).astype(BF16)
            hl_ref[:, place] = hidden
            out = out + nt(hidden, down)
            pre_grad = nn(dout_low, down) * (phi + pre * bell)
            pre_low = pre_grad.astype(BF16)
            pre_ref[:, place] = pre_low
            upbg_ref[:, place] += fold_rows(pre_low.astype(F32))
            feed_grad = feed_grad + nt(pre_low, up)
    out_ref[...] = out.astype(BF16)
    sums_ref[0:8, :] += fold_rows(feed_grad * xhat)
    sums_ref[8:16, :] += fold_rows(feed_grad)
    sums_ref[16:24, :] += fold_rows(dout)
    middle_grad = dout + normalize_back(feed_grad, gain, xhat, scale)
    mg_ref[...] = middle_grad
    branch = middle_grad.astype(BF16)
    br_ref[...] = branch
    mixed_grad = nt(branch, wo_ref[...])
    for p in range(heads // 2):
        num, den, inv = parts[p]
        mg = mixed_grad[:, LANES * p : LANES * (p + 1)]
        a = mg * inv
        b = head_sums(mg * num) * den * (inv * inv * inv) * (-1.0 / 64)
        b = pltpu.roll(b, 64, 1)
        for h in (2 * p, 2 * p + 1):
            a_low = jnp.where(mine(h, lower), a, b)
            a_ref[:, LANES * h : LANES * (h + 1)] = a_low.astype(BF16)
            lifted = (a_low * jnp.exp(column(gcol, 16 + h, rows, LANES))).astype(BF16)
            adj[h] += tn(lifted, qf_ref[:, 256 * h : 256 * (h + 1)])

    @pl.when(step == pl.num_programs(0) - 1)
    def _():
        for h in range(heads):
            final_ref[h] = shrink_state(adj[h], h)


def back_kernel(heads, hg, chunks, comm, *refs):
    refs = list(refs)

    def take(n):
        taken = refs[:n]
        del refs[:n]
        return taken

    (qf_ref, kf_ref, v_ref, uq_ref, uk_ref, rq_ref, rk_ref, a_ref, gcol_ref, grow_ref) = take(10)
    before_ref, entry_ref, after_ref, proj_ref = take(4)
    x_hbm, mg_hbm, ml_hbm, wq_hbm, wk_hbm, wv_hbm, wgt_ref, gain_ref = take(8)
    u_hbm, o_hbm, s_hbm, f_hbm = take(4) if comm else (None,) * 4
    dx_ref, w_ref, small_ref = take(3)
    usum_hbm, osum_hbm, ssum_hbm, fsum_hbm = take(4) if comm else (None,) * 4
    adj_ref, dqkv, dlogit, x_ref, mg_ref, ml_ref, wq_ref, wk_ref, wv_ref, load_sems = take(10)
    g, i = pl.program_id(0), pl.program_id(1)
    tick = g * chunks + i
    last = heads // hg * chunks - 1
    chunk = chunks - 1 - i
    here = pl.ds(pl.multiple_of(chunk * C, C), C)
    groups = heads // hg
    loads = [
        (x_hbm, x_ref),
        (mg_hbm, mg_ref),
        (ml_hbm, ml_ref),
        (wq_hbm, wq_ref),
        (wk_hbm, wk_ref),
        (wv_hbm, wv_ref),
    ]
    if comm:
        u_ref, o_ref, s_ref, f_ref, w_src, small_src = take(6)
        usum_ref, osum_ref, ssum_ref, fsum_ref, wsum_ref, smallsum_ref = take(6)
        store_sems = refs.pop(0)
        loads = [(u_hbm, u_ref), (o_hbm, o_ref), (s_hbm, s_ref), (f_hbm, f_ref)] + loads
        links = Links()
        streams, starts, stores = [], [], []

        def add(plan, source, out, final, start):
            streams.append(Stream(plan, links, source, out, take(len(plan.scratch()))))
            starts.append(start)
            stores.append((out, final))

        def store(k):
            return pltpu.make_async_copy(*stores[k], store_sems.at[k])

        plans = back_plans(u_hbm.shape, o_hbm.shape, s_hbm.shape, f_hbm.shape, w_src.shape, small_src.shape)
        n_u = u_hbm.shape[1] // plans["u"].lanes
        for k in range(n_u):
            lanes = pl.ds(k * plans["u"].lanes, plans["u"].lanes)
            add(plans["u"], u_ref.at[:, lanes], usum_ref.at[:, lanes], usum_hbm.at[:, lanes], k + 1)
        add(plans["f"], f_ref, fsum_ref, fsum_hbm, 3)
        add(plans["s"], s_ref, ssum_ref, ssum_hbm, 5)
        add(plans["o"], o_ref, osum_ref, osum_hbm, 7)
        for k in range(groups):
            for j in range(3):
                lanes = pl.ds(j * plans["w"].lanes, plans["w"].lanes)
                add(
                    plans["w"],
                    w_src.at[k, :, lanes],
                    wsum_ref.at[k, :, lanes],
                    w_ref.at[k, :, lanes],
                    (k + 1) * chunks,
                )

        def advance(now):
            for k, (stream, start) in enumerate(zip(streams, starts)):
                stage = now - start
                if 0 < stage <= stream.plan.stages:
                    stream.finish(stage - 1)
                    if stage == stream.plan.stages:
                        store(k).start()
                if 0 <= stage < stream.plan.stages:
                    stream.start(stage)

    def load(k):
        return pltpu.make_async_copy(loads[k][0], loads[k][1], load_sems.at[k])

    @pl.when(tick == 0)
    def _():
        for k in range(len(loads)):
            load(k).start()
        dlogit[...] = jnp.zeros_like(dlogit)
        if comm:
            links.greet(("core", "plane", "z"))

    if comm:
        @pl.when(tick == 1)
        def _():
            for k in range(4):
                load(k).wait()

        for now in range(1, last + 1):
            pl.when(tick == now)(partial(advance, now))

    @pl.when(i == 0)
    def _():
        for h in range(hg):
            adj_ref[h] = grow_state(after_ref, h)

    row = iota((C, C), 0)
    col = iota((C, C), 1)
    causal = row >= col
    one = jnp.ones((C, C), BF16)
    zero = jnp.zeros((C, C), BF16)
    later = jnp.where(row < col, 1.0, 0.0).astype(BF16)
    pair_sums = jnp.concatenate([later, one], axis=0)
    two_sums = jnp.concatenate(
        [jnp.concatenate([one, zero], axis=1), jnp.concatenate([zero, one], axis=1)], axis=0
    )
    lower = lower_half((C, LANES))
    gcol = gcol_ref[...]
    if groups > 1:
        gcol = jnp.where(g == 0, gcol, pltpu.roll(gcol, LANES - hg, 1))

    def grow_row(kind, h):
        return grow_ref[pl.ds(kind * heads + g * hg + h, 1), :]

    for p in range(hg // 2):
        lanes = slice(LANES * p, LANES * (p + 1))
        angle_q, angle_k, dvs, x_parts, y_parts, throughs = [], [], [], [], [], []
        v_pair = v_ref[:, lanes].astype(F32)
        values = [jnp.where(mine(h, lower), v_pair, 1.0) for h in range(2)]
        values_low = [part.astype(BF16) for part in values]
        dweights = nt(
            a_ref[:, 2 * LANES * p : 2 * LANES * (p + 1)],
            jnp.concatenate(
                [
                    jnp.concatenate([values_low[0], zero], axis=1),
                    jnp.concatenate([zero, values_low[1]], axis=1),
                ],
                axis=0,
            ),
        )
        for j in range(2):
            h = 2 * p + j
            qf = qf_ref[:, 256 * h : 256 * (h + 1)]
            kf = kf_ref[:, 256 * h : 256 * (h + 1)]
            a_low = a_ref[:, LANES * h : LANES * (h + 1)]
            a = a_low.astype(F32)
            decay = column(gcol, h, C, LANES)
            lift = jnp.exp(decay)
            coef = jnp.exp(column(gcol, 8 + h, C, LANES))
            carried = jnp.exp(gcol[0:1, 48 + h : 49 + h])
            total = jnp.exp(gcol[0:1, 56 + h : 57 + h])
            before = before_ref[0, h].astype(F32) + carried * grow_state(entry_ref, h)
            before_low = before.astype(BF16)
            adj = adj_ref[h]
            adj_low = adj.astype(BF16)
            kept = total * adj
            through = jnp.sum(kept * before, axis=0, keepdims=True)
            throughs.append(jnp.sum(through, axis=1, keepdims=True))
            pairs = jnp.where(causal, jnp.exp(decay + grow_row(0, h)), 0.0)
            keys_and_state = jnp.concatenate([kf, before_low], axis=0)
            raw_and_far = nt(qf, keys_and_state)
            raw = raw_and_far[:, :C]
            weights = (raw * pairs).astype(BF16)
            draw = dweights[:, C * j : C * (j + 1)].astype(BF16).astype(F32) * pairs
            draw_low = draw.astype(BF16)
            both = (raw * draw).astype(BF16)
            a_lift = (a * lift).astype(BF16)
            v_coef = (values[j] * coef).astype(BF16)
            dq = nn(jnp.concatenate([draw_low, a_lift], axis=1), keys_and_state)
            dk = nn(
                jnp.concatenate([draw_low.T, v_coef], axis=1),
                jnp.concatenate([qf, adj_low], axis=0),
            )
            dv_far = coef * nt(kf, adj_low)
            dv = tn(weights, a_low) + dv_far
            x_far = (a * lift * raw_and_far[:, C:]).astype(BF16)
            x_parts.append(jnp.concatenate([both, x_far], axis=1))
            y_parts.append(
                jnp.concatenate(
                    [(values[j] * dv_far).astype(BF16), (values[j] * dv).astype(BF16)], axis=1
                )
            )
            adj_ref[h] = kept + tn(a_lift, qf)
            for feats, grad, angle in ((qf, dq, angle_q), (kf, dk, angle_k)):
                f = feats.astype(F32)
                angle.append(grad[:, :LANES] * f[:, LANES:] - grad[:, LANES:] * f[:, :LANES])
            dvs.append(dv)
        upto = nn(jnp.concatenate(x_parts, axis=0), pair_sums)
        ends = nn(jnp.concatenate(y_parts, axis=0), two_sums)
        for j in range(2):
            h = 2 * p + j
            rows = slice(C * j, C * (j + 1))
            flow = jnp.where(causal, upto[rows], ends[rows, :C])
            flow = jnp.sum(flow, axis=0, keepdims=True) + throughs[j]
            own = jnp.sum(jnp.where(row == col, ends[rows, C:], 0.0), axis=0, keepdims=True)
            dlogit[g, h : h + 1, here] = grow_row(3, h) * flow - grow_row(2, h) * own
        angles = jnp.concatenate(
            [jnp.concatenate(angle_q, axis=1), jnp.concatenate(angle_k, axis=1)], axis=0
        )
        du = nt(angles.astype(BF16), proj_ref[p])
        u = jnp.concatenate([uq_ref[:, lanes], uk_ref[:, lanes]], axis=0).astype(F32)
        scale = jnp.concatenate([rq_ref[:, lanes], rk_ref[:, lanes]], axis=0)
        along = nn((u * du).astype(BF16), block_ones())
        dqk = ((2.0 * math.pi) * scale * (du - u * along)).astype(BF16)
        width = hg * 64
        dqkv[g, here, LANES * p : LANES * (p + 1)] = dqk[:C]
        dqkv[g, here, width + LANES * p : width + LANES * (p + 1)] = dqk[C:]
        dqkv[g, here, 2 * width + LANES * p : 2 * width + LANES * (p + 1)] = jnp.where(
            lower, dvs[0], dvs[1]
        ).astype(BF16)

    @pl.when(i == chunks - 1)
    def _():
        @pl.when(g == 0)
        def _():
            load(len(loads) - 4).wait()

        grads = tn(ml_ref[...], dqkv[g]).astype(BF16)
        if comm:
            w_src[g] = grads
        else:
            w_ref[g] = grads

    @pl.when(tick == last)
    def _():
        if comm:
            advance(last + 1)
        for k in range(len(loads) - 6, len(loads)):
            if k != len(loads) - 4:
                load(k).wait()
        tokens = chunks * C
        block = min(T, tokens)
        small = small_src if comm else small_ref
        rows8 = jnp.concatenate(
            [dlogit[k, 0:hg, :] for k in range(groups)]
            + [jnp.zeros((16 - heads, dlogit.shape[2]), F32)],
            axis=0,
        ).astype(BF16)
        small[...] = jnp.zeros_like(small)
        small[0:heads, :] = nn(rows8, ml_ref[...])[0:heads]
        bias_sum = jnp.sum(rows8.astype(F32), axis=1, keepdims=True)[0:heads]
        small[heads : 2 * heads, :] = jnp.broadcast_to(bias_sum, (heads, small.shape[1]))
        gain = gain_ref[...]
        now = last + 2
        for b in range(tokens // block):
            rows = slice(block * b, block * (b + 1))
            mixer_grad = tn(rows8[:, rows], wgt_ref[...])
            for k in range(groups):
                for j, ref in enumerate((wq_ref, wk_ref, wv_ref)):
                    mixer_grad = mixer_grad + nt(
                        dqkv[k, rows, hg * 64 * j : hg * 64 * (j + 1)],
                        ref[:, hg * 64 * k : hg * 64 * (k + 1)],
                    )
            xhat, scale = normalize(x_ref[rows, :].astype(F32))
            small[2 * heads : 2 * heads + 1, :] += jnp.sum(
                mixer_grad * xhat, axis=0, keepdims=True
            )
            small[2 * heads + 1 : 2 * heads + 2, :] += jnp.sum(mixer_grad, axis=0, keepdims=True)
            dx_ref[rows, :] = mg_ref[rows, :] + normalize_back(mixer_grad, gain, xhat, scale)
            if comm:
                advance(now)
                now += 1
        if comm:
            add(plans["small"], small_src, smallsum_ref, small_ref, now)
            finish = max(start + stream.plan.stages for stream, start in zip(streams, starts))
            for later_tick in range(now, finish + 1):
                advance(later_tick)
            for k, stream in enumerate(streams):
                stream.drain()
                store(k).wait()


def back_plans(u, o, s, f, w, small):
    return {
        "u": Plan(u[0], 128, BF16, *UP_PLAN),
        "o": Plan(o[0], o[1], BF16, *ALL_PLAN),
        "s": Plan(s[0], s[1], BF16, *ALL_PLAN),
        "f": Plan(f[0], f[1], F32, *SHARE_PLAN),
        "w": Plan(w[1], w[2] // 3, BF16, *ALL_PLAN),
        "small": Plan(small[0], small[1], F32, *SHARE_PLAN),
    }


def whole(shape):
    zeros = (0,) * len(shape)
    return pl.BlockSpec(shape, lambda *at: zeros, pipeline_mode=pl.Buffered(1))


ANY = pl.BlockSpec(memory_space=pl.ANY)


def call(kernel, grid, ins, outs, scratch, name, collective_id=None):
    def spec(shape, block, index):
        if block is None:
            return whole(shape)
        return block if isinstance(block, pl.BlockSpec) else pl.BlockSpec(block, index)

    params = {} if collective_id is None else {
        "collective_id": collective_id, "has_side_effects": True
    }
    return pl.pallas_call(
        kernel,
        grid=grid,
        in_specs=[spec(array.shape, block, index) for array, block, index in ins],
        out_specs=[spec(shape, block, index) for shape, _, block, index in outs],
        out_shape=[jax.ShapeDtypeStruct(shape, dtype) for shape, dtype, _, _ in outs],
        scratch_shapes=scratch,
        compiler_params=pltpu.CompilerParams(
            dimension_semantics=("arbitrary",) * len(grid), vmem_limit_bytes=VMEM, **params
        ),
        name=name,
    )(*[array for array, _, _ in ins])


def carry_over(payload, logs, forward):
    n, index = lax.axis_size("seq"), lax.axis_index("seq")
    if n == 2:
        return lax.ppermute(payload, "seq", [(0, 1)] if forward else [(1, 0)])
    everything = lax.all_gather(payload, "seq")
    every_log = lax.all_gather(logs, "seq")
    total = jnp.zeros(payload.shape, F32)
    for k in range(n) if forward else reversed(range(n)):
        ahead = (k < index) if forward else (k > index)
        new = jnp.exp(every_log[k])[:, None, None] * total + everything[k].astype(F32)
        total = jnp.where(ahead, new, total)
    return total.astype(BF16)


def local(
    inputs,
    cotangent,
    mixer_gain,
    mixer_bias,
    query_weight,
    key_weight,
    value_weight,
    gate_weight,
    gate_bias,
    output_weight,
    projections,
    start_state,
    start_norm,
    feed_gain,
    feed_bias,
    up_weight,
    up_bias,
    down_weight,
    down_bias,
):
    _, tokens, width = inputs.shape
    heads, size, feats = projections.shape
    chunks = tokens // C
    tile = min(T, tokens)
    tiles = tokens // tile
    shards = lax.axis_size("seq")
    first = lax.axis_index("seq") == 0
    x = inputs.reshape(tokens, width)
    dout = cotangent.reshape(tokens, width)

    every_up = lax.all_gather(up_weight, "seq")
    every_down = lax.all_gather(down_weight, "seq")
    every_upb = lax.all_gather(up_bias.astype(F32), "seq").reshape(1, -1)
    hidden = every_upb.shape[1]

    turns = projections * (1.0 / (2.0 * math.pi))
    high = lax.reduce_precision(turns, 8, 7)
    rest = turns - high
    zeros = jnp.zeros_like(turns)

    def pair_blocks(part):
        left = jnp.concatenate([part[0::2], zeros[0::2]], axis=2)
        right = jnp.concatenate([zeros[0::2], part[1::2]], axis=2)
        return jnp.concatenate([left, right], axis=1)

    pcat = jnp.concatenate(
        [pair_blocks(high), pair_blocks(high), pair_blocks(rest)], axis=1
    ).astype(BF16)
    wg = jnp.tile(gate_weight, (1, LANES // heads))
    wgt = gate_weight.T
    gb = jnp.tile(gate_bias, LANES // heads)[None]
    gbt = jnp.broadcast_to(gate_bias[:, None], (heads, LANES))
    start_rows = start_state.transpose(0, 2, 1)
    norm_rows = jnp.broadcast_to(start_norm[:, None, :], start_rows.shape)
    even = (jnp.arange(heads) % 2 == 0)[:, None, None]
    start = jnp.concatenate(
        [jnp.where(even, start_rows, norm_rows), jnp.where(even, norm_rows, start_rows)], axis=1
    )
    start = jnp.where(first, start, 0.0)

    def rows(n, block_rows=C):
        return (block_rows, n), lambda i: (i, 0)

    def out_rows(n, dtype, block_rows=C):
        return ((tokens, n), dtype) + rows(n, block_rows)

    def const(array):
        return (array if array.ndim > 1 else array[None], None, None)

    def keep(shape, dtype):
        return (shape, dtype, None, None)

    wide = heads * LANES
    wider = heads * 2 * feats
    ml, uq, uk, rq, rk, qf, kf, v, gcol, grow, before, final, total = call(
        partial(features_kernel, heads),
        (chunks,),
        [
            (x,) + rows(width),
            const(mixer_gain),
            const(mixer_bias),
            const(query_weight),
            const(key_weight),
            const(value_weight),
            const(wg),
            const(wgt),
            const(gb),
            const(gbt),
            const(pcat),
            const(start),
        ],
        [
            out_rows(width, BF16),
            out_rows(width, BF16),
            out_rows(width, BF16),
            out_rows(width, F32),
            out_rows(width, F32),
            out_rows(wider, BF16),
            out_rows(wider, BF16),
            out_rows(width, BF16),
            out_rows(LANES, F32),
            ((4 * heads, tokens), F32, (4 * heads, C), lambda i: (0, i)),
            (
                (chunks, heads, LANES, 2 * feats),
                BF16,
                (1, heads, LANES, 2 * feats),
                lambda i: (i, 0, 0, 0),
            ),
            keep((heads, PAY, 2 * feats), BF16),
            keep((8, LANES), F32),
        ],
        [pltpu.VMEM((heads, LANES, 2 * feats), F32), pltpu.VMEM((1, LANES), F32)],
        "features",
    )
    logs = total[0, :heads]
    entry = carry_over(final, logs, True)
    state_block = (1, heads, LANES, 2 * feats)
    (num,) = call(
        partial(inner_kernel, heads),
        (chunks,),
        [
            (qf,) + rows(wider),
            (kf,) + rows(wider),
            (v,) + rows(width),
            (gcol,) + rows(LANES),
            (grow, (4 * heads, C), lambda i: (0, i)),
            (before, state_block, lambda i: (i, 0, 0, 0)),
        ],
        [out_rows(wide, F32)],
        [],
        "inner",
    )
    out, mg, fl, hl, pre, mix, br, a, adj_final, feed_sums, upbg = call(
        partial(feed_kernel, heads, shards),
        (tiles,),
        [
            (x,) + rows(width, tile),
            (dout,) + rows(width, tile),
            (qf,) + rows(wider, tile),
            (num,) + rows(wide, tile),
            (gcol,) + rows(LANES, tile),
            const(entry),
            const(output_weight),
            const(feed_gain),
            const(feed_bias),
            const(every_up),
            const(every_upb),
            const(every_down),
            const(down_bias),
        ],
        [
            out_rows(width, BF16, tile),
            out_rows(width, F32, tile),
            out_rows(width, BF16, tile),
            out_rows(hidden, BF16, tile),
            out_rows(hidden, BF16, tile),
            out_rows(width, BF16, tile),
            out_rows(width, BF16, tile),
            out_rows(wide, BF16, tile),
            keep((heads, PAY, 2 * feats), BF16),
            keep((24, width), F32),
            keep((8, hidden), F32),
        ],
        [
            pltpu.VMEM((heads, LANES, 2 * feats), F32),
            pltpu.VMEM((heads, LANES, 2 * feats), BF16),
        ],
        "feed",
    )
    after = carry_over(adj_final, logs, False)
    down_grad = tn(dout, hl).astype(BF16)
    up_grad = tn(fl, pre).astype(BF16)
    output_grad = tn(mix, br).astype(BF16)

    feed_three = jnp.sum(feed_sums.reshape(3, 8, width), axis=1)
    upb_grad = jnp.sum(upbg, axis=0)
    begin = adj_final.astype(F32) + jnp.exp(logs)[:, None, None] * after.astype(F32)
    begin = jnp.where(first, begin, 0.0)
    state_grad = begin[:, :64].astype(BF16).reshape(heads * 64, 2 * feats)
    norm_grad = 64.0 * begin[:, 64]

    hg = GROUP_HEADS
    groups = heads // hg
    comm = (lax.axis_size("dp"), lax.axis_size("seq")) == (16, 2)

    def back_rows(n, per_group=True):
        return (C, n), lambda g, i: (chunks - 1 - i, g if per_group else 0)

    def per_group(array, *shape):
        zeros = (0,) * (len(shape) - 1)
        return (array, shape, lambda g, i: (g,) + zeros)

    def hbm(array):
        return (array, ANY, None)

    ins = [
        (qf,) + back_rows(hg * 2 * feats),
        (kf,) + back_rows(hg * 2 * feats),
        (v,) + back_rows(hg * size),
        (uq,) + back_rows(hg * size),
        (uk,) + back_rows(hg * size),
        (rq,) + back_rows(hg * size),
        (rk,) + back_rows(hg * size),
        (a,) + back_rows(hg * LANES),
        (gcol,) + back_rows(LANES, False),
        (grow, (4 * heads, C), lambda g, i: (0, chunks - 1 - i)),
        (before, (1, hg, LANES, 2 * feats), lambda g, i: (chunks - 1 - i, g, 0, 0)),
        per_group(entry, hg, PAY, 2 * feats),
        per_group(after, hg, PAY, 2 * feats),
        per_group(pcat, hg // 2, LANES, 2 * feats),
        hbm(x),
        hbm(mg),
        hbm(ml),
        hbm(query_weight),
        hbm(key_weight),
        hbm(value_weight),
        const(jnp.pad(wgt, ((0, 16 - heads), (0, 0)))),
        const(mixer_gain),
    ]
    w_shape, small_shape = (groups, width, 3 * hg * size), (32, width)

    def result(shape, dtype):
        return (shape, dtype, ANY if comm else None, None)

    outs = [keep((tokens, width), F32), result(w_shape, BF16), result(small_shape, F32)]
    scratch = [
        pltpu.VMEM((hg, LANES, 2 * feats), F32),
        pltpu.VMEM((groups, tokens, 3 * hg * size), BF16),
        pltpu.VMEM((groups, 8, tokens), F32),
        pltpu.VMEM((tokens, width), BF16),
        pltpu.VMEM((tokens, width), F32),
        pltpu.VMEM((tokens, width), BF16),
        pltpu.VMEM((width, width), BF16),
        pltpu.VMEM((width, width), BF16),
        pltpu.VMEM((width, width), BF16),
        pltpu.SemaphoreType.DMA((10,)),
    ]
    if comm:
        half = hidden // 2
        up_halves = (up_grad[:, :half], up_grad[:, half:])
        down_halves = (down_grad[:, :half], down_grad[:, half:])
        up_down = jnp.concatenate(up_halves + down_halves)
        flat = jnp.concatenate(
            [feed_three, upb_grad.reshape(-1, width), norm_grad.reshape(-1, width)]
        )
        flat = jnp.pad(flat, ((0, 16 - flat.shape[0]), (0, 0)))
        ins += [hbm(up_down), hbm(output_grad), hbm(state_grad), hbm(flat)]
        outs += [
            result((up_down.shape[0] // 2, half), BF16),
            result(output_grad.shape, BF16),
            result(state_grad.shape, BF16),
            result(flat.shape, F32),
        ]
        plans = back_plans(
            up_down.shape, output_grad.shape, state_grad.shape, flat.shape, w_shape, small_shape
        )
        scratch += [
            pltpu.VMEM(up_down.shape, BF16),
            pltpu.VMEM(output_grad.shape, BF16),
            pltpu.VMEM(state_grad.shape, BF16),
            pltpu.VMEM(flat.shape, F32),
            pltpu.VMEM(w_shape, BF16),
            pltpu.VMEM(small_shape, F32),
            pltpu.VMEM((up_down.shape[0] // 2, half), BF16),
            pltpu.VMEM(output_grad.shape, BF16),
            pltpu.VMEM(state_grad.shape, BF16),
            pltpu.VMEM(flat.shape, F32),
            pltpu.VMEM(w_shape, BF16),
            pltpu.VMEM(small_shape, F32),
            pltpu.SemaphoreType.DMA((32,)),
        ]
        for _ in range(half // plans["u"].lanes):
            scratch += plans["u"].scratch()
        for name in ("f", "s", "o") + ("w",) * (3 * groups) + ("small",):
            scratch += plans[name].scratch()
    results = call(
        partial(back_kernel, heads, hg, chunks, comm),
        (groups, chunks),
        ins,
        outs,
        scratch,
        "back",
        1 if comm else None,
    )
    dx, sum_w, small = results[:3]
    if comm:
        sum_up_down, sum_o, sum_state, flat = results[3:]
        sum_up, sum_down = sum_up_down[:width], sum_up_down[width:]
        sum_feed = flat[0:3]
        sum_upb = flat[3 : 3 + hidden // width].reshape(-1)
        sum_upb = jnp.where(first, sum_upb[:half], sum_upb[half:])
        sum_norm = flat[3 + hidden // width :][:4].reshape(heads, 2 * feats)
    else:
        halves = lax.psum_scatter(
            jnp.stack([up_grad, down_grad]), "seq", scatter_dimension=2, tiled=True
        )
        upb_half = lax.psum_scatter(upb_grad, "seq", scatter_dimension=0, tiled=True)
        (sum_up, sum_down), sum_upb = lax.psum((halves, upb_half), "dp")
        sum_w, sum_o, sum_state, small, sum_norm, sum_feed = lax.psum(
            (sum_w, output_grad, state_grad, small, norm_grad, feed_three), ("dp", "seq")
        )
    sum_w = sum_w.reshape(groups, width, 3, hg * size).transpose(2, 1, 0, 3)
    sum_q, sum_k, sum_v = sum_w.reshape(3, width, width).astype(F32)
    sum_state = sum_state.reshape(heads, size, 2 * feats).astype(F32).transpose(0, 2, 1)
    return (
        out.reshape(inputs.shape),
        dx.reshape(inputs.shape),
        small[2 * heads],
        small[2 * heads + 1],
        sum_q,
        sum_k,
        sum_v,
        small[:heads].T,
        small[heads : 2 * heads, 0],
        sum_o.astype(F32),
        sum_state,
        sum_norm,
        sum_feed[0],
        sum_feed[1],
        sum_up.astype(F32),
        sum_upb,
        sum_down.astype(F32),
        sum_feed[2],
    )


class Links:
    def __init__(self):
        self.dp, self.seq = lax.axis_index("dp"), lax.axis_index("seq")
        core, y, z = self.dp % 2, (self.dp // 2) % 2, self.dp // 4
        self.y = y
        self.at = {"core": core, "x": self.seq, "y": y, "z": z, "plane": self.seq * 2 + y}

    size = {"core": 2, "x": 2, "y": 2, "z": 4, "plane": 4}

    def partner(self, group, step):
        dp, seq = self.dp, self.seq
        if group == "core":
            return (dp + 1 - 2 * self.at["core"], seq)
        if group == "x":
            return (dp, 1 - seq)
        if group == "y":
            return (dp + 2 - 4 * self.y, seq)
        target = (self.at[group] + step) % 4
        if group == "z":
            return (dp % 4 + 4 * target, seq)
        return (dp + 2 * (target % 2 - self.y), target // 2)

    def greet(self, groups):
        barrier = pltpu.get_barrier_semaphore()
        count = 0
        for group in groups:
            for step in range(1, self.size[group]):
                pl.semaphore_signal(
                    barrier, inc=1, device_id=self.partner(group, step), device_id_type=MESH
                )
                count += 1
        pl.semaphore_wait(barrier, count)


class Plan:
    def __init__(self, rows, lanes, dtype, scatter, gather, share=()):
        self.scatter, self.gather, self.share = scatter, gather, share
        self.rows, self.lanes, self.dtype = rows, lanes, dtype
        self.groups = scatter + gather + share
        self.stages = len(self.groups)

    def scratch(self):
        shapes = []
        rows = self.rows
        for i, group in enumerate(self.scatter):
            n = Links.size[group]
            rows //= n
            shapes.append(pltpu.VMEM((n - 1, rows, self.lanes), self.dtype))
            if i < len(self.scatter) - 1:
                shapes.append(pltpu.VMEM((rows, self.lanes), self.dtype))
        for i, group in enumerate(self.share):
            shapes.append(pltpu.VMEM((Links.size[group], rows, self.lanes), self.dtype))
            if i < len(self.share) - 1:
                shapes.append(pltpu.VMEM((rows, self.lanes), self.dtype))
        for group in self.groups:
            n = Links.size[group]
            shapes.append(pltpu.SemaphoreType.DMA((n - 1,)))
            shapes.append(pltpu.SemaphoreType.DMA((n - 1,)))
        return shapes


class Stream:
    def __init__(self, plan, links, source, out, scratch):
        self.plan, self.links, self.source, self.out = plan, links, source, out
        scratch = list(scratch)
        self.landing, self.parts = [], [source]
        summed = plan.scatter + plan.share
        for i in range(len(summed)):
            self.landing.append(scratch.pop(0))
            if i < len(summed) - 1:
                self.parts.append(scratch.pop(0))
        self.sems = [(scratch.pop(0), scratch.pop(0)) for _ in range(plan.stages)]
        self.places = {}
        rows, start = out.shape[0], 0
        for group in plan.scatter:
            if group in plan.gather:
                rows //= Links.size[group]
                self.places[group] = (start, rows)
                start = start + links.at[group] * rows
        self.final = (start, rows)

    def copies(self, stage, sending):
        plan, links = self.plan, self.links
        group = plan.groups[stage]
        n, me = Links.size[group], links.at[group]
        sends, recvs = self.sems[stage]
        made = []
        for step in range(1, n):
            target, origin = (me + step) % n, (me + n - step) % n
            if plan.share:
                source = self.parts[stage]
                lands = self.landing[stage].at[me]
                arrives = self.landing[stage].at[origin]
            elif stage < len(plan.scatter):
                landing = self.landing[stage]
                rows = landing.shape[1]
                source = self.parts[stage].at[pl.ds(pl.multiple_of(target * rows, 8), rows)]
                arrives = lands = landing.at[step - 1]
            else:
                start, rows = self.places[group]
                mine_at = pl.multiple_of(start + me * rows, 8)
                theirs_at = pl.multiple_of(start + origin * rows, 8)
                source = lands = self.out.at[pl.ds(mine_at, rows)]
                arrives = self.out.at[pl.ds(theirs_at, rows)]
            made.append(
                pltpu.make_async_remote_copy(
                    src_ref=source if sending else arrives,
                    dst_ref=lands if sending else arrives,
                    send_sem=sends.at[step - 1],
                    recv_sem=recvs.at[step - 1],
                    device_id=links.partner(group, step),
                    device_id_type=MESH,
                )
            )
        return made

    def start(self, stage):
        for copy in self.copies(stage, True):
            copy.start()

    def finish(self, stage):
        plan = self.plan
        for copy in self.copies(stage, False):
            copy.wait_recv()
        if plan.share:
            landing, me = self.landing[stage], self.links.at[plan.groups[stage]]
            landing[me] = self.parts[stage][...]
            total = landing[0]
            for k in range(1, landing.shape[0]):
                total = total + landing[k]
            if stage + 1 < plan.stages:
                self.parts[stage + 1][...] = total
            else:
                self.out[...] = total
            return
        if stage >= len(plan.scatter):
            return
        landing = self.landing[stage]
        arrivals, rows, _ = landing.shape
        own = pl.multiple_of(self.links.at[plan.groups[stage]] * rows, 8)
        total = self.parts[stage][pl.ds(own, rows), :].astype(F32)
        for step in range(arrivals):
            total = total + landing[step].astype(F32)
        total = total.astype(landing.dtype)
        if stage + 1 < len(plan.scatter):
            self.parts[stage + 1][...] = total
        else:
            start, rows = self.final
            self.out[pl.ds(pl.multiple_of(start, 8), rows), :] = total

    def drain(self):
        for stage in range(self.plan.stages):
            for copy in self.copies(stage, True):
                copy.wait_send()


UP_PLAN = (("core", "x", "y", "z"), ("z", "y", "core"))
ALL_PLAN = (("core", "plane", "z"), ("z", "plane", "core"))
SHARE_PLAN = ((), (), ("core", "plane", "z"))


def solution(mesh):
    tokens = P("dp", "seq", None)
    columns = P(None, "seq")
    return jax.shard_map(
        local,
        mesh=mesh,
        in_specs=(tokens, tokens) + (P(),) * 13 + (columns, P("seq"), columns, P()),
        out_specs=(tokens, tokens) + (P(),) * 12 + (columns, P("seq"), columns, P()),
        check_vma=False,
    )
```

```python
from functools import partial
import math

import jax
import jax.numpy as jnp
from jax import lax
from jax.experimental import pallas as pl
from jax.experimental.pallas import tpu as pltpu
from jax.sharding import PartitionSpec as P

F32 = jnp.float32
BF16 = jnp.bfloat16
EPS_NORM = 1e-05
EPS_UNIT = 1e-06
GUARD = 0.0625
MESH = pl.DeviceIdType.MESH
VMEM = 56 * 1024 * 1024

C = 128
T = 256
HB = 256
GROUP_HEADS = 4
LANES = 128

SIN = (3.14158202, -5.16714278, 2.54189892, -0.55463591)
COS = (0.99999995, -4.93479286, 4.05841191, -1.33188012, 0.21969671)
ERF = (0.319381530, -0.356563782, 1.781477937, -1.821255978, 1.330274429)
ERF_P = 0.2316419
INV_SQRT_2PI = 0.3989422804014327


def nn(a, b):
    return lax.dot_general(a, b, (((1,), (0,)), ((), ())), preferred_element_type=F32)


def nt(a, b):
    return lax.dot_general(a, b, (((1,), (1,)), ((), ())), preferred_element_type=F32)


def tn(a, b):
    return lax.dot_general(a, b, (((0,), (0,)), ((), ())), preferred_element_type=F32)


def thirds(x):
    high = x.astype(BF16)
    rest = x - high.astype(F32)
    middle = rest.astype(BF16)
    return high, middle, (rest - middle.astype(F32)).astype(BF16)


def rows_up_to(x):
    n = x.shape[0]
    tri = jnp.where(iota((n, n), 0) >= iota((n, n), 1), 1.0, 0.0).astype(BF16)
    return nn(jnp.concatenate([tri] * 3, axis=1), jnp.concatenate(thirds(x), axis=0))


def lanes_up_to(x):
    n = x.shape[1]
    tri = jnp.where(iota((n, n), 0) <= iota((n, n), 1), 1.0, 0.0).astype(BF16)
    return nn(jnp.concatenate(thirds(x), axis=1), jnp.concatenate([tri] * 3, axis=0))


def iota(shape, dim):
    return lax.broadcasted_iota(jnp.int32, shape, dim)


def log_sigmoid(x):
    return jnp.minimum(x, 0.0) - jnp.log(1.0 + jnp.exp(-jnp.abs(x)))


def normalize(x):
    centred = x - jnp.mean(x, axis=-1, keepdims=True)
    scale = lax.rsqrt(jnp.mean(centred * centred, axis=-1, keepdims=True) + EPS_NORM)
    return centred * scale, scale


def normalize_back(grad, gain, xhat, scale):
    inner = grad * gain
    mean_inner = jnp.mean(inner, axis=-1, keepdims=True)
    mean_both = jnp.mean(inner * xhat, axis=-1, keepdims=True)
    return scale * (inner - mean_inner - xhat * mean_both)


def fold_rows(x):
    return jnp.sum(x.reshape(x.shape[0] // 8, 8, x.shape[1]), axis=0)


def block_ones():
    return jnp.where(
        iota((LANES, LANES), 0) // 64 == iota((LANES, LANES), 1) // 64, 1.0, 0.0
    ).astype(BF16)


def head_sums(x):
    high = x.astype(BF16)
    rest = (x - high.astype(F32)).astype(BF16)
    ones = block_ones()
    return nn(jnp.concatenate([high, rest], axis=1), jnp.concatenate([ones, ones], axis=0))


def lower_half(shape):
    return iota(shape, 1) < 64


def mine(h, lower):
    return lower if h % 2 == 0 else jnp.logical_not(lower)


def column(block, index, rows, width):
    return jnp.broadcast_to(block[:, index : index + 1], (rows, width))


def sin_cos(turns, scale):
    r = turns - jnp.floor(turns + 0.5)
    r2 = r * r
    s = (((SIN[3] * r2 + SIN[2]) * r2 + SIN[1]) * r2 + SIN[0]) * r
    k = 2.0 * scale
    c = (((k * COS[4] * r2 + k * COS[3]) * r2 + k * COS[2]) * r2 + k * COS[1]) * r2 + k * COS[0]
    return s * c, scale - (k * s) * s


class Links:
    def __init__(self):
        self.dp, self.seq = lax.axis_index("dp"), lax.axis_index("seq")
        core, y, z = self.dp % 2, (self.dp // 2) % 2, self.dp // 4
        self.y = y
        self.at = {"core": core, "y": y, "z": z, "plane": self.seq * 2 + y}
        self.at["xr"] = 0

    size = {"core": 2, "xr": 2, "y": 2, "z": 4, "plane": 4}

    def partner(self, group, step):
        dp, seq = self.dp, self.seq
        if group == "core":
            return (dp + 1 - 2 * self.at["core"], seq)
        if group == "xr":
            return (dp, 1 - seq)
        if group == "y":
            return (dp + 2 - 4 * self.y, seq)
        target = (self.at[group] + step) % 4
        if group == "z":
            return (dp % 4 + 4 * target, seq)
        return (dp + 2 * (target % 2 - self.y), target // 2)

    def greet(self, groups):
        barrier = pltpu.get_barrier_semaphore()
        count = 0
        for group in groups:
            for step in range(1, self.size[group]):
                pl.semaphore_signal(
                    barrier, inc=1, device_id=self.partner(group, step), device_id_type=MESH
                )
                count += 1
        pl.semaphore_wait(barrier, count)


class Plan:
    def __init__(self, rows, lanes, dtype, scatter, gather, share=(), pre=()):
        self.pre = pre
        self.scatter, self.gather, self.share = scatter, gather, share
        self.rows, self.lanes, self.dtype = rows, lanes, dtype
        self.groups = scatter + gather + share
        self.left = rows
        for group in scatter:
            self.left //= Links.size[group]
        self.stages = len(self.groups)

    def scratch(self):
        shapes = []
        rows = self.rows
        for i, group in enumerate(self.scatter):
            n = Links.size[group]
            rows //= n
            shapes.append(pltpu.VMEM((n - 1, rows, self.lanes), self.dtype))
            if i < len(self.scatter) - 1:
                shapes.append(pltpu.VMEM((rows, self.lanes), self.dtype))
        for i, group in enumerate(self.share):
            shapes.append(pltpu.VMEM((Links.size[group], rows, self.lanes), self.dtype))
            if i < len(self.share) - 1:
                shapes.append(pltpu.VMEM((rows, self.lanes), self.dtype))
        for group in self.groups:
            n = Links.size[group]
            shapes.append(pltpu.SemaphoreType.DMA((n - 1,)))
            shapes.append(pltpu.SemaphoreType.DMA((n - 1,)))
        return shapes


class Stream:
    def __init__(self, plan, links, source, out, scratch):
        self.plan, self.links, self.source, self.out = plan, links, source, out
        scratch = list(scratch)
        self.landing, self.parts = [], [source]
        summed = plan.scatter + plan.share
        for i in range(len(summed)):
            self.landing.append(scratch.pop(0))
            if i < len(summed) - 1:
                self.parts.append(scratch.pop(0))
        self.sems = [(scratch.pop(0), scratch.pop(0)) for _ in range(plan.stages)]
        self.places = {}
        rows, start = out.shape[0], 0
        for group in plan.pre + plan.scatter:
            if group in plan.gather:
                rows //= Links.size[group]
                self.places[group] = (start, rows)
                start = start + links.at[group] * rows
        self.final = (start, rows)

    def copies(self, stage, sending):
        plan, links = self.plan, self.links
        group = plan.groups[stage]
        n, me = Links.size[group], links.at[group]
        sends, recvs = self.sems[stage]
        made = []
        for step in range(1, n):
            target, origin = (me + step) % n, (me + n - step) % n
            if plan.share:
                source = self.parts[stage]
                lands = self.landing[stage].at[me]
                arrives = self.landing[stage].at[origin]
            elif stage < len(plan.scatter):
                landing = self.landing[stage]
                rows = landing.shape[1]
                source = self.parts[stage].at[pl.ds(pl.multiple_of(target * rows, 8), rows)]
                arrives = lands = landing.at[step - 1]
            else:
                start, rows = self.places[group]
                mine_at = pl.multiple_of(start + me * rows, 8)
                theirs_at = pl.multiple_of(start + origin * rows, 8)
                source = lands = self.out.at[pl.ds(mine_at, rows)]
                arrives = self.out.at[pl.ds(theirs_at, rows)]
            made.append(
                pltpu.make_async_remote_copy(
                    src_ref=source if sending else arrives,
                    dst_ref=lands if sending else arrives,
                    send_sem=sends.at[step - 1],
                    recv_sem=recvs.at[step - 1],
                    device_id=links.partner(group, step),
                    device_id_type=MESH,
                )
            )
        return made

    def start(self, stage):
        if stage == 0 and not (self.plan.scatter or self.plan.share):
            start, rows = self.final
            self.out[pl.ds(pl.multiple_of(start, 8), rows), :] = self.source[...]
        for copy in self.copies(stage, True):
            copy.start()

    def finish(self, stage):
        plan = self.plan
        for copy in self.copies(stage, False):
            copy.wait_recv()
        if plan.share:
            landing, me = self.landing[stage], self.links.at[plan.groups[stage]]
            landing[me] = self.parts[stage][...]
            total = landing[0]
            for k in range(1, landing.shape[0]):
                total = total + landing[k]
            if stage + 1 < plan.stages:
                self.parts[stage + 1][...] = total
            else:
                self.out[...] = total
            return
        if stage >= len(plan.scatter):
            return
        landing = self.landing[stage]
        arrivals, rows, _ = landing.shape
        own = pl.multiple_of(self.links.at[plan.groups[stage]] * rows, 8)
        total = self.parts[stage][pl.ds(own, rows), :].astype(F32)
        for step in range(arrivals):
            total = total + landing[step].astype(F32)
        total = total.astype(landing.dtype)
        if stage + 1 < len(plan.scatter):
            self.parts[stage + 1][...] = total
        else:
            start, rows = self.final
            self.out[pl.ds(pl.multiple_of(start, 8), rows), :] = total

    def drain(self):
        for stage in range(self.plan.stages):
            for copy in self.copies(stage, True):
                copy.wait_send()


ALL_PLAN = (("core", "plane", "z"), ("z", "plane", "core"))
SHARE_PLAN = ((), (), ("core", "plane", "z"))


def pick_row(block, index):
    return jnp.sum(jnp.where(iota(block.shape, 0) == index, block, 0.0), axis=0, keepdims=True)


def grow_state(rows, norm, h):
    rows = rows.astype(F32)
    norm = jnp.broadcast_to(norm, rows.shape)
    return jnp.concatenate([rows, norm] if h % 2 == 0 else [norm, rows], axis=0)


def state_part(state, h):
    return state[0:64] if h % 2 == 0 else state[64:128]


def norm_part(state, h):
    return state[64:65] if h % 2 == 0 else state[0:1]


def pack_states(states, out_ref):
    heads = len(states)
    for h, state in enumerate(states):
        out_ref[64 * h : 64 * (h + 1), :] = state_part(state, h).astype(BF16)
    norms = [norm_part(state, h) for h, state in enumerate(states)]
    pad = jnp.zeros((16 - heads, states[0].shape[1]), F32)
    out_ref[64 * heads : 64 * heads + 16, :] = jnp.concatenate(norms + [pad], axis=0).astype(BF16)


def projection_blocks(proj_ref, p, scale):
    parts = [proj_ref[2 * p + j] * scale for j in range(2)]
    highs = [part.astype(BF16) for part in parts]
    rests = [(part - high.astype(F32)).astype(BF16) for part, high in zip(parts, highs)]
    zero = jnp.zeros(highs[0].shape, BF16)

    def diagonal(pair):
        return jnp.concatenate(
            [
                jnp.concatenate([pair[0], zero], axis=1),
                jnp.concatenate([zero, pair[1]], axis=1),
            ],
            axis=0,
        )

    return diagonal(highs), diagonal(rests)


def gate_rows(wg):
    eye = jnp.where(iota((16, wg.shape[1]), 0) == iota((16, wg.shape[1]), 1), 1.0, 0.0)
    return nt(eye.astype(BF16), wg).astype(BF16)


class Taker:
    def __init__(self, refs):
        self.refs = list(refs)

    def __call__(self, n):
        taken = self.refs[:n]
        del self.refs[:n]
        return taken


class Board:
    def __init__(self, links, take, store_sems):
        self.links, self.take, self.store_sems = links, take, store_sems
        self.entries = []

    def add(self, plan, source, out, final, ticks):
        stream = Stream(plan, self.links, source, out, self.take(len(plan.scratch())))
        self.entries.append((stream, ticks, out, final))

    def store(self, k):
        _, _, out, final = self.entries[k]
        return pltpu.make_async_copy(out, final, self.store_sems.at[k])

    def advance(self, now):
        for k, (stream, ticks, _, final) in enumerate(self.entries):
            for stage, tick in enumerate(ticks):
                if tick == now:
                    if stage > 0:
                        stream.finish(stage - 1)
                    if stage < stream.plan.stages:
                        stream.start(stage)
                    elif final is not None:
                        self.store(k).start()

    def last(self):
        return max(ticks[-1] for _, ticks, _, _ in self.entries)

    def drain(self):
        for k, (stream, _, _, final) in enumerate(self.entries):
            stream.drain()
            if final is not None:
                self.store(k).wait()


def features_kernel(heads, chunks, comm, *refs):
    take = Taker(refs)
    x_ref, gain_ref, bias_ref, wq_ref, wk_ref, wv_ref = take(6)
    gate_ref, gb_smem, proj_ref, start_ref, start_norm_ref = take(5)
    up_hbm, down_hbm, upb_ref = take(3) if comm else (None,) * 3
    ml_ref, uq_ref, uk_ref, rq_ref, rk_ref, qf_ref, kf_ref, v_ref = take(8)
    gcol_ref, grow_ref, before_ref, n_ref = take(4)
    if comm:
        entry_ref, upo_hbm, downo_hbm, upbs_ref = take(4)
    else:
        final_ref, total_ref = take(2)
    state, carry, qf_s, kf_s, v_s, gcol_s, grow_s, before_s = take(8)
    wg_ref, wgt_ref, gb_ref, gbt_ref, pcat_ref = take(5)
    step = pl.program_id(0)
    chunk = lax.rem(step, chunks)

    if comm:
        sent, landed, upb_landed, sends, recvs = take(5)
        links = Links()
        core = links.at["core"]
        half = up_hbm.shape[0] // 2
        own_rows = pl.ds(pl.multiple_of(core * half, 16), half)
        other_rows = pl.ds(pl.multiple_of((1 - core) * half, 16), half)

        def remote(k, sending):
            group = "core" if k >= 4 else "xr"
            if k == 2:
                source, lands = upb_ref, upb_landed
            elif k == 3:
                source, lands = sent, landed
            else:
                into = (upo_hbm, downo_hbm)[k % 2].at[own_rows]
                source, lands = (up_hbm, down_hbm)[k % 2].at[own_rows], into
                if k >= 4:
                    source = into
                    if not sending:
                        lands = (upo_hbm, downo_hbm)[k % 2].at[other_rows]
            return pltpu.make_async_remote_copy(
                src_ref=source if sending else lands,
                dst_ref=lands,
                send_sem=sends.at[k],
                recv_sem=recvs.at[k],
                device_id=links.partner(group, 1),
                device_id_type=MESH,
            )

        @pl.when(step == 0)
        def _():
            links.greet(("core", "xr"))
            for k in (0, 1, 2):
                remote(k, True).start()

        @pl.when(step == chunks)
        def _():
            remote(3, True).start()

        @pl.when(step == chunks + chunks // 2)
        def _():
            for k in (0, 1):
                remote(k, False).wait_recv()
                remote(k + 4, True).start()

    @pl.when(step == 0)
    def _():
        carry[...] = jnp.zeros_like(carry)
        is_first = lax.axis_index("seq") == 0
        wg = gate_ref[...]
        spread = jnp.where(iota((heads, LANES), 0) == iota((heads, LANES), 1) % heads, 1.0, 0.0)
        wg_ref[...] = nn(wg, spread.astype(BF16)).astype(BF16)
        wgt_ref[...] = gate_rows(wg)[0:heads]
        lane_head = iota((1, LANES), 1) % heads
        row_head = iota((heads, LANES), 0)
        gb = jnp.zeros((1, LANES), F32)
        gbt = jnp.zeros((heads, LANES), F32)
        for h in range(heads):
            gb = jnp.where(lane_head == h, gb_smem[h], gb)
            gbt = jnp.where(row_head == h, gb_smem[h], gbt)
            begin = start_ref[h].T
            norm = jnp.broadcast_to(start_norm_ref[h : h + 1, :], begin.shape)
            both = [begin, norm] if h % 2 == 0 else [norm, begin]
            state[h] = jnp.where(is_first, jnp.concatenate(both, axis=0), 0.0)
        gb_ref[...] = gb
        gbt_ref[...] = gbt
        for p in range(heads // 2):
            high, rest = projection_blocks(proj_ref, p, 1.0 / (2.0 * math.pi))
            pcat_ref[p, 0:LANES, :] = high
            pcat_ref[p, LANES : 2 * LANES, :] = high
            pcat_ref[p, 2 * LANES : 3 * LANES, :] = rest

    lower = lower_half((C, LANES))

    @pl.when(step < chunks)
    def _():
        xhat, _ = normalize(x_ref[...].astype(F32))
        ml = (xhat * gain_ref[...] + bias_ref[...]).astype(BF16)
        ml_ref[...] = ml
        q = nn(ml, wq_ref[...])
        k = nn(ml, wk_ref[...])
        v = nn(ml, wv_ref[...])
        v_low = v.astype(BF16)
        v_ref[...] = v_low
        v_s[chunk] = v_low
        logit = nn(ml, wg_ref[...]) + gb_ref[...]
        keep = log_sigmoid(logit)
        gain_in = keep - logit
        decay = rows_up_to(keep)
        total = decay[C - 1 : C, :]
        group = iota((C, LANES), 1) // 8
        coef = total - decay + gain_in
        packed = jnp.where(group == 0, decay, coef)
        packed = jnp.where(group == 2, carry[...] + decay, packed)
        packed = jnp.where(group == 6, jnp.broadcast_to(carry[...], (C, LANES)), packed)
        packed = jnp.where(group == 7, jnp.broadcast_to(total, (C, LANES)), packed)
        gcol_ref[...] = packed
        gcol_s[chunk] = packed
        carry[...] = carry[...] + total
        if not comm:
            total_ref[...] = jnp.broadcast_to(carry[...], total_ref.shape)
        logit_row = nt(wgt_ref[...], ml) + gbt_ref[...][:, 0:1]
        keep_row = log_sigmoid(logit_row)
        decay_row = lanes_up_to(keep_row)
        rows = jnp.concatenate(
            [
                keep_row - logit_row - decay_row,
                decay_row,
                jax.nn.sigmoid(logit_row),
                jax.nn.sigmoid(-logit_row),
            ],
            axis=0,
        )
        grow_ref[...] = rows
        grow_s[chunk] = rows

        ftr_scale = 1.0 / math.sqrt(LANES)
        for p in range(heads // 2):
            lanes = slice(LANES * p, LANES * (p + 1))
            both = jnp.concatenate([q[:, lanes], k[:, lanes]], axis=0)
            scale = lax.rsqrt(head_sums(both * both) + EPS_UNIT)
            unit = both * scale
            high = unit.astype(BF16)
            rest = (unit - high.astype(F32)).astype(BF16)
            uq_ref[:, lanes] = high[:C]
            uk_ref[:, lanes] = high[C:]
            rq_ref[:, lanes] = scale[:C]
            rk_ref[:, lanes] = scale[C:]
            turns = nn(jnp.concatenate([high, rest, high], axis=1), pcat_ref[p])
            s, c = sin_cos(turns, ftr_scale)
            s = s.astype(BF16)
            c = c.astype(BF16)
            for j in range(2):
                h = 2 * p + j
                half_lanes = slice(LANES * j, LANES * (j + 1))
                feats = jnp.concatenate([s[:, half_lanes], c[:, half_lanes]], axis=1)
                place = slice(256 * h, 256 * (h + 1))
                qf_ref[:, place] = feats[:C]
                qf_s[chunk, :, place] = feats[:C]
                kf = feats[C:]
                kf_ref[:, place] = kf
                kf_s[chunk, :, place] = kf
                values = jnp.where(mine(h, lower), v[:, lanes], 1.0)
                weighted = (values * jnp.exp(column(coef, h, C, LANES))).astype(BF16)
                now = state[h]
                now_low = now.astype(BF16)
                before_ref[0, h] = now_low
                before_s[chunk, h] = now_low
                state[h] = jnp.exp(total[:, h : h + 1]) * now + tn(weighted, kf)

    @pl.when(step == chunks - 1)
    def _():
        pack_states([state[h] for h in range(heads)], sent if comm else final_ref)

    @pl.when(step >= chunks)
    def _():
        causal = iota((C, C), 0) >= iota((C, C), 1)
        gcol = gcol_s[chunk]
        for h in range(heads):
            qf = qf_s[chunk, :, 256 * h : 256 * (h + 1)]
            kf = kf_s[chunk, :, 256 * h : 256 * (h + 1)]
            p = h // 2
            v = v_s[chunk, :, LANES * p : LANES * (p + 1)].astype(F32)
            values = jnp.where(mine(h, lower), v, 1.0).astype(BF16)
            decay = column(gcol, h, C, LANES)
            pairs = jnp.where(causal, jnp.exp(decay + grow_s[chunk, h : h + 1, :]), 0.0)
            both = nt(qf, jnp.concatenate([kf, before_s[chunk, h]], axis=0))
            weights = (both[:, :C] * pairs).astype(BF16)
            n_ref[:, LANES * h : LANES * (h + 1)] = (
                nn(weights, values) + jnp.exp(decay) * both[:, C:]
            )

    if comm:
        @pl.when(step == 2 * chunks - 1)
        def _():
            for k in (2, 3, 4, 5):
                remote(k, False).wait_recv()
            later = links.seq == 1
            entry_ref[...] = jnp.where(later, landed[...].astype(F32), 0.0).astype(BF16)
            upbs_ref[0:1, :] = upb_ref[...]
            upbs_ref[1:2, :] = upb_landed[...]
            for k in range(6):
                remote(k, True).wait_send()


def feed_kernel(heads, tiles, pairs, comm, *refs):
    take = Taker(refs)
    x_ref, qf_hbm, n_ref, gcol_ref, entry_ref, wo_ref = take(6)
    gain_ref, bias_ref, downb_ref, upb_ref, dout_hbm = take(5)
    weights_hbm = take(4 if comm else 2)
    out_ref, mg_ref, a_ref = take(3)
    if comm:
        usum_hbm, *late_refs = take(1 + len(FEED_STAGES) - 1)
        os_ref, flat_ref, after_ref = take(3)
    else:
        upg_ref, downg_ref, upbg_ref, o_ref, final_ref, sums_out = take(6)
    entry, adj, middle_s, num_s, den_s, fl_s, mix_s, br_s = take(8)
    acc_s, fg_s, dout_s, up_s, down_s, hid_s, pre_s, sums_s, load_sems = take(9)
    step = pl.program_id(0)
    tokens, width = middle_s.shape
    rows = x_ref.shape[0]
    shards, _, shard_width = up_s.shape
    hb = hid_s.shape[1] // 2
    (qf_s,) = take(1)
    loads = [
        (qf_hbm.at[pl.ds(rows * t, rows)], qf_s.at[pl.ds(rows * t, rows)]) for t in range(tiles)
    ]
    loads += [(dout_hbm, dout_s)]
    if comm:
        up_own, up_other, down_own, down_other = weights_hbm
        loads += [(up_own, up_s.at[0]), (up_other, up_s.at[1])]
        loads += [(down_own, down_s.at[0]), (down_other, down_s.at[1])]
        u_src, usum_s, upbg_s, sent, landed, sends, recvs, store_sems = take(8)
        links = Links()
        board = Board(links, take, store_sems)
        for j, (plan, ticks) in enumerate(zip(feed_plans(hb), FEED_TICKS)):
            if j == 0:
                board.add(plan, u_src.at[j], usum_s, usum_hbm, ticks)
            else:
                board.add(plan, u_src.at[j], late_refs[j - 1], None, ticks)

        def exchange():
            return pltpu.make_async_remote_copy(
                src_ref=sent,
                dst_ref=landed,
                send_sem=sends,
                recv_sem=recvs,
                device_id=links.partner("xr", 1),
                device_id_type=MESH,
            )
    else:
        upbg_s = upbg_ref
        loads += [(weights_hbm[0], up_s), (weights_hbm[1], down_s)]

    def load(k):
        return pltpu.make_async_copy(loads[k][0], loads[k][1], load_sems.at[k])

    @pl.when(step == 0)
    def _():
        for k in range(len(loads)):
            load(k).start()
        adj[...] = jnp.zeros_like(adj)
        sums_s[...] = jnp.zeros_like(sums_s)
        norms = entry_ref[64 * heads : 64 * heads + 16, :].astype(F32)
        for h in range(heads):
            grown = grow_state(entry_ref[64 * h : 64 * (h + 1), :], norms[h : h + 1], h)
            entry[h] = grown.astype(BF16)
        if comm:
            links.greet(("core", "xr", "y", "z"))

    lower = lower_half((rows, LANES))

    @pl.when(step < tiles)
    def _():
        for t in range(tiles):
            pl.when(step == t)(load(t).wait)
        here = pl.ds(pl.multiple_of(step * rows, rows), rows)
        gcol = gcol_ref[...]
        mixed = []
        for p in range(heads // 2):
            lanes = slice(LANES * p, LANES * (p + 1))
            both = []
            for h in (2 * p, 2 * p + 1):
                far = nt(qf_s[here, 256 * h : 256 * (h + 1)], entry[h])
                far = far * jnp.exp(column(gcol, 16 + h, rows, LANES))
                both.append(n_ref[:, LANES * h : LANES * (h + 1)] + far)
            num = jnp.where(lower, both[0], both[1])
            den = pltpu.roll(jnp.where(lower, both[1], both[0]), 64, 1)
            num_s[here, lanes] = num
            den_s[here, lanes] = den
            mixed.append(num * lax.rsqrt(den * den + GUARD))
        mixed = jnp.concatenate(mixed, axis=1).astype(BF16)
        mix_s[here, :] = mixed
        middle = x_ref[...].astype(F32) + nn(mixed, wo_ref[...])
        middle_s[here, :] = middle
        acc_s[here, :] = middle + downb_ref[...]
        fg_s[here, :] = jnp.zeros_like(middle)
        xhat, _ = normalize(middle)
        fl_s[here, :] = (xhat * gain_ref[...] + bias_ref[...]).astype(BF16)

    @pl.when(step == tiles)
    def _():
        for k in range(tiles, len(loads)):
            load(k).wait()

    @pl.when(jnp.logical_and(step >= tiles, step < tiles + pairs))
    def _():
        j = step - tiles
        blocks = []
        for s in range(2):
            if comm:
                shard, off = s, pl.multiple_of(j * hb, hb)
            else:
                at = (2 * j + s) * hb
                shard, off = at // shard_width, pl.multiple_of(at % shard_width, hb)
            blocks.append((shard, pl.ds(off, hb)))
        ups = [up_s[shard, :, cols] for shard, cols in blocks]
        downs = [down_s[shard, :, cols] for shard, cols in blocks]
        up = jnp.concatenate(ups, axis=1)
        down = jnp.concatenate(downs, axis=1)
        if comm:
            upb = jnp.concatenate(
                [upb_ref[s : s + 1, cols] for s, (_, cols) in enumerate(blocks)], axis=1
            )
        else:
            upb = jnp.concatenate([upb_ref[shard, :, cols] for shard, cols in blocks], axis=1)
        for r in range(tokens // rows):
            if comm and r % 2 == 0:
                for k in range(pairs):
                    pl.when(j == k)(partial(board.advance, 2 * k + r // 2))
            here = slice(rows * r, rows * (r + 1))
            feed_low = fl_s[here, :]
            pre = nn(feed_low, up) + upb
            pre_grad = nn(dout_s[here, :], down)
            t = 1.0 / (1.0 + ERF_P * jnp.abs(pre))
            bell = INV_SQRT_2PI * jnp.exp(-0.5 * pre * pre)
            tail = ((((ERF[4] * t + ERF[3]) * t + ERF[2]) * t + ERF[1]) * t + ERF[0]) * t * bell
            phi = jnp.where(pre >= 0.0, 1.0 - tail, tail)
            hidden = (pre * phi).astype(BF16)
            pre_low = (pre_grad * (phi + pre * bell)).astype(BF16)
            hid_s[here, :] = hidden
            pre_s[here, :] = pre_low
            acc_s[here, :] += nt(hidden, down)
            fg_s[here, :] += nt(pre_low, up)
        up_grad = tn(fl_s[...], pre_s[...]).astype(BF16)
        down_grad = tn(dout_s[...], hid_s[...]).astype(BF16)
        bias_grad = nn(jnp.ones((16, tokens), BF16), pre_s[...])[0:1]
        for s, (shard, cols) in enumerate(blocks):
            part = slice(hb * s, hb * (s + 1))
            upbg_s[shard, :, cols] = bias_grad[:, part]
            if comm:
                u_src[j, width * s : width * (s + 1), :] = up_grad[:, part]
                u_src[j, width * (2 + s) : width * (3 + s), :] = down_grad[:, part]
            else:
                upg_ref[shard, :, cols] = up_grad[:, part]
                downg_ref[shard, :, cols] = down_grad[:, part]

    @pl.when(step >= tiles + pairs)
    def _():
        tile = step - tiles - pairs

        if comm:
            for t in range(tiles):
                pl.when(tile == t)(partial(board.advance, 2 * pairs + t))
        here = pl.ds(pl.multiple_of(tile * rows, rows), rows)
        gcol = gcol_ref[...]
        dout = dout_s[here, :].astype(F32)
        out_ref[...] = acc_s[here, :].astype(BF16)
        feed_grad = fg_s[here, :]
        xhat, scale = normalize(middle_s[here, :])
        sums_s[0:8, :] += fold_rows(feed_grad * xhat)
        sums_s[8:16, :] += fold_rows(feed_grad)
        sums_s[16:24, :] += fold_rows(dout)
        middle_grad = dout + normalize_back(feed_grad, gain_ref[...], xhat, scale)
        mg_ref[...] = middle_grad
        branch = middle_grad.astype(BF16)
        br_s[here, :] = branch
        mixed_grad = nt(branch, wo_ref[...])
        for p in range(heads // 2):
            lanes = slice(LANES * p, LANES * (p + 1))
            num, den = num_s[here, lanes], den_s[here, lanes]
            inv = lax.rsqrt(den * den + GUARD)
            mg = mixed_grad[:, lanes]
            b = head_sums(mg * num) * den * (inv * inv * inv) * (-1.0 / 64)
            b = pltpu.roll(b, 64, 1)
            for h in (2 * p, 2 * p + 1):
                a = jnp.where(mine(h, lower), mg * inv, b)
                a_ref[:, LANES * h : LANES * (h + 1)] = a.astype(BF16)
                lifted = (a * jnp.exp(column(gcol, 16 + h, rows, LANES))).astype(BF16)
                adj[h] += tn(lifted, qf_s[here, 256 * h : 256 * (h + 1)])

    @pl.when(step == 2 * tiles + pairs - 1)
    def _():
        pack_states([adj[h] for h in range(heads)], sent if comm else final_ref)
        if comm:
            exchange().start()
        output_grad = tn(mix_s[...], br_s[...]).astype(BF16)
        if not comm:
            o_ref[...] = output_grad
            sums_out[...] = sums_s[...]
            return
        os_ref[:, 0:width] = output_grad
        for later in range(2 * pairs + tiles, board.last() + 1):
            board.advance(later)
        exchange().wait_recv()
        is_first = links.seq == 0
        after_ref[...] = jnp.where(is_first, landed[...].astype(F32), 0.0).astype(BF16)
        logs = gcol_ref[rows - 1 : rows, :]
        norms = landed[64 * heads : 64 * heads + 16, :].astype(F32)
        flat_ref[...] = jnp.zeros_like(flat_ref)
        for k in range(3):
            flat_ref[k : k + 1, :] = jnp.sum(sums_s[8 * k : 8 * (k + 1), :], axis=0, keepdims=True)
        for k in range(2 * shard_width // width):
            cols = slice(width * k % shard_width, width * k % shard_width + width)
            in_first = k < shard_width // width
            own, other = upbg_s[0, :, cols], upbg_s[1, :, cols]
            flat_ref[3 + k : 4 + k, :] = jnp.where(is_first, own, other) if in_first else jnp.where(
                is_first, other, own
            )
        for h in range(heads):
            grown = grow_state(landed[64 * h : 64 * (h + 1), :], norms[h : h + 1], h)
            begin = adj[h] + jnp.exp(logs[:, 16 + h : 17 + h]) * grown
            begin = jnp.where(is_first, begin, 0.0)
            os_ref[64 * h : 64 * (h + 1), width : width + 256] = state_part(begin, h).astype(BF16)
            flat_ref[8 + h : 9 + h, 0:256] = 64.0 * norm_part(begin, h)
        exchange().wait_send()
        board.drain()


U_SCATTER, U_GATHER = ("core", "xr", "y", "z"), ("z", "y", "core")
FEED_STAGES = (7, 4, 3, 2)
FEED_TICKS = ((2, 3, 5, 7, 8, 9, 11, 12), (4, 5, 8, 10, 12), (6, 7, 10, 12), (8, 9, 13))
BACK_TICKS = ((2, 4, 6, 8), (1, 3, 5, 7, 9), (1, 3, 5, 7, 9, 11))


def feed_plans(hb):
    return [
        Plan(2048, hb, BF16, U_SCATTER[:n], U_GATHER if n > 4 else ()) for n in FEED_STAGES
    ]


def late_plans(hb):
    plans = []
    for plan, n in zip(feed_plans(hb)[1:], FEED_STAGES[1:]):
        done = [group for group in U_SCATTER[:n] if group != "xr"]
        plans.append(Plan(plan.left, hb, BF16, U_SCATTER[n:], U_GATHER, pre=tuple(done)))
    return plans


def back_kernel(heads, hg, chunks, comm, *refs):
    take = Taker(refs)
    (qf_ref, kf_ref, v_ref, uq_ref, uk_ref, rq_ref, rk_ref, a_ref, gcol_ref, grow_ref) = take(10)
    before_ref, entry_ref, entry_norm, after_ref, after_norm, proj_in = take(6)
    x_hbm, mg_hbm, ml_hbm, wq_hbm, wk_hbm, wv_hbm, gate_ref, gain_ref = take(8)
    u_hbms = take(3) if comm else ()
    os_hbm, f_hbm = take(2) if comm else (None,) * 2
    dx_ref, w_ref, small_ref = take(3)
    usum_hbm, ossum_hbm, fsum_hbm = take(3) if comm else (None,) * 3
    adj_ref, dqkv, dlogit, x_ref, mg_ref, ml_ref, wq_ref, wk_ref, wv_ref, load_sems = take(10)
    (proj_ref,) = take(1)
    g, i = pl.program_id(0), pl.program_id(1)
    tick = g * chunks + i
    last = heads // hg * chunks - 1
    chunk = chunks - 1 - i
    here = pl.ds(pl.multiple_of(chunk * C, C), C)
    groups = heads // hg
    loads = [
        (x_hbm, x_ref),
        (mg_hbm, mg_ref),
        (ml_hbm, ml_ref),
        (wq_hbm, wq_ref),
        (wk_hbm, wk_ref),
        (wv_hbm, wv_ref),
    ]
    if comm:
        u_refs = take(3)
        os_ref, f_ref, w_src, small_src = take(4)
        usum_ref, ossum_ref, fsum_ref, wsum_ref, smallsum_ref = take(5)
        (store_sems,) = take(1)
        loads = list(zip(u_hbms, u_refs)) + [(os_hbm, os_ref), (f_hbm, f_ref)] + loads
        early_loads = len(loads) - 6
        links = Links()
        board = Board(links, take, store_sems)
        plans = back_plans(os_hbm.shape, f_hbm.shape, w_src.shape, small_src.shape)

        def stages(start, gaps):
            ticks = [start]
            for gap in gaps:
                ticks.append(ticks[-1] + gap)
            return ticks

        for j, (plan, ticks) in enumerate(zip(late_plans(usum_ref.shape[2]), BACK_TICKS)):
            board.add(plan, u_refs[j], usum_ref.at[j], usum_hbm.at[j], ticks)
        board.add(plans["os"], os_ref, ossum_ref, ossum_hbm, OS_TICKS)
        board.add(plans["f"], f_ref, fsum_ref, fsum_hbm, F_TICKS)
        for k in range(groups):
            final = k + 1 == groups
            pieces = W_PIECES if final else 1
            lanes_each = w_src.shape[2] // pieces
            for j in range(pieces):
                lanes = pl.ds(j * lanes_each, lanes_each)
                board.add(
                    plans["w_last" if final else "w"],
                    w_src.at[k, :, lanes],
                    wsum_ref.at[k, :, lanes],
                    w_ref.at[k, :, lanes],
                    [last + 1 + i + (j if i else 0) for i in range(7)] if final else W_TICKS,
                )
        advance = board.advance

    def load(k):
        return pltpu.make_async_copy(loads[k][0], loads[k][1], load_sems.at[k])

    @pl.when(tick == 0)
    def _():
        for k in range(len(loads)):
            load(k).start()
        dlogit[...] = jnp.zeros_like(dlogit)
        if comm:
            links.greet(("core", "plane", "z"))

    if comm:
        @pl.when(tick == 1)
        def _():
            for k in range(early_loads):
                load(k).wait()

        for now in range(1, last + 1):
            pl.when(tick == now)(partial(advance, now))

    @pl.when(i == 0)
    def _():
        for p in range(hg // 2):
            proj_ref[p] = projection_blocks(proj_in, p, 1.0 / (2.0 * math.pi))[0]
        norms = after_norm[...].astype(F32)
        for h in range(hg):
            norm = pick_row(norms, g * hg + h)
            adj_ref[h] = grow_state(after_ref[64 * h : 64 * (h + 1), :], norm, h)

    row = iota((C, C), 0)
    col = iota((C, C), 1)
    causal = row >= col
    one = jnp.ones((C, C), BF16)
    zero = jnp.zeros((C, C), BF16)
    later = jnp.where(row < col, 1.0, 0.0).astype(BF16)
    pair_sums = jnp.concatenate([later, one], axis=0)
    two_sums = jnp.concatenate(
        [jnp.concatenate([one, zero], axis=1), jnp.concatenate([zero, one], axis=1)], axis=0
    )
    lower = lower_half((C, LANES))
    entry_norms = entry_norm[...].astype(F32)
    gcol = gcol_ref[...]
    if groups > 1:
        gcol = jnp.where(g == 0, gcol, pltpu.roll(gcol, LANES - hg, 1))

    def grow_row(kind, h):
        return grow_ref[pl.ds(kind * heads + g * hg + h, 1), :]

    for p in range(hg // 2):
        lanes = slice(LANES * p, LANES * (p + 1))
        angle_q, angle_k, dvs, x_parts, y_parts, throughs = [], [], [], [], [], []
        v_pair = v_ref[:, lanes].astype(F32)
        values = [jnp.where(mine(h, lower), v_pair, 1.0) for h in range(2)]
        values_low = [part.astype(BF16) for part in values]
        dweights = nt(
            a_ref[:, 2 * LANES * p : 2 * LANES * (p + 1)],
            jnp.concatenate(
                [
                    jnp.concatenate([values_low[0], zero], axis=1),
                    jnp.concatenate([zero, values_low[1]], axis=1),
                ],
                axis=0,
            ),
        )
        for j in range(2):
            h = 2 * p + j
            qf = qf_ref[:, 256 * h : 256 * (h + 1)]
            kf = kf_ref[:, 256 * h : 256 * (h + 1)]
            a_low = a_ref[:, LANES * h : LANES * (h + 1)]
            a = a_low.astype(F32)
            decay = column(gcol, h, C, LANES)
            lift = jnp.exp(decay)
            coef = jnp.exp(column(gcol, 8 + h, C, LANES))
            carried = jnp.exp(gcol[0:1, 48 + h : 49 + h])
            total = jnp.exp(gcol[0:1, 56 + h : 57 + h])
            entry = grow_state(
                entry_ref[64 * h : 64 * (h + 1), :], pick_row(entry_norms, g * hg + h), h
            )
            before = before_ref[0, h].astype(F32) + carried * entry
            before_low = before.astype(BF16)
            adj = adj_ref[h]
            adj_low = adj.astype(BF16)
            kept = total * adj
            through = jnp.sum(kept * before, axis=0, keepdims=True)
            throughs.append(jnp.sum(through, axis=1, keepdims=True))
            pairs = jnp.where(causal, jnp.exp(decay + grow_row(0, h)), 0.0)
            keys_and_state = jnp.concatenate([kf, before_low], axis=0)
            raw_and_far = nt(qf, keys_and_state)
            raw = raw_and_far[:, :C]
            weights = (raw * pairs).astype(BF16)
            draw = dweights[:, C * j : C * (j + 1)].astype(BF16).astype(F32) * pairs
            draw_low = draw.astype(BF16)
            both = (raw * draw).astype(BF16)
            a_lift = (a * lift).astype(BF16)
            v_coef = (values[j] * coef).astype(BF16)
            dq = nn(jnp.concatenate([draw_low, a_lift], axis=1), keys_and_state)
            dk = nn(
                jnp.concatenate([draw_low.T, v_coef], axis=1),
                jnp.concatenate([qf, adj_low], axis=0),
            )
            dv_far = coef * nt(kf, adj_low)
            dv = tn(weights, a_low) + dv_far
            x_far = (a * lift * raw_and_far[:, C:]).astype(BF16)
            x_parts.append(jnp.concatenate([both, x_far], axis=1))
            y_parts.append(
                jnp.concatenate(
                    [(values[j] * dv_far).astype(BF16), (values[j] * dv).astype(BF16)], axis=1
                )
            )
            adj_ref[h] = kept + tn(a_lift, qf)
            for feats, grad, angle in ((qf, dq, angle_q), (kf, dk, angle_k)):
                f = feats.astype(F32)
                angle.append(grad[:, :LANES] * f[:, LANES:] - grad[:, LANES:] * f[:, :LANES])
            dvs.append(dv)
        upto = nn(jnp.concatenate(x_parts, axis=0), pair_sums)
        ends = nn(jnp.concatenate(y_parts, axis=0), two_sums)
        for j in range(2):
            h = 2 * p + j
            rows = slice(C * j, C * (j + 1))
            flow = jnp.where(causal, upto[rows], ends[rows, :C])
            flow = jnp.sum(flow, axis=0, keepdims=True) + throughs[j]
            own = jnp.sum(jnp.where(row == col, ends[rows, C:], 0.0), axis=0, keepdims=True)
            dlogit[g, h : h + 1, here] = grow_row(3, h) * flow - grow_row(2, h) * own
        angles = jnp.concatenate(
            [jnp.concatenate(angle_q, axis=1), jnp.concatenate(angle_k, axis=1)], axis=0
        )
        du = nt(angles.astype(BF16), proj_ref[p])
        u = jnp.concatenate([uq_ref[:, lanes], uk_ref[:, lanes]], axis=0).astype(F32)
        scale = jnp.concatenate([rq_ref[:, lanes], rk_ref[:, lanes]], axis=0)
        along = nn((u * du).astype(BF16), block_ones())
        dqk = ((2.0 * math.pi) * scale * (du - u * along)).astype(BF16)
        width = hg * 64
        dqkv[g, here, LANES * p : LANES * (p + 1)] = dqk[:C]
        dqkv[g, here, width + LANES * p : width + LANES * (p + 1)] = dqk[C:]
        dqkv[g, here, 2 * width + LANES * p : 2 * width + LANES * (p + 1)] = jnp.where(
            lower, dvs[0], dvs[1]
        ).astype(BF16)

    @pl.when(i == chunks - 1)
    def _():
        @pl.when(g == 0)
        def _():
            load(len(loads) - 4).wait()

        grads = tn(ml_ref[...], dqkv[g]).astype(BF16)
        if comm:
            w_src[g] = grads
        else:
            w_ref[g] = grads

    @pl.when(tick == last)
    def _():
        if comm:
            advance(last + 1)
        for k in range(len(loads) - 6, len(loads)):
            if k != len(loads) - 4:
                load(k).wait()
        tokens = chunks * C
        block = min(T, tokens)
        small = small_src if comm else small_ref
        rows8 = jnp.concatenate(
            [dlogit[k, 0:hg, :] for k in range(groups)]
            + [jnp.zeros((16 - heads, dlogit.shape[2]), F32)],
            axis=0,
        ).astype(BF16)
        small[...] = jnp.zeros_like(small)
        small[0:heads, :] = nn(rows8, ml_ref[...])[0:heads]
        bias_sum = nt(jnp.ones(rows8.shape, BF16), rows8)[0:1]
        small[heads : heads + 1, 0:16] = bias_sum
        gate_low = gate_rows(gate_ref[...])
        gain = gain_ref[...]
        now = last + 2
        for b in range(tokens // block):
            rows = slice(block * b, block * (b + 1))
            mixer_grad = tn(rows8[:, rows], gate_low)
            for k in range(groups):
                for j, ref in enumerate((wq_ref, wk_ref, wv_ref)):
                    mixer_grad = mixer_grad + nt(
                        dqkv[k, rows, hg * 64 * j : hg * 64 * (j + 1)],
                        ref[:, hg * 64 * k : hg * 64 * (k + 1)],
                    )
            xhat, scale = normalize(x_ref[rows, :].astype(F32))
            small[2 * heads : 2 * heads + 1, :] += jnp.sum(
                mixer_grad * xhat, axis=0, keepdims=True
            )
            small[2 * heads + 1 : 2 * heads + 2, :] += jnp.sum(mixer_grad, axis=0, keepdims=True)
            dx_ref[rows, :] = mg_ref[rows, :] + normalize_back(mixer_grad, gain, xhat, scale)
            if comm:
                advance(now)
                now += 1
        if comm:
            board.add(
                plans["small"], small_src, smallsum_ref, small_ref, [now, now + 1, now + 2, now + 3]
            )
            for later_tick in range(now, board.last() + 1):
                advance(later_tick)
            board.drain()


OS_TICKS = (2, 4, 7, 9, 11, 14, 16)
F_TICKS = (6, 8, 10, 12)
W_TICKS = (8, 10, 12, 14, 16, 18, 20)
W_PIECES = 3


def back_plans(os, f, w, small):
    return {
        "os": Plan(os[0], os[1], BF16, *ALL_PLAN),
        "f": Plan(f[0], f[1], F32, *SHARE_PLAN),
        "w": Plan(w[1], w[2], BF16, *ALL_PLAN),
        "w_last": Plan(w[1], w[2] // W_PIECES, BF16, *ALL_PLAN),
        "small": Plan(small[0], small[1], F32, *SHARE_PLAN),
    }


def whole(shape):
    zeros = (0,) * len(shape)
    return pl.BlockSpec(shape, lambda *at: zeros, pipeline_mode=pl.Buffered(1))


ANY = pl.BlockSpec(memory_space=pl.ANY)


def call(kernel, grid, ins, outs, scratch, name, collective_id=None):
    def spec(shape, block, index):
        if block is None:
            return whole(shape)
        return block if isinstance(block, pl.BlockSpec) else pl.BlockSpec(block, index)

    params = {} if collective_id is None else {
        "collective_id": collective_id, "has_side_effects": True
    }
    return pl.pallas_call(
        kernel,
        grid=grid,
        in_specs=[spec(array.shape, block, index) for array, block, index in ins],
        out_specs=[spec(shape, block, index) for shape, _, block, index in outs],
        out_shape=[jax.ShapeDtypeStruct(shape, dtype) for shape, dtype, _, _ in outs],
        scratch_shapes=scratch,
        compiler_params=pltpu.CompilerParams(
            dimension_semantics=("arbitrary",) * len(grid), vmem_limit_bytes=VMEM, **params
        ),
        name=name,
    )(*[array for array, _, _ in ins])


def finish_kernel(u_ref, late_ref, w_ref, os_ref, up_ref, down_ref, q_ref, k_ref, v_ref, o_ref, s_ref):
    hb = u_ref.shape[2]
    for part, ref in enumerate((up_ref, down_ref)):
        ref[:, 0:hb] = u_ref[part].astype(F32)
        for k in range(late_ref.shape[0]):
            ref[:, hb * (k + 1) : hb * (k + 2)] = late_ref[k, part].astype(F32)
    groups, _, lanes = w_ref.shape
    each = lanes // 3
    for part, ref in enumerate((q_ref, k_ref, v_ref)):
        for k in range(groups):
            ref[:, each * k : each * (k + 1)] = w_ref[k, :, each * part : each * (part + 1)].astype(F32)
    width = o_ref.shape[1]
    o_ref[...] = os_ref[:, 0:width].astype(F32)
    for k in range(s_ref.shape[0]):
        s_ref[k] = os_ref[64 * k : 64 * (k + 1), width:].astype(F32).T


def finish(heads, sum_u, sum_late, sum_w, out_state, small):
    width = sum_w.shape[1]
    steps = 4
    rows = width // steps
    late, _, hb = sum_late.shape
    feats = out_state.shape[1] - width
    square = ((width, width), F32, (rows, width), lambda i: (i, 0))
    wide = ((width, (late + 1) * hb), F32, (rows, (late + 1) * hb), lambda i: (i, 0))
    return call(
        finish_kernel,
        (steps,),
        [
            (sum_u.reshape(2, width, hb), (2, rows, hb), lambda i: (0, i, 0)),
            (sum_late.reshape(late, 2, width, hb), (late, 2, rows, hb), lambda i: (0, 0, i, 0)),
            (sum_w, (sum_w.shape[0], rows, sum_w.shape[2]), lambda i: (0, i, 0)),
            (out_state, (rows, width + feats), lambda i: (i, 0)),
        ],
        [wide, wide, square, square, square, square]
        + [((heads, feats, 64), F32, (heads // steps, feats, 64), lambda i: (i, 0, 0))],
        [],
        "finish",
    )


def carry_over(payload, logs, forward):
    n, index = lax.axis_size("seq"), lax.axis_index("seq")
    everything = lax.all_gather(payload, "seq")
    every_log = lax.all_gather(logs, "seq")
    heads = logs.shape[0]
    row = jnp.arange(payload.shape[0])
    head = jnp.where(row < 64 * heads, row // 64, jnp.minimum(row - 64 * heads, heads - 1))
    total = jnp.zeros(payload.shape, F32)
    for k in range(n) if forward else reversed(range(n)):
        ahead = (k < index) if forward else (k > index)
        new = jnp.exp(every_log[k])[head][:, None] * total + everything[k].astype(F32)
        total = jnp.where(ahead, new, total)
    return total.astype(BF16)


def local(
    inputs,
    cotangent,
    mixer_gain,
    mixer_bias,
    query_weight,
    key_weight,
    value_weight,
    gate_weight,
    gate_bias,
    output_weight,
    projections,
    start_state,
    start_norm,
    feed_gain,
    feed_bias,
    up_weight,
    up_bias,
    down_weight,
    down_bias,
):
    _, tokens, width = inputs.shape
    heads, size, feats = projections.shape
    chunks = tokens // C
    tile = min(T, tokens)
    tiles = tokens // tile
    shards = lax.axis_size("seq")
    first = lax.axis_index("seq") == 0
    comm = (lax.axis_size("dp"), shards) == (16, 2)
    x = inputs.reshape(tokens, width)
    dout = cotangent.reshape(tokens, width)
    shard_width = up_weight.shape[1]
    hidden = shard_width * shards
    hb = min(HB, shard_width)
    pairs = hidden // (2 * hb)
    wide = heads * LANES
    wider = heads * 2 * feats
    pay_shape = (heads * 64 + 16, 2 * feats)

    def const(array):
        return (array if array.ndim > 1 else array[None], None, None)

    def keep(shape, dtype):
        return (shape, dtype, None, None)

    def hbm(array):
        return (array, ANY, None)

    def result(shape, dtype):
        return (shape, dtype, ANY, None)

    def vmem(*shape, dtype=BF16):
        return pltpu.VMEM(shape, dtype)

    def early(n):
        return (C, n), lambda i: (jnp.minimum(i, chunks - 1), 0)

    def out_early(n, dtype):
        return ((tokens, n), dtype) + early(n)

    ins = [(x,) + early(width)]
    ins += [const(part) for part in (mixer_gain, mixer_bias, query_weight, key_weight)]
    ins += [
        const(value_weight),
        const(gate_weight),
        (gate_bias, pl.BlockSpec(memory_space=pltpu.SMEM), None),
        const(projections),
        const(start_state),
        const(start_norm),
    ]
    outs = [out_early(width, BF16)] * 3 + [out_early(width, F32)] * 2
    outs += [out_early(wider, BF16)] * 2 + [out_early(width, BF16), out_early(LANES, F32)]
    outs += [
        (
            (4 * heads, tokens),
            F32,
            (4 * heads, C),
            lambda i: (0, jnp.minimum(i, chunks - 1)),
        ),
        (
            (chunks, heads, LANES, 2 * feats),
            BF16,
            (1, heads, LANES, 2 * feats),
            lambda i: (jnp.minimum(i, chunks - 1), 0, 0, 0),
        ),
        ((tokens, wide), F32, (C, wide), lambda i: (jnp.maximum(i - chunks, 0), 0)),
    ]
    scratch = [
        vmem(heads, LANES, 2 * feats, dtype=F32),
        vmem(1, LANES, dtype=F32),
        vmem(chunks, C, wider),
        vmem(chunks, C, wider),
        vmem(chunks, C, width),
        vmem(chunks, C, LANES, dtype=F32),
        vmem(chunks, 4 * heads, C, dtype=F32),
        vmem(chunks, heads, LANES, 2 * feats),
        vmem(width, LANES),
        vmem(heads, width),
        vmem(1, LANES, dtype=F32),
        vmem(heads, LANES, dtype=F32),
        vmem(heads // 2, 3 * LANES, 2 * feats),
    ]
    upb = up_bias.astype(F32)[None]
    if comm:
        ins += [hbm(up_weight), hbm(down_weight), const(upb)]
        outs += [
            keep(pay_shape, BF16),
            result(up_weight.shape, BF16),
            result(down_weight.shape, BF16),
            keep((2, shard_width), F32),
        ]
        scratch += [
            vmem(*pay_shape),
            vmem(*pay_shape),
            vmem(1, shard_width, dtype=F32),
            pltpu.SemaphoreType.DMA((6,)),
            pltpu.SemaphoreType.DMA((6,)),
        ]
    else:
        outs += [keep(pay_shape, BF16), keep((8, LANES), F32)]
    found = call(
        partial(features_kernel, heads, chunks, comm),
        (2 * chunks,),
        ins,
        outs,
        scratch,
        "features",
        1 if comm else None,
    )
    ml, uq, uk, rq, rk, qf, kf, v, gcol, grow, before, num = found[:12]
    if comm:
        entry, up_other, down_other, upb = found[12:]
        weights = (up_weight, up_other, down_weight, down_other)
    else:
        final, total = found[12:]
        logs = total[0, :heads]
        entry = carry_over(final, logs, True)
        weights = (lax.all_gather(up_weight, "seq"), lax.all_gather(down_weight, "seq"))
        upb = lax.all_gather(upb, "seq")

    steps = 2 * tiles + pairs

    def first_last(n):
        def index(i):
            late = jnp.maximum(i - tiles - pairs, 0)
            return (jnp.where(i < tiles + pairs, jnp.minimum(i, tiles - 1), late), 0)

        return (tile, n), index

    def only_first(n):
        return (tile, n), lambda i: (jnp.minimum(i, tiles - 1), 0)

    def only_last(n, dtype):
        return (
            (tokens, n),
            dtype,
            (tile, n),
            lambda i: (jnp.maximum(i - tiles - pairs, 0), 0),
        )

    ins = [
        (x,) + only_first(width),
        hbm(qf),
        (num,) + only_first(wide),
        (gcol,) + first_last(LANES),
        const(entry),
        const(output_weight),
        const(feed_gain),
        const(feed_bias),
        const(down_bias),
        const(upb),
        hbm(dout),
    ] + [hbm(part) for part in weights]
    outs = [only_last(width, BF16), only_last(width, F32), only_last(wide, BF16)]
    scratch = [
        vmem(heads, LANES, 2 * feats),
        vmem(heads, LANES, 2 * feats, dtype=F32),
        vmem(tokens, width, dtype=F32),
        vmem(tokens, width, dtype=F32),
        vmem(tokens, width, dtype=F32),
        vmem(tokens, width),
        vmem(tokens, width),
        vmem(tokens, width),
        vmem(tokens, width, dtype=F32),
        vmem(tokens, width, dtype=F32),
        vmem(tokens, width),
        vmem(shards, width, shard_width),
        vmem(shards, width, shard_width),
        vmem(tokens, 2 * hb),
        vmem(tokens, 2 * hb),
        vmem(24, width, dtype=F32),
        pltpu.SemaphoreType.DMA((5 + tiles,)),
        vmem(tokens, wider),
    ]
    if comm:
        plans = feed_plans(hb)
        outs += [
            result((2 * width, hb), BF16),
            *[keep((plan.left, hb), BF16) for plan in plans[1:]],
            keep((width, width + 2 * feats), BF16),
            keep((16, width), F32),
            keep(pay_shape, BF16),
        ]
        scratch += [
            vmem(pairs, 4 * width, hb),
            vmem(2 * width, hb),
            vmem(shards, 1, shard_width, dtype=F32),
            vmem(*pay_shape),
            vmem(*pay_shape),
            pltpu.SemaphoreType.DMA,
            pltpu.SemaphoreType.DMA,
            pltpu.SemaphoreType.DMA((pairs,)),
        ]
        for plan in plans:
            scratch += plan.scratch()
    else:
        outs += [
            keep((shards, width, shard_width), BF16),
            keep((shards, width, shard_width), BF16),
            keep((shards, 1, shard_width), F32),
            keep((width, width), BF16),
            keep(pay_shape, BF16),
            keep((24, width), F32),
        ]
    found = call(
        partial(feed_kernel, heads, tiles, pairs, comm),
        (steps,),
        ins,
        outs,
        scratch,
        "feed",
        2 if comm else None,
    )
    out, mg, a = found[:3]
    if comm:
        sum_u, *u_late = found[3:7]
        out_state, flat, after = found[7:]
    else:
        up_grad, down_grad, upb_grad, output_grad, adj_final, feed_sums = found[3:]
        after = carry_over(adj_final, logs, False)
        feed_three = jnp.sum(feed_sums.reshape(3, 8, width), axis=1)
        begin = adj_final.astype(F32)
        row = jnp.arange(pay_shape[0])
        head = jnp.where(row < 64 * heads, row // 64, jnp.minimum(row - 64 * heads, heads - 1))
        begin = begin + jnp.exp(logs)[head][:, None] * after.astype(F32)
        begin = jnp.where(first, begin, 0.0)
        state_grad = begin[: heads * 64].astype(BF16)
        norm_grad = 64.0 * begin[heads * 64 : heads * 65]

    hg = GROUP_HEADS
    groups = heads // hg

    def back_rows(n, per_group=True):
        return (C, n), lambda g, i: (chunks - 1 - i, g if per_group else 0)

    def per_group(array, *shape):
        zeros = (0,) * (len(shape) - 1)
        return (array, shape, lambda g, i: (g,) + zeros)

    def states(array):
        return [
            (array, (hg * 64, 2 * feats), lambda g, i: (g, 0)),
            (array, (16, 2 * feats), lambda g, i: (heads * 4, 0)),
        ]

    ins = [
        (qf,) + back_rows(hg * 2 * feats),
        (kf,) + back_rows(hg * 2 * feats),
        (v,) + back_rows(hg * size),
        (uq,) + back_rows(hg * size),
        (uk,) + back_rows(hg * size),
        (rq,) + back_rows(hg * size),
        (rk,) + back_rows(hg * size),
        (a,) + back_rows(hg * LANES),
        (gcol,) + back_rows(LANES, False),
        (grow, (4 * heads, C), lambda g, i: (0, chunks - 1 - i)),
        (before, (1, hg, LANES, 2 * feats), lambda g, i: (chunks - 1 - i, g, 0, 0)),
    ]
    ins += states(entry) + states(after)
    ins += [
        per_group(projections, hg, size, feats),
        hbm(x),
        hbm(mg),
        hbm(ml),
        hbm(query_weight),
        hbm(key_weight),
        hbm(value_weight),
        const(gate_weight),
        const(mixer_gain),
    ]
    w_shape, small_shape = (groups, width, 3 * hg * size), (32, width)

    def sums(shape, dtype):
        return result(shape, dtype) if comm else keep(shape, dtype)

    outs = [keep((tokens, width), F32), sums(w_shape, BF16), sums(small_shape, F32)]
    scratch = [
        vmem(hg, LANES, 2 * feats, dtype=F32),
        vmem(groups, tokens, 3 * hg * size),
        vmem(groups, 8, tokens, dtype=F32),
        vmem(tokens, width),
        vmem(tokens, width, dtype=F32),
        vmem(tokens, width),
        vmem(width, width),
        vmem(width, width),
        vmem(width, width),
        pltpu.SemaphoreType.DMA((11,)),
        vmem(hg // 2, LANES, 2 * feats),
    ]
    if comm:
        ins += [hbm(part) for part in (*u_late, out_state, flat)]
        summed = [
            ((len(u_late), 2 * width, hb), BF16),
            (out_state.shape, BF16),
            (flat.shape, F32),
        ]
        outs += [result(*part) for part in summed]
        scratch += [vmem(*part.shape) for part in u_late]
        scratch += [
            vmem(*out_state.shape),
            vmem(*flat.shape, dtype=F32),
            vmem(*w_shape),
            vmem(*small_shape, dtype=F32),
        ]
        scratch += [vmem(*shape, dtype=dtype) for shape, dtype in summed]
        scratch += [vmem(*w_shape), vmem(*small_shape, dtype=F32)]
        plans = back_plans(out_state.shape, flat.shape, w_shape, small_shape)
        plans = late_plans(hb) + [
            plans[name]
            for name in ("os", "f") + ("w",) * (groups - 1) + ("w_last",) * W_PIECES + ("small",)
        ]
        scratch += [pltpu.SemaphoreType.DMA((len(plans),))]
        for plan in plans:
            scratch += plan.scratch()
    found = call(
        partial(back_kernel, heads, hg, chunks, comm),
        (groups, chunks),
        ins,
        outs,
        scratch,
        "back",
        3 if comm else None,
    )
    dx, sum_w, small = found[:3]
    if comm:
        sum_late, out_state, flat = found[3:]
        results = finish(heads, sum_u, sum_late, sum_w, out_state, small)
        sum_up, sum_down, sum_q, sum_k, sum_v, sum_o, sum_state = results
        sum_feed = flat[0:3]
        sum_upb = flat[3 : 3 + hidden // width].reshape(-1)
        sum_upb = jnp.where(first, sum_upb[:shard_width], sum_upb[shard_width:])
        sum_norm = flat[8 : 8 + heads, : 2 * feats]
    else:
        own = lax.psum_scatter(
            jnp.stack([up_grad, down_grad]), "seq", scatter_dimension=1, tiled=True
        )
        upb_own = lax.psum_scatter(upb_grad, "seq", scatter_dimension=0, tiled=True)
        (sum_up, sum_down), sum_upb = lax.psum((own[:, 0], upb_own.reshape(-1)), "dp")
        sum_w, sum_o, sum_state, small, sum_norm, sum_feed = lax.psum(
            (sum_w, output_grad, state_grad, small, norm_grad, feed_three), ("dp", "seq")
        )
        sum_w = sum_w.reshape(groups, width, 3, hg * size).transpose(2, 1, 0, 3)
        sum_q, sum_k, sum_v = sum_w.reshape(3, width, width).astype(F32)
        sum_state = sum_state.reshape(heads, size, 2 * feats).astype(F32).transpose(0, 2, 1)
    return (
        out.reshape(inputs.shape),
        dx.reshape(inputs.shape),
        small[2 * heads],
        small[2 * heads + 1],
        sum_q,
        sum_k,
        sum_v,
        small[:heads].T,
        small[heads, :heads],
        sum_o.astype(F32),
        sum_state,
        sum_norm,
        sum_feed[0],
        sum_feed[1],
        sum_up.astype(F32),
        sum_upb,
        sum_down.astype(F32),
        sum_feed[2],
    )


def solution(mesh):
    tokens = P("dp", "seq", None)
    columns = P(None, "seq")
    return jax.shard_map(
        local,
        mesh=mesh,
        in_specs=(tokens, tokens) + (P(),) * 13 + (columns, P("seq"), columns, P()),
        out_specs=(tokens, tokens) + (P(),) * 12 + (columns, P("seq"), columns, P()),
        check_vma=False,
    )
```

```python
from functools import partial
import math

import jax
import jax.numpy as jnp
from jax import lax
from jax.experimental import pallas as pl
from jax.experimental.pallas import tpu as pltpu
from jax.sharding import PartitionSpec as P

F32 = jnp.float32
BF16 = jnp.bfloat16
EPS_NORM = 1e-05
EPS_UNIT = 1e-06
GUARD = 0.0625
MESH = pl.DeviceIdType.MESH
VMEM = 56 * 1024 * 1024

C = 128
T = 256
HB = 256
INNER_HEADS = 8
WEIGHT_STEPS = (4, 6, 8, 11)
SPAN = 2
GROUP_HEADS = 4
LANES = 128

SIN = (3.14158202, -5.16714278, 2.54189892, -0.55463591)
COS = (0.99999995, -4.93479286, 4.05841191, -1.33188012, 0.21969671)
ERF = (0.319381530, -0.356563782, 1.781477937, -1.821255978, 1.330274429)
ERF_P = 0.2316419
INV_SQRT_2PI = 0.3989422804014327


def nn(a, b):
    return lax.dot_general(a, b, (((1,), (0,)), ((), ())), preferred_element_type=F32)


def nt(a, b):
    return lax.dot_general(a, b, (((1,), (1,)), ((), ())), preferred_element_type=F32)


def tn(a, b):
    return lax.dot_general(a, b, (((0,), (0,)), ((), ())), preferred_element_type=F32)


def thirds(x):
    high = x.astype(BF16)
    rest = x - high.astype(F32)
    middle = rest.astype(BF16)
    return high, middle, (rest - middle.astype(F32)).astype(BF16)


def rows_up_to(x):
    n = x.shape[0]
    tri = jnp.where(iota((n, n), 0) >= iota((n, n), 1), 1.0, 0.0).astype(BF16)
    return nn(jnp.concatenate([tri] * 3, axis=1), jnp.concatenate(thirds(x), axis=0))


def lanes_up_to(x):
    n = x.shape[1]
    tri = jnp.where(iota((n, n), 0) <= iota((n, n), 1), 1.0, 0.0).astype(BF16)
    return nn(jnp.concatenate(thirds(x), axis=1), jnp.concatenate([tri] * 3, axis=0))


def iota(shape, dim):
    return lax.broadcasted_iota(jnp.int32, shape, dim)


def log_sigmoid(x):
    return jnp.minimum(x, 0.0) - jnp.log(1.0 + jnp.exp(-jnp.abs(x)))


def normalize(x):
    centred = x - jnp.mean(x, axis=-1, keepdims=True)
    scale = lax.rsqrt(jnp.mean(centred * centred, axis=-1, keepdims=True) + EPS_NORM)
    return centred * scale, scale


def normalize_back(grad, gain, xhat, scale):
    inner = grad * gain
    mean_inner = jnp.mean(inner, axis=-1, keepdims=True)
    mean_both = jnp.mean(inner * xhat, axis=-1, keepdims=True)
    return scale * (inner - mean_inner - xhat * mean_both)


def fold_rows(x):
    return jnp.sum(x.reshape(x.shape[0] // 8, 8, x.shape[1]), axis=0)


def block_ones():
    return jnp.where(
        iota((LANES, LANES), 0) // 64 == iota((LANES, LANES), 1) // 64, 1.0, 0.0
    ).astype(BF16)


def head_sums(x):
    high = x.astype(BF16)
    rest = (x - high.astype(F32)).astype(BF16)
    ones = block_ones()
    return nn(jnp.concatenate([high, rest], axis=1), jnp.concatenate([ones, ones], axis=0))


def lower_half(shape):
    return iota(shape, 1) < 64


def mine(h, lower):
    return lower if h % 2 == 0 else jnp.logical_not(lower)


def column(block, index, rows, width):
    return jnp.broadcast_to(block[:, index : index + 1], (rows, width))


def sin_cos(turns, scale):
    r = turns - jnp.floor(turns + 0.5)
    r2 = r * r
    s = (((SIN[3] * r2 + SIN[2]) * r2 + SIN[1]) * r2 + SIN[0]) * r
    k = 2.0 * scale
    c = (((k * COS[4] * r2 + k * COS[3]) * r2 + k * COS[2]) * r2 + k * COS[1]) * r2 + k * COS[0]
    return s * c, scale - (k * s) * s


class Links:
    def __init__(self):
        self.dp, self.seq = lax.axis_index("dp"), lax.axis_index("seq")
        core, y, z = self.dp % 2, (self.dp // 2) % 2, self.dp // 4
        self.y = y
        self.at = {"core": core, "y": y, "z": z, "plane": self.seq * 2 + y}
        self.at["xr"] = 0

    size = {"core": 2, "xr": 2, "y": 2, "z": 4, "plane": 4}

    def partner(self, group, step):
        dp, seq = self.dp, self.seq
        if group == "core":
            return (dp + 1 - 2 * self.at["core"], seq)
        if group == "xr":
            return (dp, 1 - seq)
        if group == "y":
            return (dp + 2 - 4 * self.y, seq)
        target = (self.at[group] + step) % 4
        if group == "z":
            return (dp % 4 + 4 * target, seq)
        return (dp + 2 * (target % 2 - self.y), target // 2)

    def greet(self, groups):
        barrier = pltpu.get_barrier_semaphore()
        count = 0
        for group in groups:
            for step in range(1, self.size[group]):
                pl.semaphore_signal(
                    barrier, inc=1, device_id=self.partner(group, step), device_id_type=MESH
                )
                count += 1
        pl.semaphore_wait(barrier, count)


class Plan:
    def __init__(self, rows, lanes, dtype, scatter, gather, share=(), pre=()):
        self.pre = pre
        self.scatter, self.gather, self.share = scatter, gather, share
        self.rows, self.lanes, self.dtype = rows, lanes, dtype
        self.groups = scatter + gather + share
        self.left = rows
        for group in scatter:
            self.left //= Links.size[group]
        self.stages = len(self.groups)

    def scratch(self):
        shapes = []
        rows = self.rows
        for i, group in enumerate(self.scatter):
            n = Links.size[group]
            rows //= n
            shapes.append(pltpu.VMEM((n - 1, rows, self.lanes), self.dtype))
            if i < len(self.scatter) - 1:
                shapes.append(pltpu.VMEM((rows, self.lanes), self.dtype))
        for i, group in enumerate(self.share):
            shapes.append(pltpu.VMEM((Links.size[group], rows, self.lanes), self.dtype))
            if i < len(self.share) - 1:
                shapes.append(pltpu.VMEM((rows, self.lanes), self.dtype))
        for group in self.groups:
            n = Links.size[group]
            shapes.append(pltpu.SemaphoreType.DMA((n - 1,)))
            shapes.append(pltpu.SemaphoreType.DMA((n - 1,)))
        return shapes


class Stream:
    def __init__(self, plan, links, source, out, scratch):
        self.plan, self.links, self.source, self.out = plan, links, source, out
        scratch = list(scratch)
        self.landing, self.parts = [], [source]
        summed = plan.scatter + plan.share
        for i in range(len(summed)):
            self.landing.append(scratch.pop(0))
            if i < len(summed) - 1:
                self.parts.append(scratch.pop(0))
        self.sems = [(scratch.pop(0), scratch.pop(0)) for _ in range(plan.stages)]
        self.places = {}
        rows, start = out.shape[0], 0
        for group in plan.pre + plan.scatter:
            if group in plan.gather:
                rows //= Links.size[group]
                self.places[group] = (start, rows)
                start = start + links.at[group] * rows
        self.final = (start, rows)

    def copies(self, stage, sending):
        plan, links = self.plan, self.links
        group = plan.groups[stage]
        n, me = Links.size[group], links.at[group]
        sends, recvs = self.sems[stage]
        made = []
        for step in range(1, n):
            target, origin = (me + step) % n, (me + n - step) % n
            if plan.share:
                source = self.parts[stage]
                lands = self.landing[stage].at[me]
                arrives = self.landing[stage].at[origin]
            elif stage < len(plan.scatter):
                landing = self.landing[stage]
                rows = landing.shape[1]
                source = self.parts[stage].at[pl.ds(pl.multiple_of(target * rows, 8), rows)]
                arrives = lands = landing.at[step - 1]
            else:
                start, rows = self.places[group]
                mine_at = pl.multiple_of(start + me * rows, 8)
                theirs_at = pl.multiple_of(start + origin * rows, 8)
                source = lands = self.out.at[pl.ds(mine_at, rows)]
                arrives = self.out.at[pl.ds(theirs_at, rows)]
            made.append(
                pltpu.make_async_remote_copy(
                    src_ref=source if sending else arrives,
                    dst_ref=lands if sending else arrives,
                    send_sem=sends.at[step - 1],
                    recv_sem=recvs.at[step - 1],
                    device_id=links.partner(group, step),
                    device_id_type=MESH,
                )
            )
        return made

    def start(self, stage):
        if stage == 0 and not (self.plan.scatter or self.plan.share):
            start, rows = self.final
            self.out[pl.ds(pl.multiple_of(start, 8), rows), :] = self.source[...]
        for copy in self.copies(stage, True):
            copy.start()

    def finish(self, stage):
        plan = self.plan
        for copy in self.copies(stage, False):
            copy.wait_recv()
        if plan.share:
            landing, me = self.landing[stage], self.links.at[plan.groups[stage]]
            landing[me] = self.parts[stage][...]
            total = landing[0]
            for k in range(1, landing.shape[0]):
                total = total + landing[k]
            if stage + 1 < plan.stages:
                self.parts[stage + 1][...] = total
            else:
                self.out[...] = total
            return
        if stage >= len(plan.scatter):
            return
        landing = self.landing[stage]
        arrivals, rows, _ = landing.shape
        own = self.links.at[plan.groups[stage]] * rows
        into, start = self.out, self.final[0]
        if stage + 1 < len(plan.scatter):
            into, start = self.parts[stage + 1], 0
        block = min(rows, SUM_ROWS)

        def add_block(k, carry):
            at = k * block
            total = self.parts[stage][pl.ds(pl.multiple_of(own + at, 16), block), :].astype(F32)
            for step in range(arrivals):
                total = total + landing[step, pl.ds(pl.multiple_of(at, 16), block), :].astype(F32)
            into[pl.ds(pl.multiple_of(start + at, 16), block), :] = total.astype(landing.dtype)
            return carry

        lax.fori_loop(0, rows // block, add_block, 0)

    def drain(self):
        for stage in range(self.plan.stages):
            for copy in self.copies(stage, True):
                copy.wait_send()


ALL_PLAN = (("core", "plane", "z"), ("z", "plane", "core"))
SHARE_PLAN = ((), (), ("core", "plane", "z"))


def pick_row(block, index):
    return jnp.sum(jnp.where(iota(block.shape, 0) == index, block, 0.0), axis=0, keepdims=True)


def grow_state(rows, norm, h):
    rows = rows.astype(F32)
    norm = jnp.broadcast_to(norm, rows.shape)
    return jnp.concatenate([rows, norm] if h % 2 == 0 else [norm, rows], axis=0)


def state_part(state, h):
    return state[0:64] if h % 2 == 0 else state[64:128]


def norm_part(state, h):
    return state[64:65] if h % 2 == 0 else state[0:1]


def pack_states(states, out_ref):
    heads = len(states)
    for h, state in enumerate(states):
        out_ref[64 * h : 64 * (h + 1), :] = state_part(state, h).astype(BF16)
    norms = [norm_part(state, h) for h, state in enumerate(states)]
    pad = jnp.zeros((16 - heads, states[0].shape[1]), F32)
    out_ref[64 * heads : 64 * heads + 16, :] = jnp.concatenate(norms + [pad], axis=0).astype(BF16)


def projection_blocks(proj_ref, p, scale):
    parts = [proj_ref[2 * p + j] * scale for j in range(2)]
    highs = [part.astype(BF16) for part in parts]
    rests = [(part - high.astype(F32)).astype(BF16) for part, high in zip(parts, highs)]
    zero = jnp.zeros(highs[0].shape, BF16)

    def diagonal(pair):
        return jnp.concatenate(
            [
                jnp.concatenate([pair[0], zero], axis=1),
                jnp.concatenate([zero, pair[1]], axis=1),
            ],
            axis=0,
        )

    return diagonal(highs), diagonal(rests)


def gate_rows(wg):
    eye = jnp.where(iota((16, wg.shape[1]), 0) == iota((16, wg.shape[1]), 1), 1.0, 0.0)
    return nt(eye.astype(BF16), wg).astype(BF16)


class Taker:
    def __init__(self, refs):
        self.refs = list(refs)

    def __call__(self, n):
        taken = self.refs[:n]
        del self.refs[:n]
        return taken


class Board:
    def __init__(self, links, take, store_sems):
        self.links, self.take, self.store_sems = links, take, store_sems
        self.entries = []

    def add(self, plan, source, out, final, ticks):
        stream = Stream(plan, self.links, source, out, self.take(len(plan.scratch())))
        self.entries.append((stream, ticks, out, final))

    def store(self, k):
        _, _, out, final = self.entries[k]
        return pltpu.make_async_copy(out, final, self.store_sems.at[k])

    def advance(self, now):
        for k, (stream, ticks, _, final) in enumerate(self.entries):
            for stage, tick in enumerate(ticks):
                if tick == now:
                    if stage > 0:
                        stream.finish(stage - 1)
                    if stage < stream.plan.stages:
                        stream.start(stage)
                    elif final is not None:
                        self.store(k).start()

    def last(self):
        return max(ticks[-1] for _, ticks, _, _ in self.entries)

    def drain(self):
        for k, (stream, _, _, final) in enumerate(self.entries):
            stream.drain()
            if final is not None:
                self.store(k).wait()


def features_kernel(heads, chunks, comm, *refs):
    take = Taker(refs)
    x_ref, gain_ref, bias_ref, wq_ref, wk_ref, wv_ref = take(6)
    gate_ref, gb_smem, proj_ref, start_ref, start_norm_ref = take(5)
    up_hbm, down_hbm, upb_ref = take(3) if comm else (None,) * 3
    ml_ref, uq_ref, uk_ref, rq_ref, rk_ref, qf_ref, kf_ref, v_ref = take(8)
    gcol_ref, grow_ref, before_ref, n_ref = take(4)
    if comm:
        entry_ref, upo_hbm, downo_hbm, upbs_ref = take(4)
    else:
        final_ref, total_ref = take(2)
    state, carry, qf_s, kf_s, v_s, gcol_s, grow_s, before_s = take(8)
    wg_ref, wgt_ref, gb_ref, gbt_ref, pcat_ref = take(5)
    step = pl.program_id(0)
    chunk = lax.rem(step, chunks)

    if comm:
        sent, landed, upb_landed, sends, recvs = take(5)
        links = Links()
        core, y = links.at["core"], links.at["y"]
        part = up_hbm.shape[0] // 4
        here = pl.ds(pl.multiple_of((2 * core + y) * part, 16), part)
        there = pl.ds(pl.multiple_of((2 * core + 1 - y) * part, 16), part)
        own_half = pl.ds(pl.multiple_of(2 * core * part, 16), 2 * part)
        other_half = pl.ds(pl.multiple_of(2 * (1 - core) * part, 16), 2 * part)

        def remote(k, sending):
            group = ("xr", "y", "core")[k // 2] if k < 6 else "xr"
            if k == 6:
                source, lands = upb_ref, upb_landed
            elif k == 7:
                source, lands = sent, landed
            else:
                mine_ref, theirs_ref = ((up_hbm, upo_hbm), (down_hbm, downo_hbm))[k % 2]
                if k < 2:
                    source, lands = mine_ref.at[here], theirs_ref.at[here]
                elif k < 4:
                    source = theirs_ref.at[here]
                    lands = source if sending else theirs_ref.at[there]
                else:
                    source = theirs_ref.at[own_half]
                    lands = source if sending else theirs_ref.at[other_half]
            return pltpu.make_async_remote_copy(
                src_ref=source if sending else lands,
                dst_ref=lands,
                send_sem=sends.at[k],
                recv_sem=recvs.at[k],
                device_id=links.partner(group, 1),
                device_id_type=MESH,
            )

        @pl.when(step == 0)
        def _():
            links.greet(("core", "xr", "y"))
            for k in (6, 0, 1):
                remote(k, True).start()

        @pl.when(step == chunks)
        def _():
            remote(7, True).start()

        for k, ready in zip(range(4), WEIGHT_STEPS):
            @pl.when(step == ready * chunks // 8)
            def _(k=k):
                remote(k, False).wait_recv()
                remote(k + 2, True).start()

    @pl.when(step == 0)
    def _():
        carry[...] = jnp.zeros_like(carry)
        is_first = lax.axis_index("seq") == 0
        wg = gate_ref[...]
        spread = jnp.where(iota((heads, LANES), 0) == iota((heads, LANES), 1) % heads, 1.0, 0.0)
        wg_ref[...] = nn(wg, spread.astype(BF16)).astype(BF16)
        wgt_ref[...] = gate_rows(wg)[0:heads]
        lane_head = iota((1, LANES), 1) % heads
        row_head = iota((heads, LANES), 0)
        gb = jnp.zeros((1, LANES), F32)
        gbt = jnp.zeros((heads, LANES), F32)
        for h in range(heads):
            gb = jnp.where(lane_head == h, gb_smem[h], gb)
            gbt = jnp.where(row_head == h, gb_smem[h], gbt)
            begin = start_ref[h].T
            norm = jnp.broadcast_to(start_norm_ref[h : h + 1, :], begin.shape)
            both = [begin, norm] if h % 2 == 0 else [norm, begin]
            state[h] = jnp.where(is_first, jnp.concatenate(both, axis=0), 0.0)
        gb_ref[...] = gb
        gbt_ref[...] = gbt
        for p in range(heads // 2):
            high, rest = projection_blocks(proj_ref, p, 1.0 / (2.0 * math.pi))
            pcat_ref[p, 0:LANES, :] = high
            pcat_ref[p, LANES : 2 * LANES, :] = high
            pcat_ref[p, 2 * LANES : 3 * LANES, :] = rest

    lower = lower_half((C, LANES))

    @pl.when(step < chunks)
    def _():
        xhat, _ = normalize(x_ref[...].astype(F32))
        ml = (xhat * gain_ref[...] + bias_ref[...]).astype(BF16)
        ml_ref[...] = ml
        q = nn(ml, wq_ref[...])
        k = nn(ml, wk_ref[...])
        v = nn(ml, wv_ref[...])
        v_low = v.astype(BF16)
        v_ref[...] = v_low
        v_s[chunk] = v_low
        logit = nn(ml, wg_ref[...]) + gb_ref[...]
        keep = log_sigmoid(logit)
        gain_in = keep - logit
        decay = rows_up_to(keep)
        total = decay[C - 1 : C, :]
        group = iota((C, LANES), 1) // 8
        coef = total - decay + gain_in
        packed = jnp.where(group == 0, decay, coef)
        packed = jnp.where(group == 2, carry[...] + decay, packed)
        packed = jnp.where(group == 6, jnp.broadcast_to(carry[...], (C, LANES)), packed)
        packed = jnp.where(group == 7, jnp.broadcast_to(total, (C, LANES)), packed)
        gcol_ref[...] = packed
        gcol_s[chunk] = packed
        carry[...] = carry[...] + total
        if not comm:
            total_ref[...] = jnp.broadcast_to(carry[...], total_ref.shape)
        logit_row = nt(wgt_ref[...], ml) + gbt_ref[...][:, 0:1]
        keep_row = log_sigmoid(logit_row)
        decay_row = lanes_up_to(keep_row)
        rows = jnp.concatenate(
            [
                keep_row - logit_row - decay_row,
                decay_row,
                jax.nn.sigmoid(logit_row),
                jax.nn.sigmoid(-logit_row),
            ],
            axis=0,
        )
        grow_ref[...] = rows
        grow_s[chunk] = rows

        ftr_scale = 1.0 / math.sqrt(LANES)
        pairs = range(heads // 2)
        lanes_of = [slice(LANES * p, LANES * (p + 1)) for p in pairs]
        boths = [jnp.concatenate([q[:, at], k[:, at]], axis=0) for at in lanes_of]
        scales = [lax.rsqrt(head_sums(both * both) + EPS_UNIT) for both in boths]
        all_turns = []
        for p in pairs:
            unit = boths[p] * scales[p]
            high = unit.astype(BF16)
            rest = (unit - high.astype(F32)).astype(BF16)
            uq_ref[:, lanes_of[p]] = high[:C]
            uk_ref[:, lanes_of[p]] = high[C:]
            rq_ref[:, lanes_of[p]] = scales[p][:C]
            rk_ref[:, lanes_of[p]] = scales[p][C:]
            all_turns.append(nn(jnp.concatenate([high, rest, high], axis=1), pcat_ref[p]))
        for p in pairs:
            s, c = sin_cos(all_turns[p], ftr_scale)
            s = s.astype(BF16)
            c = c.astype(BF16)
            for j in range(2):
                h = 2 * p + j
                half_lanes = slice(LANES * j, LANES * (j + 1))
                feats = jnp.concatenate([s[:, half_lanes], c[:, half_lanes]], axis=1)
                place = slice(256 * h, 256 * (h + 1))
                qf_ref[:, place] = feats[:C]
                qf_s[chunk, :, place] = feats[:C]
                kf = feats[C:]
                kf_ref[:, place] = kf
                kf_s[chunk, :, place] = kf
                values = jnp.where(mine(h, lower), v[:, lanes_of[p]], 1.0)
                weighted = (values * jnp.exp(column(coef, h, C, LANES))).astype(BF16)
                now = state[h]
                now_low = now.astype(BF16)
                before_ref[0, h] = now_low
                before_s[chunk, h] = now_low
                state[h] = jnp.exp(total[:, h : h + 1]) * now + tn(weighted, kf)

    @pl.when(step == chunks - 1)
    def _():
        pack_states([state[h] for h in range(heads)], sent if comm else final_ref)

    @pl.when(step >= chunks)
    def _():
        causal = iota((C, C), 0) >= iota((C, C), 1)
        gcol = gcol_s[chunk]
        for first in range(0, heads, INNER_HEADS):
            some = range(first, first + INNER_HEADS)
            boths = []
            for h in some:
                place = slice(256 * h, 256 * (h + 1))
                keys = jnp.concatenate([kf_s[chunk, :, place], before_s[chunk, h]], axis=0)
                boths.append(nt(qf_s[chunk, :, place], keys))
            decays = [column(gcol, h, C, LANES) for h in some]
            weights = []
            for h, both, decay in zip(some, boths, decays):
                pairs = jnp.where(causal, jnp.exp(decay + grow_s[chunk, h : h + 1, :]), 0.0)
                weights.append((both[:, :C] * pairs).astype(BF16))
            for k, h in enumerate(some):
                lanes = slice(LANES * (h // 2), LANES * (h // 2 + 1))
                v = v_s[chunk, :, lanes].astype(F32)
                values = jnp.where(mine(h, lower), v, 1.0).astype(BF16)
                n_ref[:, LANES * h : LANES * (h + 1)] = (
                    nn(weights[k], values) + jnp.exp(decays[k]) * boths[k][:, C:]
                )

    if comm:
        @pl.when(step == 2 * chunks - 1)
        def _():
            for k in (4, 5, 6, 7):
                remote(k, False).wait_recv()
            later = links.seq == 1
            entry_ref[...] = jnp.where(later, landed[...].astype(F32), 0.0).astype(BF16)
            upbs_ref[0:1, :] = upb_ref[...]
            upbs_ref[1:2, :] = upb_landed[...]
            for k in range(8):
                remote(k, True).wait_send()


def feed_kernel(heads, tiles, pairs, comm, *refs):
    take = Taker(refs)
    x_ref, qf_hbm, n_ref, gcol_ref, entry_ref, wo_ref = take(6)
    gain_ref, bias_ref, downb_ref, upb_ref, dout_hbm = take(5)
    weights_hbm = take(4 if comm else 2)
    out_ref, mg_ref, a_ref = take(3)
    if comm:
        late_refs = take(len(FEED_STAGES))
        os_ref, flat_ref, after_ref = take(3)
    else:
        upg_ref, downg_ref, upbg_ref, o_ref, final_ref, sums_out = take(6)
    entry, adj, middle_s, num_s, den_s, fl_s, mix_s, br_s = take(8)
    acc_s, fg_s, dout_s, up_s, down_s, hid_s, pre_s, sums_s, load_sems = take(9)
    step = pl.program_id(0)
    tokens, width = middle_s.shape
    rows = x_ref.shape[0]
    shards, _, shard_width = up_s.shape
    hb = hid_s.shape[1] // 2
    (qf_s,) = take(1)
    loads = [
        (qf_hbm.at[pl.ds(rows * t, rows)], qf_s.at[pl.ds(rows * t, rows)]) for t in range(tiles)
    ]
    loads += [(dout_hbm, dout_s)]
    if comm:
        up_own, up_other, down_own, down_other = weights_hbm
        loads += [(up_own, up_s.at[0]), (up_other, up_s.at[1])]
        loads += [(down_own, down_s.at[0]), (down_other, down_s.at[1])]
        u_src, upbg_s, sent, landed, sends, recvs = take(6)
        links = Links()
        board = Board(links, take, None)
        for j, (plan, ticks) in enumerate(zip(feed_plans(hb), FEED_TICKS)):
            board.add(plan, u_src.at[j], late_refs[j], None, ticks)

        def exchange():
            return pltpu.make_async_remote_copy(
                src_ref=sent,
                dst_ref=landed,
                send_sem=sends,
                recv_sem=recvs,
                device_id=links.partner("xr", 1),
                device_id_type=MESH,
            )
    else:
        upbg_s = upbg_ref
        loads += [(weights_hbm[0], up_s), (weights_hbm[1], down_s)]

    def load(k):
        return pltpu.make_async_copy(loads[k][0], loads[k][1], load_sems.at[k])

    @pl.when(step == 0)
    def _():
        for k in range(len(loads)):
            load(k).start()
        adj[...] = jnp.zeros_like(adj)
        sums_s[...] = jnp.zeros_like(sums_s)
        norms = entry_ref[64 * heads : 64 * heads + 16, :].astype(F32)
        for h in range(heads):
            grown = grow_state(entry_ref[64 * h : 64 * (h + 1), :], norms[h : h + 1], h)
            entry[h] = grown.astype(BF16)
        if comm:
            links.greet(("core", "xr", "y", "z"))

    lower = lower_half((rows, LANES))

    @pl.when(step < tiles)
    def _():
        for t in range(tiles):
            pl.when(step == t)(load(t).wait)
        here = pl.ds(pl.multiple_of(step * rows, rows), rows)
        gcol = gcol_ref[...]
        fars = [nt(qf_s[here, 256 * h : 256 * (h + 1)], entry[h]) for h in range(heads)]
        mixed = []
        for p in range(heads // 2):
            lanes = slice(LANES * p, LANES * (p + 1))
            both = []
            for h in (2 * p, 2 * p + 1):
                far = fars[h] * jnp.exp(column(gcol, 16 + h, rows, LANES))
                both.append(n_ref[:, LANES * h : LANES * (h + 1)] + far)
            num = jnp.where(lower, both[0], both[1])
            den = pltpu.roll(jnp.where(lower, both[1], both[0]), 64, 1)
            num_s[here, lanes] = num
            den_s[here, lanes] = den
            mixed.append(num * lax.rsqrt(den * den + GUARD))
        mixed = jnp.concatenate(mixed, axis=1).astype(BF16)
        mix_s[here, :] = mixed
        middle = x_ref[...].astype(F32) + nn(mixed, wo_ref[...])
        middle_s[here, :] = middle
        acc_s[here, :] = middle + downb_ref[...]
        fg_s[here, :] = jnp.zeros_like(middle)
        xhat, _ = normalize(middle)
        fl_s[here, :] = (xhat * gain_ref[...] + bias_ref[...]).astype(BF16)

    @pl.when(step == tiles)
    def _():
        for k in range(tiles, len(loads)):
            load(k).wait()

    @pl.when(jnp.logical_and(step >= tiles, step < tiles + pairs))
    def _():
        j = step - tiles
        blocks = []
        for s in range(2):
            if comm:
                shard, off = s, pl.multiple_of(j * hb, hb)
            else:
                at = (2 * j + s) * hb
                shard, off = at // shard_width, pl.multiple_of(at % shard_width, hb)
            blocks.append((shard, pl.ds(off, hb)))
        ups = [up_s[shard, :, cols] for shard, cols in blocks]
        downs = [down_s[shard, :, cols] for shard, cols in blocks]
        up = jnp.concatenate(ups, axis=1)
        down = jnp.concatenate(downs, axis=1)
        if comm:
            upb = jnp.concatenate(
                [upb_ref[s : s + 1, cols] for s, (_, cols) in enumerate(blocks)], axis=1
            )
        else:
            upb = jnp.concatenate([upb_ref[shard, :, cols] for shard, cols in blocks], axis=1)
        for r in range(tokens // rows):
            if comm and r % 2 == 0:
                for k in range(pairs):
                    pl.when(j == k)(partial(board.advance, 2 * k + r // 2))
            here = slice(rows * r, rows * (r + 1))
            feed_low = fl_s[here, :]
            pre = nn(feed_low, up) + upb
            pre_grad = nn(dout_s[here, :], down)
            t = 1.0 / (1.0 + ERF_P * jnp.abs(pre))
            bell = INV_SQRT_2PI * jnp.exp(-0.5 * pre * pre)
            tail = ((((ERF[4] * t + ERF[3]) * t + ERF[2]) * t + ERF[1]) * t + ERF[0]) * t * bell
            phi = jnp.where(pre >= 0.0, 1.0 - tail, tail)
            hidden = (pre * phi).astype(BF16)
            pre_low = (pre_grad * (phi + pre * bell)).astype(BF16)
            hid_s[here, :] = hidden
            pre_s[here, :] = pre_low
            acc_s[here, :] += nt(hidden, down)
            fg_s[here, :] += nt(pre_low, up)
        up_grad = tn(fl_s[...], pre_s[...]).astype(BF16)
        down_grad = tn(dout_s[...], hid_s[...]).astype(BF16)
        bias_grad = nn(jnp.ones((16, tokens), BF16), pre_s[...])[0:1]
        for s, (shard, cols) in enumerate(blocks):
            part = slice(hb * s, hb * (s + 1))
            upbg_s[shard, :, cols] = bias_grad[:, part]
            if comm:
                u_src[j, width * s : width * (s + 1), :] = up_grad[:, part]
                u_src[j, width * (2 + s) : width * (3 + s), :] = down_grad[:, part]
            else:
                upg_ref[shard, :, cols] = up_grad[:, part]
                downg_ref[shard, :, cols] = down_grad[:, part]

    @pl.when(step >= tiles + pairs)
    def _():
        tile = step - tiles - pairs

        if comm:
            for t in range(tiles):
                pl.when(tile == t)(partial(board.advance, 2 * pairs + t))
        here = pl.ds(pl.multiple_of(tile * rows, rows), rows)
        gcol = gcol_ref[...]
        dout = dout_s[here, :].astype(F32)
        out_ref[...] = acc_s[here, :].astype(BF16)
        feed_grad = fg_s[here, :]
        xhat, scale = normalize(middle_s[here, :])
        sums_s[0:8, :] += fold_rows(feed_grad * xhat)
        sums_s[8:16, :] += fold_rows(feed_grad)
        sums_s[16:24, :] += fold_rows(dout)
        middle_grad = dout + normalize_back(feed_grad, gain_ref[...], xhat, scale)
        mg_ref[...] = middle_grad
        branch = middle_grad.astype(BF16)
        br_s[here, :] = branch
        mixed_grad = nt(branch, wo_ref[...])
        lanes_of = [slice(LANES * p, LANES * (p + 1)) for p in range(heads // 2)]
        alongs = [head_sums(mixed_grad[:, lanes] * num_s[here, lanes]) for lanes in lanes_of]
        lifts = []
        for p, lanes in enumerate(lanes_of):
            den = den_s[here, lanes]
            inv = lax.rsqrt(den * den + GUARD)
            b = alongs[p] * den * (inv * inv * inv) * (-1.0 / 64)
            b = pltpu.roll(b, 64, 1)
            for h in (2 * p, 2 * p + 1):
                a = jnp.where(mine(h, lower), mixed_grad[:, lanes] * inv, b)
                a_ref[:, LANES * h : LANES * (h + 1)] = a.astype(BF16)
                lifts.append((a * jnp.exp(column(gcol, 16 + h, rows, LANES))).astype(BF16))
        for h in range(heads):
            adj[h] += tn(lifts[h], qf_s[here, 256 * h : 256 * (h + 1)])

    @pl.when(step == 2 * tiles + pairs - 1)
    def _():
        pack_states([adj[h] for h in range(heads)], sent if comm else final_ref)
        if comm:
            exchange().start()
        output_grad = tn(mix_s[...], br_s[...]).astype(BF16)
        if not comm:
            o_ref[...] = output_grad
            sums_out[...] = sums_s[...]
            return
        os_ref[:, 0:width] = output_grad
        for later in range(2 * pairs + tiles, board.last() + 1):
            board.advance(later)
        exchange().wait_recv()
        is_first = links.seq == 0
        after_ref[...] = jnp.where(is_first, landed[...].astype(F32), 0.0).astype(BF16)
        logs = gcol_ref[rows - 1 : rows, :]
        norms = landed[64 * heads : 64 * heads + 16, :].astype(F32)
        flat_ref[...] = jnp.zeros_like(flat_ref)
        for k in range(3):
            flat_ref[k : k + 1, :] = jnp.sum(sums_s[8 * k : 8 * (k + 1), :], axis=0, keepdims=True)
        for k in range(2 * shard_width // width):
            cols = slice(width * k % shard_width, width * k % shard_width + width)
            in_first = k < shard_width // width
            own, other = upbg_s[0, :, cols], upbg_s[1, :, cols]
            flat_ref[3 + k : 4 + k, :] = jnp.where(is_first, own, other) if in_first else jnp.where(
                is_first, other, own
            )
        for h in range(heads):
            grown = grow_state(landed[64 * h : 64 * (h + 1), :], norms[h : h + 1], h)
            begin = adj[h] + jnp.exp(logs[:, 16 + h : 17 + h]) * grown
            begin = jnp.where(is_first, begin, 0.0)
            os_ref[64 * h : 64 * (h + 1), width : width + 256] = state_part(begin, h).astype(BF16)
            flat_ref[8 + h : 9 + h, 0:256] = 64.0 * norm_part(begin, h)
        exchange().wait_send()
        board.drain()


U_SCATTER, U_GATHER = ("core", "xr", "y", "z"), ("z", "y", "core")
FEED_STAGES = (4, 3, 2, 1)
FEED_TICKS = ((2, 3, 6, 8, 11), (4, 6, 9, 12), (6, 8, 12), (8, 10))
BACK_TICKS = ((2, 4, 6, 7), (1, 3, 5, 7, 8), (1, 3, 5, 7, 8, 9), (1, 3, 5, 7, 8, 9, 10))


def feed_plans(hb):
    return [Plan(2048, hb, BF16, U_SCATTER[:n], ()) for n in FEED_STAGES]


def late_plans(hb):
    plans = []
    for plan, n in zip(feed_plans(hb), FEED_STAGES):
        done = [group for group in U_SCATTER[:n] if group != "xr"]
        plans.append(Plan(plan.left, hb, BF16, U_SCATTER[n:], U_GATHER, pre=tuple(done)))
    return plans


def back_kernel(heads, hg, span, chunks, comm, *refs):
    take = Taker(refs)
    (qf_ref, kf_ref, v_ref, uq_ref, uk_ref, rq_ref, rk_ref, a_ref, gcol_ref, grow_ref) = take(10)
    before_ref, entry_ref, entry_norm, after_ref, after_norm, proj_in = take(6)
    x_hbm, mg_hbm, ml_hbm, wq_hbm, wk_hbm, wv_hbm, gate_ref, gain_ref = take(8)
    u_hbms = take(len(FEED_STAGES)) if comm else ()
    os_hbm, f_hbm = take(2) if comm else (None,) * 2
    dx_ref, w_ref, small_ref = take(3)
    usum_hbm, ossum_hbm, fsum_hbm = take(3) if comm else (None,) * 3
    adj_ref, dqkv, dlogit, x_ref, mg_ref, ml_ref, wq_ref, wk_ref, wv_ref, load_sems = take(10)
    (proj_ref,) = take(1)
    g, i = pl.program_id(0), pl.program_id(1)
    tick = g * chunks + i
    last = heads // hg * chunks - 1
    first_row = (chunks - 1 - i) * (span * C)
    here = pl.ds(pl.multiple_of(first_row, C), span * C)
    groups = heads // hg
    loads = [
        (x_hbm, x_ref),
        (mg_hbm, mg_ref),
        (ml_hbm, ml_ref),
        (wq_hbm, wq_ref),
        (wk_hbm, wk_ref),
        (wv_hbm, wv_ref),
    ]
    if comm:
        u_refs = take(len(FEED_STAGES))
        os_ref, f_ref, w_src, small_src = take(4)
        usum_ref, ossum_ref, fsum_ref, wsum_ref, smallsum_ref = take(5)
        (store_sems,) = take(1)
        loads = list(zip(u_hbms, u_refs)) + [(os_hbm, os_ref), (f_hbm, f_ref)] + loads
        early_loads = len(loads) - 6
        links = Links()
        board = Board(links, take, store_sems)
        plans = back_plans(os_hbm.shape, f_hbm.shape, w_src.shape, small_src.shape)

        def stages(start, gaps):
            ticks = [start]
            for gap in gaps:
                ticks.append(ticks[-1] + gap)
            return ticks

        for j, (plan, ticks) in enumerate(zip(late_plans(usum_ref.shape[2]), BACK_TICKS)):
            board.add(plan, u_refs[j], usum_ref.at[j], usum_hbm.at[j], ticks)
        board.add(plans["os"], os_ref, ossum_ref, ossum_hbm, OS_TICKS)
        board.add(plans["f"], f_ref, fsum_ref, fsum_hbm, F_TICKS)
        for k in range(groups):
            final = k + 1 == groups
            pieces = W_PIECES if final else 1
            lanes_each = w_src.shape[2] // pieces
            for j in range(pieces):
                lanes = pl.ds(j * lanes_each, lanes_each)
                board.add(
                    plans["w_last" if final else "w"],
                    w_src.at[k, :, lanes],
                    wsum_ref.at[k, :, lanes],
                    w_ref.at[k, :, lanes],
                    [last + 1 + i for i in range(7)] if final else W_TICKS,
                )
        advance = board.advance

    def load(k):
        return pltpu.make_async_copy(loads[k][0], loads[k][1], load_sems.at[k])

    @pl.when(tick == 0)
    def _():
        for k in range(len(loads)):
            load(k).start()
        dlogit[...] = jnp.zeros_like(dlogit)
        if comm:
            links.greet(("core", "plane", "z"))

    if comm:
        @pl.when(tick == 1)
        def _():
            for k in range(early_loads):
                load(k).wait()

        for now in range(1, last + 1):
            pl.when(tick == now)(partial(advance, now))

    @pl.when(i == 0)
    def _():
        for p in range(hg // 2):
            proj_ref[p] = projection_blocks(proj_in, p, 1.0 / (2.0 * math.pi))[0]
        norms = after_norm[...].astype(F32)
        for h in range(hg):
            norm = pick_row(norms, g * hg + h)
            adj_ref[h] = grow_state(after_ref[64 * h : 64 * (h + 1), :], norm, h)

    row = iota((C, C), 0)
    col = iota((C, C), 1)
    causal = row >= col
    one = jnp.ones((C, C), BF16)
    zero = jnp.zeros((C, C), BF16)
    later = jnp.where(row < col, 1.0, 0.0).astype(BF16)
    pair_sums = jnp.concatenate([later, one], axis=0)
    two_sums = jnp.concatenate(
        [jnp.concatenate([one, zero], axis=1), jnp.concatenate([zero, one], axis=1)], axis=0
    )
    lower = lower_half((C, LANES))
    entry_norms = entry_norm[...].astype(F32)
    gcol = gcol_ref[...]
    if groups > 1:
        gcol = jnp.where(g == 0, gcol, pltpu.roll(gcol, LANES - hg, 1))

    def grow_row(kind, h):
        return grow_ref[pl.ds(kind * heads + g * hg + h, 1), :]

    width = hg * 64
    pairs_of_heads = range(hg // 2)
    lanes_of = [slice(LANES * p, LANES * (p + 1)) for p in pairs_of_heads]
    items = [(u, h) for u in reversed(range(span)) for h in range(hg)]
    numbers = range(len(items))
    rows_of = [slice(C * u, C * (u + 1)) for u in range(span)]
    qfs = [qf_ref[rows_of[u], 256 * h : 256 * (h + 1)] for u, h in items]
    kfs = [kf_ref[rows_of[u], 256 * h : 256 * (h + 1)] for u, h in items]
    a_lows = [a_ref[rows_of[u], LANES * h : LANES * (h + 1)] for u, h in items]
    values = [
        jnp.where(mine(h, lower), v_ref[rows_of[u], lanes_of[h // 2]].astype(F32), 1.0)
        for u, h in items
    ]
    values_low = [part.astype(BF16) for part in values]
    lifts = [jnp.exp(column(gcol[rows_of[u]], h, C, LANES)) for u, h in items]
    a_lifts = [(a_lows[k].astype(F32) * lifts[k]).astype(BF16) for k in numbers]
    dweights = []
    for k in numbers[::2]:
        u, h = items[k]
        top = jnp.concatenate([values_low[k], zero], axis=1)
        bottom = jnp.concatenate([zero, values_low[k + 1]], axis=1)
        both = nt(
            a_ref[rows_of[u], LANES * h : LANES * (h + 2)],
            jnp.concatenate([top, bottom], axis=0),
        )
        dweights += [both[:, :C], both[:, C:]]
    adj_lows, throughs, keys_and_states = [], [], []
    raws, fars, dv_fars = [], [], []
    for k, (u, h) in enumerate(items):
        carried = jnp.exp(gcol[C * u : C * u + 1, 48 + h : 49 + h])
        total = jnp.exp(gcol[C * u : C * u + 1, 56 + h : 57 + h])
        entry = grow_state(
            entry_ref[64 * h : 64 * (h + 1), :], pick_row(entry_norms, g * hg + h), h
        )
        before = before_ref[u, h].astype(F32) + carried * entry
        adj = adj_ref[h]
        adj_lows.append(adj.astype(BF16))
        kept = total * adj
        through = jnp.sum(kept * before, axis=0, keepdims=True)
        throughs.append(jnp.sum(through, axis=1, keepdims=True))
        keys_and_states.append(jnp.concatenate([kfs[k], before.astype(BF16)], axis=0))
        raw_and_far = nt(qfs[k], keys_and_states[k])
        raws.append(raw_and_far[:, :C])
        fars.append(raw_and_far[:, C:])
        dv_fars.append(nt(kfs[k], adj_lows[k]))
        if u > 0:
            adj_ref[h] = kept + tn(a_lifts[k], qfs[k])
        else:
            adj_ref[h] = kept
    coefs = [jnp.exp(column(gcol[rows_of[u]], 8 + h, C, LANES)) for u, h in items]
    weights, draws, boths, v_coefs = [], [], [], []
    for k, (u, h) in enumerate(items):
        gap = column(gcol[rows_of[u]], h, C, LANES) + grow_row(0, h)[:, rows_of[u]]
        pairs = jnp.where(causal, jnp.exp(gap), 0.0)
        weights.append((raws[k] * pairs).astype(BF16))
        draw = dweights[k].astype(BF16).astype(F32) * pairs
        draws.append(draw.astype(BF16))
        boths.append((raws[k] * draw).astype(BF16))
        v_coefs.append((values[k] * coefs[k]).astype(BF16))
    dqs, dks, dvs = [], [], []
    for k in numbers:
        dqs.append(nn(jnp.concatenate([draws[k], a_lifts[k]], axis=1), keys_and_states[k]))
        dks.append(
            nn(
                jnp.concatenate([draws[k].T, v_coefs[k]], axis=1),
                jnp.concatenate([qfs[k], adj_lows[k]], axis=0),
            )
        )
        dvs.append(tn(weights[k], a_lows[k]))
        if items[k][0] == 0:
            adj_ref[items[k][1]] += tn(a_lifts[k], qfs[k])
    x_parts, y_parts = [], []
    for k in numbers:
        dv_far = coefs[k] * dv_fars[k]
        dvs[k] = dvs[k] + dv_far
        x_far = (a_lows[k].astype(F32) * lifts[k] * fars[k]).astype(BF16)
        x_parts.append(jnp.concatenate([boths[k], x_far], axis=1))
        y_far = (values[k] * dv_far).astype(BF16)
        y_parts.append(jnp.concatenate([y_far, (values[k] * dvs[k]).astype(BF16)], axis=1))
    upto = nn(jnp.concatenate(x_parts, axis=0), pair_sums)
    ends = nn(jnp.concatenate(y_parts, axis=0), two_sums)
    dus = []
    for p in pairs_of_heads:
        angles = []
        for feats, grads in ((qfs, dqs), (kfs, dks)):
            for u in range(span):
                row_angles = []
                for k, item in enumerate(items):
                    if item[0] == u and item[1] // 2 == p:
                        f, grad = feats[k].astype(F32), grads[k]
                        row_angles.append(
                            grad[:, :LANES] * f[:, LANES:] - grad[:, LANES:] * f[:, :LANES]
                        )
                angles.append(jnp.concatenate(row_angles, axis=1))
        dus.append(nt(jnp.concatenate(angles, axis=0).astype(BF16), proj_ref[p]))
    for k, (u, h) in enumerate(items):
        rows = slice(C * k, C * (k + 1))
        flow = jnp.where(causal, upto[rows], ends[rows, :C])
        flow = jnp.sum(flow, axis=0, keepdims=True) + throughs[k]
        own = jnp.sum(jnp.where(row == col, ends[rows, C:], 0.0), axis=0, keepdims=True)
        stay, leave = grow_row(2, h)[:, rows_of[u]], grow_row(3, h)[:, rows_of[u]]
        at = pl.ds(pl.multiple_of(first_row + C * u, C), C)
        dlogit[g, h : h + 1, at] = leave * flow - stay * own
    for p, lanes in enumerate(lanes_of):
        u = jnp.concatenate([uq_ref[:, lanes], uk_ref[:, lanes]], axis=0).astype(F32)
        scale = jnp.concatenate([rq_ref[:, lanes], rk_ref[:, lanes]], axis=0)
        along = nn((u * dus[p]).astype(BF16), block_ones())
        dqk = ((2.0 * math.pi) * scale * (dus[p] - u * along)).astype(BF16)
        dqkv[g, here, LANES * p : LANES * (p + 1)] = dqk[: span * C]
        dqkv[g, here, width + LANES * p : width + LANES * (p + 1)] = dqk[span * C :]
        for k, (u, h) in enumerate(items):
            if h == 2 * p:
                at = pl.ds(pl.multiple_of(first_row + C * u, C), C)
                dqkv[g, at, 2 * width + LANES * p : 2 * width + LANES * (p + 1)] = jnp.where(
                    lower, dvs[k], dvs[k + 1]
                ).astype(BF16)

    @pl.when(i == chunks - 1)
    def _():
        @pl.when(g == 0)
        def _():
            load(len(loads) - 4).wait()

        grads = tn(ml_ref[...], dqkv[g]).astype(BF16)
        if comm:
            w_src[g] = grads
        else:
            w_ref[g] = grads

    @pl.when(tick == last)
    def _():
        if comm:
            advance(last + 1)
        for k in range(len(loads) - 6, len(loads)):
            if k != len(loads) - 4:
                load(k).wait()
        tokens = chunks * span * C
        block = min(T, tokens)
        small = small_src if comm else small_ref
        rows8 = jnp.concatenate(
            [dlogit[k, 0:hg, :] for k in range(groups)]
            + [jnp.zeros((16 - heads, dlogit.shape[2]), F32)],
            axis=0,
        ).astype(BF16)
        small[...] = jnp.zeros_like(small)
        small[0:heads, :] = nn(rows8, ml_ref[...])[0:heads]
        bias_sum = nt(jnp.ones(rows8.shape, BF16), rows8)[0:1]
        small[heads : heads + 1, 0:16] = bias_sum
        gate_low = gate_rows(gate_ref[...])
        gain = gain_ref[...]
        now = last + 2
        for b in range(tokens // block):
            rows = slice(block * b, block * (b + 1))
            mixer_grad = tn(rows8[:, rows], gate_low)
            for k in range(groups):
                for j, ref in enumerate((wq_ref, wk_ref, wv_ref)):
                    mixer_grad = mixer_grad + nt(
                        dqkv[k, rows, hg * 64 * j : hg * 64 * (j + 1)],
                        ref[:, hg * 64 * k : hg * 64 * (k + 1)],
                    )
            xhat, scale = normalize(x_ref[rows, :].astype(F32))
            small[heads + 1 : heads + 2, :] += jnp.sum(
                mixer_grad * xhat, axis=0, keepdims=True
            )
            small[heads + 2 : heads + 3, :] += jnp.sum(mixer_grad, axis=0, keepdims=True)
            dx_ref[rows, :] = mg_ref[rows, :] + normalize_back(mixer_grad, gain, xhat, scale)
            if comm and b % 2 == 1 and b + 1 < tokens // block:
                advance(now)
                now += 1
        if comm:
            board.add(
                plans["small"], small_src, smallsum_ref, small_ref, [now, now + 1, now + 2, now + 3]
            )
            for later_tick in range(now, board.last() + 1):
                advance(later_tick)
            board.drain()


OS_TICKS = (1, 3, 6, 8, 9, 10, 11)
F_TICKS = (2, 4, 6, 8)
W_TICKS = (4, 6, 8, 9, 10, 11, 12)
W_PIECES = 3
SUM_ROWS = 16


def back_plans(os, f, w, small):
    return {
        "os": Plan(os[0], os[1], BF16, *ALL_PLAN),
        "f": Plan(f[0], f[1], F32, *SHARE_PLAN),
        "w": Plan(w[1], w[2], BF16, *ALL_PLAN),
        "w_last": Plan(w[1], w[2] // W_PIECES, BF16, *ALL_PLAN),
        "small": Plan(small[0], small[1], F32, *SHARE_PLAN),
    }


def whole(shape):
    zeros = (0,) * len(shape)
    return pl.BlockSpec(shape, lambda *at: zeros, pipeline_mode=pl.Buffered(1))


ANY = pl.BlockSpec(memory_space=pl.ANY)


def call(kernel, grid, ins, outs, scratch, name, collective_id=None):
    def spec(shape, block, index):
        if block is None:
            return whole(shape)
        return block if isinstance(block, pl.BlockSpec) else pl.BlockSpec(block, index)

    params = {} if collective_id is None else {
        "collective_id": collective_id, "has_side_effects": True
    }
    return pl.pallas_call(
        kernel,
        grid=grid,
        in_specs=[spec(array.shape, block, index) for array, block, index in ins],
        out_specs=[spec(shape, block, index) for shape, _, block, index in outs],
        out_shape=[jax.ShapeDtypeStruct(shape, dtype) for shape, dtype, _, _ in outs],
        scratch_shapes=scratch,
        compiler_params=pltpu.CompilerParams(
            dimension_semantics=("arbitrary",) * len(grid), vmem_limit_bytes=VMEM, **params
        ),
        name=name,
    )(*[array for array, _, _ in ins])


def finish_kernel(
    late_ref, w_ref, os_ref, up_ref, down_ref, q_ref, k_ref, v_ref, o_ref, s_ref
):
    hb = late_ref.shape[3]
    for part, ref in enumerate((up_ref, down_ref)):
        for k in range(late_ref.shape[0]):
            ref[:, hb * k : hb * (k + 1)] = late_ref[k, part].astype(F32)
    groups, _, lanes = w_ref.shape
    each = lanes // 3
    for part, ref in enumerate((q_ref, k_ref, v_ref)):
        for k in range(groups):
            ref[:, each * k : each * (k + 1)] = w_ref[k, :, each * part : each * (part + 1)].astype(F32)
    width = o_ref.shape[1]
    o_ref[...] = os_ref[:, 0:width].astype(F32)
    for k in range(s_ref.shape[0]):
        s_ref[k] = os_ref[64 * k : 64 * (k + 1), width:].astype(F32).T


def finish(heads, sum_late, sum_w, out_state):
    width = sum_w.shape[1]
    steps = 4
    rows = width // steps
    late, _, hb = sum_late.shape
    feats = out_state.shape[1] - width
    square = ((width, width), F32, (rows, width), lambda i: (i, 0))
    wide = ((width, late * hb), F32, (rows, late * hb), lambda i: (i, 0))
    return call(
        finish_kernel,
        (steps,),
        [
            (sum_late.reshape(late, 2, width, hb), (late, 2, rows, hb), lambda i: (0, 0, i, 0)),
            (sum_w, (sum_w.shape[0], rows, sum_w.shape[2]), lambda i: (0, i, 0)),
            (out_state, (rows, width + feats), lambda i: (i, 0)),
        ],
        [wide, wide, square, square, square, square]
        + [((heads, feats, 64), F32, (heads // steps, feats, 64), lambda i: (i, 0, 0))],
        [],
        "finish",
    )


def carry_over(payload, logs, forward):
    n, index = lax.axis_size("seq"), lax.axis_index("seq")
    everything = lax.all_gather(payload, "seq")
    every_log = lax.all_gather(logs, "seq")
    heads = logs.shape[0]
    row = jnp.arange(payload.shape[0])
    head = jnp.where(row < 64 * heads, row // 64, jnp.minimum(row - 64 * heads, heads - 1))
    total = jnp.zeros(payload.shape, F32)
    for k in range(n) if forward else reversed(range(n)):
        ahead = (k < index) if forward else (k > index)
        new = jnp.exp(every_log[k])[head][:, None] * total + everything[k].astype(F32)
        total = jnp.where(ahead, new, total)
    return total.astype(BF16)


def local(
    inputs,
    cotangent,
    mixer_gain,
    mixer_bias,
    query_weight,
    key_weight,
    value_weight,
    gate_weight,
    gate_bias,
    output_weight,
    projections,
    start_state,
    start_norm,
    feed_gain,
    feed_bias,
    up_weight,
    up_bias,
    down_weight,
    down_bias,
):
    _, tokens, width = inputs.shape
    heads, size, feats = projections.shape
    chunks = tokens // C
    tile = min(T, tokens)
    tiles = tokens // tile
    shards = lax.axis_size("seq")
    first = lax.axis_index("seq") == 0
    comm = (lax.axis_size("dp"), shards) == (16, 2)
    x = inputs.reshape(tokens, width)
    dout = cotangent.reshape(tokens, width)
    shard_width = up_weight.shape[1]
    hidden = shard_width * shards
    hb = min(HB, shard_width)
    pairs = hidden // (2 * hb)
    wide = heads * LANES
    wider = heads * 2 * feats
    pay_shape = (heads * 64 + 16, 2 * feats)

    def const(array):
        return (array if array.ndim > 1 else array[None], None, None)

    def keep(shape, dtype):
        return (shape, dtype, None, None)

    def hbm(array):
        return (array, ANY, None)

    def result(shape, dtype):
        return (shape, dtype, ANY, None)

    def vmem(*shape, dtype=BF16):
        return pltpu.VMEM(shape, dtype)

    def early(n):
        return (C, n), lambda i: (jnp.minimum(i, chunks - 1), 0)

    def out_early(n, dtype):
        return ((tokens, n), dtype) + early(n)

    ins = [(x,) + early(width)]
    ins += [const(part) for part in (mixer_gain, mixer_bias, query_weight, key_weight)]
    ins += [
        const(value_weight),
        const(gate_weight),
        (gate_bias, pl.BlockSpec(memory_space=pltpu.SMEM), None),
        const(projections),
        const(start_state),
        const(start_norm),
    ]
    outs = [out_early(width, BF16)] * 3 + [out_early(width, F32)] * 2
    outs += [out_early(wider, BF16)] * 2 + [out_early(width, BF16), out_early(LANES, F32)]
    outs += [
        (
            (4 * heads, tokens),
            F32,
            (4 * heads, C),
            lambda i: (0, jnp.minimum(i, chunks - 1)),
        ),
        (
            (chunks, heads, LANES, 2 * feats),
            BF16,
            (1, heads, LANES, 2 * feats),
            lambda i: (jnp.minimum(i, chunks - 1), 0, 0, 0),
        ),
        ((tokens, wide), F32, (C, wide), lambda i: (jnp.maximum(i - chunks, 0), 0)),
    ]
    scratch = [
        vmem(heads, LANES, 2 * feats, dtype=F32),
        vmem(1, LANES, dtype=F32),
        vmem(chunks, C, wider),
        vmem(chunks, C, wider),
        vmem(chunks, C, width),
        vmem(chunks, C, LANES, dtype=F32),
        vmem(chunks, 4 * heads, C, dtype=F32),
        vmem(chunks, heads, LANES, 2 * feats),
        vmem(width, LANES),
        vmem(heads, width),
        vmem(1, LANES, dtype=F32),
        vmem(heads, LANES, dtype=F32),
        vmem(heads // 2, 3 * LANES, 2 * feats),
    ]
    upb = up_bias.astype(F32)[None]
    if comm:
        ins += [hbm(up_weight), hbm(down_weight), const(upb)]
        outs += [
            keep(pay_shape, BF16),
            result(up_weight.shape, BF16),
            result(down_weight.shape, BF16),
            keep((2, shard_width), F32),
        ]
        scratch += [
            vmem(*pay_shape),
            vmem(*pay_shape),
            vmem(1, shard_width, dtype=F32),
            pltpu.SemaphoreType.DMA((8,)),
            pltpu.SemaphoreType.DMA((8,)),
        ]
    else:
        outs += [keep(pay_shape, BF16), keep((8, LANES), F32)]
    found = call(
        partial(features_kernel, heads, chunks, comm),
        (2 * chunks,),
        ins,
        outs,
        scratch,
        "features",
        1 if comm else None,
    )
    ml, uq, uk, rq, rk, qf, kf, v, gcol, grow, before, num = found[:12]
    if comm:
        entry, up_other, down_other, upb = found[12:]
        weights = (up_weight, up_other, down_weight, down_other)
    else:
        final, total = found[12:]
        logs = total[0, :heads]
        entry = carry_over(final, logs, True)
        weights = (lax.all_gather(up_weight, "seq"), lax.all_gather(down_weight, "seq"))
        upb = lax.all_gather(upb, "seq")

    steps = 2 * tiles + pairs

    def first_last(n):
        def index(i):
            late = jnp.maximum(i - tiles - pairs, 0)
            return (jnp.where(i < tiles + pairs, jnp.minimum(i, tiles - 1), late), 0)

        return (tile, n), index

    def only_first(n):
        return (tile, n), lambda i: (jnp.minimum(i, tiles - 1), 0)

    def only_last(n, dtype):
        return (
            (tokens, n),
            dtype,
            (tile, n),
            lambda i: (jnp.maximum(i - tiles - pairs, 0), 0),
        )

    ins = [
        (x,) + only_first(width),
        hbm(qf),
        (num,) + only_first(wide),
        (gcol,) + first_last(LANES),
        const(entry),
        const(output_weight),
        const(feed_gain),
        const(feed_bias),
        const(down_bias),
        const(upb),
        hbm(dout),
    ] + [hbm(part) for part in weights]
    outs = [only_last(width, BF16), only_last(width, F32), only_last(wide, BF16)]
    scratch = [
        vmem(heads, LANES, 2 * feats),
        vmem(heads, LANES, 2 * feats, dtype=F32),
        vmem(tokens, width, dtype=F32),
        vmem(tokens, width, dtype=F32),
        vmem(tokens, width, dtype=F32),
        vmem(tokens, width),
        vmem(tokens, width),
        vmem(tokens, width),
        vmem(tokens, width, dtype=F32),
        vmem(tokens, width, dtype=F32),
        vmem(tokens, width),
        vmem(shards, width, shard_width),
        vmem(shards, width, shard_width),
        vmem(tokens, 2 * hb),
        vmem(tokens, 2 * hb),
        vmem(24, width, dtype=F32),
        pltpu.SemaphoreType.DMA((5 + tiles,)),
        vmem(tokens, wider),
    ]
    if comm:
        plans = feed_plans(hb)
        outs += [
            *[keep((plan.left, hb), BF16) for plan in plans],
            keep((width, width + 2 * feats), BF16),
            keep((16, width), F32),
            keep(pay_shape, BF16),
        ]
        scratch += [
            vmem(pairs, 4 * width, hb),
            vmem(shards, 1, shard_width, dtype=F32),
            vmem(*pay_shape),
            vmem(*pay_shape),
            pltpu.SemaphoreType.DMA,
            pltpu.SemaphoreType.DMA,
        ]
        for plan in plans:
            scratch += plan.scratch()
    else:
        outs += [
            keep((shards, width, shard_width), BF16),
            keep((shards, width, shard_width), BF16),
            keep((shards, 1, shard_width), F32),
            keep((width, width), BF16),
            keep(pay_shape, BF16),
            keep((24, width), F32),
        ]
    found = call(
        partial(feed_kernel, heads, tiles, pairs, comm),
        (steps,),
        ins,
        outs,
        scratch,
        "feed",
        2 if comm else None,
    )
    out, mg, a = found[:3]
    if comm:
        u_late = found[3:-3]
        out_state, flat, after = found[-3:]
    else:
        up_grad, down_grad, upb_grad, output_grad, adj_final, feed_sums = found[3:]
        after = carry_over(adj_final, logs, False)
        feed_three = jnp.sum(feed_sums.reshape(3, 8, width), axis=1)
        begin = adj_final.astype(F32)
        row = jnp.arange(pay_shape[0])
        head = jnp.where(row < 64 * heads, row // 64, jnp.minimum(row - 64 * heads, heads - 1))
        begin = begin + jnp.exp(logs)[head][:, None] * after.astype(F32)
        begin = jnp.where(first, begin, 0.0)
        state_grad = begin[: heads * 64].astype(BF16)
        norm_grad = 64.0 * begin[heads * 64 : heads * 65]

    hg = GROUP_HEADS
    groups = heads // hg
    span = min(SPAN, chunks)
    blocks = chunks // span

    def back_rows(n, per_group=True):
        return (span * C, n), lambda g, i: (blocks - 1 - i, g if per_group else 0)

    def per_group(array, *shape):
        zeros = (0,) * (len(shape) - 1)
        return (array, shape, lambda g, i: (g,) + zeros)

    def states(array):
        return [
            (array, (hg * 64, 2 * feats), lambda g, i: (g, 0)),
            (array, (16, 2 * feats), lambda g, i: (heads * 4, 0)),
        ]

    ins = [
        (qf,) + back_rows(hg * 2 * feats),
        (kf,) + back_rows(hg * 2 * feats),
        (v,) + back_rows(hg * size),
        (uq,) + back_rows(hg * size),
        (uk,) + back_rows(hg * size),
        (rq,) + back_rows(hg * size),
        (rk,) + back_rows(hg * size),
        (a,) + back_rows(hg * LANES),
        (gcol,) + back_rows(LANES, False),
        (grow, (4 * heads, span * C), lambda g, i: (0, blocks - 1 - i)),
        (before, (span, hg, LANES, 2 * feats), lambda g, i: (blocks - 1 - i, g, 0, 0)),
    ]
    ins += states(entry) + states(after)
    ins += [
        per_group(projections, hg, size, feats),
        hbm(x),
        hbm(mg),
        hbm(ml),
        hbm(query_weight),
        hbm(key_weight),
        hbm(value_weight),
        const(gate_weight),
        const(mixer_gain),
    ]
    w_shape, small_shape = (groups, width, 3 * hg * size), (16, width)

    def sums(shape, dtype):
        return result(shape, dtype) if comm else keep(shape, dtype)

    outs = [keep((tokens, width), F32), sums(w_shape, BF16), sums(small_shape, F32)]
    scratch = [
        vmem(hg, LANES, 2 * feats, dtype=F32),
        vmem(groups, tokens, 3 * hg * size),
        vmem(groups, 8, tokens, dtype=F32),
        vmem(tokens, width),
        vmem(tokens, width, dtype=F32),
        vmem(tokens, width),
        vmem(width, width),
        vmem(width, width),
        vmem(width, width),
        pltpu.SemaphoreType.DMA((12,)),
        vmem(hg // 2, LANES, 2 * feats),
    ]
    if comm:
        ins += [hbm(part) for part in (*u_late, out_state, flat)]
        summed = [
            ((len(u_late), 2 * width, hb), BF16),
            (out_state.shape, BF16),
            (flat.shape, F32),
        ]
        outs += [result(*part) for part in summed]
        scratch += [vmem(*part.shape) for part in u_late]
        scratch += [
            vmem(*out_state.shape),
            vmem(*flat.shape, dtype=F32),
            vmem(*w_shape),
            vmem(*small_shape, dtype=F32),
        ]
        scratch += [vmem(*shape, dtype=dtype) for shape, dtype in summed]
        scratch += [vmem(*w_shape), vmem(*small_shape, dtype=F32)]
        plans = back_plans(out_state.shape, flat.shape, w_shape, small_shape)
        plans = late_plans(hb) + [
            plans[name]
            for name in ("os", "f") + ("w",) * (groups - 1) + ("w_last",) * W_PIECES + ("small",)
        ]
        scratch += [pltpu.SemaphoreType.DMA((len(plans),))]
        for plan in plans:
            scratch += plan.scratch()
    found = call(
        partial(back_kernel, heads, hg, span, blocks, comm),
        (groups, blocks),
        ins,
        outs,
        scratch,
        "back",
        3 if comm else None,
    )
    dx, sum_w, small = found[:3]
    if comm:
        sum_late, out_state, flat = found[3:]
        results = finish(heads, sum_late, sum_w, out_state)
        sum_up, sum_down, sum_q, sum_k, sum_v, sum_o, sum_state = results
        sum_feed = flat[0:3]
        sum_upb = flat[3 : 3 + hidden // width].reshape(-1)
        sum_upb = jnp.where(first, sum_upb[:shard_width], sum_upb[shard_width:])
        sum_norm = flat[8 : 8 + heads, : 2 * feats]
    else:
        own = lax.psum_scatter(
            jnp.stack([up_grad, down_grad]), "seq", scatter_dimension=1, tiled=True
        )
        upb_own = lax.psum_scatter(upb_grad, "seq", scatter_dimension=0, tiled=True)
        (sum_up, sum_down), sum_upb = lax.psum((own[:, 0], upb_own.reshape(-1)), "dp")
        sum_w, sum_o, sum_state, small, sum_norm, sum_feed = lax.psum(
            (sum_w, output_grad, state_grad, small, norm_grad, feed_three), ("dp", "seq")
        )
        sum_w = sum_w.reshape(groups, width, 3, hg * size).transpose(2, 1, 0, 3)
        sum_q, sum_k, sum_v = sum_w.reshape(3, width, width).astype(F32)
        sum_state = sum_state.reshape(heads, size, 2 * feats).astype(F32).transpose(0, 2, 1)
    return (
        out.reshape(inputs.shape),
        dx.reshape(inputs.shape),
        small[heads + 1],
        small[heads + 2],
        sum_q,
        sum_k,
        sum_v,
        small[:heads].T,
        small[heads, :heads],
        sum_o.astype(F32),
        sum_state,
        sum_norm,
        sum_feed[0],
        sum_feed[1],
        sum_up.astype(F32),
        sum_upb,
        sum_down.astype(F32),
        sum_feed[2],
    )


def solution(mesh):
    tokens = P("dp", "seq", None)
    columns = P(None, "seq")
    return jax.shard_map(
        local,
        mesh=mesh,
        in_specs=(tokens, tokens) + (P(),) * 13 + (columns, P("seq"), columns, P()),
        out_specs=(tokens, tokens) + (P(),) * 12 + (columns, P("seq"), columns, P()),
        check_vma=False,
    )
```

```python
from functools import partial
import math

import jax
import jax.numpy as jnp
from jax import lax
from jax.experimental import pallas as pl
from jax.experimental.pallas import tpu as pltpu
from jax.sharding import PartitionSpec as P

F32 = jnp.float32
BF16 = jnp.bfloat16
EPS_NORM = 1e-05
EPS_UNIT = 1e-06
GUARD = 0.0625
MESH = pl.DeviceIdType.MESH
VMEM = 56 * 1024 * 1024

C = 128
T = 256
FEED_ROWS = 512
HB = 256
INNER_HEADS = 8
WEIGHT_STEPS = (2, 3, 5, 8)
SPAN = 2
GROUP_HEADS = 4
LANES = 128

SIN = (3.14158202, -5.16714278, 2.54189892, -0.55463591)
COS = (0.99999995, -4.93479286, 4.05841191, -1.33188012, 0.21969671)
ERF = (0.319381530, -0.356563782, 1.781477937, -1.821255978, 1.330274429)
ERF_P = 0.2316419
INV_SQRT_2PI = 0.3989422804014327


def nn(a, b):
    return lax.dot_general(a, b, (((1,), (0,)), ((), ())), preferred_element_type=F32)


def nt(a, b):
    return lax.dot_general(a, b, (((1,), (1,)), ((), ())), preferred_element_type=F32)


def tn(a, b):
    return lax.dot_general(a, b, (((0,), (0,)), ((), ())), preferred_element_type=F32)


def thirds(x):
    high = x.astype(BF16)
    rest = x - high.astype(F32)
    middle = rest.astype(BF16)
    return high, middle, (rest - middle.astype(F32)).astype(BF16)


def rows_up_to(x):
    n = x.shape[0]
    tri = jnp.where(iota((n, n), 0) >= iota((n, n), 1), 1.0, 0.0).astype(BF16)
    return nn(jnp.concatenate([tri] * 3, axis=1), jnp.concatenate(thirds(x), axis=0))


def lanes_up_to(x):
    n = x.shape[1]
    tri = jnp.where(iota((n, n), 0) <= iota((n, n), 1), 1.0, 0.0).astype(BF16)
    return nn(jnp.concatenate(thirds(x), axis=1), jnp.concatenate([tri] * 3, axis=0))


def iota(shape, dim):
    return lax.broadcasted_iota(jnp.int32, shape, dim)


def log_sigmoid(x):
    return jnp.minimum(x, 0.0) - jnp.log(1.0 + jnp.exp(-jnp.abs(x)))


def normalize(x):
    centred = x - jnp.mean(x, axis=-1, keepdims=True)
    scale = lax.rsqrt(jnp.mean(centred * centred, axis=-1, keepdims=True) + EPS_NORM)
    return centred * scale, scale


def normalize_back(grad, gain, xhat, scale):
    inner = grad * gain
    mean_inner = jnp.mean(inner, axis=-1, keepdims=True)
    mean_both = jnp.mean(inner * xhat, axis=-1, keepdims=True)
    return scale * (inner - mean_inner - xhat * mean_both)


def fold_rows(x):
    return jnp.sum(x.reshape(x.shape[0] // 8, 8, x.shape[1]), axis=0)


def block_ones():
    return jnp.where(
        iota((LANES, LANES), 0) // 64 == iota((LANES, LANES), 1) // 64, 1.0, 0.0
    ).astype(BF16)


def head_sums(x):
    high = x.astype(BF16)
    rest = (x - high.astype(F32)).astype(BF16)
    ones = block_ones()
    return nn(jnp.concatenate([high, rest], axis=1), jnp.concatenate([ones, ones], axis=0))


def lower_half(shape):
    return iota(shape, 1) < 64


def mine(h, lower):
    return lower if h % 2 == 0 else jnp.logical_not(lower)


def column(block, index, rows, width):
    return jnp.broadcast_to(block[:, index : index + 1], (rows, width))


def sin_cos(turns, scale):
    r = turns - jnp.floor(turns + 0.5)
    r2 = r * r
    s = (((SIN[3] * r2 + SIN[2]) * r2 + SIN[1]) * r2 + SIN[0]) * r
    k = 2.0 * scale
    c = (((k * COS[4] * r2 + k * COS[3]) * r2 + k * COS[2]) * r2 + k * COS[1]) * r2 + k * COS[0]
    return s * c, scale - (k * s) * s


class Links:
    def __init__(self):
        self.dp, self.seq = lax.axis_index("dp"), lax.axis_index("seq")
        core, y, z = self.dp % 2, (self.dp // 2) % 2, self.dp // 4
        self.y = y
        self.at = {"core": core, "y": y, "z": z, "plane": self.seq * 2 + y}
        self.at["xr"] = 0

    size = {"core": 2, "xr": 2, "y": 2, "z": 4, "plane": 4}

    def partner(self, group, step):
        dp, seq = self.dp, self.seq
        if group == "core":
            return (dp + 1 - 2 * self.at["core"], seq)
        if group == "xr":
            return (dp, 1 - seq)
        if group == "y":
            return (dp + 2 - 4 * self.y, seq)
        target = (self.at[group] + step) % 4
        if group == "z":
            return (dp % 4 + 4 * target, seq)
        return (dp + 2 * (target % 2 - self.y), target // 2)

    def greet(self, groups):
        barrier = pltpu.get_barrier_semaphore()
        count = 0
        for group in groups:
            for step in range(1, self.size[group]):
                pl.semaphore_signal(
                    barrier, inc=1, device_id=self.partner(group, step), device_id_type=MESH
                )
                count += 1
        pl.semaphore_wait(barrier, count)


class Plan:
    def __init__(self, rows, lanes, dtype, scatter, gather, share=(), pre=()):
        self.pre = pre
        self.scatter, self.gather, self.share = scatter, gather, share
        self.rows, self.lanes, self.dtype = rows, lanes, dtype
        self.groups = scatter + gather + share
        self.left = rows
        for group in scatter:
            self.left //= Links.size[group]
        self.stages = len(self.groups)

    def scratch(self):
        shapes = []
        rows = self.rows
        for i, group in enumerate(self.scatter):
            n = Links.size[group]
            rows //= n
            shapes.append(pltpu.VMEM((n - 1, rows, self.lanes), self.dtype))
            if i < len(self.scatter) - 1:
                shapes.append(pltpu.VMEM((rows, self.lanes), self.dtype))
        for i, group in enumerate(self.share):
            shapes.append(pltpu.VMEM((Links.size[group], rows, self.lanes), self.dtype))
            if i < len(self.share) - 1:
                shapes.append(pltpu.VMEM((rows, self.lanes), self.dtype))
        for group in self.groups:
            n = Links.size[group]
            shapes.append(pltpu.SemaphoreType.DMA((n - 1,)))
            shapes.append(pltpu.SemaphoreType.DMA((n - 1,)))
        return shapes


class Stream:
    def __init__(self, plan, links, source, out, scratch):
        self.plan, self.links, self.source, self.out = plan, links, source, out
        scratch = list(scratch)
        self.landing, self.parts = [], [source]
        summed = plan.scatter + plan.share
        for i in range(len(summed)):
            self.landing.append(scratch.pop(0))
            if i < len(summed) - 1:
                self.parts.append(scratch.pop(0))
        self.sems = [(scratch.pop(0), scratch.pop(0)) for _ in range(plan.stages)]
        self.places = {}
        rows, start = out.shape[0], 0
        for group in plan.pre + plan.scatter:
            if group in plan.gather:
                rows //= Links.size[group]
                self.places[group] = (start, rows)
                start = start + links.at[group] * rows
        self.final = (start, rows)

    def copies(self, stage, sending):
        plan, links = self.plan, self.links
        group = plan.groups[stage]
        n, me = Links.size[group], links.at[group]
        sends, recvs = self.sems[stage]
        made = []
        for step in range(1, n):
            target, origin = (me + step) % n, (me + n - step) % n
            if plan.share:
                source = self.parts[stage]
                lands = self.landing[stage].at[me]
                arrives = self.landing[stage].at[origin]
            elif stage < len(plan.scatter):
                landing = self.landing[stage]
                rows = landing.shape[1]
                source = self.parts[stage].at[pl.ds(pl.multiple_of(target * rows, 8), rows)]
                arrives = lands = landing.at[step - 1]
            else:
                start, rows = self.places[group]
                mine_at = pl.multiple_of(start + me * rows, 8)
                theirs_at = pl.multiple_of(start + origin * rows, 8)
                source = lands = self.out.at[pl.ds(mine_at, rows)]
                arrives = self.out.at[pl.ds(theirs_at, rows)]
            made.append(
                pltpu.make_async_remote_copy(
                    src_ref=source if sending else arrives,
                    dst_ref=lands if sending else arrives,
                    send_sem=sends.at[step - 1],
                    recv_sem=recvs.at[step - 1],
                    device_id=links.partner(group, step),
                    device_id_type=MESH,
                )
            )
        return made

    def start(self, stage):
        if stage == 0 and not (self.plan.scatter or self.plan.share):
            start, rows = self.final
            self.out[pl.ds(pl.multiple_of(start, 8), rows), :] = self.source[...]
        for copy in self.copies(stage, True):
            copy.start()

    def finish(self, stage):
        plan = self.plan
        for copy in self.copies(stage, False):
            copy.wait_recv()
        if plan.share:
            landing, me = self.landing[stage], self.links.at[plan.groups[stage]]
            landing[me] = self.parts[stage][...]
            total = landing[0]
            for k in range(1, landing.shape[0]):
                total = total + landing[k]
            if stage + 1 < plan.stages:
                self.parts[stage + 1][...] = total
            else:
                self.out[...] = total
            return
        if stage >= len(plan.scatter):
            return
        landing = self.landing[stage]
        arrivals, rows, _ = landing.shape
        own = self.links.at[plan.groups[stage]] * rows
        into, start = self.out, self.final[0]
        if stage + 1 < len(plan.scatter):
            into, start = self.parts[stage + 1], 0
        block = min(rows, SUM_ROWS)

        def add_block(k, carry):
            at = k * block
            total = self.parts[stage][pl.ds(pl.multiple_of(own + at, 16), block), :].astype(F32)
            for step in range(arrivals):
                total = total + landing[step, pl.ds(pl.multiple_of(at, 16), block), :].astype(F32)
            into[pl.ds(pl.multiple_of(start + at, 16), block), :] = total.astype(landing.dtype)
            return carry

        lax.fori_loop(0, rows // block, add_block, 0)

    def drain(self):
        for stage in range(self.plan.stages):
            for copy in self.copies(stage, True):
                copy.wait_send()


ALL_PLAN = (("core", "plane", "z"), ("z", "plane", "core"))
SHARE_PLAN = ((), (), ("core", "plane", "z"))


def pick_row(block, index):
    return jnp.sum(jnp.where(iota(block.shape, 0) == index, block, 0.0), axis=0, keepdims=True)


def grow_state(rows, norm, h):
    rows = rows.astype(F32)
    norm = jnp.broadcast_to(norm, rows.shape)
    return jnp.concatenate([rows, norm] if h % 2 == 0 else [norm, rows], axis=0)


def state_part(state, h):
    return state[0:64] if h % 2 == 0 else state[64:128]


def norm_part(state, h):
    return state[64:65] if h % 2 == 0 else state[0:1]


def pack_states(states, out_ref):
    heads = len(states)
    for h, state in enumerate(states):
        out_ref[64 * h : 64 * (h + 1), :] = state_part(state, h).astype(BF16)
    norms = [norm_part(state, h) for h, state in enumerate(states)]
    pad = jnp.zeros((16 - heads, states[0].shape[1]), F32)
    out_ref[64 * heads : 64 * heads + 16, :] = jnp.concatenate(norms + [pad], axis=0).astype(BF16)


def projection_blocks(proj_ref, p, scale):
    parts = [proj_ref[2 * p + j] * scale for j in range(2)]
    highs = [part.astype(BF16) for part in parts]
    rests = [(part - high.astype(F32)).astype(BF16) for part, high in zip(parts, highs)]
    zero = jnp.zeros(highs[0].shape, BF16)

    def diagonal(pair):
        return jnp.concatenate(
            [
                jnp.concatenate([pair[0], zero], axis=1),
                jnp.concatenate([zero, pair[1]], axis=1),
            ],
            axis=0,
        )

    return diagonal(highs), diagonal(rests)


class Taker:
    def __init__(self, refs):
        self.refs = list(refs)

    def __call__(self, n):
        taken = self.refs[:n]
        del self.refs[:n]
        return taken


class Board:
    def __init__(self, links, take, store_sems):
        self.links, self.take, self.store_sems = links, take, store_sems
        self.entries = []

    def add(self, plan, source, out, final, ticks):
        stream = Stream(plan, self.links, source, out, self.take(len(plan.scratch())))
        self.entries.append((stream, ticks, out, final))

    def store(self, k):
        _, _, out, final = self.entries[k]
        return pltpu.make_async_copy(out, final, self.store_sems.at[k])

    def advance(self, now):
        for k, (stream, ticks, _, final) in enumerate(self.entries):
            for stage, tick in enumerate(ticks):
                if tick == now:
                    if stage > 0:
                        stream.finish(stage - 1)
                    if stage < stream.plan.stages:
                        stream.start(stage)
                    elif final is not None:
                        self.store(k).start()

    def last(self):
        return max(ticks[-1] for _, ticks, _, _ in self.entries)

    def drain(self):
        for k, (stream, _, _, final) in enumerate(self.entries):
            stream.drain()
            if final is not None:
                self.store(k).wait()


def features_kernel(heads, span, blocks, comm, *refs):
    take = Taker(refs)
    x_ref, gain_ref, bias_ref, wq_ref, wk_ref, wv_ref = take(6)
    gate_ref, gb_smem, proj_ref, start_ref, start_norm_ref = take(5)
    up_hbm, down_hbm, upb_ref = take(3) if comm else (None,) * 3
    ml_ref, uq_ref, uk_ref, rq_ref, rk_ref, qf_ref, kf_ref, v_ref = take(8)
    gcol_ref, grow_ref, before_ref, n_ref = take(4)
    if comm:
        entry_ref, upo_hbm, downo_hbm, upbs_ref = take(4)
    else:
        final_ref, total_ref = take(2)
    state, carry, qf_s, kf_s, v_s, gcol_s, grow_s, before_s = take(8)
    wg_ref, gb_ref, gbt_ref, pcat_ref = take(4)
    step = pl.program_id(0)
    chunks = span * blocks
    full = span * C

    if comm:
        sent, landed, upb_landed, sends, recvs = take(5)
        links = Links()
        core, y = links.at["core"], links.at["y"]
        part = up_hbm.shape[0] // 4
        here = pl.ds(pl.multiple_of((2 * core + y) * part, 16), part)
        there = pl.ds(pl.multiple_of((2 * core + 1 - y) * part, 16), part)
        own_half = pl.ds(pl.multiple_of(2 * core * part, 16), 2 * part)
        other_half = pl.ds(pl.multiple_of(2 * (1 - core) * part, 16), 2 * part)

        def remote(k, sending):
            group = ("xr", "y", "core")[k // 2] if k < 6 else "xr"
            if k == 6:
                source, lands = upb_ref, upb_landed
            elif k == 7:
                source, lands = sent, landed
            else:
                mine_ref, theirs_ref = ((up_hbm, upo_hbm), (down_hbm, downo_hbm))[k % 2]
                if k < 2:
                    source, lands = mine_ref.at[here], theirs_ref.at[here]
                elif k < 4:
                    source = theirs_ref.at[here]
                    lands = source if sending else theirs_ref.at[there]
                else:
                    source = theirs_ref.at[own_half]
                    lands = source if sending else theirs_ref.at[other_half]
            return pltpu.make_async_remote_copy(
                src_ref=source if sending else lands,
                dst_ref=lands,
                send_sem=sends.at[k],
                recv_sem=recvs.at[k],
                device_id=links.partner(group, 1),
                device_id_type=MESH,
            )

        @pl.when(step == 0)
        def _():
            links.greet(("core", "xr", "y"))
            for k in (6, 0, 1):
                remote(k, True).start()

        @pl.when(step == blocks)
        def _():
            remote(7, True).start()

        for k, ready in zip(range(4), WEIGHT_STEPS):
            @pl.when(step == ready)
            def _(k=k):
                remote(k, False).wait_recv()
                remote(k + 2, True).start()

    @pl.when(step == 0)
    def _():
        carry[...] = jnp.zeros_like(carry)
        is_first = lax.axis_index("seq") == 0
        spread = jnp.where(iota((LANES, heads), 0) % heads == iota((LANES, heads), 1), 1.0, 0.0)
        wg_ref[...] = nn(spread.astype(BF16), gate_ref[...]).astype(BF16)
        lane_head = iota((1, LANES), 1) % heads
        row_head = iota((heads, LANES), 0)
        gb = jnp.zeros((1, LANES), F32)
        gbt = jnp.zeros((heads, LANES), F32)
        for h in range(heads):
            gb = jnp.where(lane_head == h, gb_smem[h], gb)
            gbt = jnp.where(row_head == h, gb_smem[h], gbt)
            begin = start_ref[h]
            norm = jnp.broadcast_to(start_norm_ref[h : h + 1, :], begin.shape)
            both = [begin, norm] if h % 2 == 0 else [norm, begin]
            state[h] = jnp.where(is_first, jnp.concatenate(both, axis=0), 0.0)
        gb_ref[...] = gb
        gbt_ref[...] = gbt
        for p in range(heads // 2):
            high, rest = projection_blocks(proj_ref, p, 1.0 / (2.0 * math.pi))
            pcat_ref[p, 0:LANES, :] = high
            pcat_ref[p, LANES : 2 * LANES, :] = high
            pcat_ref[p, 2 * LANES : 3 * LANES, :] = rest

    lower = lower_half((C, LANES))

    @pl.when(step < blocks)
    def _():
        xhat, _ = normalize(x_ref[...].astype(F32))
        ml = (xhat * gain_ref[...] + bias_ref[...]).astype(BF16)
        ml_ref[...] = ml
        q = nn(ml, wq_ref[...])
        k = nn(ml, wk_ref[...])
        v = nn(ml, wv_ref[...])
        v_low = v.astype(BF16)
        v_ref[...] = v_low
        rows_of = [slice(C * u, C * (u + 1)) for u in range(span)]
        logit = nt(ml, wg_ref[...]) + gb_ref[...]
        keep = log_sigmoid(logit)
        logit_row = nt(gate_ref[...], ml) + gbt_ref[...][:, 0:1]
        keep_row = log_sigmoid(logit_row)

        ftr_scale = 1.0 / math.sqrt(LANES)
        pairs = range(heads // 2)
        lanes_of = [slice(LANES * p, LANES * (p + 1)) for p in pairs]
        boths = [jnp.concatenate([q[:, at], k[:, at]], axis=0) for at in lanes_of]
        scales = [lax.rsqrt(head_sums(both * both) + EPS_UNIT) for both in boths]
        all_turns = []
        for p in pairs:
            unit = boths[p] * scales[p]
            high = unit.astype(BF16)
            rest = (unit - high.astype(F32)).astype(BF16)
            uq_ref[:, lanes_of[p]] = high[:full]
            uk_ref[:, lanes_of[p]] = high[full:]
            rq_ref[:, lanes_of[p]] = scales[p][:full]
            rk_ref[:, lanes_of[p]] = scales[p][full:]
            all_turns.append(nn(jnp.concatenate([high, rest, high], axis=1), pcat_ref[p]))
        coefs, totals = [], []
        group = iota((C, LANES), 1) // 8
        for u, rows in enumerate(rows_of):
            decay = rows_up_to(keep[rows])
            total = decay[C - 1 : C, :]
            coef = total - decay + keep[rows] - logit[rows]
            packed = jnp.where(group == 0, decay, coef)
            packed = jnp.where(group == 2, carry[...] + decay, packed)
            packed = jnp.where(group == 6, jnp.broadcast_to(carry[...], (C, LANES)), packed)
            packed = jnp.where(group == 7, jnp.broadcast_to(total, (C, LANES)), packed)
            gcol_ref[rows, :] = packed
            gcol_s[span * step + u] = packed
            carry[...] = carry[...] + total
            coefs.append(coef)
            totals.append(total)
            gate_rows = jnp.concatenate(
                [
                    keep_row[:, rows] - logit_row[:, rows] - lanes_up_to(keep_row[:, rows]),
                    jax.nn.sigmoid(logit_row[:, rows]),
                    jax.nn.sigmoid(-logit_row[:, rows]),
                ],
                axis=0,
            )
            grow_ref[:, rows] = gate_rows
            grow_s[span * step + u] = gate_rows
        if not comm:
            total_ref[...] = jnp.broadcast_to(carry[...], total_ref.shape)
        for p in pairs:
            s, c = sin_cos(all_turns[p], ftr_scale)
            s = s.astype(BF16)
            c = c.astype(BF16)
            for j in range(2):
                h = 2 * p + j
                half_lanes = slice(LANES * j, LANES * (j + 1))
                feats = jnp.concatenate([s[:, half_lanes], c[:, half_lanes]], axis=1)
                place = slice(256 * h, 256 * (h + 1))
                qf_ref[:, place] = feats[:full]
                kf_ref[:, place] = feats[full:]
                for u, rows in enumerate(rows_of):
                    at = span * step + u
                    kf = feats[full + C * u : full + C * (u + 1)]
                    qf_s[at, :, place] = feats[rows]
                    kf_s[at, :, place] = kf
                    v_s[at, :, lanes_of[p]] = v_low[rows, lanes_of[p]]
                    values = jnp.where(mine(h, lower), v[rows, lanes_of[p]], 1.0)
                    weighted = values * jnp.exp(column(coefs[u], h, C, LANES))
                    now = state[h]
                    now_low = now.astype(BF16)
                    before_ref[u, h] = now_low
                    before_s[at, h] = now_low
                    state[h] = jnp.exp(totals[u][:, h : h + 1]) * now + tn(weighted.astype(BF16), kf)

    @pl.when(step == blocks - 1)
    def _():
        pack_states([state[h] for h in range(heads)], sent if comm else final_ref)

    @pl.when(step >= blocks)
    def _():
        chunk = step - blocks
        causal = iota((C, C), 0) >= iota((C, C), 1)
        gcol = gcol_s[chunk]
        for first in range(0, heads, INNER_HEADS):
            some = range(first, first + INNER_HEADS)
            boths = []
            for h in some:
                place = slice(256 * h, 256 * (h + 1))
                keys = jnp.concatenate([kf_s[chunk, :, place], before_s[chunk, h]], axis=0)
                boths.append(nt(qf_s[chunk, :, place], keys))
            decays = [column(gcol, h, C, LANES) for h in some]
            weights = []
            for h, both, decay in zip(some, boths, decays):
                pairs = jnp.where(causal, jnp.exp(decay + grow_s[chunk, h : h + 1, :]), 0.0)
                weights.append((both[:, :C] * pairs).astype(BF16))
            for k, h in enumerate(some):
                lanes = slice(LANES * (h // 2), LANES * (h // 2 + 1))
                v = v_s[chunk, :, lanes].astype(F32)
                values = jnp.where(mine(h, lower), v, 1.0).astype(BF16)
                n_ref[:, LANES * h : LANES * (h + 1)] = (
                    nn(weights[k], values) + jnp.exp(decays[k]) * boths[k][:, C:]
                )

    if comm:
        @pl.when(step == blocks + chunks - 1)
        def _():
            for k in (4, 5, 6, 7):
                remote(k, False).wait_recv()
            later = links.seq == 1
            entry_ref[...] = jnp.where(later, landed[...].astype(F32), 0.0).astype(BF16)
            upbs_ref[0:1, :] = upb_ref[...]
            upbs_ref[1:2, :] = upb_landed[...]
            for k in range(8):
                remote(k, True).wait_send()


def feed_kernel(heads, tiles, pairs, comm, *refs):
    take = Taker(refs)
    x_ref, qf_hbm, n_ref, gcol_ref, entry_ref, wo_ref = take(6)
    gain_ref, bias_ref, downb_ref, upb_ref, dout_hbm = take(5)
    weights_hbm = take(4 if comm else 2)
    out_ref, mg_ref, a_ref = take(3)
    if comm:
        late_refs = take(len(FEED_STAGES))
        os_ref, flat_ref, after_ref = take(3)
    else:
        upg_ref, downg_ref, upbg_ref, o_ref, final_ref, sums_out = take(6)
    entry, adj, middle_s, num_s, den_s, fl_s, mix_s, br_s = take(8)
    acc_s, fg_s, dout_s, up_s, down_s, hid_s, pre_s, sums_s, load_sems = take(9)
    step = pl.program_id(0)
    tokens, width = middle_s.shape
    rows = x_ref.shape[0]
    shards, _, shard_width = up_s.shape
    hb = hid_s.shape[1] // 2
    (qf_s,) = take(1)
    loads = [
        (qf_hbm.at[pl.ds(rows * t, rows)], qf_s.at[pl.ds(rows * t, rows)]) for t in range(tiles)
    ]
    loads += [(dout_hbm, dout_s)]
    if comm:
        up_own, up_other, down_own, down_other = weights_hbm
        loads += [(up_own, up_s.at[0]), (up_other, up_s.at[1])]
        loads += [(down_own, down_s.at[0]), (down_other, down_s.at[1])]
        u_src, upbg_s, sent, landed, sends, recvs = take(6)
        links = Links()
        board = Board(links, take, None)
        for j, (plan, ticks) in enumerate(zip(feed_plans(hb), FEED_TICKS)):
            board.add(plan, u_src.at[j], late_refs[j], None, ticks)

        def exchange():
            return pltpu.make_async_remote_copy(
                src_ref=sent,
                dst_ref=landed,
                send_sem=sends,
                recv_sem=recvs,
                device_id=links.partner("xr", 1),
                device_id_type=MESH,
            )
    else:
        upbg_s = upbg_ref
        loads += [(weights_hbm[0], up_s), (weights_hbm[1], down_s)]

    def load(k):
        return pltpu.make_async_copy(loads[k][0], loads[k][1], load_sems.at[k])

    @pl.when(step == 0)
    def _():
        for k in range(len(loads)):
            load(k).start()
        adj[...] = jnp.zeros_like(adj)
        sums_s[...] = jnp.zeros_like(sums_s)
        norms = entry_ref[64 * heads : 64 * heads + 16, :].astype(F32)
        for h in range(heads):
            grown = grow_state(entry_ref[64 * h : 64 * (h + 1), :], norms[h : h + 1], h)
            entry[h] = grown.astype(BF16)
        if comm:
            links.greet(("core", "xr", "y", "z"))

    lower = lower_half((rows, LANES))

    @pl.when(step < tiles)
    def _():
        for t in range(tiles):
            pl.when(step == t)(load(t).wait)
        here = pl.ds(pl.multiple_of(step * rows, rows), rows)
        gcol = gcol_ref[...]
        fars = [nt(qf_s[here, 256 * h : 256 * (h + 1)], entry[h]) for h in range(heads)]
        mixed = []
        for p in range(heads // 2):
            lanes = slice(LANES * p, LANES * (p + 1))
            both = []
            for h in (2 * p, 2 * p + 1):
                far = fars[h] * jnp.exp(column(gcol, 16 + h, rows, LANES))
                both.append(n_ref[:, LANES * h : LANES * (h + 1)] + far)
            num = jnp.where(lower, both[0], both[1])
            den = pltpu.roll(jnp.where(lower, both[1], both[0]), 64, 1)
            num_s[here, lanes] = num
            den_s[here, lanes] = den
            mixed.append(num * lax.rsqrt(den * den + GUARD))
        mixed = jnp.concatenate(mixed, axis=1).astype(BF16)
        mix_s[here, :] = mixed
        middle = x_ref[...].astype(F32) + nn(mixed, wo_ref[...])
        middle_s[here, :] = middle
        acc_s[here, :] = middle + downb_ref[...]
        fg_s[here, :] = jnp.zeros_like(middle)
        xhat, _ = normalize(middle)
        fl_s[here, :] = (xhat * gain_ref[...] + bias_ref[...]).astype(BF16)

    @pl.when(step == tiles)
    def _():
        for k in range(tiles, len(loads)):
            load(k).wait()

    @pl.when(jnp.logical_and(step >= tiles, step < tiles + pairs))
    def _():
        j = step - tiles
        blocks = []
        for s in range(2):
            if comm:
                shard, off = s, pl.multiple_of(j * hb, hb)
            else:
                at = (2 * j + s) * hb
                shard, off = at // shard_width, pl.multiple_of(at % shard_width, hb)
            blocks.append((shard, pl.ds(off, hb)))
        ups = [up_s[shard, :, cols] for shard, cols in blocks]
        downs = [down_s[shard, :, cols] for shard, cols in blocks]
        up = jnp.concatenate(ups, axis=1)
        down = jnp.concatenate(downs, axis=1)
        if comm:
            upb = jnp.concatenate(
                [upb_ref[s : s + 1, cols] for s, (_, cols) in enumerate(blocks)], axis=1
            )
        else:
            upb = jnp.concatenate([upb_ref[shard, :, cols] for shard, cols in blocks], axis=1)
        if comm:
            for k in range(pairs):
                pl.when(j == k)(partial(board.advance, 2 * k))
        many = min(FEED_ROWS, tokens)
        for r in range(tokens // many):
            here = slice(many * r, many * (r + 1))
            feed_low = fl_s[here, :]
            pre = nn(feed_low, up) + upb
            pre_grad = nn(dout_s[here, :], down)
            t = 1.0 / (1.0 + ERF_P * jnp.abs(pre))
            bell = INV_SQRT_2PI * jnp.exp(-0.5 * pre * pre)
            tail = ((((ERF[4] * t + ERF[3]) * t + ERF[2]) * t + ERF[1]) * t + ERF[0]) * t * bell
            phi = jnp.where(pre >= 0.0, 1.0 - tail, tail)
            hidden = (pre * phi).astype(BF16)
            pre_low = (pre_grad * (phi + pre * bell)).astype(BF16)
            hid_s[here, :] = hidden
            pre_s[here, :] = pre_low
            acc_s[here, :] += nt(hidden, down)
            fg_s[here, :] += nt(pre_low, up)
        up_grad = tn(fl_s[...], pre_s[...]).astype(BF16)
        down_grad = tn(dout_s[...], hid_s[...]).astype(BF16)
        bias_grad = nn(jnp.ones((16, tokens), BF16), pre_s[...])[0:1]
        for s, (shard, cols) in enumerate(blocks):
            part = slice(hb * s, hb * (s + 1))
            upbg_s[shard, :, cols] = bias_grad[:, part]
            if comm:
                u_src[j, width * s : width * (s + 1), :] = up_grad[:, part]
                u_src[j, width * (2 + s) : width * (3 + s), :] = down_grad[:, part]
            else:
                upg_ref[shard, :, cols] = up_grad[:, part]
                downg_ref[shard, :, cols] = down_grad[:, part]

    @pl.when(step >= tiles + pairs)
    def _():
        tile = step - tiles - pairs

        if comm:
            for t in range(tiles):
                pl.when(tile == t)(partial(board.advance, 2 * pairs + t))
        here = pl.ds(pl.multiple_of(tile * rows, rows), rows)
        gcol = gcol_ref[...]
        dout = dout_s[here, :].astype(F32)
        out_ref[...] = acc_s[here, :].astype(BF16)
        feed_grad = fg_s[here, :]
        xhat, scale = normalize(middle_s[here, :])
        sums_s[0:8, :] += fold_rows(feed_grad * xhat)
        sums_s[8:16, :] += fold_rows(feed_grad)
        sums_s[16:24, :] += fold_rows(dout)
        middle_grad = dout + normalize_back(feed_grad, gain_ref[...], xhat, scale)
        mg_ref[...] = middle_grad
        branch = middle_grad.astype(BF16)
        br_s[here, :] = branch
        mixed_grad = nt(branch, wo_ref[...])
        lanes_of = [slice(LANES * p, LANES * (p + 1)) for p in range(heads // 2)]
        alongs = [head_sums(mixed_grad[:, lanes] * num_s[here, lanes]) for lanes in lanes_of]
        lifts = []
        for p, lanes in enumerate(lanes_of):
            den = den_s[here, lanes]
            inv = lax.rsqrt(den * den + GUARD)
            b = alongs[p] * den * (inv * inv * inv) * (-1.0 / 64)
            b = pltpu.roll(b, 64, 1)
            for h in (2 * p, 2 * p + 1):
                a = jnp.where(mine(h, lower), mixed_grad[:, lanes] * inv, b)
                a_ref[:, LANES * h : LANES * (h + 1)] = a.astype(BF16)
                lifts.append((a * jnp.exp(column(gcol, 16 + h, rows, LANES))).astype(BF16))
        for h in range(heads):
            adj[h] += tn(lifts[h], qf_s[here, 256 * h : 256 * (h + 1)])

    @pl.when(step == 2 * tiles + pairs - 1)
    def _():
        pack_states([adj[h] for h in range(heads)], sent if comm else final_ref)
        if comm:
            exchange().start()
        output_grad = tn(mix_s[...], br_s[...]).astype(BF16)
        if not comm:
            o_ref[...] = output_grad
            sums_out[...] = sums_s[...]
            return
        os_ref[:, 0:width] = output_grad
        for later in range(2 * pairs + tiles, board.last() + 1):
            board.advance(later)
        exchange().wait_recv()
        is_first = links.seq == 0
        after_ref[...] = jnp.where(is_first, landed[...].astype(F32), 0.0).astype(BF16)
        logs = gcol_ref[rows - 1 : rows, :]
        norms = landed[64 * heads : 64 * heads + 16, :].astype(F32)
        flat_ref[...] = jnp.zeros_like(flat_ref)
        for k in range(3):
            flat_ref[k : k + 1, :] = jnp.sum(sums_s[8 * k : 8 * (k + 1), :], axis=0, keepdims=True)
        for k in range(2 * shard_width // width):
            cols = slice(width * k % shard_width, width * k % shard_width + width)
            in_first = k < shard_width // width
            own, other = upbg_s[0, :, cols], upbg_s[1, :, cols]
            flat_ref[3 + k : 4 + k, :] = jnp.where(is_first, own, other) if in_first else jnp.where(
                is_first, other, own
            )
        for h in range(heads):
            grown = grow_state(landed[64 * h : 64 * (h + 1), :], norms[h : h + 1], h)
            begin = adj[h] + jnp.exp(logs[:, 16 + h : 17 + h]) * grown
            begin = jnp.where(is_first, begin, 0.0)
            os_ref[64 * h : 64 * (h + 1), width : width + 256] = state_part(begin, h).astype(BF16)
            flat_ref[8 + h : 9 + h, 0:256] = 64.0 * norm_part(begin, h)
        exchange().wait_send()
        board.drain()


U_SCATTER, U_GATHER = ("core", "xr", "y", "z"), ("z", "y", "core")
FEED_STAGES = (4, 3, 2, 1)
FEED_TICKS = ((2, 4, 6, 8, 11), (4, 6, 9, 12), (6, 8, 12), (8, 10))
BACK_TICKS = ((2, 4, 6, 7), (1, 3, 5, 7, 8), (1, 3, 5, 7, 8, 9), (1, 3, 5, 7, 8, 9, 10))


def feed_plans(hb):
    return [Plan(2048, hb, BF16, U_SCATTER[:n], ()) for n in FEED_STAGES]


def late_plans(hb):
    plans = []
    for plan, n in zip(feed_plans(hb), FEED_STAGES):
        done = [group for group in U_SCATTER[:n] if group != "xr"]
        plans.append(Plan(plan.left, hb, BF16, U_SCATTER[n:], U_GATHER, pre=tuple(done)))
    return plans


def back_kernel(heads, hg, span, chunks, comm, *refs):
    take = Taker(refs)
    (qf_ref, kf_ref, v_ref, uq_ref, uk_ref, rq_ref, rk_ref, a_ref, gcol_ref, grow_ref) = take(10)
    before_ref, entry_ref, entry_norm, after_ref, after_norm, proj_in = take(6)
    x_hbm, mg_hbm, ml_hbm, wq_hbm, wk_hbm, wv_hbm, gate_ref, gain_ref = take(8)
    u_hbms = take(len(FEED_STAGES)) if comm else ()
    os_hbm, f_hbm = take(2) if comm else (None,) * 2
    dx_ref, w_ref, small_ref = take(3)
    usum_hbm, ossum_hbm, fsum_hbm = take(3) if comm else (None,) * 3
    adj_ref, dqkv, dlogit, x_ref, mg_ref, ml_ref, wq_ref, wk_ref, wv_ref, load_sems = take(10)
    (proj_ref,) = take(1)
    g, i = pl.program_id(0), pl.program_id(1)
    tick = g * chunks + i
    last = heads // hg * chunks - 1
    first_row = (chunks - 1 - i) * (span * C)
    here = pl.ds(pl.multiple_of(first_row, C), span * C)
    groups = heads // hg
    loads = [
        (x_hbm, x_ref),
        (mg_hbm, mg_ref),
        (ml_hbm, ml_ref),
        (wq_hbm, wq_ref),
        (wk_hbm, wk_ref),
        (wv_hbm, wv_ref),
    ]
    if comm:
        u_refs = take(len(FEED_STAGES))
        os_ref, f_ref, w_src, small_src = take(4)
        usum_ref, ossum_ref, fsum_ref, wsum_ref, smallsum_ref = take(5)
        (store_sems,) = take(1)
        loads = list(zip(u_hbms, u_refs)) + [(os_hbm, os_ref), (f_hbm, f_ref)] + loads
        early_loads = len(loads) - 6
        links = Links()
        board = Board(links, take, store_sems)
        plans = back_plans(os_hbm.shape, f_hbm.shape, w_src.shape, small_src.shape)

        def stages(start, gaps):
            ticks = [start]
            for gap in gaps:
                ticks.append(ticks[-1] + gap)
            return ticks

        for k in reversed(range(groups)):
            final = k + 1 == groups
            pieces = W_PIECES if final else 1
            lanes_each = w_src.shape[2] // pieces
            for j in range(pieces):
                lanes = pl.ds(j * lanes_each, lanes_each)
                board.add(
                    plans["w_last" if final else "w"],
                    w_src.at[k, :, lanes],
                    wsum_ref.at[k, :, lanes],
                    w_ref.at[k, :, lanes],
                    [last + 1 + i for i in range(7)]
                    if final
                    else [(k + 1) * chunks + gap for gap in W_GAPS],
                )
        for j, (plan, ticks) in enumerate(zip(late_plans(usum_ref.shape[2]), BACK_TICKS)):
            board.add(plan, u_refs[j], usum_ref.at[j], usum_hbm.at[j], ticks)
        board.add(plans["os"], os_ref, ossum_ref, ossum_hbm, OS_TICKS)
        board.add(plans["f"], f_ref, fsum_ref, fsum_hbm, F_TICKS)
        advance = board.advance

    def load(k):
        return pltpu.make_async_copy(loads[k][0], loads[k][1], load_sems.at[k])

    @pl.when(tick == 0)
    def _():
        for k in range(len(loads)):
            load(k).start()
        dlogit[...] = jnp.zeros_like(dlogit)
        if comm:
            links.greet(("core", "plane", "z"))

    if comm:
        @pl.when(tick == 1)
        def _():
            for k in range(early_loads):
                load(k).wait()

        for now in range(1, last + 1):
            pl.when(tick == now)(partial(advance, now))

    @pl.when(i == 0)
    def _():
        for p in range(hg // 2):
            proj_ref[p] = projection_blocks(proj_in, p, 1.0 / (2.0 * math.pi))[0]
        norms = after_norm[...].astype(F32)
        for h in range(hg):
            norm = pick_row(norms, g * hg + h)
            adj_ref[h] = grow_state(after_ref[64 * h : 64 * (h + 1), :], norm, h)

    row = iota((C, C), 0)
    col = iota((C, C), 1)
    causal = row >= col
    one = jnp.ones((C, C), BF16)
    zero = jnp.zeros((C, C), BF16)
    later = jnp.where(row < col, 1.0, 0.0).astype(BF16)
    pair_sums = jnp.concatenate([later, one], axis=0)
    two_sums = jnp.concatenate(
        [jnp.concatenate([one, zero], axis=1), jnp.concatenate([zero, one], axis=1)], axis=0
    )
    lower = lower_half((C, LANES))
    entry_norms = entry_norm[...].astype(F32)
    gcol = gcol_ref[...]
    if groups > 1:
        gcol = jnp.where(g == 0, gcol, pltpu.roll(gcol, LANES - hg, 1))

    def grow_row(kind, h):
        return grow_ref[pl.ds(kind * heads + g * hg + h, 1), :]

    width = hg * 64
    pairs_of_heads = range(hg // 2)
    lanes_of = [slice(LANES * p, LANES * (p + 1)) for p in pairs_of_heads]
    items = [(u, h) for u in reversed(range(span)) for h in range(hg)]
    numbers = range(len(items))
    rows_of = [slice(C * u, C * (u + 1)) for u in range(span)]
    qfs = [qf_ref[rows_of[u], 256 * h : 256 * (h + 1)] for u, h in items]
    kfs = [kf_ref[rows_of[u], 256 * h : 256 * (h + 1)] for u, h in items]
    a_lows = [a_ref[rows_of[u], LANES * h : LANES * (h + 1)] for u, h in items]
    values = [
        jnp.where(mine(h, lower), v_ref[rows_of[u], lanes_of[h // 2]].astype(F32), 1.0)
        for u, h in items
    ]
    values_low = [part.astype(BF16) for part in values]
    lifts = [jnp.exp(column(gcol[rows_of[u]], h, C, LANES)) for u, h in items]
    a_lifts = [(a_lows[k].astype(F32) * lifts[k]).astype(BF16) for k in numbers]
    dweights = []
    for k in numbers[::2]:
        u, h = items[k]
        top = jnp.concatenate([values_low[k], zero], axis=1)
        bottom = jnp.concatenate([zero, values_low[k + 1]], axis=1)
        both = nt(
            a_ref[rows_of[u], LANES * h : LANES * (h + 2)],
            jnp.concatenate([top, bottom], axis=0),
        )
        dweights += [both[:, :C], both[:, C:]]
    adj_lows, throughs, keys_and_states = [], [], []
    raws, fars, dv_fars = [], [], []
    for k, (u, h) in enumerate(items):
        carried = jnp.exp(gcol[C * u : C * u + 1, 48 + h : 49 + h])
        total = jnp.exp(gcol[C * u : C * u + 1, 56 + h : 57 + h])
        entry = grow_state(
            entry_ref[64 * h : 64 * (h + 1), :], pick_row(entry_norms, g * hg + h), h
        )
        before = before_ref[u, h].astype(F32) + carried * entry
        adj = adj_ref[h]
        adj_lows.append(adj.astype(BF16))
        kept = total * adj
        through = jnp.sum(kept * before, axis=0, keepdims=True)
        throughs.append(jnp.sum(through, axis=1, keepdims=True))
        keys_and_states.append(jnp.concatenate([kfs[k], before.astype(BF16)], axis=0))
        raw_and_far = nt(qfs[k], keys_and_states[k])
        raws.append(raw_and_far[:, :C])
        fars.append(raw_and_far[:, C:])
        dv_fars.append(nt(kfs[k], adj_lows[k]))
        if u > 0:
            adj_ref[h] = kept + tn(a_lifts[k], qfs[k])
        else:
            adj_ref[h] = kept
    coefs = [jnp.exp(column(gcol[rows_of[u]], 8 + h, C, LANES)) for u, h in items]
    weights, draws, boths, v_coefs = [], [], [], []
    for k, (u, h) in enumerate(items):
        gap = column(gcol[rows_of[u]], h, C, LANES) + grow_row(0, h)[:, rows_of[u]]
        pairs = jnp.where(causal, jnp.exp(gap), 0.0)
        weights.append((raws[k] * pairs).astype(BF16))
        draw = dweights[k].astype(BF16).astype(F32) * pairs
        draws.append(draw.astype(BF16))
        boths.append((raws[k] * draw).astype(BF16))
        v_coefs.append((values[k] * coefs[k]).astype(BF16))
    dqs, dks, dvs = [], [], []
    for k in numbers:
        dqs.append(nn(jnp.concatenate([draws[k], a_lifts[k]], axis=1), keys_and_states[k]))
        dks.append(
            nn(
                jnp.concatenate([draws[k].T, v_coefs[k]], axis=1),
                jnp.concatenate([qfs[k], adj_lows[k]], axis=0),
            )
        )
        dvs.append(tn(weights[k], a_lows[k]))
        if items[k][0] == 0:
            adj_ref[items[k][1]] += tn(a_lifts[k], qfs[k])
    x_parts, y_parts = [], []
    for k in numbers:
        dv_far = coefs[k] * dv_fars[k]
        dvs[k] = dvs[k] + dv_far
        x_far = (a_lows[k].astype(F32) * lifts[k] * fars[k]).astype(BF16)
        x_parts.append(jnp.concatenate([boths[k], x_far], axis=1))
        y_far = (values[k] * dv_far).astype(BF16)
        y_parts.append(jnp.concatenate([y_far, (values[k] * dvs[k]).astype(BF16)], axis=1))
    upto = nn(jnp.concatenate(x_parts, axis=0), pair_sums)
    ends = nn(jnp.concatenate(y_parts, axis=0), two_sums)
    dus = []
    for p in pairs_of_heads:
        angles = []
        for feats, grads in ((qfs, dqs), (kfs, dks)):
            for u in range(span):
                row_angles = []
                for k, item in enumerate(items):
                    if item[0] == u and item[1] // 2 == p:
                        f, grad = feats[k].astype(F32), grads[k]
                        row_angles.append(
                            grad[:, :LANES] * f[:, LANES:] - grad[:, LANES:] * f[:, :LANES]
                        )
                angles.append(jnp.concatenate(row_angles, axis=1))
        dus.append(nt(jnp.concatenate(angles, axis=0).astype(BF16), proj_ref[p]))
    for k, (u, h) in enumerate(items):
        rows = slice(C * k, C * (k + 1))
        flow = jnp.where(causal, upto[rows], ends[rows, :C])
        flow = jnp.sum(flow, axis=0, keepdims=True) + throughs[k]
        own = jnp.sum(jnp.where(row == col, ends[rows, C:], 0.0), axis=0, keepdims=True)
        stay, leave = grow_row(1, h)[:, rows_of[u]], grow_row(2, h)[:, rows_of[u]]
        at = pl.ds(pl.multiple_of(first_row + C * u, C), C)
        dlogit[g, h : h + 1, at] = leave * flow - stay * own
    for p, lanes in enumerate(lanes_of):
        u = jnp.concatenate([uq_ref[:, lanes], uk_ref[:, lanes]], axis=0).astype(F32)
        scale = jnp.concatenate([rq_ref[:, lanes], rk_ref[:, lanes]], axis=0)
        along = nn((u * dus[p]).astype(BF16), block_ones())
        dqk = ((2.0 * math.pi) * scale * (dus[p] - u * along)).astype(BF16)
        dqkv[g, here, LANES * p : LANES * (p + 1)] = dqk[: span * C]
        dqkv[g, here, width + LANES * p : width + LANES * (p + 1)] = dqk[span * C :]
        for k, (u, h) in enumerate(items):
            if h == 2 * p:
                at = pl.ds(pl.multiple_of(first_row + C * u, C), C)
                dqkv[g, at, 2 * width + LANES * p : 2 * width + LANES * (p + 1)] = jnp.where(
                    lower, dvs[k], dvs[k + 1]
                ).astype(BF16)

    @pl.when(i == chunks - 1)
    def _():
        @pl.when(g == 0)
        def _():
            load(len(loads) - 4).wait()

        grads = tn(ml_ref[...], dqkv[g]).astype(BF16)
        if comm:
            w_src[g] = grads
        else:
            w_ref[g] = grads

    @pl.when(tick == last)
    def _():
        if comm:
            advance(last + 1)
        for k in range(len(loads) - 6, len(loads)):
            if k != len(loads) - 4:
                load(k).wait()
        tokens = chunks * span * C
        block = min(T, tokens)
        small = small_src if comm else small_ref
        rows8 = jnp.concatenate(
            [dlogit[k, 0:hg, :] for k in range(groups)]
            + [jnp.zeros((16 - heads, dlogit.shape[2]), F32)],
            axis=0,
        ).astype(BF16)
        small[...] = jnp.zeros_like(small)
        small[0:heads, :] = nn(rows8, ml_ref[...])[0:heads]
        bias_sum = nt(jnp.ones(rows8.shape, BF16), rows8)[0:1]
        small[heads : heads + 1, 0:16] = bias_sum
        gain = gain_ref[...]
        now = last + 2
        for b in range(tokens // block):
            rows = slice(block * b, block * (b + 1))
            mixer_grad = tn(rows8[0:heads, rows], gate_ref[...])
            for k in range(groups):
                for j, ref in enumerate((wq_ref, wk_ref, wv_ref)):
                    mixer_grad = mixer_grad + nt(
                        dqkv[k, rows, hg * 64 * j : hg * 64 * (j + 1)],
                        ref[:, hg * 64 * k : hg * 64 * (k + 1)],
                    )
            xhat, scale = normalize(x_ref[rows, :].astype(F32))
            small[heads + 1 : heads + 2, :] += jnp.sum(
                mixer_grad * xhat, axis=0, keepdims=True
            )
            small[heads + 2 : heads + 3, :] += jnp.sum(mixer_grad, axis=0, keepdims=True)
            dx_ref[rows, :] = mg_ref[rows, :] + normalize_back(mixer_grad, gain, xhat, scale)
            if comm and b % 2 == 1 and b + 1 < tokens // block:
                advance(now)
                now += 1
        if comm:
            board.add(
                plans["small"], small_src, smallsum_ref, small_ref, [now, now + 1, now + 2, now + 3]
            )
            for later_tick in range(now, board.last() + 1):
                advance(later_tick)
            board.drain()


OS_TICKS = (1, 3, 5, 7, 8, 9, 10)
F_TICKS = (5, 7, 8, 9)
W_GAPS = (0, 2, 4, 5, 6, 7, 8)
W_PIECES = 3
SUM_ROWS = 16


def back_plans(os, f, w, small):
    return {
        "os": Plan(os[0], os[1], BF16, *ALL_PLAN),
        "f": Plan(f[0], f[1], F32, *SHARE_PLAN),
        "w": Plan(w[1], w[2], BF16, *ALL_PLAN),
        "w_last": Plan(w[1], w[2] // W_PIECES, BF16, *ALL_PLAN),
        "small": Plan(small[0], small[1], F32, *SHARE_PLAN),
    }


def whole(shape):
    zeros = (0,) * len(shape)
    return pl.BlockSpec(shape, lambda *at: zeros, pipeline_mode=pl.Buffered(1))


ANY = pl.BlockSpec(memory_space=pl.ANY)


def call(kernel, grid, ins, outs, scratch, name, collective_id=None):
    def spec(shape, block, index):
        if block is None:
            return whole(shape)
        return block if isinstance(block, pl.BlockSpec) else pl.BlockSpec(block, index)

    params = {} if collective_id is None else {
        "collective_id": collective_id, "has_side_effects": True
    }
    return pl.pallas_call(
        kernel,
        grid=grid,
        in_specs=[spec(array.shape, block, index) for array, block, index in ins],
        out_specs=[spec(shape, block, index) for shape, _, block, index in outs],
        out_shape=[jax.ShapeDtypeStruct(shape, dtype) for shape, dtype, _, _ in outs],
        scratch_shapes=scratch,
        compiler_params=pltpu.CompilerParams(
            dimension_semantics=("arbitrary",) * len(grid), vmem_limit_bytes=VMEM, **params
        ),
        name=name,
    )(*[array for array, _, _ in ins])


def finish_kernel(
    late_ref, w_ref, os_ref, up_ref, down_ref, q_ref, k_ref, v_ref, o_ref, s_ref
):
    hb = late_ref.shape[3]
    for part, ref in enumerate((up_ref, down_ref)):
        for k in range(late_ref.shape[0]):
            ref[:, hb * k : hb * (k + 1)] = late_ref[k, part].astype(F32)
    groups, _, lanes = w_ref.shape
    each = lanes // 3
    for part, ref in enumerate((q_ref, k_ref, v_ref)):
        for k in range(groups):
            ref[:, each * k : each * (k + 1)] = w_ref[k, :, each * part : each * (part + 1)].astype(F32)
    width = o_ref.shape[1]
    o_ref[...] = os_ref[:, 0:width].astype(F32)
    for k in range(s_ref.shape[0]):
        s_ref[k] = os_ref[64 * k : 64 * (k + 1), width:].astype(F32)


def finish(heads, sum_late, sum_w, out_state):
    width = sum_w.shape[1]
    steps = 4
    rows = width // steps
    late, _, hb = sum_late.shape
    feats = out_state.shape[1] - width
    square = ((width, width), F32, (rows, width), lambda i: (i, 0))
    wide = ((width, late * hb), F32, (rows, late * hb), lambda i: (i, 0))
    return call(
        finish_kernel,
        (steps,),
        [
            (sum_late.reshape(late, 2, width, hb), (late, 2, rows, hb), lambda i: (0, 0, i, 0)),
            (sum_w, (sum_w.shape[0], rows, sum_w.shape[2]), lambda i: (0, i, 0)),
            (out_state, (rows, width + feats), lambda i: (i, 0)),
        ],
        [wide, wide, square, square, square, square]
        + [((heads, 64, feats), F32, (heads // steps, 64, feats), lambda i: (i, 0, 0))],
        [],
        "finish",
    )


def carry_over(payload, logs, forward):
    n, index = lax.axis_size("seq"), lax.axis_index("seq")
    everything = lax.all_gather(payload, "seq")
    every_log = lax.all_gather(logs, "seq")
    heads = logs.shape[0]
    row = jnp.arange(payload.shape[0])
    head = jnp.where(row < 64 * heads, row // 64, jnp.minimum(row - 64 * heads, heads - 1))
    total = jnp.zeros(payload.shape, F32)
    for k in range(n) if forward else reversed(range(n)):
        ahead = (k < index) if forward else (k > index)
        new = jnp.exp(every_log[k])[head][:, None] * total + everything[k].astype(F32)
        total = jnp.where(ahead, new, total)
    return total.astype(BF16)


def local(
    inputs,
    cotangent,
    mixer_gain,
    mixer_bias,
    query_weight,
    key_weight,
    value_weight,
    gate_weight,
    gate_bias,
    output_weight,
    projections,
    start_state,
    start_norm,
    feed_gain,
    feed_bias,
    up_weight,
    up_bias,
    down_weight,
    down_bias,
):
    _, tokens, width = inputs.shape
    heads, size, feats = projections.shape
    chunks = tokens // C
    span = min(SPAN, chunks)
    blocks = chunks // span
    tile = min(T, tokens)
    tiles = tokens // tile
    shards = lax.axis_size("seq")
    first = lax.axis_index("seq") == 0
    comm = (lax.axis_size("dp"), shards) == (16, 2)
    gate_rows = gate_weight.T
    x = inputs.reshape(tokens, width)
    dout = cotangent.reshape(tokens, width)
    shard_width = up_weight.shape[1]
    hidden = shard_width * shards
    hb = min(HB, shard_width)
    pairs = hidden // (2 * hb)
    wide = heads * LANES
    wider = heads * 2 * feats
    pay_shape = (heads * 64 + 16, 2 * feats)

    def const(array):
        return (array if array.ndim > 1 else array[None], None, None)

    def keep(shape, dtype):
        return (shape, dtype, None, None)

    def hbm(array):
        return (array, ANY, None)

    def result(shape, dtype):
        return (shape, dtype, ANY, None)

    def vmem(*shape, dtype=BF16):
        return pltpu.VMEM(shape, dtype)

    def early(n):
        return (span * C, n), lambda i: (jnp.minimum(i, blocks - 1), 0)

    def out_early(n, dtype):
        return ((tokens, n), dtype) + early(n)

    ins = [(x,) + early(width)]
    ins += [const(part) for part in (mixer_gain, mixer_bias, query_weight, key_weight)]
    ins += [
        const(value_weight),
        const(gate_rows),
        (gate_bias, pl.BlockSpec(memory_space=pltpu.SMEM), None),
        const(projections),
        const(start_state.transpose(0, 2, 1)),
        const(start_norm),
    ]
    outs = [out_early(width, BF16)] * 3 + [out_early(width, F32)] * 2
    outs += [out_early(wider, BF16)] * 2 + [out_early(width, BF16), out_early(LANES, F32)]
    outs += [
        (
            (3 * heads, tokens),
            F32,
            (3 * heads, span * C),
            lambda i: (0, jnp.minimum(i, blocks - 1)),
        ),
        (
            (chunks, heads, LANES, 2 * feats),
            BF16,
            (span, heads, LANES, 2 * feats),
            lambda i: (jnp.minimum(i, blocks - 1), 0, 0, 0),
        ),
        ((tokens, wide), F32, (C, wide), lambda i: (jnp.maximum(i - blocks, 0), 0)),
    ]
    scratch = [
        vmem(heads, LANES, 2 * feats, dtype=F32),
        vmem(1, LANES, dtype=F32),
        vmem(chunks, C, wider),
        vmem(chunks, C, wider),
        vmem(chunks, C, width),
        vmem(chunks, C, LANES, dtype=F32),
        vmem(chunks, 3 * heads, C, dtype=F32),
        vmem(chunks, heads, LANES, 2 * feats),
        vmem(LANES, width),
        vmem(1, LANES, dtype=F32),
        vmem(heads, LANES, dtype=F32),
        vmem(heads // 2, 3 * LANES, 2 * feats),
    ]
    upb = up_bias.astype(F32)[None]
    if comm:
        ins += [hbm(up_weight), hbm(down_weight), const(upb)]
        outs += [
            keep(pay_shape, BF16),
            result(up_weight.shape, BF16),
            result(down_weight.shape, BF16),
            keep((2, shard_width), F32),
        ]
        scratch += [
            vmem(*pay_shape),
            vmem(*pay_shape),
            vmem(1, shard_width, dtype=F32),
            pltpu.SemaphoreType.DMA((8,)),
            pltpu.SemaphoreType.DMA((8,)),
        ]
    else:
        outs += [keep(pay_shape, BF16), keep((8, LANES), F32)]
    found = call(
        partial(features_kernel, heads, span, blocks, comm),
        (blocks + chunks,),
        ins,
        outs,
        scratch,
        "features",
        1 if comm else None,
    )
    ml, uq, uk, rq, rk, qf, kf, v, gcol, grow, before, num = found[:12]
    if comm:
        entry, up_other, down_other, upb = found[12:]
        weights = (up_weight, up_other, down_weight, down_other)
    else:
        final, total = found[12:]
        logs = total[0, :heads]
        entry = carry_over(final, logs, True)
        weights = (lax.all_gather(up_weight, "seq"), lax.all_gather(down_weight, "seq"))
        upb = lax.all_gather(upb, "seq")

    steps = 2 * tiles + pairs

    def first_last(n):
        def index(i):
            late = jnp.maximum(i - tiles - pairs, 0)
            return (jnp.where(i < tiles + pairs, jnp.minimum(i, tiles - 1), late), 0)

        return (tile, n), index

    def only_first(n):
        return (tile, n), lambda i: (jnp.minimum(i, tiles - 1), 0)

    def only_last(n, dtype):
        return (
            (tokens, n),
            dtype,
            (tile, n),
            lambda i: (jnp.maximum(i - tiles - pairs, 0), 0),
        )

    ins = [
        (x,) + only_first(width),
        hbm(qf),
        (num,) + only_first(wide),
        (gcol,) + first_last(LANES),
        const(entry),
        const(output_weight),
        const(feed_gain),
        const(feed_bias),
        const(down_bias),
        const(upb),
        hbm(dout),
    ] + [hbm(part) for part in weights]
    outs = [only_last(width, BF16), only_last(width, F32), only_last(wide, BF16)]
    scratch = [
        vmem(heads, LANES, 2 * feats),
        vmem(heads, LANES, 2 * feats, dtype=F32),
        vmem(tokens, width, dtype=F32),
        vmem(tokens, width, dtype=F32),
        vmem(tokens, width, dtype=F32),
        vmem(tokens, width),
        vmem(tokens, width),
        vmem(tokens, width),
        vmem(tokens, width, dtype=F32),
        vmem(tokens, width, dtype=F32),
        vmem(tokens, width),
        vmem(shards, width, shard_width),
        vmem(shards, width, shard_width),
        vmem(tokens, 2 * hb),
        vmem(tokens, 2 * hb),
        vmem(24, width, dtype=F32),
        pltpu.SemaphoreType.DMA((5 + tiles,)),
        vmem(tokens, wider),
    ]
    if comm:
        plans = feed_plans(hb)
        outs += [
            *[keep((plan.left, hb), BF16) for plan in plans],
            keep((width, width + 2 * feats), BF16),
            keep((16, width), F32),
            keep(pay_shape, BF16),
        ]
        scratch += [
            vmem(pairs, 4 * width, hb),
            vmem(shards, 1, shard_width, dtype=F32),
            vmem(*pay_shape),
            vmem(*pay_shape),
            pltpu.SemaphoreType.DMA,
            pltpu.SemaphoreType.DMA,
        ]
        for plan in plans:
            scratch += plan.scratch()
    else:
        outs += [
            keep((shards, width, shard_width), BF16),
            keep((shards, width, shard_width), BF16),
            keep((shards, 1, shard_width), F32),
            keep((width, width), BF16),
            keep(pay_shape, BF16),
            keep((24, width), F32),
        ]
    found = call(
        partial(feed_kernel, heads, tiles, pairs, comm),
        (steps,),
        ins,
        outs,
        scratch,
        "feed",
        2 if comm else None,
    )
    out, mg, a = found[:3]
    if comm:
        u_late = found[3:-3]
        out_state, flat, after = found[-3:]
    else:
        up_grad, down_grad, upb_grad, output_grad, adj_final, feed_sums = found[3:]
        after = carry_over(adj_final, logs, False)
        feed_three = jnp.sum(feed_sums.reshape(3, 8, width), axis=1)
        begin = adj_final.astype(F32)
        row = jnp.arange(pay_shape[0])
        head = jnp.where(row < 64 * heads, row // 64, jnp.minimum(row - 64 * heads, heads - 1))
        begin = begin + jnp.exp(logs)[head][:, None] * after.astype(F32)
        begin = jnp.where(first, begin, 0.0)
        state_grad = begin[: heads * 64].astype(BF16)
        norm_grad = 64.0 * begin[heads * 64 : heads * 65]

    hg = GROUP_HEADS
    groups = heads // hg
    def back_rows(n, per_group=True):
        return (span * C, n), lambda g, i: (blocks - 1 - i, g if per_group else 0)

    def per_group(array, *shape):
        zeros = (0,) * (len(shape) - 1)
        return (array, shape, lambda g, i: (g,) + zeros)

    def states(array):
        return [
            (array, (hg * 64, 2 * feats), lambda g, i: (g, 0)),
            (array, (16, 2 * feats), lambda g, i: (heads * 4, 0)),
        ]

    ins = [
        (qf,) + back_rows(hg * 2 * feats),
        (kf,) + back_rows(hg * 2 * feats),
        (v,) + back_rows(hg * size),
        (uq,) + back_rows(hg * size),
        (uk,) + back_rows(hg * size),
        (rq,) + back_rows(hg * size),
        (rk,) + back_rows(hg * size),
        (a,) + back_rows(hg * LANES),
        (gcol,) + back_rows(LANES, False),
        (grow, (3 * heads, span * C), lambda g, i: (0, blocks - 1 - i)),
        (before, (span, hg, LANES, 2 * feats), lambda g, i: (blocks - 1 - i, g, 0, 0)),
    ]
    ins += states(entry) + states(after)
    ins += [
        per_group(projections, hg, size, feats),
        hbm(x),
        hbm(mg),
        hbm(ml),
        hbm(query_weight),
        hbm(key_weight),
        hbm(value_weight),
        const(gate_rows),
        const(mixer_gain),
    ]
    w_shape, small_shape = (groups, width, 3 * hg * size), (16, width)

    def sums(shape, dtype):
        return result(shape, dtype) if comm else keep(shape, dtype)

    outs = [keep((tokens, width), F32), sums(w_shape, BF16), sums(small_shape, F32)]
    scratch = [
        vmem(hg, LANES, 2 * feats, dtype=F32),
        vmem(groups, tokens, 3 * hg * size),
        vmem(groups, 8, tokens, dtype=F32),
        vmem(tokens, width),
        vmem(tokens, width, dtype=F32),
        vmem(tokens, width),
        vmem(width, width),
        vmem(width, width),
        vmem(width, width),
        pltpu.SemaphoreType.DMA((12,)),
        vmem(hg // 2, LANES, 2 * feats),
    ]
    if comm:
        ins += [hbm(part) for part in (*u_late, out_state, flat)]
        summed = [
            ((len(u_late), 2 * width, hb), BF16),
            (out_state.shape, BF16),
            (flat.shape, F32),
        ]
        outs += [result(*part) for part in summed]
        scratch += [vmem(*part.shape) for part in u_late]
        scratch += [
            vmem(*out_state.shape),
            vmem(*flat.shape, dtype=F32),
            vmem(*w_shape),
            vmem(*small_shape, dtype=F32),
        ]
        scratch += [vmem(*shape, dtype=dtype) for shape, dtype in summed]
        scratch += [vmem(*w_shape), vmem(*small_shape, dtype=F32)]
        plans = back_plans(out_state.shape, flat.shape, w_shape, small_shape)
        first_names = ("w_last",) * W_PIECES + ("w",) * (groups - 1)
        plans = (
            [plans[name] for name in first_names]
            + late_plans(hb)
            + [plans[name] for name in ("os", "f", "small")]
        )
        scratch += [pltpu.SemaphoreType.DMA((len(plans),))]
        for plan in plans:
            scratch += plan.scratch()
    found = call(
        partial(back_kernel, heads, hg, span, blocks, comm),
        (groups, blocks),
        ins,
        outs,
        scratch,
        "back",
        3 if comm else None,
    )
    dx, sum_w, small = found[:3]
    if comm:
        sum_late, out_state, flat = found[3:]
        results = finish(heads, sum_late, sum_w, out_state)
        sum_up, sum_down, sum_q, sum_k, sum_v, sum_o, sum_state = results
        sum_feed = flat[0:3]
        sum_upb = flat[3 : 3 + hidden // width].reshape(-1)
        sum_upb = jnp.where(first, sum_upb[:shard_width], sum_upb[shard_width:])
        sum_norm = flat[8 : 8 + heads, : 2 * feats]
    else:
        own = lax.psum_scatter(
            jnp.stack([up_grad, down_grad]), "seq", scatter_dimension=1, tiled=True
        )
        upb_own = lax.psum_scatter(upb_grad, "seq", scatter_dimension=0, tiled=True)
        (sum_up, sum_down), sum_upb = lax.psum((own[:, 0], upb_own.reshape(-1)), "dp")
        sum_w, sum_o, sum_state, small, sum_norm, sum_feed = lax.psum(
            (sum_w, output_grad, state_grad, small, norm_grad, feed_three), ("dp", "seq")
        )
        sum_w = sum_w.reshape(groups, width, 3, hg * size).transpose(2, 1, 0, 3)
        sum_q, sum_k, sum_v = sum_w.reshape(3, width, width).astype(F32)
        sum_state = sum_state.reshape(heads, size, 2 * feats).astype(F32)
    return (
        out.reshape(inputs.shape),
        dx.reshape(inputs.shape),
        small[heads + 1],
        small[heads + 2],
        sum_q,
        sum_k,
        sum_v,
        small[:heads].T,
        small[heads, :heads],
        sum_o.astype(F32),
        sum_state.transpose(0, 2, 1),
        sum_norm,
        sum_feed[0],
        sum_feed[1],
        sum_up.astype(F32),
        sum_upb,
        sum_down.astype(F32),
        sum_feed[2],
    )


def solution(mesh):
    tokens = P("dp", "seq", None)
    columns = P(None, "seq")
    return jax.shard_map(
        local,
        mesh=mesh,
        in_specs=(tokens, tokens) + (P(),) * 13 + (columns, P("seq"), columns, P()),
        out_specs=(tokens, tokens) + (P(),) * 12 + (columns, P("seq"), columns, P()),
        check_vma=False,
    )
```

```python
from functools import partial
import math

import jax
import jax.numpy as jnp
from jax import lax
from jax.experimental import pallas as pl
from jax.experimental.pallas import tpu as pltpu
from jax.sharding import PartitionSpec as P

F32 = jnp.float32
BF16 = jnp.bfloat16
EPS_NORM = 1e-05
EPS_UNIT = 1e-06
GUARD = 0.0625
MESH = pl.DeviceIdType.MESH
VMEM = 56 * 1024 * 1024

C = 128
T = 256
FEED_ROWS = 512
HB = 256
INNER_HEADS = 8
WEIGHT_STEPS = (2, 3, 5, 8)
SPAN = 2
GROUP_HEADS = 4
LANES = 128

SIN = (3.14158202, -5.16714278, 2.54189892, -0.55463591)
COS = (0.99999995, -4.93479286, 4.05841191, -1.33188012, 0.21969671)
ERF = (0.319381530, -0.356563782, 1.781477937, -1.821255978, 1.330274429)
ERF_P = 0.2316419
INV_SQRT_2PI = 0.3989422804014327


def nn(a, b):
    return lax.dot_general(a, b, (((1,), (0,)), ((), ())), preferred_element_type=F32)


def nt(a, b):
    return lax.dot_general(a, b, (((1,), (1,)), ((), ())), preferred_element_type=F32)


def tn(a, b):
    return lax.dot_general(a, b, (((0,), (0,)), ((), ())), preferred_element_type=F32)


def thirds(x):
    high = x.astype(BF16)
    rest = x - high.astype(F32)
    middle = rest.astype(BF16)
    return high, middle, (rest - middle.astype(F32)).astype(BF16)


def rows_up_to(x):
    n = x.shape[0]
    tri = jnp.where(iota((n, n), 0) >= iota((n, n), 1), 1.0, 0.0).astype(BF16)
    return nn(jnp.concatenate([tri] * 3, axis=1), jnp.concatenate(thirds(x), axis=0))


def lanes_up_to(x):
    n = x.shape[1]
    tri = jnp.where(iota((n, n), 0) <= iota((n, n), 1), 1.0, 0.0).astype(BF16)
    return nn(jnp.concatenate(thirds(x), axis=1), jnp.concatenate([tri] * 3, axis=0))


def iota(shape, dim):
    return lax.broadcasted_iota(jnp.int32, shape, dim)


def log_sigmoid(x):
    return jnp.minimum(x, 0.0) - jnp.log(1.0 + jnp.exp(-jnp.abs(x)))


def normalize(x):
    centred = x - jnp.mean(x, axis=-1, keepdims=True)
    scale = lax.rsqrt(jnp.mean(centred * centred, axis=-1, keepdims=True) + EPS_NORM)
    return centred * scale, scale


def normalize_back(grad, gain, xhat, scale):
    inner = grad * gain
    mean_inner = jnp.mean(inner, axis=-1, keepdims=True)
    mean_both = jnp.mean(inner * xhat, axis=-1, keepdims=True)
    return scale * (inner - mean_inner - xhat * mean_both)


def fold_rows(x):
    return jnp.sum(x.reshape(x.shape[0] // 8, 8, x.shape[1]), axis=0)


def block_ones():
    return jnp.where(
        iota((LANES, LANES), 0) // 64 == iota((LANES, LANES), 1) // 64, 1.0, 0.0
    ).astype(BF16)


def head_sums(x):
    high = x.astype(BF16)
    rest = (x - high.astype(F32)).astype(BF16)
    ones = block_ones()
    return nn(jnp.concatenate([high, rest], axis=1), jnp.concatenate([ones, ones], axis=0))


def lower_half(shape):
    return iota(shape, 1) < 64


def mine(h, lower):
    return lower if h % 2 == 0 else jnp.logical_not(lower)


def column(block, index, rows, width):
    return jnp.broadcast_to(block[:, index : index + 1], (rows, width))


def sin_cos(turns, scale):
    r = turns - jnp.floor(turns + 0.5)
    r2 = r * r
    s = (((SIN[3] * r2 + SIN[2]) * r2 + SIN[1]) * r2 + SIN[0]) * r
    k = 2.0 * scale
    c = (((k * COS[4] * r2 + k * COS[3]) * r2 + k * COS[2]) * r2 + k * COS[1]) * r2 + k * COS[0]
    return s * c, scale - (k * s) * s


class Links:
    def __init__(self):
        self.dp, self.seq = lax.axis_index("dp"), lax.axis_index("seq")
        core, y, z = self.dp % 2, (self.dp // 2) % 2, self.dp // 4
        self.y = y
        self.at = {"core": core, "y": y, "z": z, "plane": self.seq * 2 + y}
        self.at["xr"] = 0

    size = {"core": 2, "xr": 2, "y": 2, "z": 4, "plane": 4}

    def partner(self, group, step):
        dp, seq = self.dp, self.seq
        if group == "core":
            return (dp + 1 - 2 * self.at["core"], seq)
        if group == "xr":
            return (dp, 1 - seq)
        if group == "y":
            return (dp + 2 - 4 * self.y, seq)
        target = (self.at[group] + step) % 4
        if group == "z":
            return (dp % 4 + 4 * target, seq)
        return (dp + 2 * (target % 2 - self.y), target // 2)

    def greet(self, groups):
        barrier = pltpu.get_barrier_semaphore()
        count = 0
        for group in groups:
            for step in range(1, self.size[group]):
                pl.semaphore_signal(
                    barrier, inc=1, device_id=self.partner(group, step), device_id_type=MESH
                )
                count += 1
        pl.semaphore_wait(barrier, count)


class Plan:
    def __init__(self, rows, lanes, dtype, scatter, gather, share=(), pre=()):
        self.pre = pre
        self.scatter, self.gather, self.share = scatter, gather, share
        self.rows, self.lanes, self.dtype = rows, lanes, dtype
        self.groups = scatter + gather + share
        self.left = rows
        for group in scatter:
            self.left //= Links.size[group]
        self.stages = len(self.groups)

    def scratch(self):
        shapes = []
        rows = self.rows
        for i, group in enumerate(self.scatter):
            n = Links.size[group]
            rows //= n
            shapes.append(pltpu.VMEM((n - 1, rows, self.lanes), self.dtype))
            if i < len(self.scatter) - 1:
                shapes.append(pltpu.VMEM((rows, self.lanes), self.dtype))
        for i, group in enumerate(self.share):
            shapes.append(pltpu.VMEM((Links.size[group], rows, self.lanes), self.dtype))
            if i < len(self.share) - 1:
                shapes.append(pltpu.VMEM((rows, self.lanes), self.dtype))
        for group in self.groups:
            n = Links.size[group]
            shapes.append(pltpu.SemaphoreType.DMA((n - 1,)))
            shapes.append(pltpu.SemaphoreType.DMA((n - 1,)))
        return shapes


class Stream:
    def __init__(self, plan, links, source, out, scratch):
        self.plan, self.links, self.source, self.out = plan, links, source, out
        scratch = list(scratch)
        self.landing, self.parts = [], [source]
        summed = plan.scatter + plan.share
        for i in range(len(summed)):
            self.landing.append(scratch.pop(0))
            if i < len(summed) - 1:
                self.parts.append(scratch.pop(0))
        self.sems = [(scratch.pop(0), scratch.pop(0)) for _ in range(plan.stages)]
        self.places = {}
        rows, start = out.shape[0], 0
        for group in plan.pre + plan.scatter:
            if group in plan.gather:
                rows //= Links.size[group]
                self.places[group] = (start, rows)
                start = start + links.at[group] * rows
        self.final = (start, rows)

    def copies(self, stage, sending):
        plan, links = self.plan, self.links
        group = plan.groups[stage]
        n, me = Links.size[group], links.at[group]
        sends, recvs = self.sems[stage]
        made = []
        for step in range(1, n):
            target, origin = (me + step) % n, (me + n - step) % n
            if plan.share:
                source = self.parts[stage]
                lands = self.landing[stage].at[me]
                arrives = self.landing[stage].at[origin]
            elif stage < len(plan.scatter):
                landing = self.landing[stage]
                rows = landing.shape[1]
                source = self.parts[stage].at[pl.ds(pl.multiple_of(target * rows, 8), rows)]
                arrives = lands = landing.at[step - 1]
            else:
                start, rows = self.places[group]
                mine_at = pl.multiple_of(start + me * rows, 8)
                theirs_at = pl.multiple_of(start + origin * rows, 8)
                source = lands = self.out.at[pl.ds(mine_at, rows)]
                arrives = self.out.at[pl.ds(theirs_at, rows)]
            made.append(
                pltpu.make_async_remote_copy(
                    src_ref=source if sending else arrives,
                    dst_ref=lands if sending else arrives,
                    send_sem=sends.at[step - 1],
                    recv_sem=recvs.at[step - 1],
                    device_id=links.partner(group, step),
                    device_id_type=MESH,
                )
            )
        return made

    def start(self, stage):
        if stage == 0 and not (self.plan.scatter or self.plan.share):
            start, rows = self.final
            self.out[pl.ds(pl.multiple_of(start, 8), rows), :] = self.source[...]
        for copy in self.copies(stage, True):
            copy.start()

    def finish(self, stage):
        plan = self.plan
        for copy in self.copies(stage, False):
            copy.wait_recv()
        if plan.share:
            landing, me = self.landing[stage], self.links.at[plan.groups[stage]]
            landing[me] = self.parts[stage][...]
            total = landing[0]
            for k in range(1, landing.shape[0]):
                total = total + landing[k]
            if stage + 1 < plan.stages:
                self.parts[stage + 1][...] = total
            else:
                self.out[...] = total
            return
        if stage >= len(plan.scatter):
            return
        landing = self.landing[stage]
        arrivals, rows, _ = landing.shape
        own = self.links.at[plan.groups[stage]] * rows
        into, start = self.out, self.final[0]
        if stage + 1 < len(plan.scatter):
            into, start = self.parts[stage + 1], 0
        block = min(rows, SUM_ROWS)

        def add_block(k, carry):
            at = k * block
            total = self.parts[stage][pl.ds(pl.multiple_of(own + at, 16), block), :].astype(F32)
            for step in range(arrivals):
                total = total + landing[step, pl.ds(pl.multiple_of(at, 16), block), :].astype(F32)
            into[pl.ds(pl.multiple_of(start + at, 16), block), :] = total.astype(landing.dtype)
            return carry

        lax.fori_loop(0, rows // block, add_block, 0)

    def drain(self):
        for stage in range(self.plan.stages):
            for copy in self.copies(stage, True):
                copy.wait_send()


ALL_PLAN = (("core", "plane", "z"), ("z", "plane", "core"))
SHARE_PLAN = ((), (), ("core", "plane", "z"))


def pick_row(block, index):
    return jnp.sum(jnp.where(iota(block.shape, 0) == index, block, 0.0), axis=0, keepdims=True)


def grow_state(rows, norm, h):
    rows = rows.astype(F32)
    norm = jnp.broadcast_to(norm, rows.shape)
    return jnp.concatenate([rows, norm] if h % 2 == 0 else [norm, rows], axis=0)


def state_part(state, h):
    return state[0:64] if h % 2 == 0 else state[64:128]


def norm_part(state, h):
    return state[64:65] if h % 2 == 0 else state[0:1]


def pack_states(states, out_ref):
    heads = len(states)
    for h, state in enumerate(states):
        out_ref[64 * h : 64 * (h + 1), :] = state_part(state, h).astype(BF16)
    norms = [norm_part(state, h) for h, state in enumerate(states)]
    pad = jnp.zeros((16 - heads, states[0].shape[1]), F32)
    out_ref[64 * heads : 64 * heads + 16, :] = jnp.concatenate(norms + [pad], axis=0).astype(BF16)


def projection_blocks(proj_ref, p, scale):
    parts = [proj_ref[2 * p + j] * scale for j in range(2)]
    highs = [part.astype(BF16) for part in parts]
    rests = [(part - high.astype(F32)).astype(BF16) for part, high in zip(parts, highs)]
    zero = jnp.zeros(highs[0].shape, BF16)

    def diagonal(pair):
        return jnp.concatenate(
            [
                jnp.concatenate([pair[0], zero], axis=1),
                jnp.concatenate([zero, pair[1]], axis=1),
            ],
            axis=0,
        )

    return diagonal(highs), diagonal(rests)


class Taker:
    def __init__(self, refs):
        self.refs = list(refs)

    def __call__(self, n):
        taken = self.refs[:n]
        del self.refs[:n]
        return taken


class Board:
    def __init__(self, links, take, store_sems):
        self.links, self.take, self.store_sems = links, take, store_sems
        self.entries = []

    def add(self, plan, source, out, final, ticks):
        stream = Stream(plan, self.links, source, out, self.take(len(plan.scratch())))
        self.entries.append((stream, ticks, out, final))

    def store(self, k):
        _, _, out, final = self.entries[k]
        return pltpu.make_async_copy(out, final, self.store_sems.at[k])

    def advance(self, now):
        for k, (stream, ticks, _, final) in enumerate(self.entries):
            for stage, tick in enumerate(ticks):
                if tick == now:
                    if stage > 0:
                        stream.finish(stage - 1)
                    if stage < stream.plan.stages:
                        stream.start(stage)
                    elif final is not None:
                        self.store(k).start()

    def last(self):
        return max(ticks[-1] for _, ticks, _, _ in self.entries)

    def drain(self):
        for k, (stream, _, _, final) in enumerate(self.entries):
            stream.drain()
            if final is not None:
                self.store(k).wait()


def features_kernel(heads, span, blocks, comm, *refs):
    take = Taker(refs)
    x_ref, gain_ref, bias_ref, wq_ref, wk_ref, wv_ref = take(6)
    gate_ref, gb_smem, proj_ref, start_ref, start_norm_ref = take(5)
    up_hbm, down_hbm, upb_ref = take(3) if comm else (None,) * 3
    ml_ref, uq_ref, uk_ref, rq_ref, rk_ref, qf_ref, kf_ref, v_ref = take(8)
    gcol_ref, grow_ref, before_ref, n_ref = take(4)
    if comm:
        entry_ref, upo_hbm, downo_hbm, upbs_ref = take(4)
    else:
        final_ref, total_ref = take(2)
    state, carry, qf_s, kf_s, v_s, gcol_s, grow_s, before_s = take(8)
    wg_ref, gb_ref, gbt_ref, pcat_ref = take(4)
    step = pl.program_id(0)
    chunks = span * blocks
    full = span * C

    if comm:
        sent, landed, upb_own, upb_landed, sends, recvs = take(6)
        links = Links()
        core, y = links.at["core"], links.at["y"]
        part = up_hbm.shape[0] // 4
        here = pl.ds(pl.multiple_of((2 * core + y) * part, 16), part)
        there = pl.ds(pl.multiple_of((2 * core + 1 - y) * part, 16), part)
        own_half = pl.ds(pl.multiple_of(2 * core * part, 16), 2 * part)
        other_half = pl.ds(pl.multiple_of(2 * (1 - core) * part, 16), 2 * part)

        def remote(k, sending):
            group = ("xr", "y", "core")[k // 2] if k < 6 else "xr"
            if k == 6:
                source, lands = upb_own, upb_landed
            elif k == 7:
                source, lands = sent, landed
            else:
                mine_ref, theirs_ref = ((up_hbm, upo_hbm), (down_hbm, downo_hbm))[k % 2]
                if k < 2:
                    source, lands = mine_ref.at[here], theirs_ref.at[here]
                elif k < 4:
                    source = theirs_ref.at[here]
                    lands = source if sending else theirs_ref.at[there]
                else:
                    source = theirs_ref.at[own_half]
                    lands = source if sending else theirs_ref.at[other_half]
            return pltpu.make_async_remote_copy(
                src_ref=source if sending else lands,
                dst_ref=lands,
                send_sem=sends.at[k],
                recv_sem=recvs.at[k],
                device_id=links.partner(group, 1),
                device_id_type=MESH,
            )

        @pl.when(step == 0)
        def _():
            links.greet(("core", "xr", "y"))
            upb_own[...] = upb_ref[...].astype(F32)
            for k in (6, 0, 1):
                remote(k, True).start()

        @pl.when(step == blocks)
        def _():
            remote(7, True).start()

        for k, ready in zip(range(4), WEIGHT_STEPS):
            @pl.when(step == ready)
            def _(k=k):
                remote(k, False).wait_recv()
                remote(k + 2, True).start()

    @pl.when(step == 0)
    def _():
        carry[...] = jnp.zeros_like(carry)
        is_first = lax.axis_index("seq") == 0
        spread = jnp.where(iota((LANES, heads), 0) % heads == iota((LANES, heads), 1), 1.0, 0.0)
        wg_ref[...] = nn(spread.astype(BF16), gate_ref[...]).astype(BF16)
        lane_head = iota((1, LANES), 1) % heads
        row_head = iota((heads, LANES), 0)
        gb = jnp.zeros((1, LANES), F32)
        gbt = jnp.zeros((heads, LANES), F32)
        for h in range(heads):
            gb = jnp.where(lane_head == h, gb_smem[h], gb)
            gbt = jnp.where(row_head == h, gb_smem[h], gbt)
            begin = start_ref[h]
            norm = jnp.broadcast_to(start_norm_ref[h : h + 1, :], begin.shape)
            both = [begin, norm] if h % 2 == 0 else [norm, begin]
            state[h] = jnp.where(is_first, jnp.concatenate(both, axis=0), 0.0)
        gb_ref[...] = gb
        gbt_ref[...] = gbt
        for p in range(heads // 2):
            high, rest = projection_blocks(proj_ref, p, 1.0 / (2.0 * math.pi))
            pcat_ref[p, 0:LANES, :] = high
            pcat_ref[p, LANES : 2 * LANES, :] = high
            pcat_ref[p, 2 * LANES : 3 * LANES, :] = rest

    lower = lower_half((C, LANES))

    @pl.when(step < blocks)
    def _():
        xhat, _ = normalize(x_ref[...].astype(F32))
        ml = (xhat * gain_ref[...] + bias_ref[...]).astype(BF16)
        ml_ref[...] = ml
        q = nn(ml, wq_ref[...])
        k = nn(ml, wk_ref[...])
        v = nn(ml, wv_ref[...])
        v_low = v.astype(BF16)
        v_ref[...] = v_low
        rows_of = [slice(C * u, C * (u + 1)) for u in range(span)]
        logit = nt(ml, wg_ref[...]) + gb_ref[...]
        keep = log_sigmoid(logit)
        logit_row = nt(gate_ref[...], ml) + gbt_ref[...][:, 0:1]
        keep_row = log_sigmoid(logit_row)

        ftr_scale = 1.0 / math.sqrt(LANES)
        pairs = range(heads // 2)
        lanes_of = [slice(LANES * p, LANES * (p + 1)) for p in pairs]
        boths = [jnp.concatenate([q[:, at], k[:, at]], axis=0) for at in lanes_of]
        scales = [lax.rsqrt(head_sums(both * both) + EPS_UNIT) for both in boths]
        all_turns = []
        for p in pairs:
            unit = boths[p] * scales[p]
            high = unit.astype(BF16)
            rest = (unit - high.astype(F32)).astype(BF16)
            uq_ref[:, lanes_of[p]] = high[:full]
            uk_ref[:, lanes_of[p]] = high[full:]
            rq_ref[:, lanes_of[p]] = scales[p][:full]
            rk_ref[:, lanes_of[p]] = scales[p][full:]
            all_turns.append(nn(jnp.concatenate([high, rest, high], axis=1), pcat_ref[p]))
        coefs, totals = [], []
        group = iota((C, LANES), 1) // 8
        for u, rows in enumerate(rows_of):
            decay = rows_up_to(keep[rows])
            total = decay[C - 1 : C, :]
            coef = total - decay + keep[rows] - logit[rows]
            packed = jnp.where(group == 0, decay, coef)
            packed = jnp.where(group == 2, carry[...] + decay, packed)
            packed = jnp.where(group == 6, jnp.broadcast_to(carry[...], (C, LANES)), packed)
            packed = jnp.where(group == 7, jnp.broadcast_to(total, (C, LANES)), packed)
            gcol_ref[rows, :] = packed
            gcol_s[span * step + u] = packed
            carry[...] = carry[...] + total
            coefs.append(coef)
            totals.append(total)
            gate_rows = jnp.concatenate(
                [
                    keep_row[:, rows] - logit_row[:, rows] - lanes_up_to(keep_row[:, rows]),
                    jax.nn.sigmoid(logit_row[:, rows]),
                    jax.nn.sigmoid(-logit_row[:, rows]),
                ],
                axis=0,
            )
            grow_ref[:, rows] = gate_rows
            grow_s[span * step + u] = gate_rows
        if not comm:
            total_ref[...] = jnp.broadcast_to(carry[...], total_ref.shape)
        for p in pairs:
            s, c = sin_cos(all_turns[p], ftr_scale)
            s = s.astype(BF16)
            c = c.astype(BF16)
            for j in range(2):
                h = 2 * p + j
                half_lanes = slice(LANES * j, LANES * (j + 1))
                feats = jnp.concatenate([s[:, half_lanes], c[:, half_lanes]], axis=1)
                place = slice(256 * h, 256 * (h + 1))
                qf_ref[:, place] = feats[:full]
                kf_ref[:, place] = feats[full:]
                for u, rows in enumerate(rows_of):
                    at = span * step + u
                    kf = feats[full + C * u : full + C * (u + 1)]
                    qf_s[at, :, place] = feats[rows]
                    kf_s[at, :, place] = kf
                    v_s[at, :, lanes_of[p]] = v_low[rows, lanes_of[p]]
                    values = jnp.where(mine(h, lower), v[rows, lanes_of[p]], 1.0)
                    weighted = values * jnp.exp(column(coefs[u], h, C, LANES))
                    now = state[h]
                    now_low = now.astype(BF16)
                    before_ref[u, h] = now_low
                    before_s[at, h] = now_low
                    state[h] = jnp.exp(totals[u][:, h : h + 1]) * now + tn(weighted.astype(BF16), kf)

    @pl.when(step == blocks - 1)
    def _():
        pack_states([state[h] for h in range(heads)], sent if comm else final_ref)

    @pl.when(step >= blocks)
    def _():
        chunk = step - blocks
        causal = iota((C, C), 0) >= iota((C, C), 1)
        gcol = gcol_s[chunk]
        for first in range(0, heads, INNER_HEADS):
            some = range(first, first + INNER_HEADS)
            boths = []
            for h in some:
                place = slice(256 * h, 256 * (h + 1))
                keys = jnp.concatenate([kf_s[chunk, :, place], before_s[chunk, h]], axis=0)
                boths.append(nt(qf_s[chunk, :, place], keys))
            decays = [column(gcol, h, C, LANES) for h in some]
            weights = []
            for h, both, decay in zip(some, boths, decays):
                pairs = jnp.where(causal, jnp.exp(decay + grow_s[chunk, h : h + 1, :]), 0.0)
                weights.append((both[:, :C] * pairs).astype(BF16))
            for k, h in enumerate(some):
                lanes = slice(LANES * (h // 2), LANES * (h // 2 + 1))
                v = v_s[chunk, :, lanes].astype(F32)
                values = jnp.where(mine(h, lower), v, 1.0).astype(BF16)
                n_ref[:, LANES * h : LANES * (h + 1)] = (
                    nn(weights[k], values) + jnp.exp(decays[k]) * boths[k][:, C:]
                )

    if comm:
        @pl.when(step == blocks + chunks - 1)
        def _():
            for k in (4, 5, 6, 7):
                remote(k, False).wait_recv()
            later = links.seq == 1
            entry_ref[...] = jnp.where(later, landed[...].astype(F32), 0.0).astype(BF16)
            upbs_ref[0:1, :] = upb_own[...]
            upbs_ref[1:2, :] = upb_landed[...]
            for k in range(8):
                remote(k, True).wait_send()


def feed_kernel(heads, tiles, pairs, comm, *refs):
    take = Taker(refs)
    x_ref, qf_hbm, n_ref, gcol_ref, entry_ref, wo_ref = take(6)
    gain_ref, bias_ref, downb_ref, upb_ref, dout_hbm = take(5)
    weights_hbm = take(4 if comm else 2)
    out_ref, mg_ref, a_ref = take(3)
    if comm:
        late_refs = take(len(FEED_STAGES))
        os_ref, flat_ref, after_ref = take(3)
    else:
        upg_ref, downg_ref, upbg_ref, o_ref, final_ref, sums_out = take(6)
    entry, adj, middle_s, num_s, den_s, fl_s, mix_s, br_s = take(8)
    acc_s, fg_s, dout_s, up_s, down_s, hid_s, pre_s, sums_s, load_sems = take(9)
    step = pl.program_id(0)
    tokens, width = middle_s.shape
    rows = x_ref.shape[0]
    shards, _, shard_width = up_s.shape
    hb = hid_s.shape[1] // 2
    (qf_s,) = take(1)
    loads = [
        (qf_hbm.at[pl.ds(rows * t, rows)], qf_s.at[pl.ds(rows * t, rows)]) for t in range(tiles)
    ]
    loads += [(dout_hbm, dout_s)]
    if comm:
        up_own, up_other, down_own, down_other = weights_hbm
        loads += [(up_own, up_s.at[0]), (up_other, up_s.at[1])]
        loads += [(down_own, down_s.at[0]), (down_other, down_s.at[1])]
        u_src, upbg_s, sent, landed, sends, recvs = take(6)
        links = Links()
        board = Board(links, take, None)
        for j, (plan, ticks) in enumerate(zip(feed_plans(hb), FEED_TICKS)):
            board.add(plan, u_src.at[j], late_refs[j], None, ticks)

        def exchange():
            return pltpu.make_async_remote_copy(
                src_ref=sent,
                dst_ref=landed,
                send_sem=sends,
                recv_sem=recvs,
                device_id=links.partner("xr", 1),
                device_id_type=MESH,
            )
    else:
        upbg_s = upbg_ref
        loads += [(weights_hbm[0], up_s), (weights_hbm[1], down_s)]

    def load(k):
        return pltpu.make_async_copy(loads[k][0], loads[k][1], load_sems.at[k])

    @pl.when(step == 0)
    def _():
        for k in range(len(loads)):
            load(k).start()
        adj[...] = jnp.zeros_like(adj)
        sums_s[...] = jnp.zeros_like(sums_s)
        norms = entry_ref[64 * heads : 64 * heads + 16, :].astype(F32)
        for h in range(heads):
            grown = grow_state(entry_ref[64 * h : 64 * (h + 1), :], norms[h : h + 1], h)
            entry[h] = grown.astype(BF16)
        if comm:
            links.greet(("core", "xr", "y", "z"))

    lower = lower_half((rows, LANES))

    @pl.when(step < tiles)
    def _():
        for t in range(tiles):
            pl.when(step == t)(load(t).wait)
        here = pl.ds(pl.multiple_of(step * rows, rows), rows)
        gcol = gcol_ref[...]
        fars = [nt(qf_s[here, 256 * h : 256 * (h + 1)], entry[h]) for h in range(heads)]
        mixed = []
        for p in range(heads // 2):
            lanes = slice(LANES * p, LANES * (p + 1))
            both = []
            for h in (2 * p, 2 * p + 1):
                far = fars[h] * jnp.exp(column(gcol, 16 + h, rows, LANES))
                both.append(n_ref[:, LANES * h : LANES * (h + 1)] + far)
            num = jnp.where(lower, both[0], both[1])
            den = pltpu.roll(jnp.where(lower, both[1], both[0]), 64, 1)
            num_s[here, lanes] = num
            den_s[here, lanes] = den
            mixed.append(num * lax.rsqrt(den * den + GUARD))
        mixed = jnp.concatenate(mixed, axis=1).astype(BF16)
        mix_s[here, :] = mixed
        middle = x_ref[...].astype(F32) + nn(mixed, wo_ref[...])
        middle_s[here, :] = middle
        acc_s[here, :] = middle + downb_ref[...]
        fg_s[here, :] = jnp.zeros_like(middle)
        xhat, _ = normalize(middle)
        fl_s[here, :] = (xhat * gain_ref[...] + bias_ref[...]).astype(BF16)

    @pl.when(step == tiles)
    def _():
        for k in range(tiles, len(loads)):
            load(k).wait()

    @pl.when(jnp.logical_and(step >= tiles, step < tiles + pairs))
    def _():
        j = step - tiles
        blocks = []
        for s in range(2):
            if comm:
                shard, off = s, pl.multiple_of(j * hb, hb)
            else:
                at = (2 * j + s) * hb
                shard, off = at // shard_width, pl.multiple_of(at % shard_width, hb)
            blocks.append((shard, pl.ds(off, hb)))
        ups = [up_s[shard, :, cols] for shard, cols in blocks]
        downs = [down_s[shard, :, cols] for shard, cols in blocks]
        up = jnp.concatenate(ups, axis=1)
        down = jnp.concatenate(downs, axis=1)
        if comm:
            upb = jnp.concatenate(
                [upb_ref[s : s + 1, cols] for s, (_, cols) in enumerate(blocks)], axis=1
            )
        else:
            upb = jnp.concatenate([upb_ref[shard, :, cols] for shard, cols in blocks], axis=1)
        if comm:
            for k in range(pairs):
                pl.when(j == k)(partial(board.advance, 2 * k))
        many = min(FEED_ROWS, tokens)
        for r in range(tokens // many):
            here = slice(many * r, many * (r + 1))
            feed_low = fl_s[here, :]
            pre = nn(feed_low, up) + upb
            pre_grad = nn(dout_s[here, :], down)
            t = 1.0 / (1.0 + ERF_P * jnp.abs(pre))
            bell = INV_SQRT_2PI * jnp.exp(-0.5 * pre * pre)
            tail = ((((ERF[4] * t + ERF[3]) * t + ERF[2]) * t + ERF[1]) * t + ERF[0]) * t * bell
            phi = jnp.where(pre >= 0.0, 1.0 - tail, tail)
            hidden = (pre * phi).astype(BF16)
            pre_low = (pre_grad * (phi + pre * bell)).astype(BF16)
            hid_s[here, :] = hidden
            pre_s[here, :] = pre_low
            acc_s[here, :] += nt(hidden, down)
            fg_s[here, :] += nt(pre_low, up)
        up_grad = tn(fl_s[...], pre_s[...]).astype(BF16)
        down_grad = tn(dout_s[...], hid_s[...]).astype(BF16)
        bias_grad = nn(jnp.ones((16, tokens), BF16), pre_s[...])[0:1]
        for s, (shard, cols) in enumerate(blocks):
            part = slice(hb * s, hb * (s + 1))
            upbg_s[shard, :, cols] = bias_grad[:, part]
            if comm:
                u_src[j, width * s : width * (s + 1), :] = up_grad[:, part]
                u_src[j, width * (2 + s) : width * (3 + s), :] = down_grad[:, part]
            else:
                upg_ref[shard, :, cols] = up_grad[:, part]
                downg_ref[shard, :, cols] = down_grad[:, part]

    @pl.when(step >= tiles + pairs)
    def _():
        tile = step - tiles - pairs

        if comm:
            for t in range(tiles):
                pl.when(tile == t)(partial(board.advance, 2 * pairs + t))
        here = pl.ds(pl.multiple_of(tile * rows, rows), rows)
        gcol = gcol_ref[...]
        dout = dout_s[here, :].astype(F32)
        out_ref[...] = acc_s[here, :].astype(BF16)
        feed_grad = fg_s[here, :]
        xhat, scale = normalize(middle_s[here, :])
        sums_s[0:8, :] += fold_rows(feed_grad * xhat)
        sums_s[8:16, :] += fold_rows(feed_grad)
        sums_s[16:24, :] += fold_rows(dout)
        middle_grad = dout + normalize_back(feed_grad, gain_ref[...], xhat, scale)
        mg_ref[...] = middle_grad
        branch = middle_grad.astype(BF16)
        br_s[here, :] = branch
        mixed_grad = nt(branch, wo_ref[...])
        lanes_of = [slice(LANES * p, LANES * (p + 1)) for p in range(heads // 2)]
        alongs = [head_sums(mixed_grad[:, lanes] * num_s[here, lanes]) for lanes in lanes_of]
        lifts = []
        for p, lanes in enumerate(lanes_of):
            den = den_s[here, lanes]
            inv = lax.rsqrt(den * den + GUARD)
            b = alongs[p] * den * (inv * inv * inv) * (-1.0 / 64)
            b = pltpu.roll(b, 64, 1)
            for h in (2 * p, 2 * p + 1):
                a = jnp.where(mine(h, lower), mixed_grad[:, lanes] * inv, b)
                a_ref[:, LANES * h : LANES * (h + 1)] = a.astype(BF16)
                lifts.append((a * jnp.exp(column(gcol, 16 + h, rows, LANES))).astype(BF16))
        for h in range(heads):
            adj[h] += tn(lifts[h], qf_s[here, 256 * h : 256 * (h + 1)])

    @pl.when(step == 2 * tiles + pairs - 1)
    def _():
        pack_states([adj[h] for h in range(heads)], sent if comm else final_ref)
        if comm:
            exchange().start()
        output_grad = tn(mix_s[...], br_s[...]).astype(BF16)
        if not comm:
            o_ref[...] = output_grad
            sums_out[...] = sums_s[...]
            return
        os_ref[:, 0:width] = output_grad
        for later in range(2 * pairs + tiles, board.last() + 1):
            board.advance(later)
        exchange().wait_recv()
        is_first = links.seq == 0
        after_ref[...] = jnp.where(is_first, landed[...].astype(F32), 0.0).astype(BF16)
        logs = gcol_ref[rows - 1 : rows, :]
        norms = landed[64 * heads : 64 * heads + 16, :].astype(F32)
        flat_ref[...] = jnp.zeros_like(flat_ref)
        for k in range(3):
            flat_ref[k : k + 1, :] = jnp.sum(sums_s[8 * k : 8 * (k + 1), :], axis=0, keepdims=True)
        for k in range(2 * shard_width // width):
            cols = slice(width * k % shard_width, width * k % shard_width + width)
            in_first = k < shard_width // width
            own, other = upbg_s[0, :, cols], upbg_s[1, :, cols]
            flat_ref[3 + k : 4 + k, :] = jnp.where(is_first, own, other) if in_first else jnp.where(
                is_first, other, own
            )
        for h in range(heads):
            grown = grow_state(landed[64 * h : 64 * (h + 1), :], norms[h : h + 1], h)
            begin = adj[h] + jnp.exp(logs[:, 16 + h : 17 + h]) * grown
            begin = jnp.where(is_first, begin, 0.0)
            os_ref[64 * h : 64 * (h + 1), width : width + 256] = state_part(begin, h).astype(BF16)
            flat_ref[8 + h : 9 + h, 0:256] = 64.0 * norm_part(begin, h)
        exchange().wait_send()
        board.drain()


U_SCATTER, U_GATHER = ("core", "xr", "y", "z"), ("z", "y", "core")
FEED_STAGES = (4, 3, 2, 1)
FEED_TICKS = ((2, 4, 6, 8, 11), (4, 6, 9, 12), (6, 8, 12), (8, 10))
BACK_TICKS = ((2, 4, 6, 7), (1, 3, 5, 7, 8), (1, 3, 5, 7, 8, 9), (1, 3, 5, 7, 8, 9, 10))


def feed_plans(hb):
    return [Plan(2048, hb, BF16, U_SCATTER[:n], ()) for n in FEED_STAGES]


def late_plans(hb):
    plans = []
    for plan, n in zip(feed_plans(hb), FEED_STAGES):
        done = [group for group in U_SCATTER[:n] if group != "xr"]
        plans.append(Plan(plan.left, hb, BF16, U_SCATTER[n:], U_GATHER, pre=tuple(done)))
    return plans


def back_kernel(heads, hg, span, chunks, comm, *refs):
    take = Taker(refs)
    (qf_ref, kf_ref, v_ref, uq_ref, uk_ref, rq_ref, rk_ref, a_ref, gcol_ref, grow_ref) = take(10)
    before_ref, entry_ref, entry_norm, after_ref, after_norm, proj_in = take(6)
    x_hbm, mg_hbm, ml_hbm, wq_hbm, wk_hbm, wv_hbm, gate_ref, gain_ref = take(8)
    u_hbms = take(len(FEED_STAGES)) if comm else ()
    os_hbm, f_hbm = take(2) if comm else (None,) * 2
    dx_ref, w_ref, small_ref = take(3)
    usum_hbm, ossum_hbm, fsum_hbm = take(3) if comm else (None,) * 3
    adj_ref, dqkv, dlogit, x_ref, mg_ref, ml_ref, wq_ref, wk_ref, wv_ref, load_sems = take(10)
    (proj_ref,) = take(1)
    g, i = pl.program_id(0), pl.program_id(1)
    tick = g * chunks + i
    last = heads // hg * chunks - 1
    first_row = (chunks - 1 - i) * (span * C)
    here = pl.ds(pl.multiple_of(first_row, C), span * C)
    groups = heads // hg
    loads = [
        (x_hbm, x_ref),
        (mg_hbm, mg_ref),
        (ml_hbm, ml_ref),
        (wq_hbm, wq_ref),
        (wk_hbm, wk_ref),
        (wv_hbm, wv_ref),
    ]
    if comm:
        u_refs = take(len(FEED_STAGES))
        os_ref, f_ref, w_src, small_src = take(4)
        usum_ref, ossum_ref, fsum_ref, wsum_ref, smallsum_ref = take(5)
        (store_sems,) = take(1)
        loads = list(zip(u_hbms, u_refs)) + [(os_hbm, os_ref), (f_hbm, f_ref)] + loads
        early_loads = len(loads) - 6
        links = Links()
        board = Board(links, take, store_sems)
        plans = back_plans(os_hbm.shape, f_hbm.shape, w_src.shape, small_src.shape)

        def stages(start, gaps):
            ticks = [start]
            for gap in gaps:
                ticks.append(ticks[-1] + gap)
            return ticks

        for k in reversed(range(groups)):
            final = k + 1 == groups
            pieces = W_PIECES if final else 1
            lanes_each = w_src.shape[2] // pieces
            for j in range(pieces):
                lanes = pl.ds(j * lanes_each, lanes_each)
                board.add(
                    plans["w_last" if final else "w"],
                    w_src.at[k, :, lanes],
                    wsum_ref.at[k, :, lanes],
                    w_ref.at[k, :, lanes],
                    [last + 1 + i for i in range(7)]
                    if final
                    else [(k + 1) * chunks + gap for gap in W_GAPS],
                )
        for j, (plan, ticks) in enumerate(zip(late_plans(usum_ref.shape[2]), BACK_TICKS)):
            board.add(plan, u_refs[j], usum_ref.at[j], usum_hbm.at[j], ticks)
        board.add(plans["os"], os_ref, ossum_ref, ossum_hbm, OS_TICKS)
        board.add(plans["f"], f_ref, fsum_ref, fsum_hbm, F_TICKS)
        advance = board.advance

    def load(k):
        return pltpu.make_async_copy(loads[k][0], loads[k][1], load_sems.at[k])

    @pl.when(tick == 0)
    def _():
        for k in range(len(loads)):
            load(k).start()
        dlogit[...] = jnp.zeros_like(dlogit)
        if comm:
            links.greet(("core", "plane", "z"))

    if comm:
        @pl.when(tick == 1)
        def _():
            for k in range(early_loads):
                load(k).wait()

        for now in range(1, last + 1):
            pl.when(tick == now)(partial(advance, now))

    @pl.when(i == 0)
    def _():
        for p in range(hg // 2):
            proj_ref[p] = projection_blocks(proj_in, p, 1.0 / (2.0 * math.pi))[0]
        norms = after_norm[...].astype(F32)
        for h in range(hg):
            norm = pick_row(norms, g * hg + h)
            adj_ref[h] = grow_state(after_ref[64 * h : 64 * (h + 1), :], norm, h)

    row = iota((C, C), 0)
    col = iota((C, C), 1)
    causal = row >= col
    one = jnp.ones((C, C), BF16)
    zero = jnp.zeros((C, C), BF16)
    later = jnp.where(row < col, 1.0, 0.0).astype(BF16)
    pair_sums = jnp.concatenate([later, one], axis=0)
    two_sums = jnp.concatenate(
        [jnp.concatenate([one, zero], axis=1), jnp.concatenate([zero, one], axis=1)], axis=0
    )
    lower = lower_half((C, LANES))
    entry_norms = entry_norm[...].astype(F32)
    gcol = gcol_ref[...]
    if groups > 1:
        gcol = jnp.where(g == 0, gcol, pltpu.roll(gcol, LANES - hg, 1))

    def grow_row(kind, h):
        return grow_ref[pl.ds(kind * heads + g * hg + h, 1), :]

    width = hg * 64
    pairs_of_heads = range(hg // 2)
    lanes_of = [slice(LANES * p, LANES * (p + 1)) for p in pairs_of_heads]
    items = [(u, h) for u in reversed(range(span)) for h in range(hg)]
    numbers = range(len(items))
    rows_of = [slice(C * u, C * (u + 1)) for u in range(span)]
    qfs = [qf_ref[rows_of[u], 256 * h : 256 * (h + 1)] for u, h in items]
    kfs = [kf_ref[rows_of[u], 256 * h : 256 * (h + 1)] for u, h in items]
    a_lows = [a_ref[rows_of[u], LANES * h : LANES * (h + 1)] for u, h in items]
    values = [
        jnp.where(mine(h, lower), v_ref[rows_of[u], lanes_of[h // 2]].astype(F32), 1.0)
        for u, h in items
    ]
    values_low = [part.astype(BF16) for part in values]
    lifts = [jnp.exp(column(gcol[rows_of[u]], h, C, LANES)) for u, h in items]
    a_lifts = [(a_lows[k].astype(F32) * lifts[k]).astype(BF16) for k in numbers]
    dweights = []
    for k in numbers[::2]:
        u, h = items[k]
        top = jnp.concatenate([values_low[k], zero], axis=1)
        bottom = jnp.concatenate([zero, values_low[k + 1]], axis=1)
        both = nt(
            a_ref[rows_of[u], LANES * h : LANES * (h + 2)],
            jnp.concatenate([top, bottom], axis=0),
        )
        dweights += [both[:, :C], both[:, C:]]
    adj_lows, throughs, keys_and_states = [], [], []
    raws, fars, dv_fars = [], [], []
    for k, (u, h) in enumerate(items):
        carried = jnp.exp(gcol[C * u : C * u + 1, 48 + h : 49 + h])
        total = jnp.exp(gcol[C * u : C * u + 1, 56 + h : 57 + h])
        entry = grow_state(
            entry_ref[64 * h : 64 * (h + 1), :], pick_row(entry_norms, g * hg + h), h
        )
        before = before_ref[u, h].astype(F32) + carried * entry
        adj = adj_ref[h]
        adj_lows.append(adj.astype(BF16))
        kept = total * adj
        through = jnp.sum(kept * before, axis=0, keepdims=True)
        throughs.append(jnp.sum(through, axis=1, keepdims=True))
        keys_and_states.append(jnp.concatenate([kfs[k], before.astype(BF16)], axis=0))
        raw_and_far = nt(qfs[k], keys_and_states[k])
        raws.append(raw_and_far[:, :C])
        fars.append(raw_and_far[:, C:])
        dv_fars.append(nt(kfs[k], adj_lows[k]))
        if u > 0:
            adj_ref[h] = kept + tn(a_lifts[k], qfs[k])
        else:
            adj_ref[h] = kept
    coefs = [jnp.exp(column(gcol[rows_of[u]], 8 + h, C, LANES)) for u, h in items]
    weights, draws, boths, v_coefs = [], [], [], []
    for k, (u, h) in enumerate(items):
        gap = column(gcol[rows_of[u]], h, C, LANES) + grow_row(0, h)[:, rows_of[u]]
        pairs = jnp.where(causal, jnp.exp(gap), 0.0)
        weights.append((raws[k] * pairs).astype(BF16))
        draw = dweights[k].astype(BF16).astype(F32) * pairs
        draws.append(draw.astype(BF16))
        boths.append((raws[k] * draw).astype(BF16))
        v_coefs.append((values[k] * coefs[k]).astype(BF16))
    dqs, dks, dvs = [], [], []
    for k in numbers:
        dqs.append(nn(jnp.concatenate([draws[k], a_lifts[k]], axis=1), keys_and_states[k]))
        dks.append(
            nn(
                jnp.concatenate([draws[k].T, v_coefs[k]], axis=1),
                jnp.concatenate([qfs[k], adj_lows[k]], axis=0),
            )
        )
        dvs.append(tn(weights[k], a_lows[k]))
        if items[k][0] == 0:
            adj_ref[items[k][1]] += tn(a_lifts[k], qfs[k])
    x_parts, y_parts = [], []
    for k in numbers:
        dv_far = coefs[k] * dv_fars[k]
        dvs[k] = dvs[k] + dv_far
        x_far = (a_lows[k].astype(F32) * lifts[k] * fars[k]).astype(BF16)
        x_parts.append(jnp.concatenate([boths[k], x_far], axis=1))
        y_far = (values[k] * dv_far).astype(BF16)
        y_parts.append(jnp.concatenate([y_far, (values[k] * dvs[k]).astype(BF16)], axis=1))
    upto = nn(jnp.concatenate(x_parts, axis=0), pair_sums)
    ends = nn(jnp.concatenate(y_parts, axis=0), two_sums)
    dus = []
    for p in pairs_of_heads:
        angles = []
        for feats, grads in ((qfs, dqs), (kfs, dks)):
            for u in range(span):
                row_angles = []
                for k, item in enumerate(items):
                    if item[0] == u and item[1] // 2 == p:
                        f, grad = feats[k].astype(F32), grads[k]
                        row_angles.append(
                            grad[:, :LANES] * f[:, LANES:] - grad[:, LANES:] * f[:, :LANES]
                        )
                angles.append(jnp.concatenate(row_angles, axis=1))
        dus.append(nt(jnp.concatenate(angles, axis=0).astype(BF16), proj_ref[p]))
    for k, (u, h) in enumerate(items):
        rows = slice(C * k, C * (k + 1))
        flow = jnp.where(causal, upto[rows], ends[rows, :C])
        flow = jnp.sum(flow, axis=0, keepdims=True) + throughs[k]
        own = jnp.sum(jnp.where(row == col, ends[rows, C:], 0.0), axis=0, keepdims=True)
        stay, leave = grow_row(1, h)[:, rows_of[u]], grow_row(2, h)[:, rows_of[u]]
        at = pl.ds(pl.multiple_of(first_row + C * u, C), C)
        dlogit[g, h : h + 1, at] = leave * flow - stay * own
    for p, lanes in enumerate(lanes_of):
        u = jnp.concatenate([uq_ref[:, lanes], uk_ref[:, lanes]], axis=0).astype(F32)
        scale = jnp.concatenate([rq_ref[:, lanes], rk_ref[:, lanes]], axis=0)
        along = nn((u * dus[p]).astype(BF16), block_ones())
        dqk = ((2.0 * math.pi) * scale * (dus[p] - u * along)).astype(BF16)
        dqkv[g, here, LANES * p : LANES * (p + 1)] = dqk[: span * C]
        dqkv[g, here, width + LANES * p : width + LANES * (p + 1)] = dqk[span * C :]
        for k, (u, h) in enumerate(items):
            if h == 2 * p:
                at = pl.ds(pl.multiple_of(first_row + C * u, C), C)
                dqkv[g, at, 2 * width + LANES * p : 2 * width + LANES * (p + 1)] = jnp.where(
                    lower, dvs[k], dvs[k + 1]
                ).astype(BF16)

    @pl.when(i == chunks - 1)
    def _():
        @pl.when(g == 0)
        def _():
            load(len(loads) - 4).wait()

        grads = tn(ml_ref[...], dqkv[g]).astype(BF16)
        if comm:
            w_src[g] = grads
        else:
            w_ref[g] = grads

    @pl.when(tick == last)
    def _():
        if comm:
            advance(last + 1)
        for k in range(len(loads) - 6, len(loads)):
            if k != len(loads) - 4:
                load(k).wait()
        tokens = chunks * span * C
        block = min(T, tokens)
        small = small_src if comm else small_ref
        rows8 = jnp.concatenate(
            [dlogit[k, 0:hg, :] for k in range(groups)]
            + [jnp.zeros((16 - heads, dlogit.shape[2]), F32)],
            axis=0,
        ).astype(BF16)
        small[...] = jnp.zeros_like(small)
        small[0:heads, :] = nn(rows8, ml_ref[...])[0:heads]
        bias_sum = nt(jnp.ones(rows8.shape, BF16), rows8)[0:1]
        small[heads : heads + 1, 0:16] = bias_sum
        gain = gain_ref[...]
        now = last + 2
        for b in range(tokens // block):
            rows = slice(block * b, block * (b + 1))
            mixer_grad = tn(rows8[0:heads, rows], gate_ref[...])
            for k in range(groups):
                for j, ref in enumerate((wq_ref, wk_ref, wv_ref)):
                    mixer_grad = mixer_grad + nt(
                        dqkv[k, rows, hg * 64 * j : hg * 64 * (j + 1)],
                        ref[:, hg * 64 * k : hg * 64 * (k + 1)],
                    )
            xhat, scale = normalize(x_ref[rows, :].astype(F32))
            small[heads + 1 : heads + 2, :] += jnp.sum(
                mixer_grad * xhat, axis=0, keepdims=True
            )
            small[heads + 2 : heads + 3, :] += jnp.sum(mixer_grad, axis=0, keepdims=True)
            dx_ref[rows, :] = mg_ref[rows, :] + normalize_back(mixer_grad, gain, xhat, scale)
            if comm and b % 2 == 1 and b + 1 < tokens // block:
                advance(now)
                now += 1
        if comm:
            board.add(
                plans["small"], small_src, smallsum_ref, small_ref, [now, now + 1, now + 2, now + 3]
            )
            for later_tick in range(now, board.last() + 1):
                advance(later_tick)
            board.drain()


OS_TICKS = (1, 3, 5, 7, 8, 9, 10)
F_TICKS = (5, 7, 8, 9)
W_GAPS = (0, 2, 4, 5, 6, 7, 8)
W_PIECES = 3
SUM_ROWS = 16


def back_plans(os, f, w, small):
    return {
        "os": Plan(os[0], os[1], BF16, *ALL_PLAN),
        "f": Plan(f[0], f[1], F32, *SHARE_PLAN),
        "w": Plan(w[1], w[2], BF16, *ALL_PLAN),
        "w_last": Plan(w[1], w[2] // W_PIECES, BF16, *ALL_PLAN),
        "small": Plan(small[0], small[1], F32, *SHARE_PLAN),
    }


def whole(shape):
    zeros = (0,) * len(shape)
    return pl.BlockSpec(shape, lambda *at: zeros, pipeline_mode=pl.Buffered(1))


ANY = pl.BlockSpec(memory_space=pl.ANY)


def call(kernel, grid, ins, outs, scratch, name, collective_id=None):
    def spec(shape, block, index):
        if block is None:
            return whole(shape)
        return block if isinstance(block, pl.BlockSpec) else pl.BlockSpec(block, index)

    params = {} if collective_id is None else {
        "collective_id": collective_id, "has_side_effects": True
    }
    return pl.pallas_call(
        kernel,
        grid=grid,
        in_specs=[spec(array.shape, block, index) for array, block, index in ins],
        out_specs=[spec(shape, block, index) for shape, _, block, index in outs],
        out_shape=[jax.ShapeDtypeStruct(shape, dtype) for shape, dtype, _, _ in outs],
        scratch_shapes=scratch,
        compiler_params=pltpu.CompilerParams(
            dimension_semantics=("arbitrary",) * len(grid), vmem_limit_bytes=VMEM, **params
        ),
        name=name,
    )(*[array for array, _, _ in ins])


def finish_kernel(heads, *refs):
    take = Taker(refs)
    late_ref, w_ref, os_ref, flat_ref, small_ref = take(5)
    up_ref, down_ref, q_ref, k_ref, v_ref, o_ref, s_ref = take(7)
    vectors, (upb_ref, norm_ref, gate_ref, gate_bias_ref) = take(5), take(4)

    @pl.when(pl.program_id(0) == 0)
    def _():
        def spread(row, ref, first):
            for k in range(row.shape[1] // LANES):
                ref[first + k : first + k + 1, :] = row[:, LANES * k : LANES * (k + 1)]

        flat, small = flat_ref[...], small_ref[...]
        rows = [small[heads + 1 : heads + 2], small[heads + 2 : heads + 3]]
        rows += [flat[k : k + 1] for k in range(3)]
        for row, ref in zip(rows, vectors):
            spread(row, ref, 0)
        is_first = lax.axis_index("seq") == 0
        half = upb_ref.shape[0] * LANES // flat.shape[1]
        for k in range(half):
            row = jnp.where(is_first, flat[3 + k : 4 + k], flat[3 + half + k : 4 + half + k])
            spread(row, upb_ref, k * (flat.shape[1] // LANES))
        norm_ref[...] = flat[8 : 8 + heads, 0 : norm_ref.shape[1]]
        gate_ref[...] = small[0:heads]
        gate_bias_ref[...] = small[heads : heads + 1, 0:heads]

    hb = late_ref.shape[3]
    for part, ref in enumerate((up_ref, down_ref)):
        for k in range(late_ref.shape[0]):
            ref[:, hb * k : hb * (k + 1)] = late_ref[k, part].astype(F32)
    groups, _, lanes = w_ref.shape
    each = lanes // 3
    for part, ref in enumerate((q_ref, k_ref, v_ref)):
        for k in range(groups):
            ref[:, each * k : each * (k + 1)] = w_ref[k, :, each * part : each * (part + 1)].astype(F32)
    width = o_ref.shape[1]
    o_ref[...] = os_ref[:, 0:width].astype(F32)
    for k in range(s_ref.shape[0]):
        s_ref[k] = os_ref[64 * k : 64 * (k + 1), width:].astype(F32)


def finish(heads, sum_late, sum_w, out_state, flat, small):
    width = sum_w.shape[1]
    steps = 4
    rows = width // steps
    late, _, hb = sum_late.shape
    feats = out_state.shape[1] - width
    square = ((width, width), F32, (rows, width), lambda i: (i, 0))
    wide = ((width, late * hb), F32, (rows, late * hb), lambda i: (i, 0))
    return call(
        partial(finish_kernel, heads),
        (steps,),
        [
            (sum_late.reshape(late, 2, width, hb), (late, 2, rows, hb), lambda i: (0, 0, i, 0)),
            (sum_w, (sum_w.shape[0], rows, sum_w.shape[2]), lambda i: (0, i, 0)),
            (out_state, (rows, width + feats), lambda i: (i, 0)),
            (flat, None, None),
            (small, None, None),
        ],
        [wide, wide, square, square, square, square]
        + [((heads, 64, feats), F32, (heads // steps, 64, feats), lambda i: (i, 0, 0))]
        + [((width // LANES, LANES), F32, None, None)] * 5
        + [
            ((late * hb // LANES, LANES), F32, None, None),
            ((heads, feats), F32, None, None),
            ((heads, width), F32, None, None),
            ((1, heads), F32, None, None),
        ],
        [],
        "finish",
    )


def carry_over(payload, logs, forward):
    n, index = lax.axis_size("seq"), lax.axis_index("seq")
    everything = lax.all_gather(payload, "seq")
    every_log = lax.all_gather(logs, "seq")
    heads = logs.shape[0]
    row = jnp.arange(payload.shape[0])
    head = jnp.where(row < 64 * heads, row // 64, jnp.minimum(row - 64 * heads, heads - 1))
    total = jnp.zeros(payload.shape, F32)
    for k in range(n) if forward else reversed(range(n)):
        ahead = (k < index) if forward else (k > index)
        new = jnp.exp(every_log[k])[head][:, None] * total + everything[k].astype(F32)
        total = jnp.where(ahead, new, total)
    return total.astype(BF16)


def local(
    inputs,
    cotangent,
    mixer_gain,
    mixer_bias,
    query_weight,
    key_weight,
    value_weight,
    gate_weight,
    gate_bias,
    output_weight,
    projections,
    start_state,
    start_norm,
    feed_gain,
    feed_bias,
    up_weight,
    up_bias,
    down_weight,
    down_bias,
):
    _, tokens, width = inputs.shape
    heads, size, feats = projections.shape
    chunks = tokens // C
    span = min(SPAN, chunks)
    blocks = chunks // span
    tile = min(T, tokens)
    tiles = tokens // tile
    shards = lax.axis_size("seq")
    first = lax.axis_index("seq") == 0
    comm = (lax.axis_size("dp"), shards) == (16, 2)
    gate_rows = gate_weight.T
    x = inputs.reshape(tokens, width)
    dout = cotangent.reshape(tokens, width)
    shard_width = up_weight.shape[1]
    hidden = shard_width * shards
    hb = min(HB, shard_width)
    pairs = hidden // (2 * hb)
    wide = heads * LANES
    wider = heads * 2 * feats
    pay_shape = (heads * 64 + 16, 2 * feats)

    def const(array):
        return (array if array.ndim > 1 else array[None], None, None)

    def keep(shape, dtype):
        return (shape, dtype, None, None)

    def hbm(array):
        return (array, ANY, None)

    def result(shape, dtype):
        return (shape, dtype, ANY, None)

    def vmem(*shape, dtype=BF16):
        return pltpu.VMEM(shape, dtype)

    def early(n):
        return (span * C, n), lambda i: (jnp.minimum(i, blocks - 1), 0)

    def out_early(n, dtype):
        return ((tokens, n), dtype) + early(n)

    ins = [(x,) + early(width)]
    ins += [const(part) for part in (mixer_gain, mixer_bias, query_weight, key_weight)]
    ins += [
        const(value_weight),
        const(gate_rows),
        (gate_bias, pl.BlockSpec(memory_space=pltpu.SMEM), None),
        const(projections),
        const(start_state.transpose(0, 2, 1)),
        const(start_norm),
    ]
    outs = [out_early(width, BF16)] * 3 + [out_early(width, F32)] * 2
    outs += [out_early(wider, BF16)] * 2 + [out_early(width, BF16), out_early(LANES, F32)]
    outs += [
        (
            (3 * heads, tokens),
            F32,
            (3 * heads, span * C),
            lambda i: (0, jnp.minimum(i, blocks - 1)),
        ),
        (
            (chunks, heads, LANES, 2 * feats),
            BF16,
            (span, heads, LANES, 2 * feats),
            lambda i: (jnp.minimum(i, blocks - 1), 0, 0, 0),
        ),
        ((tokens, wide), F32, (C, wide), lambda i: (jnp.maximum(i - blocks, 0), 0)),
    ]
    scratch = [
        vmem(heads, LANES, 2 * feats, dtype=F32),
        vmem(1, LANES, dtype=F32),
        vmem(chunks, C, wider),
        vmem(chunks, C, wider),
        vmem(chunks, C, width),
        vmem(chunks, C, LANES, dtype=F32),
        vmem(chunks, 3 * heads, C, dtype=F32),
        vmem(chunks, heads, LANES, 2 * feats),
        vmem(LANES, width),
        vmem(1, LANES, dtype=F32),
        vmem(heads, LANES, dtype=F32),
        vmem(heads // 2, 3 * LANES, 2 * feats),
    ]
    if comm:
        ins += [hbm(up_weight), hbm(down_weight), const(up_bias)]
        outs += [
            keep(pay_shape, BF16),
            result(up_weight.shape, BF16),
            result(down_weight.shape, BF16),
            keep((2, shard_width), F32),
        ]
        scratch += [
            vmem(*pay_shape),
            vmem(*pay_shape),
            vmem(1, shard_width, dtype=F32),
            vmem(1, shard_width, dtype=F32),
            pltpu.SemaphoreType.DMA((8,)),
            pltpu.SemaphoreType.DMA((8,)),
        ]
    else:
        outs += [keep(pay_shape, BF16), keep((8, LANES), F32)]
    found = call(
        partial(features_kernel, heads, span, blocks, comm),
        (blocks + chunks,),
        ins,
        outs,
        scratch,
        "features",
        1 if comm else None,
    )
    ml, uq, uk, rq, rk, qf, kf, v, gcol, grow, before, num = found[:12]
    if comm:
        entry, up_other, down_other, upb = found[12:]
        weights = (up_weight, up_other, down_weight, down_other)
    else:
        final, total = found[12:]
        logs = total[0, :heads]
        entry = carry_over(final, logs, True)
        weights = (lax.all_gather(up_weight, "seq"), lax.all_gather(down_weight, "seq"))
        upb = lax.all_gather(up_bias.astype(F32)[None], "seq")

    steps = 2 * tiles + pairs

    def first_last(n):
        def index(i):
            late = jnp.maximum(i - tiles - pairs, 0)
            return (jnp.where(i < tiles + pairs, jnp.minimum(i, tiles - 1), late), 0)

        return (tile, n), index

    def only_first(n):
        return (tile, n), lambda i: (jnp.minimum(i, tiles - 1), 0)

    def only_last(n, dtype):
        return (
            (tokens, n),
            dtype,
            (tile, n),
            lambda i: (jnp.maximum(i - tiles - pairs, 0), 0),
        )

    ins = [
        (x,) + only_first(width),
        hbm(qf),
        (num,) + only_first(wide),
        (gcol,) + first_last(LANES),
        const(entry),
        const(output_weight),
        const(feed_gain),
        const(feed_bias),
        const(down_bias),
        const(upb),
        hbm(dout),
    ] + [hbm(part) for part in weights]
    outs = [only_last(width, BF16), only_last(width, F32), only_last(wide, BF16)]
    scratch = [
        vmem(heads, LANES, 2 * feats),
        vmem(heads, LANES, 2 * feats, dtype=F32),
        vmem(tokens, width, dtype=F32),
        vmem(tokens, width, dtype=F32),
        vmem(tokens, width, dtype=F32),
        vmem(tokens, width),
        vmem(tokens, width),
        vmem(tokens, width),
        vmem(tokens, width, dtype=F32),
        vmem(tokens, width, dtype=F32),
        vmem(tokens, width),
        vmem(shards, width, shard_width),
        vmem(shards, width, shard_width),
        vmem(tokens, 2 * hb),
        vmem(tokens, 2 * hb),
        vmem(24, width, dtype=F32),
        pltpu.SemaphoreType.DMA((5 + tiles,)),
        vmem(tokens, wider),
    ]
    if comm:
        plans = feed_plans(hb)
        outs += [
            *[keep((plan.left, hb), BF16) for plan in plans],
            keep((width, width + 2 * feats), BF16),
            keep((16, width), F32),
            keep(pay_shape, BF16),
        ]
        scratch += [
            vmem(pairs, 4 * width, hb),
            vmem(shards, 1, shard_width, dtype=F32),
            vmem(*pay_shape),
            vmem(*pay_shape),
            pltpu.SemaphoreType.DMA,
            pltpu.SemaphoreType.DMA,
        ]
        for plan in plans:
            scratch += plan.scratch()
    else:
        outs += [
            keep((shards, width, shard_width), BF16),
            keep((shards, width, shard_width), BF16),
            keep((shards, 1, shard_width), F32),
            keep((width, width), BF16),
            keep(pay_shape, BF16),
            keep((24, width), F32),
        ]
    found = call(
        partial(feed_kernel, heads, tiles, pairs, comm),
        (steps,),
        ins,
        outs,
        scratch,
        "feed",
        2 if comm else None,
    )
    out, mg, a = found[:3]
    if comm:
        u_late = found[3:-3]
        out_state, flat, after = found[-3:]
    else:
        up_grad, down_grad, upb_grad, output_grad, adj_final, feed_sums = found[3:]
        after = carry_over(adj_final, logs, False)
        feed_three = jnp.sum(feed_sums.reshape(3, 8, width), axis=1)
        begin = adj_final.astype(F32)
        row = jnp.arange(pay_shape[0])
        head = jnp.where(row < 64 * heads, row // 64, jnp.minimum(row - 64 * heads, heads - 1))
        begin = begin + jnp.exp(logs)[head][:, None] * after.astype(F32)
        begin = jnp.where(first, begin, 0.0)
        state_grad = begin[: heads * 64].astype(BF16)
        norm_grad = 64.0 * begin[heads * 64 : heads * 65]

    hg = GROUP_HEADS
    groups = heads // hg
    def back_rows(n, per_group=True):
        return (span * C, n), lambda g, i: (blocks - 1 - i, g if per_group else 0)

    def per_group(array, *shape):
        zeros = (0,) * (len(shape) - 1)
        return (array, shape, lambda g, i: (g,) + zeros)

    def states(array):
        return [
            (array, (hg * 64, 2 * feats), lambda g, i: (g, 0)),
            (array, (16, 2 * feats), lambda g, i: (heads * 4, 0)),
        ]

    ins = [
        (qf,) + back_rows(hg * 2 * feats),
        (kf,) + back_rows(hg * 2 * feats),
        (v,) + back_rows(hg * size),
        (uq,) + back_rows(hg * size),
        (uk,) + back_rows(hg * size),
        (rq,) + back_rows(hg * size),
        (rk,) + back_rows(hg * size),
        (a,) + back_rows(hg * LANES),
        (gcol,) + back_rows(LANES, False),
        (grow, (3 * heads, span * C), lambda g, i: (0, blocks - 1 - i)),
        (before, (span, hg, LANES, 2 * feats), lambda g, i: (blocks - 1 - i, g, 0, 0)),
    ]
    ins += states(entry) + states(after)
    ins += [
        per_group(projections, hg, size, feats),
        hbm(x),
        hbm(mg),
        hbm(ml),
        hbm(query_weight),
        hbm(key_weight),
        hbm(value_weight),
        const(gate_rows),
        const(mixer_gain),
    ]
    w_shape, small_shape = (groups, width, 3 * hg * size), (16, width)

    def sums(shape, dtype):
        return result(shape, dtype) if comm else keep(shape, dtype)

    outs = [keep((tokens, width), F32), sums(w_shape, BF16), sums(small_shape, F32)]
    scratch = [
        vmem(hg, LANES, 2 * feats, dtype=F32),
        vmem(groups, tokens, 3 * hg * size),
        vmem(groups, 8, tokens, dtype=F32),
        vmem(tokens, width),
        vmem(tokens, width, dtype=F32),
        vmem(tokens, width),
        vmem(width, width),
        vmem(width, width),
        vmem(width, width),
        pltpu.SemaphoreType.DMA((12,)),
        vmem(hg // 2, LANES, 2 * feats),
    ]
    if comm:
        ins += [hbm(part) for part in (*u_late, out_state, flat)]
        summed = [
            ((len(u_late), 2 * width, hb), BF16),
            (out_state.shape, BF16),
            (flat.shape, F32),
        ]
        outs += [result(*part) for part in summed]
        scratch += [vmem(*part.shape) for part in u_late]
        scratch += [
            vmem(*out_state.shape),
            vmem(*flat.shape, dtype=F32),
            vmem(*w_shape),
            vmem(*small_shape, dtype=F32),
        ]
        scratch += [vmem(*shape, dtype=dtype) for shape, dtype in summed]
        scratch += [vmem(*w_shape), vmem(*small_shape, dtype=F32)]
        plans = back_plans(out_state.shape, flat.shape, w_shape, small_shape)
        first_names = ("w_last",) * W_PIECES + ("w",) * (groups - 1)
        plans = (
            [plans[name] for name in first_names]
            + late_plans(hb)
            + [plans[name] for name in ("os", "f", "small")]
        )
        scratch += [pltpu.SemaphoreType.DMA((len(plans),))]
        for plan in plans:
            scratch += plan.scratch()
    found = call(
        partial(back_kernel, heads, hg, span, blocks, comm),
        (groups, blocks),
        ins,
        outs,
        scratch,
        "back",
        3 if comm else None,
    )
    dx, sum_w, small = found[:3]
    if comm:
        sum_late, out_state, flat = found[3:]
        results = finish(heads, sum_late, sum_w, out_state, flat, small)
        sum_up, sum_down, sum_q, sum_k, sum_v, sum_o, sum_state = results[:7]
        mixer_two, sum_feed = results[7:9], results[9:12]
        sum_upb, sum_norm, sum_gate, gate_bias_sum = results[12:]
        gate_bias_sum = gate_bias_sum.reshape(-1)
    else:
        own = lax.psum_scatter(
            jnp.stack([up_grad, down_grad]), "seq", scatter_dimension=1, tiled=True
        )
        upb_own = lax.psum_scatter(upb_grad, "seq", scatter_dimension=0, tiled=True)
        (sum_up, sum_down), sum_upb = lax.psum((own[:, 0], upb_own.reshape(-1)), "dp")
        sum_w, sum_o, sum_state, small, sum_norm, sum_feed = lax.psum(
            (sum_w, output_grad, state_grad, small, norm_grad, feed_three), ("dp", "seq")
        )
        mixer_two = (small[heads + 1], small[heads + 2])
        sum_gate, gate_bias_sum = small[:heads], small[heads, :heads]
        sum_w = sum_w.reshape(groups, width, 3, hg * size).transpose(2, 1, 0, 3)
        sum_q, sum_k, sum_v = sum_w.reshape(3, width, width).astype(F32)
        sum_state = sum_state.reshape(heads, size, 2 * feats).astype(F32)
    return (
        out.reshape(inputs.shape),
        dx.reshape(inputs.shape),
        mixer_two[0].reshape(-1),
        mixer_two[1].reshape(-1),
        sum_q,
        sum_k,
        sum_v,
        sum_gate.T,
        gate_bias_sum,
        sum_o.astype(F32),
        sum_state.transpose(0, 2, 1),
        sum_norm,
        sum_feed[0].reshape(-1),
        sum_feed[1].reshape(-1),
        sum_up.astype(F32),
        sum_upb.reshape(-1),
        sum_down.astype(F32),
        sum_feed[2].reshape(-1),
    )


def solution(mesh):
    tokens = P("dp", "seq", None)
    columns = P(None, "seq")
    return jax.shard_map(
        local,
        mesh=mesh,
        in_specs=(tokens, tokens) + (P(),) * 13 + (columns, P("seq"), columns, P()),
        out_specs=(tokens, tokens) + (P(),) * 12 + (columns, P("seq"), columns, P()),
        check_vma=False,
    )
```

```python
from functools import partial
import math

import jax
import jax.numpy as jnp
from jax import lax
from jax.experimental import pallas as pl
from jax.experimental.pallas import tpu as pltpu
from jax.sharding import PartitionSpec as P

F32 = jnp.float32
BF16 = jnp.bfloat16
EPS_NORM = 1e-05
EPS_UNIT = 1e-06
GUARD = 0.0625
MESH = pl.DeviceIdType.MESH
VMEM = 56 * 1024 * 1024

C = 128
T = 256
FEED_ROWS = 512
HB = 256
INNER_HEADS = 8
WEIGHT_STEPS = (2, 3, 5, 8)
SPAN = 2
GROUP_HEADS = 4
LANES = 128

SIN = (3.14158202, -5.16714278, 2.54189892, -0.55463591)
COS = (0.99999995, -4.93479286, 4.05841191, -1.33188012, 0.21969671)
ERF = (0.319381530, -0.356563782, 1.781477937, -1.821255978, 1.330274429)
ERF_P = 0.2316419
INV_SQRT_2PI = 0.3989422804014327


def nn(a, b):
    return lax.dot_general(a, b, (((1,), (0,)), ((), ())), preferred_element_type=F32)


def nt(a, b):
    return lax.dot_general(a, b, (((1,), (1,)), ((), ())), preferred_element_type=F32)


def tn(a, b):
    return lax.dot_general(a, b, (((0,), (0,)), ((), ())), preferred_element_type=F32)


def thirds(x):
    high = x.astype(BF16)
    rest = x - high.astype(F32)
    middle = rest.astype(BF16)
    return high, middle, (rest - middle.astype(F32)).astype(BF16)


def rows_up_to(x):
    n = x.shape[0]
    tri = jnp.where(iota((n, n), 0) >= iota((n, n), 1), 1.0, 0.0).astype(BF16)
    return nn(jnp.concatenate([tri] * 3, axis=1), jnp.concatenate(thirds(x), axis=0))


def lanes_up_to(x):
    n = x.shape[1]
    tri = jnp.where(iota((n, n), 0) <= iota((n, n), 1), 1.0, 0.0).astype(BF16)
    return nn(jnp.concatenate(thirds(x), axis=1), jnp.concatenate([tri] * 3, axis=0))


def iota(shape, dim):
    return lax.broadcasted_iota(jnp.int32, shape, dim)


def log_sigmoid(x):
    return jnp.minimum(x, 0.0) - jnp.log(1.0 + jnp.exp(-jnp.abs(x)))


def normalize(x):
    centred = x - jnp.mean(x, axis=-1, keepdims=True)
    scale = lax.rsqrt(jnp.mean(centred * centred, axis=-1, keepdims=True) + EPS_NORM)
    return centred * scale, scale


def normalize_back(grad, gain, xhat, scale):
    inner = grad * gain
    mean_inner = jnp.mean(inner, axis=-1, keepdims=True)
    mean_both = jnp.mean(inner * xhat, axis=-1, keepdims=True)
    return scale * (inner - mean_inner - xhat * mean_both)


def fold_rows(x):
    return jnp.sum(x.reshape(x.shape[0] // 8, 8, x.shape[1]), axis=0)


def block_ones():
    return jnp.where(
        iota((LANES, LANES), 0) // 64 == iota((LANES, LANES), 1) // 64, 1.0, 0.0
    ).astype(BF16)


def head_sums(x):
    high = x.astype(BF16)
    rest = (x - high.astype(F32)).astype(BF16)
    ones = block_ones()
    return nn(jnp.concatenate([high, rest], axis=1), jnp.concatenate([ones, ones], axis=0))


def lower_half(shape):
    return iota(shape, 1) < 64


def mine(h, lower):
    return lower if h % 2 == 0 else jnp.logical_not(lower)


def column(block, index, rows, width):
    return jnp.broadcast_to(block[:, index : index + 1], (rows, width))


def sin_cos(turns, scale):
    r = turns - jnp.floor(turns + 0.5)
    r2 = r * r
    s = (((SIN[3] * r2 + SIN[2]) * r2 + SIN[1]) * r2 + SIN[0]) * r
    k = 2.0 * scale
    c = (((k * COS[4] * r2 + k * COS[3]) * r2 + k * COS[2]) * r2 + k * COS[1]) * r2 + k * COS[0]
    return s * c, scale - (k * s) * s


class Links:
    def __init__(self):
        self.dp, self.seq = lax.axis_index("dp"), lax.axis_index("seq")
        core, y, z = self.dp % 2, (self.dp // 2) % 2, self.dp // 4
        self.y = y
        self.at = {"core": core, "y": y, "z": z, "plane": self.seq * 2 + y}
        self.at["xr"] = 0

    size = {"core": 2, "xr": 2, "y": 2, "z": 4, "plane": 4}

    def partner(self, group, step):
        dp, seq = self.dp, self.seq
        if group == "core":
            return (dp + 1 - 2 * self.at["core"], seq)
        if group == "xr":
            return (dp, 1 - seq)
        if group == "y":
            return (dp + 2 - 4 * self.y, seq)
        target = (self.at[group] + step) % 4
        if group == "z":
            return (dp % 4 + 4 * target, seq)
        return (dp + 2 * (target % 2 - self.y), target // 2)

    def greet(self, groups):
        barrier = pltpu.get_barrier_semaphore()
        count = 0
        for group in groups:
            for step in range(1, self.size[group]):
                pl.semaphore_signal(
                    barrier, inc=1, device_id=self.partner(group, step), device_id_type=MESH
                )
                count += 1
        pl.semaphore_wait(barrier, count)


class Plan:
    def __init__(self, rows, lanes, dtype, scatter, gather, share=(), pre=()):
        self.pre = pre
        self.scatter, self.gather, self.share = scatter, gather, share
        self.rows, self.lanes, self.dtype = rows, lanes, dtype
        self.groups = scatter + gather + share
        self.left = rows
        for group in scatter:
            self.left //= Links.size[group]
        self.stages = len(self.groups)

    def scratch(self):
        shapes = []
        rows = self.rows
        for i, group in enumerate(self.scatter):
            n = Links.size[group]
            rows //= n
            shapes.append(pltpu.VMEM((n - 1, rows, self.lanes), self.dtype))
            if i < len(self.scatter) - 1:
                shapes.append(pltpu.VMEM((rows, self.lanes), self.dtype))
        for i, group in enumerate(self.share):
            shapes.append(pltpu.VMEM((Links.size[group], rows, self.lanes), self.dtype))
            if i < len(self.share) - 1:
                shapes.append(pltpu.VMEM((rows, self.lanes), self.dtype))
        for group in self.groups:
            n = Links.size[group]
            shapes.append(pltpu.SemaphoreType.DMA((n - 1,)))
            shapes.append(pltpu.SemaphoreType.DMA((n - 1,)))
        return shapes


class Stream:
    def __init__(self, plan, links, source, out, scratch):
        self.plan, self.links, self.source, self.out = plan, links, source, out
        scratch = list(scratch)
        self.landing, self.parts = [], [source]
        summed = plan.scatter + plan.share
        for i in range(len(summed)):
            self.landing.append(scratch.pop(0))
            if i < len(summed) - 1:
                self.parts.append(scratch.pop(0))
        self.sems = [(scratch.pop(0), scratch.pop(0)) for _ in range(plan.stages)]
        self.places = {}
        rows, start = out.shape[0], 0
        for group in plan.pre + plan.scatter:
            if group in plan.gather:
                rows //= Links.size[group]
                self.places[group] = (start, rows)
                start = start + links.at[group] * rows
        self.final = (start, rows)

    def copies(self, stage, sending):
        plan, links = self.plan, self.links
        group = plan.groups[stage]
        n, me = Links.size[group], links.at[group]
        sends, recvs = self.sems[stage]
        made = []
        for step in range(1, n):
            target, origin = (me + step) % n, (me + n - step) % n
            if plan.share:
                source = self.parts[stage]
                lands = self.landing[stage].at[me]
                arrives = self.landing[stage].at[origin]
            elif stage < len(plan.scatter):
                landing = self.landing[stage]
                rows = landing.shape[1]
                source = self.parts[stage].at[pl.ds(pl.multiple_of(target * rows, 8), rows)]
                arrives = lands = landing.at[step - 1]
            else:
                start, rows = self.places[group]
                mine_at = pl.multiple_of(start + me * rows, 8)
                theirs_at = pl.multiple_of(start + origin * rows, 8)
                source = lands = self.out.at[pl.ds(mine_at, rows)]
                arrives = self.out.at[pl.ds(theirs_at, rows)]
            made.append(
                pltpu.make_async_remote_copy(
                    src_ref=source if sending else arrives,
                    dst_ref=lands if sending else arrives,
                    send_sem=sends.at[step - 1],
                    recv_sem=recvs.at[step - 1],
                    device_id=links.partner(group, step),
                    device_id_type=MESH,
                )
            )
        return made

    def start(self, stage):
        if stage == 0 and not (self.plan.scatter or self.plan.share):
            start, rows = self.final
            self.out[pl.ds(pl.multiple_of(start, 8), rows), :] = self.source[...]
        for copy in self.copies(stage, True):
            copy.start()

    def finish(self, stage):
        plan = self.plan
        for copy in self.copies(stage, False):
            copy.wait_recv()
        if plan.share:
            landing, me = self.landing[stage], self.links.at[plan.groups[stage]]
            landing[me] = self.parts[stage][...]
            total = landing[0]
            for k in range(1, landing.shape[0]):
                total = total + landing[k]
            if stage + 1 < plan.stages:
                self.parts[stage + 1][...] = total
            else:
                self.out[...] = total
            return
        if stage >= len(plan.scatter):
            return
        landing = self.landing[stage]
        arrivals, rows, _ = landing.shape
        own = self.links.at[plan.groups[stage]] * rows
        into, start = self.out, self.final[0]
        if stage + 1 < len(plan.scatter):
            into, start = self.parts[stage + 1], 0
        block = min(rows, SUM_ROWS)

        def add_block(k, carry):
            at = k * block
            total = self.parts[stage][pl.ds(pl.multiple_of(own + at, 16), block), :].astype(F32)
            for step in range(arrivals):
                total = total + landing[step, pl.ds(pl.multiple_of(at, 16), block), :].astype(F32)
            into[pl.ds(pl.multiple_of(start + at, 16), block), :] = total.astype(landing.dtype)
            return carry

        lax.fori_loop(0, rows // block, add_block, 0)

    def drain(self):
        for stage in range(self.plan.stages):
            for copy in self.copies(stage, True):
                copy.wait_send()


ALL_PLAN = (("core", "plane", "z"), ("z", "plane", "core"))
SHARE_PLAN = ((), (), ("core", "plane", "z"))


def pick_row(block, index):
    return jnp.sum(jnp.where(iota(block.shape, 0) == index, block, 0.0), axis=0, keepdims=True)


def grow_state(rows, norm, h):
    rows = rows.astype(F32)
    norm = jnp.broadcast_to(norm, rows.shape)
    return jnp.concatenate([rows, norm] if h % 2 == 0 else [norm, rows], axis=0)


def state_part(state, h):
    return state[0:64] if h % 2 == 0 else state[64:128]


def norm_part(state, h):
    return state[64:65] if h % 2 == 0 else state[0:1]


def pack_states(states, out_ref):
    heads = len(states)
    for h, state in enumerate(states):
        out_ref[64 * h : 64 * (h + 1), :] = state_part(state, h).astype(BF16)
    norms = [norm_part(state, h) for h, state in enumerate(states)]
    pad = jnp.zeros((16 - heads, states[0].shape[1]), F32)
    out_ref[64 * heads : 64 * heads + 16, :] = jnp.concatenate(norms + [pad], axis=0).astype(BF16)


def projection_blocks(proj_ref, p, scale):
    parts = [proj_ref[2 * p + j] * scale for j in range(2)]
    highs = [part.astype(BF16) for part in parts]
    rests = [(part - high.astype(F32)).astype(BF16) for part, high in zip(parts, highs)]
    zero = jnp.zeros(highs[0].shape, BF16)

    def diagonal(pair):
        return jnp.concatenate(
            [
                jnp.concatenate([pair[0], zero], axis=1),
                jnp.concatenate([zero, pair[1]], axis=1),
            ],
            axis=0,
        )

    return diagonal(highs), diagonal(rests)


class Taker:
    def __init__(self, refs):
        self.refs = list(refs)

    def __call__(self, n):
        taken = self.refs[:n]
        del self.refs[:n]
        return taken


class Board:
    def __init__(self, links, take, store_sems):
        self.links, self.take, self.store_sems = links, take, store_sems
        self.entries = []

    def add(self, plan, source, out, final, ticks):
        stream = Stream(plan, self.links, source, out, self.take(len(plan.scratch())))
        self.entries.append((stream, ticks, out, final))

    def store(self, k):
        _, _, out, final = self.entries[k]
        return pltpu.make_async_copy(out, final, self.store_sems.at[k])

    def advance(self, now):
        for k, (stream, ticks, _, final) in enumerate(self.entries):
            for stage, tick in enumerate(ticks):
                if tick == now:
                    if stage > 0:
                        stream.finish(stage - 1)
                    if stage < stream.plan.stages:
                        stream.start(stage)
                    elif final is not None:
                        self.store(k).start()

    def last(self):
        return max(ticks[-1] for _, ticks, _, _ in self.entries)

    def drain(self):
        for k, (stream, _, _, final) in enumerate(self.entries):
            stream.drain()
            if final is not None:
                self.store(k).wait()


def features_kernel(heads, span, blocks, comm, *refs):
    take = Taker(refs)
    x_ref, gain_ref, bias_ref, wq_ref, wk_ref, wv_ref = take(6)
    gate_ref, gb_smem, proj_ref, start_ref, start_norm_ref = take(5)
    up_hbm, down_hbm, upb_ref = take(3) if comm else (None,) * 3
    ml_ref, uq_ref, uk_ref, rq_ref, rk_ref, qf_ref, kf_ref, v_ref = take(8)
    gcol_ref, grow_ref, before_ref, n_ref = take(4)
    if comm:
        entry_ref, upo_hbm, downo_hbm, upbs_ref = take(4)
    else:
        final_ref, total_ref = take(2)
    state, carry, qf_s, kf_s, v_s, gcol_s, grow_s, before_s = take(8)
    wg_ref, gb_ref, gbt_ref, pcat_ref = take(4)
    step = pl.program_id(0)
    chunks = span * blocks
    full = span * C

    if comm:
        sent, landed, upb_own, upb_landed, sends, recvs = take(6)
        links = Links()
        core, y = links.at["core"], links.at["y"]
        part = up_hbm.shape[0] // 4
        here = pl.ds(pl.multiple_of((2 * core + y) * part, 16), part)
        there = pl.ds(pl.multiple_of((2 * core + 1 - y) * part, 16), part)
        own_half = pl.ds(pl.multiple_of(2 * core * part, 16), 2 * part)
        other_half = pl.ds(pl.multiple_of(2 * (1 - core) * part, 16), 2 * part)

        def remote(k, sending):
            group = ("xr", "y", "core")[k // 2] if k < 6 else "xr"
            if k == 6:
                source, lands = upb_own, upb_landed
            elif k == 7:
                source, lands = sent, landed
            else:
                mine_ref, theirs_ref = ((up_hbm, upo_hbm), (down_hbm, downo_hbm))[k % 2]
                if k < 2:
                    source, lands = mine_ref.at[here], theirs_ref.at[here]
                elif k < 4:
                    source = theirs_ref.at[here]
                    lands = source if sending else theirs_ref.at[there]
                else:
                    source = theirs_ref.at[own_half]
                    lands = source if sending else theirs_ref.at[other_half]
            return pltpu.make_async_remote_copy(
                src_ref=source if sending else lands,
                dst_ref=lands,
                send_sem=sends.at[k],
                recv_sem=recvs.at[k],
                device_id=links.partner(group, 1),
                device_id_type=MESH,
            )

        @pl.when(step == 0)
        def _():
            links.greet(("core", "xr", "y"))
            upb_own[...] = upb_ref[...].astype(F32)
            for k in (6, 0, 1):
                remote(k, True).start()

        @pl.when(step == blocks)
        def _():
            remote(7, True).start()

        for k, ready in zip(range(4), WEIGHT_STEPS):
            @pl.when(step == ready)
            def _(k=k):
                remote(k, False).wait_recv()
                remote(k + 2, True).start()

    @pl.when(step == 0)
    def _():
        carry[...] = jnp.zeros_like(carry)
        is_first = lax.axis_index("seq") == 0
        spread = jnp.where(iota((LANES, heads), 0) % heads == iota((LANES, heads), 1), 1.0, 0.0)
        wg_ref[...] = nn(spread.astype(BF16), gate_ref[...]).astype(BF16)
        lane_head = iota((1, LANES), 1) % heads
        row_head = iota((heads, LANES), 0)
        gb = jnp.zeros((1, LANES), F32)
        gbt = jnp.zeros((heads, LANES), F32)
        for h in range(heads):
            gb = jnp.where(lane_head == h, gb_smem[h], gb)
            gbt = jnp.where(row_head == h, gb_smem[h], gbt)
            begin = start_ref[h]
            norm = jnp.broadcast_to(start_norm_ref[h : h + 1, :], begin.shape)
            both = [begin, norm] if h % 2 == 0 else [norm, begin]
            state[h] = jnp.where(is_first, jnp.concatenate(both, axis=0), 0.0)
        gb_ref[...] = gb
        gbt_ref[...] = gbt
        for p in range(heads // 2):
            high, rest = projection_blocks(proj_ref, p, 1.0 / (2.0 * math.pi))
            pcat_ref[p, 0:LANES, :] = high
            pcat_ref[p, LANES : 2 * LANES, :] = high
            pcat_ref[p, 2 * LANES : 3 * LANES, :] = rest

    lower = lower_half((C, LANES))

    @pl.when(step < blocks)
    def _():
        xhat, _ = normalize(x_ref[...].astype(F32))
        ml = (xhat * gain_ref[...] + bias_ref[...]).astype(BF16)
        ml_ref[...] = ml
        q = nn(ml, wq_ref[...])
        k = nn(ml, wk_ref[...])
        v = nn(ml, wv_ref[...])
        v_low = v.astype(BF16)
        v_ref[...] = v_low
        rows_of = [slice(C * u, C * (u + 1)) for u in range(span)]
        logit = nt(ml, wg_ref[...]) + gb_ref[...]
        keep = log_sigmoid(logit)
        logit_row = nt(gate_ref[...], ml) + gbt_ref[...][:, 0:1]
        keep_row = log_sigmoid(logit_row)

        ftr_scale = 1.0 / math.sqrt(LANES)
        pairs = range(heads // 2)
        lanes_of = [slice(LANES * p, LANES * (p + 1)) for p in pairs]
        boths = [jnp.concatenate([q[:, at], k[:, at]], axis=0) for at in lanes_of]
        scales = [lax.rsqrt(head_sums(both * both) + EPS_UNIT) for both in boths]
        all_turns = []
        for p in pairs:
            unit = boths[p] * scales[p]
            high = unit.astype(BF16)
            rest = (unit - high.astype(F32)).astype(BF16)
            uq_ref[:, lanes_of[p]] = high[:full]
            uk_ref[:, lanes_of[p]] = high[full:]
            rq_ref[:, lanes_of[p]] = scales[p][:full]
            rk_ref[:, lanes_of[p]] = scales[p][full:]
            all_turns.append(nn(jnp.concatenate([high, rest, high], axis=1), pcat_ref[p]))
        coefs, totals = [], []
        group = iota((C, LANES), 1) // 8
        for u, rows in enumerate(rows_of):
            decay = rows_up_to(keep[rows])
            total = decay[C - 1 : C, :]
            coef = total - decay + keep[rows] - logit[rows]
            packed = jnp.where(group == 0, decay, coef)
            packed = jnp.where(group == 2, carry[...] + decay, packed)
            packed = jnp.where(group == 6, jnp.broadcast_to(carry[...], (C, LANES)), packed)
            packed = jnp.where(group == 7, jnp.broadcast_to(total, (C, LANES)), packed)
            gcol_ref[rows, :] = packed
            gcol_s[span * step + u] = packed
            carry[...] = carry[...] + total
            coefs.append(coef)
            totals.append(total)
            gate_rows = jnp.concatenate(
                [
                    keep_row[:, rows] - logit_row[:, rows] - lanes_up_to(keep_row[:, rows]),
                    jax.nn.sigmoid(logit_row[:, rows]),
                    jax.nn.sigmoid(-logit_row[:, rows]),
                ],
                axis=0,
            )
            grow_ref[:, rows] = gate_rows
            grow_s[span * step + u] = gate_rows
        if not comm:
            total_ref[...] = jnp.broadcast_to(carry[...], total_ref.shape)
        for p in pairs:
            s, c = sin_cos(all_turns[p], ftr_scale)
            s = s.astype(BF16)
            c = c.astype(BF16)
            for j in range(2):
                h = 2 * p + j
                half_lanes = slice(LANES * j, LANES * (j + 1))
                feats = jnp.concatenate([s[:, half_lanes], c[:, half_lanes]], axis=1)
                place = slice(256 * h, 256 * (h + 1))
                qf_ref[:, place] = feats[:full]
                kf_ref[:, place] = feats[full:]
                for u, rows in enumerate(rows_of):
                    at = span * step + u
                    kf = feats[full + C * u : full + C * (u + 1)]
                    qf_s[at, :, place] = feats[rows]
                    kf_s[at, :, place] = kf
                    v_s[at, :, lanes_of[p]] = v_low[rows, lanes_of[p]]
                    values = jnp.where(mine(h, lower), v[rows, lanes_of[p]], 1.0)
                    weighted = values * jnp.exp(column(coefs[u], h, C, LANES))
                    now = state[h]
                    now_low = now.astype(BF16)
                    before_ref[u, h] = now_low
                    before_s[at, h] = now_low
                    state[h] = jnp.exp(totals[u][:, h : h + 1]) * now + tn(weighted.astype(BF16), kf)

    @pl.when(step == blocks - 1)
    def _():
        pack_states([state[h] for h in range(heads)], sent if comm else final_ref)

    @pl.when(step >= blocks)
    def _():
        chunk = step - blocks
        causal = iota((C, C), 0) >= iota((C, C), 1)
        gcol = gcol_s[chunk]
        for first in range(0, heads, INNER_HEADS):
            some = range(first, first + INNER_HEADS)
            boths = []
            for h in some:
                place = slice(256 * h, 256 * (h + 1))
                keys = jnp.concatenate([kf_s[chunk, :, place], before_s[chunk, h]], axis=0)
                boths.append(nt(qf_s[chunk, :, place], keys))
            decays = [column(gcol, h, C, LANES) for h in some]
            weights = []
            for h, both, decay in zip(some, boths, decays):
                pairs = jnp.where(causal, jnp.exp(decay + grow_s[chunk, h : h + 1, :]), 0.0)
                weights.append((both[:, :C] * pairs).astype(BF16))
            for k, h in enumerate(some):
                lanes = slice(LANES * (h // 2), LANES * (h // 2 + 1))
                v = v_s[chunk, :, lanes].astype(F32)
                values = jnp.where(mine(h, lower), v, 1.0).astype(BF16)
                n_ref[:, LANES * h : LANES * (h + 1)] = (
                    nn(weights[k], values) + jnp.exp(decays[k]) * boths[k][:, C:]
                )

    if comm:
        @pl.when(step == blocks + chunks - 1)
        def _():
            for k in (4, 5, 6, 7):
                remote(k, False).wait_recv()
            later = links.seq == 1
            entry_ref[...] = jnp.where(later, landed[...].astype(F32), 0.0).astype(BF16)
            upbs_ref[0:1, :] = upb_own[...]
            upbs_ref[1:2, :] = upb_landed[...]
            for k in range(8):
                remote(k, True).wait_send()


def feed_kernel(heads, tiles, pairs, comm, *refs):
    take = Taker(refs)
    x_ref, qf_hbm, n_ref, gcol_ref, entry_ref, wo_ref = take(6)
    gain_ref, bias_ref, downb_ref, upb_ref, dout_hbm = take(5)
    weights_hbm = take(4 if comm else 2)
    out_ref, mg_ref, a_ref = take(3)
    if comm:
        late_refs = take(len(FEED_STAGES))
        os_ref, flat_ref, after_ref = take(3)
    else:
        upg_ref, downg_ref, upbg_ref, o_ref, final_ref, sums_out = take(6)
    entry, adj, middle_s, num_s, den_s, fl_s, mix_s, br_s = take(8)
    acc_s, fg_s, dout_s, up_s, down_s, hid_s, pre_s, sums_s, load_sems = take(9)
    step = pl.program_id(0)
    tokens, width = middle_s.shape
    rows = x_ref.shape[0]
    shards, _, shard_width = up_s.shape
    hb = hid_s.shape[1] // 2
    (qf_s,) = take(1)
    loads = [
        (qf_hbm.at[pl.ds(rows * t, rows)], qf_s.at[pl.ds(rows * t, rows)]) for t in range(tiles)
    ]
    loads += [(dout_hbm, dout_s)]
    if comm:
        up_own, up_other, down_own, down_other = weights_hbm
        loads += [(up_own, up_s.at[0]), (up_other, up_s.at[1])]
        loads += [(down_own, down_s.at[0]), (down_other, down_s.at[1])]
        u_src, upbg_s, sent, landed, sends, recvs = take(6)
        links = Links()
        board = Board(links, take, None)
        for j, (plan, ticks) in enumerate(zip(feed_plans(hb), FEED_TICKS)):
            board.add(plan, u_src.at[j], late_refs[j], None, ticks)

        def exchange():
            return pltpu.make_async_remote_copy(
                src_ref=sent,
                dst_ref=landed,
                send_sem=sends,
                recv_sem=recvs,
                device_id=links.partner("xr", 1),
                device_id_type=MESH,
            )
    else:
        upbg_s = upbg_ref
        loads += [(weights_hbm[0], up_s), (weights_hbm[1], down_s)]

    def load(k):
        return pltpu.make_async_copy(loads[k][0], loads[k][1], load_sems.at[k])

    @pl.when(step == 0)
    def _():
        for k in range(len(loads)):
            load(k).start()
        adj[...] = jnp.zeros_like(adj)
        sums_s[...] = jnp.zeros_like(sums_s)
        norms = entry_ref[64 * heads : 64 * heads + 16, :].astype(F32)
        for h in range(heads):
            grown = grow_state(entry_ref[64 * h : 64 * (h + 1), :], norms[h : h + 1], h)
            entry[h] = grown.astype(BF16)
        if comm:
            links.greet(("core", "xr", "y", "z"))

    lower = lower_half((rows, LANES))

    @pl.when(step < tiles)
    def _():
        for t in range(tiles):
            pl.when(step == t)(load(t).wait)
        here = pl.ds(pl.multiple_of(step * rows, rows), rows)
        gcol = gcol_ref[...]
        fars = [nt(qf_s[here, 256 * h : 256 * (h + 1)], entry[h]) for h in range(heads)]
        mixed = []
        for p in range(heads // 2):
            lanes = slice(LANES * p, LANES * (p + 1))
            both = []
            for h in (2 * p, 2 * p + 1):
                far = fars[h] * jnp.exp(column(gcol, 16 + h, rows, LANES))
                both.append(n_ref[:, LANES * h : LANES * (h + 1)] + far)
            num = jnp.where(lower, both[0], both[1])
            den = pltpu.roll(jnp.where(lower, both[1], both[0]), 64, 1)
            num_s[here, lanes] = num
            den_s[here, lanes] = den
            mixed.append(num * lax.rsqrt(den * den + GUARD))
        mixed = jnp.concatenate(mixed, axis=1).astype(BF16)
        mix_s[here, :] = mixed
        middle = x_ref[...].astype(F32) + nn(mixed, wo_ref[...])
        middle_s[here, :] = middle
        acc_s[here, :] = middle + downb_ref[...]
        fg_s[here, :] = jnp.zeros_like(middle)
        xhat, _ = normalize(middle)
        fl_s[here, :] = (xhat * gain_ref[...] + bias_ref[...]).astype(BF16)

    @pl.when(step == tiles)
    def _():
        for k in range(tiles, len(loads)):
            load(k).wait()

    @pl.when(jnp.logical_and(step >= tiles, step < tiles + pairs))
    def _():
        j = step - tiles
        blocks = []
        for s in range(2):
            if comm:
                shard, off = s, pl.multiple_of(j * hb, hb)
            else:
                at = (2 * j + s) * hb
                shard, off = at // shard_width, pl.multiple_of(at % shard_width, hb)
            blocks.append((shard, pl.ds(off, hb)))
        ups = [up_s[shard, :, cols] for shard, cols in blocks]
        downs = [down_s[shard, :, cols] for shard, cols in blocks]
        up = jnp.concatenate(ups, axis=1)
        down = jnp.concatenate(downs, axis=1)
        if comm:
            upb = jnp.concatenate(
                [upb_ref[s : s + 1, cols] for s, (_, cols) in enumerate(blocks)], axis=1
            )
        else:
            upb = jnp.concatenate([upb_ref[shard, :, cols] for shard, cols in blocks], axis=1)
        if comm:
            for k in range(pairs):
                pl.when(j == k)(partial(board.advance, 2 * k))
        many = min(FEED_ROWS, tokens)
        for r in range(tokens // many):
            here = slice(many * r, many * (r + 1))
            feed_low = fl_s[here, :]
            pre = nn(feed_low, up) + upb
            pre_grad = nn(dout_s[here, :], down)
            t = 1.0 / (1.0 + ERF_P * jnp.abs(pre))
            bell = INV_SQRT_2PI * jnp.exp(-0.5 * pre * pre)
            tail = ((((ERF[4] * t + ERF[3]) * t + ERF[2]) * t + ERF[1]) * t + ERF[0]) * t * bell
            phi = jnp.where(pre >= 0.0, 1.0 - tail, tail)
            hidden = (pre * phi).astype(BF16)
            pre_low = (pre_grad * (phi + pre * bell)).astype(BF16)
            hid_s[here, :] = hidden
            pre_s[here, :] = pre_low
            acc_s[here, :] += nt(hidden, down)
            fg_s[here, :] += nt(pre_low, up)
        up_grad = tn(fl_s[...], pre_s[...]).astype(BF16)
        down_grad = tn(dout_s[...], hid_s[...]).astype(BF16)
        bias_grad = nn(jnp.ones((16, tokens), BF16), pre_s[...])[0:1]
        for s, (shard, cols) in enumerate(blocks):
            part = slice(hb * s, hb * (s + 1))
            upbg_s[shard, :, cols] = bias_grad[:, part]
            if comm:
                u_src[j, width * s : width * (s + 1), :] = up_grad[:, part]
                u_src[j, width * (2 + s) : width * (3 + s), :] = down_grad[:, part]
            else:
                upg_ref[shard, :, cols] = up_grad[:, part]
                downg_ref[shard, :, cols] = down_grad[:, part]

    @pl.when(step >= tiles + pairs)
    def _():
        tile = step - tiles - pairs

        if comm:
            for t in range(tiles):
                pl.when(tile == t)(partial(board.advance, 2 * pairs + t))
        here = pl.ds(pl.multiple_of(tile * rows, rows), rows)
        gcol = gcol_ref[...]
        dout = dout_s[here, :].astype(F32)
        out_ref[...] = acc_s[here, :].astype(BF16)
        feed_grad = fg_s[here, :]
        xhat, scale = normalize(middle_s[here, :])
        sums_s[0:8, :] += fold_rows(feed_grad * xhat)
        sums_s[8:16, :] += fold_rows(feed_grad)
        sums_s[16:24, :] += fold_rows(dout)
        middle_grad = dout + normalize_back(feed_grad, gain_ref[...], xhat, scale)
        mg_ref[...] = middle_grad
        branch = middle_grad.astype(BF16)
        br_s[here, :] = branch
        mixed_grad = nt(branch, wo_ref[...])
        lanes_of = [slice(LANES * p, LANES * (p + 1)) for p in range(heads // 2)]
        alongs = [head_sums(mixed_grad[:, lanes] * num_s[here, lanes]) for lanes in lanes_of]
        lifts = []
        for p, lanes in enumerate(lanes_of):
            den = den_s[here, lanes]
            inv = lax.rsqrt(den * den + GUARD)
            b = alongs[p] * den * (inv * inv * inv) * (-1.0 / 64)
            b = pltpu.roll(b, 64, 1)
            for h in (2 * p, 2 * p + 1):
                a = jnp.where(mine(h, lower), mixed_grad[:, lanes] * inv, b)
                a_ref[:, LANES * h : LANES * (h + 1)] = a.astype(BF16)
                lifts.append((a * jnp.exp(column(gcol, 16 + h, rows, LANES))).astype(BF16))
        for h in range(heads):
            adj[h] += tn(lifts[h], qf_s[here, 256 * h : 256 * (h + 1)])

    @pl.when(step == 2 * tiles + pairs - 1)
    def _():
        pack_states([adj[h] for h in range(heads)], sent if comm else final_ref)
        if comm:
            exchange().start()
        output_grad = tn(mix_s[...], br_s[...]).astype(BF16)
        if not comm:
            o_ref[...] = output_grad
            sums_out[...] = sums_s[...]
            return
        os_ref[:, 0:width] = output_grad
        for later in range(2 * pairs + tiles, board.last() + 1):
            board.advance(later)
        exchange().wait_recv()
        is_first = links.seq == 0
        after_ref[...] = jnp.where(is_first, landed[...].astype(F32), 0.0).astype(BF16)
        logs = gcol_ref[rows - 1 : rows, :]
        norms = landed[64 * heads : 64 * heads + 16, :].astype(F32)
        flat_ref[...] = jnp.zeros_like(flat_ref)
        for k in range(3):
            flat_ref[k : k + 1, :] = jnp.sum(sums_s[8 * k : 8 * (k + 1), :], axis=0, keepdims=True)
        for k in range(2 * shard_width // width):
            cols = slice(width * k % shard_width, width * k % shard_width + width)
            in_first = k < shard_width // width
            own, other = upbg_s[0, :, cols], upbg_s[1, :, cols]
            flat_ref[3 + k : 4 + k, :] = jnp.where(is_first, own, other) if in_first else jnp.where(
                is_first, other, own
            )
        for h in range(heads):
            grown = grow_state(landed[64 * h : 64 * (h + 1), :], norms[h : h + 1], h)
            begin = adj[h] + jnp.exp(logs[:, 16 + h : 17 + h]) * grown
            begin = jnp.where(is_first, begin, 0.0)
            os_ref[64 * h : 64 * (h + 1), width : width + 256] = state_part(begin, h).astype(BF16)
            flat_ref[8 + h : 9 + h, 0:256] = 64.0 * norm_part(begin, h)
        exchange().wait_send()
        board.drain()


U_SCATTER, U_GATHER = ("core", "xr", "y", "z"), ("z", "y", "core")
FEED_STAGES = (4, 3, 2, 1)
FEED_TICKS = ((2, 4, 6, 8, 11), (4, 6, 9, 12), (6, 8, 12), (8, 10))
BACK_TICKS = ((2, 4, 6, 7), (1, 3, 5, 7, 8), (1, 3, 5, 7, 8, 9), (1, 3, 5, 7, 8, 9, 10))


def feed_plans(hb):
    return [Plan(2048, hb, BF16, U_SCATTER[:n], ()) for n in FEED_STAGES]


def late_plans(hb):
    plans = []
    for plan, n in zip(feed_plans(hb), FEED_STAGES):
        done = [group for group in U_SCATTER[:n] if group != "xr"]
        plans.append(Plan(plan.left, hb, BF16, U_SCATTER[n:], U_GATHER, pre=tuple(done)))
    return plans


def back_kernel(heads, hg, span, chunks, comm, *refs):
    take = Taker(refs)
    (qf_ref, kf_ref, v_ref, uq_ref, uk_ref, rq_ref, rk_ref, a_ref, gcol_ref, grow_ref) = take(10)
    before_ref, entry_ref, entry_norm, after_ref, after_norm, proj_in = take(6)
    x_hbm, mg_hbm, ml_hbm, wq_hbm, wk_hbm, wv_hbm, gate_ref, gain_ref = take(8)
    u_hbms = take(len(FEED_STAGES)) if comm else ()
    os_hbm, f_hbm = take(2) if comm else (None,) * 2
    dx_ref, w_ref, small_ref = take(3)
    usum_hbm, ossum_hbm, fsum_hbm = take(3) if comm else (None,) * 3
    adj_ref, dqkv, dlogit, x_ref, mg_ref, ml_ref, wq_ref, wk_ref, wv_ref, load_sems = take(10)
    (proj_ref,) = take(1)
    g, i = pl.program_id(0), pl.program_id(1)
    tick = g * chunks + i
    last = heads // hg * chunks - 1
    first_row = (chunks - 1 - i) * (span * C)
    here = pl.ds(pl.multiple_of(first_row, C), span * C)
    groups = heads // hg
    loads = [
        (x_hbm, x_ref),
        (mg_hbm, mg_ref),
        (ml_hbm, ml_ref),
        (wq_hbm, wq_ref),
        (wk_hbm, wk_ref),
        (wv_hbm, wv_ref),
    ]
    if comm:
        u_refs = take(len(FEED_STAGES))
        os_ref, f_ref, w_src, small_src = take(4)
        usum_ref, ossum_ref, fsum_ref, wsum_ref, smallsum_ref = take(5)
        (store_sems,) = take(1)
        loads = list(zip(u_hbms, u_refs)) + [(os_hbm, os_ref), (f_hbm, f_ref)] + loads
        early_loads = len(loads) - 6
        links = Links()
        board = Board(links, take, store_sems)
        plans = back_plans(os_hbm.shape, f_hbm.shape, w_src.shape, small_src.shape)

        def stages(start, gaps):
            ticks = [start]
            for gap in gaps:
                ticks.append(ticks[-1] + gap)
            return ticks

        for k in reversed(range(groups)):
            final = k + 1 == groups
            pieces = W_PIECES if final else 1
            lanes_each = w_src.shape[2] // pieces
            for j in range(pieces):
                lanes = pl.ds(j * lanes_each, lanes_each)
                board.add(
                    plans["w_last" if final else "w"],
                    w_src.at[k, :, lanes],
                    wsum_ref.at[k, :, lanes],
                    w_ref.at[k, :, lanes],
                    [last + 1 + i for i in range(7)]
                    if final
                    else [(k + 1) * chunks + gap for gap in W_GAPS],
                )
        for j, (plan, ticks) in enumerate(zip(late_plans(usum_ref.shape[2]), BACK_TICKS)):
            board.add(plan, u_refs[j], usum_ref.at[j], usum_hbm.at[j], ticks)
        board.add(plans["os"], os_ref, ossum_ref, ossum_hbm, OS_TICKS)
        board.add(plans["f"], f_ref, fsum_ref, fsum_hbm, F_TICKS)
        advance = board.advance

    def load(k):
        return pltpu.make_async_copy(loads[k][0], loads[k][1], load_sems.at[k])

    @pl.when(tick == 0)
    def _():
        for k in range(len(loads)):
            load(k).start()
        dlogit[...] = jnp.zeros_like(dlogit)
        if comm:
            links.greet(("core", "plane", "z"))

    if comm:
        @pl.when(tick == 1)
        def _():
            for k in range(early_loads):
                load(k).wait()

        for now in range(1, last + 1):
            pl.when(tick == now)(partial(advance, now))

    @pl.when(i == 0)
    def _():
        for p in range(hg // 2):
            proj_ref[p] = projection_blocks(proj_in, p, 1.0 / (2.0 * math.pi))[0]
        norms = after_norm[...].astype(F32)
        for h in range(hg):
            norm = pick_row(norms, g * hg + h)
            adj_ref[h] = grow_state(after_ref[64 * h : 64 * (h + 1), :], norm, h)

    row = iota((C, C), 0)
    col = iota((C, C), 1)
    causal = row >= col
    one = jnp.ones((C, C), BF16)
    zero = jnp.zeros((C, C), BF16)
    later = jnp.where(row < col, 1.0, 0.0).astype(BF16)
    pair_sums = jnp.concatenate([later, one], axis=0)
    two_sums = jnp.concatenate(
        [jnp.concatenate([one, zero], axis=1), jnp.concatenate([zero, one], axis=1)], axis=0
    )
    lower = lower_half((C, LANES))
    entry_norms = entry_norm[...].astype(F32)
    gcol = gcol_ref[...]
    if groups > 1:
        gcol = jnp.where(g == 0, gcol, pltpu.roll(gcol, LANES - hg, 1))

    def grow_row(kind, h):
        return grow_ref[pl.ds(kind * heads + g * hg + h, 1), :]

    width = hg * 64
    pairs_of_heads = range(hg // 2)
    lanes_of = [slice(LANES * p, LANES * (p + 1)) for p in pairs_of_heads]
    items = [(u, h) for u in reversed(range(span)) for h in range(hg)]
    numbers = range(len(items))
    rows_of = [slice(C * u, C * (u + 1)) for u in range(span)]
    qfs = [qf_ref[rows_of[u], 256 * h : 256 * (h + 1)] for u, h in items]
    kfs = [kf_ref[rows_of[u], 256 * h : 256 * (h + 1)] for u, h in items]
    a_lows = [a_ref[rows_of[u], LANES * h : LANES * (h + 1)] for u, h in items]
    values = [
        jnp.where(mine(h, lower), v_ref[rows_of[u], lanes_of[h // 2]].astype(F32), 1.0)
        for u, h in items
    ]
    values_low = [part.astype(BF16) for part in values]
    lifts = [jnp.exp(column(gcol[rows_of[u]], h, C, LANES)) for u, h in items]
    a_lifts = [(a_lows[k].astype(F32) * lifts[k]).astype(BF16) for k in numbers]
    dweights = []
    for k in numbers[::2]:
        u, h = items[k]
        top = jnp.concatenate([values_low[k], zero], axis=1)
        bottom = jnp.concatenate([zero, values_low[k + 1]], axis=1)
        both = nt(
            a_ref[rows_of[u], LANES * h : LANES * (h + 2)],
            jnp.concatenate([top, bottom], axis=0),
        )
        dweights += [both[:, :C], both[:, C:]]
    adj_lows, throughs, keys_and_states = [], [], []
    raws, fars, dv_fars = [], [], []
    for k, (u, h) in enumerate(items):
        carried = jnp.exp(gcol[C * u : C * u + 1, 48 + h : 49 + h])
        total = jnp.exp(gcol[C * u : C * u + 1, 56 + h : 57 + h])
        entry = grow_state(
            entry_ref[64 * h : 64 * (h + 1), :], pick_row(entry_norms, g * hg + h), h
        )
        before = before_ref[u, h].astype(F32) + carried * entry
        adj = adj_ref[h]
        adj_lows.append(adj.astype(BF16))
        kept = total * adj
        through = jnp.sum(kept * before, axis=0, keepdims=True)
        throughs.append(jnp.sum(through, axis=1, keepdims=True))
        keys_and_states.append(jnp.concatenate([kfs[k], before.astype(BF16)], axis=0))
        raw_and_far = nt(qfs[k], keys_and_states[k])
        raws.append(raw_and_far[:, :C])
        fars.append(raw_and_far[:, C:])
        dv_fars.append(nt(kfs[k], adj_lows[k]))
        if u > 0:
            adj_ref[h] = kept + tn(a_lifts[k], qfs[k])
        else:
            adj_ref[h] = kept
    coefs = [jnp.exp(column(gcol[rows_of[u]], 8 + h, C, LANES)) for u, h in items]
    weights, draws, boths, v_coefs = [], [], [], []
    for k, (u, h) in enumerate(items):
        gap = column(gcol[rows_of[u]], h, C, LANES) + grow_row(0, h)[:, rows_of[u]]
        pairs = jnp.where(causal, jnp.exp(gap), 0.0)
        weights.append((raws[k] * pairs).astype(BF16))
        draw = dweights[k].astype(BF16).astype(F32) * pairs
        draws.append(draw.astype(BF16))
        boths.append((raws[k] * draw).astype(BF16))
        v_coefs.append((values[k] * coefs[k]).astype(BF16))
    dqs, dks, dvs = [], [], []
    for k in numbers:
        dqs.append(nn(jnp.concatenate([draws[k], a_lifts[k]], axis=1), keys_and_states[k]))
        dks.append(
            nn(
                jnp.concatenate([draws[k].T, v_coefs[k]], axis=1),
                jnp.concatenate([qfs[k], adj_lows[k]], axis=0),
            )
        )
        dvs.append(tn(weights[k], a_lows[k]))
        if items[k][0] == 0:
            adj_ref[items[k][1]] += tn(a_lifts[k], qfs[k])
    x_parts, y_parts = [], []
    for k in numbers:
        dv_far = coefs[k] * dv_fars[k]
        dvs[k] = dvs[k] + dv_far
        x_far = (a_lows[k].astype(F32) * lifts[k] * fars[k]).astype(BF16)
        x_parts.append(jnp.concatenate([boths[k], x_far], axis=1))
        y_far = (values[k] * dv_far).astype(BF16)
        y_parts.append(jnp.concatenate([y_far, (values[k] * dvs[k]).astype(BF16)], axis=1))
    upto = nn(jnp.concatenate(x_parts, axis=0), pair_sums)
    ends = nn(jnp.concatenate(y_parts, axis=0), two_sums)
    dus = []
    for p in pairs_of_heads:
        angles = []
        for feats, grads in ((qfs, dqs), (kfs, dks)):
            for u in range(span):
                row_angles = []
                for k, item in enumerate(items):
                    if item[0] == u and item[1] // 2 == p:
                        f, grad = feats[k].astype(F32), grads[k]
                        row_angles.append(
                            grad[:, :LANES] * f[:, LANES:] - grad[:, LANES:] * f[:, :LANES]
                        )
                angles.append(jnp.concatenate(row_angles, axis=1))
        dus.append(nt(jnp.concatenate(angles, axis=0).astype(BF16), proj_ref[p]))
    for k, (u, h) in enumerate(items):
        rows = slice(C * k, C * (k + 1))
        flow = jnp.where(causal, upto[rows], ends[rows, :C])
        flow = jnp.sum(flow, axis=0, keepdims=True) + throughs[k]
        own = jnp.sum(jnp.where(row == col, ends[rows, C:], 0.0), axis=0, keepdims=True)
        stay, leave = grow_row(1, h)[:, rows_of[u]], grow_row(2, h)[:, rows_of[u]]
        at = pl.ds(pl.multiple_of(first_row + C * u, C), C)
        dlogit[g, h : h + 1, at] = leave * flow - stay * own
    for p, lanes in enumerate(lanes_of):
        u = jnp.concatenate([uq_ref[:, lanes], uk_ref[:, lanes]], axis=0).astype(F32)
        scale = jnp.concatenate([rq_ref[:, lanes], rk_ref[:, lanes]], axis=0)
        along = nn((u * dus[p]).astype(BF16), block_ones())
        dqk = ((2.0 * math.pi) * scale * (dus[p] - u * along)).astype(BF16)
        dqkv[g, here, LANES * p : LANES * (p + 1)] = dqk[: span * C]
        dqkv[g, here, width + LANES * p : width + LANES * (p + 1)] = dqk[span * C :]
        for k, (u, h) in enumerate(items):
            if h == 2 * p:
                at = pl.ds(pl.multiple_of(first_row + C * u, C), C)
                dqkv[g, at, 2 * width + LANES * p : 2 * width + LANES * (p + 1)] = jnp.where(
                    lower, dvs[k], dvs[k + 1]
                ).astype(BF16)

    @pl.when(i == chunks - 1)
    def _():
        @pl.when(g == 0)
        def _():
            load(len(loads) - 4).wait()

        grads = tn(ml_ref[...], dqkv[g]).astype(BF16)
        if comm:
            w_src[g] = grads
        else:
            w_ref[g] = grads

    @pl.when(tick == last)
    def _():
        if comm:
            advance(last + 1)
        for k in range(len(loads) - 6, len(loads)):
            if k != len(loads) - 4:
                load(k).wait()
        tokens = chunks * span * C
        block = min(T, tokens)
        small = small_src if comm else small_ref
        rows8 = jnp.concatenate(
            [dlogit[k, 0:hg, :] for k in range(groups)]
            + [jnp.zeros((16 - heads, dlogit.shape[2]), F32)],
            axis=0,
        ).astype(BF16)
        small[...] = jnp.zeros_like(small)
        small[0:heads, :] = nn(rows8, ml_ref[...])[0:heads]
        bias_sum = nt(jnp.ones(rows8.shape, BF16), rows8)[0:1]
        small[heads : heads + 1, 0:16] = bias_sum
        gain = gain_ref[...]
        now = last + 2
        for b in range(tokens // block):
            rows = slice(block * b, block * (b + 1))
            mixer_grad = tn(rows8[0:heads, rows], gate_ref[...])
            for k in range(groups):
                for j, ref in enumerate((wq_ref, wk_ref, wv_ref)):
                    mixer_grad = mixer_grad + nt(
                        dqkv[k, rows, hg * 64 * j : hg * 64 * (j + 1)],
                        ref[:, hg * 64 * k : hg * 64 * (k + 1)],
                    )
            xhat, scale = normalize(x_ref[rows, :].astype(F32))
            small[heads + 1 : heads + 2, :] += jnp.sum(
                mixer_grad * xhat, axis=0, keepdims=True
            )
            small[heads + 2 : heads + 3, :] += jnp.sum(mixer_grad, axis=0, keepdims=True)
            dx_ref[rows, :] = mg_ref[rows, :] + normalize_back(mixer_grad, gain, xhat, scale)
        if comm:
            board.add(
                plans["small"], small_src, smallsum_ref, small_ref, [now, now + 1, now + 2, now + 3]
            )
            for later_tick in range(now, board.last() + 1):
                advance(later_tick)
            board.drain()


OS_TICKS = (1, 3, 5, 7, 8, 9, 10)
F_TICKS = (5, 7, 8, 9)
W_GAPS = (0, 2, 4, 5, 6, 7, 8)
W_PIECES = 3
SUM_ROWS = 64


def back_plans(os, f, w, small):
    return {
        "os": Plan(os[0], os[1], BF16, *ALL_PLAN),
        "f": Plan(f[0], f[1], F32, *SHARE_PLAN),
        "w": Plan(w[1], w[2], BF16, *ALL_PLAN),
        "w_last": Plan(w[1], w[2] // W_PIECES, BF16, *ALL_PLAN),
        "small": Plan(small[0], small[1], F32, *SHARE_PLAN),
    }


def whole(shape):
    zeros = (0,) * len(shape)
    return pl.BlockSpec(shape, lambda *at: zeros, pipeline_mode=pl.Buffered(1))


ANY = pl.BlockSpec(memory_space=pl.ANY)


def call(kernel, grid, ins, outs, scratch, name, collective_id=None):
    def spec(shape, block, index):
        if block is None:
            return whole(shape)
        return block if isinstance(block, pl.BlockSpec) else pl.BlockSpec(block, index)

    params = {} if collective_id is None else {
        "collective_id": collective_id, "has_side_effects": True
    }
    return pl.pallas_call(
        kernel,
        grid=grid,
        in_specs=[spec(array.shape, block, index) for array, block, index in ins],
        out_specs=[spec(shape, block, index) for shape, _, block, index in outs],
        out_shape=[jax.ShapeDtypeStruct(shape, dtype) for shape, dtype, _, _ in outs],
        scratch_shapes=scratch,
        compiler_params=pltpu.CompilerParams(
            dimension_semantics=("arbitrary",) * len(grid), vmem_limit_bytes=VMEM, **params
        ),
        name=name,
    )(*[array for array, _, _ in ins])


def finish_kernel(heads, *refs):
    take = Taker(refs)
    late_ref, w_ref, os_ref, flat_ref, small_ref = take(5)
    up_ref, down_ref, q_ref, k_ref, v_ref, o_ref, s_ref = take(7)
    vectors, (upb_ref, norm_ref, gate_ref, gate_bias_ref) = take(5), take(4)

    @pl.when(pl.program_id(0) == 0)
    def _():
        def spread(row, ref, first):
            for k in range(row.shape[1] // LANES):
                ref[first + k : first + k + 1, :] = row[:, LANES * k : LANES * (k + 1)]

        flat, small = flat_ref[...], small_ref[...]
        rows = [small[heads + 1 : heads + 2], small[heads + 2 : heads + 3]]
        rows += [flat[k : k + 1] for k in range(3)]
        for row, ref in zip(rows, vectors):
            spread(row, ref, 0)
        is_first = lax.axis_index("seq") == 0
        half = upb_ref.shape[0] * LANES // flat.shape[1]
        for k in range(half):
            row = jnp.where(is_first, flat[3 + k : 4 + k], flat[3 + half + k : 4 + half + k])
            spread(row, upb_ref, k * (flat.shape[1] // LANES))
        norm_ref[...] = flat[8 : 8 + heads, 0 : norm_ref.shape[1]]
        gate_ref[...] = small[0:heads]
        gate_bias_ref[...] = small[heads : heads + 1, 0:heads]

    hb = late_ref.shape[3]
    for part, ref in enumerate((up_ref, down_ref)):
        for k in range(late_ref.shape[0]):
            ref[:, hb * k : hb * (k + 1)] = late_ref[k, part].astype(F32)
    groups, _, lanes = w_ref.shape
    each = lanes // 3
    for part, ref in enumerate((q_ref, k_ref, v_ref)):
        for k in range(groups):
            ref[:, each * k : each * (k + 1)] = w_ref[k, :, each * part : each * (part + 1)].astype(F32)
    width = o_ref.shape[1]
    o_ref[...] = os_ref[:, 0:width].astype(F32)
    for k in range(s_ref.shape[0]):
        s_ref[k] = os_ref[64 * k : 64 * (k + 1), width:].astype(F32)


def finish(heads, sum_late, sum_w, out_state, flat, small):
    width = sum_w.shape[1]
    steps = 4
    rows = width // steps
    late, _, hb = sum_late.shape
    feats = out_state.shape[1] - width
    square = ((width, width), F32, (rows, width), lambda i: (i, 0))
    wide = ((width, late * hb), F32, (rows, late * hb), lambda i: (i, 0))
    return call(
        partial(finish_kernel, heads),
        (steps,),
        [
            (sum_late.reshape(late, 2, width, hb), (late, 2, rows, hb), lambda i: (0, 0, i, 0)),
            (sum_w, (sum_w.shape[0], rows, sum_w.shape[2]), lambda i: (0, i, 0)),
            (out_state, (rows, width + feats), lambda i: (i, 0)),
            (flat, None, None),
            (small, None, None),
        ],
        [wide, wide, square, square, square, square]
        + [((heads, 64, feats), F32, (heads // steps, 64, feats), lambda i: (i, 0, 0))]
        + [((width // LANES, LANES), F32, None, None)] * 5
        + [
            ((late * hb // LANES, LANES), F32, None, None),
            ((heads, feats), F32, None, None),
            ((heads, width), F32, None, None),
            ((1, heads), F32, None, None),
        ],
        [],
        "finish",
    )


def carry_over(payload, logs, forward):
    n, index = lax.axis_size("seq"), lax.axis_index("seq")
    everything = lax.all_gather(payload, "seq")
    every_log = lax.all_gather(logs, "seq")
    heads = logs.shape[0]
    row = jnp.arange(payload.shape[0])
    head = jnp.where(row < 64 * heads, row // 64, jnp.minimum(row - 64 * heads, heads - 1))
    total = jnp.zeros(payload.shape, F32)
    for k in range(n) if forward else reversed(range(n)):
        ahead = (k < index) if forward else (k > index)
        new = jnp.exp(every_log[k])[head][:, None] * total + everything[k].astype(F32)
        total = jnp.where(ahead, new, total)
    return total.astype(BF16)


def local(
    inputs,
    cotangent,
    mixer_gain,
    mixer_bias,
    query_weight,
    key_weight,
    value_weight,
    gate_weight,
    gate_bias,
    output_weight,
    projections,
    start_state,
    start_norm,
    feed_gain,
    feed_bias,
    up_weight,
    up_bias,
    down_weight,
    down_bias,
):
    _, tokens, width = inputs.shape
    heads, size, feats = projections.shape
    chunks = tokens // C
    span = min(SPAN, chunks)
    blocks = chunks // span
    tile = min(T, tokens)
    tiles = tokens // tile
    shards = lax.axis_size("seq")
    first = lax.axis_index("seq") == 0
    comm = (lax.axis_size("dp"), shards) == (16, 2)
    gate_rows = gate_weight.T
    x = inputs.reshape(tokens, width)
    dout = cotangent.reshape(tokens, width)
    shard_width = up_weight.shape[1]
    hidden = shard_width * shards
    hb = min(HB, shard_width)
    pairs = hidden // (2 * hb)
    wide = heads * LANES
    wider = heads * 2 * feats
    pay_shape = (heads * 64 + 16, 2 * feats)

    def const(array):
        return (array if array.ndim > 1 else array[None], None, None)

    def keep(shape, dtype):
        return (shape, dtype, None, None)

    def hbm(array):
        return (array, ANY, None)

    def result(shape, dtype):
        return (shape, dtype, ANY, None)

    def vmem(*shape, dtype=BF16):
        return pltpu.VMEM(shape, dtype)

    def early(n):
        return (span * C, n), lambda i: (jnp.minimum(i, blocks - 1), 0)

    def out_early(n, dtype):
        return ((tokens, n), dtype) + early(n)

    ins = [(x,) + early(width)]
    ins += [const(part) for part in (mixer_gain, mixer_bias, query_weight, key_weight)]
    ins += [
        const(value_weight),
        const(gate_rows),
        (gate_bias, pl.BlockSpec(memory_space=pltpu.SMEM), None),
        const(projections),
        const(start_state.transpose(0, 2, 1)),
        const(start_norm),
    ]
    outs = [out_early(width, BF16)] * 3 + [out_early(width, F32)] * 2
    outs += [out_early(wider, BF16)] * 2 + [out_early(width, BF16), out_early(LANES, F32)]
    outs += [
        (
            (3 * heads, tokens),
            F32,
            (3 * heads, span * C),
            lambda i: (0, jnp.minimum(i, blocks - 1)),
        ),
        (
            (chunks, heads, LANES, 2 * feats),
            BF16,
            (span, heads, LANES, 2 * feats),
            lambda i: (jnp.minimum(i, blocks - 1), 0, 0, 0),
        ),
        ((tokens, wide), F32, (C, wide), lambda i: (jnp.maximum(i - blocks, 0), 0)),
    ]
    scratch = [
        vmem(heads, LANES, 2 * feats, dtype=F32),
        vmem(1, LANES, dtype=F32),
        vmem(chunks, C, wider),
        vmem(chunks, C, wider),
        vmem(chunks, C, width),
        vmem(chunks, C, LANES, dtype=F32),
        vmem(chunks, 3 * heads, C, dtype=F32),
        vmem(chunks, heads, LANES, 2 * feats),
        vmem(LANES, width),
        vmem(1, LANES, dtype=F32),
        vmem(heads, LANES, dtype=F32),
        vmem(heads // 2, 3 * LANES, 2 * feats),
    ]
    if comm:
        ins += [hbm(up_weight), hbm(down_weight), const(up_bias)]
        outs += [
            keep(pay_shape, BF16),
            result(up_weight.shape, BF16),
            result(down_weight.shape, BF16),
            keep((2, shard_width), F32),
        ]
        scratch += [
            vmem(*pay_shape),
            vmem(*pay_shape),
            vmem(1, shard_width, dtype=F32),
            vmem(1, shard_width, dtype=F32),
            pltpu.SemaphoreType.DMA((8,)),
            pltpu.SemaphoreType.DMA((8,)),
        ]
    else:
        outs += [keep(pay_shape, BF16), keep((8, LANES), F32)]
    found = call(
        partial(features_kernel, heads, span, blocks, comm),
        (blocks + chunks,),
        ins,
        outs,
        scratch,
        "features",
        1 if comm else None,
    )
    ml, uq, uk, rq, rk, qf, kf, v, gcol, grow, before, num = found[:12]
    if comm:
        entry, up_other, down_other, upb = found[12:]
        weights = (up_weight, up_other, down_weight, down_other)
    else:
        final, total = found[12:]
        logs = total[0, :heads]
        entry = carry_over(final, logs, True)
        weights = (lax.all_gather(up_weight, "seq"), lax.all_gather(down_weight, "seq"))
        upb = lax.all_gather(up_bias.astype(F32)[None], "seq")

    steps = 2 * tiles + pairs

    def first_last(n):
        def index(i):
            late = jnp.maximum(i - tiles - pairs, 0)
            return (jnp.where(i < tiles + pairs, jnp.minimum(i, tiles - 1), late), 0)

        return (tile, n), index

    def only_first(n):
        return (tile, n), lambda i: (jnp.minimum(i, tiles - 1), 0)

    def only_last(n, dtype):
        return (
            (tokens, n),
            dtype,
            (tile, n),
            lambda i: (jnp.maximum(i - tiles - pairs, 0), 0),
        )

    ins = [
        (x,) + only_first(width),
        hbm(qf),
        (num,) + only_first(wide),
        (gcol,) + first_last(LANES),
        const(entry),
        const(output_weight),
        const(feed_gain),
        const(feed_bias),
        const(down_bias),
        const(upb),
        hbm(dout),
    ] + [hbm(part) for part in weights]
    outs = [only_last(width, BF16), only_last(width, F32), only_last(wide, BF16)]
    scratch = [
        vmem(heads, LANES, 2 * feats),
        vmem(heads, LANES, 2 * feats, dtype=F32),
        vmem(tokens, width, dtype=F32),
        vmem(tokens, width, dtype=F32),
        vmem(tokens, width, dtype=F32),
        vmem(tokens, width),
        vmem(tokens, width),
        vmem(tokens, width),
        vmem(tokens, width, dtype=F32),
        vmem(tokens, width, dtype=F32),
        vmem(tokens, width),
        vmem(shards, width, shard_width),
        vmem(shards, width, shard_width),
        vmem(tokens, 2 * hb),
        vmem(tokens, 2 * hb),
        vmem(24, width, dtype=F32),
        pltpu.SemaphoreType.DMA((5 + tiles,)),
        vmem(tokens, wider),
    ]
    if comm:
        plans = feed_plans(hb)
        outs += [
            *[keep((plan.left, hb), BF16) for plan in plans],
            keep((width, width + 2 * feats), BF16),
            keep((16, width), F32),
            keep(pay_shape, BF16),
        ]
        scratch += [
            vmem(pairs, 4 * width, hb),
            vmem(shards, 1, shard_width, dtype=F32),
            vmem(*pay_shape),
            vmem(*pay_shape),
            pltpu.SemaphoreType.DMA,
            pltpu.SemaphoreType.DMA,
        ]
        for plan in plans:
            scratch += plan.scratch()
    else:
        outs += [
            keep((shards, width, shard_width), BF16),
            keep((shards, width, shard_width), BF16),
            keep((shards, 1, shard_width), F32),
            keep((width, width), BF16),
            keep(pay_shape, BF16),
            keep((24, width), F32),
        ]
    found = call(
        partial(feed_kernel, heads, tiles, pairs, comm),
        (steps,),
        ins,
        outs,
        scratch,
        "feed",
        2 if comm else None,
    )
    out, mg, a = found[:3]
    if comm:
        u_late = found[3:-3]
        out_state, flat, after = found[-3:]
    else:
        up_grad, down_grad, upb_grad, output_grad, adj_final, feed_sums = found[3:]
        after = carry_over(adj_final, logs, False)
        feed_three = jnp.sum(feed_sums.reshape(3, 8, width), axis=1)
        begin = adj_final.astype(F32)
        row = jnp.arange(pay_shape[0])
        head = jnp.where(row < 64 * heads, row // 64, jnp.minimum(row - 64 * heads, heads - 1))
        begin = begin + jnp.exp(logs)[head][:, None] * after.astype(F32)
        begin = jnp.where(first, begin, 0.0)
        state_grad = begin[: heads * 64].astype(BF16)
        norm_grad = 64.0 * begin[heads * 64 : heads * 65]

    hg = GROUP_HEADS
    groups = heads // hg
    def back_rows(n, per_group=True):
        return (span * C, n), lambda g, i: (blocks - 1 - i, g if per_group else 0)

    def per_group(array, *shape):
        zeros = (0,) * (len(shape) - 1)
        return (array, shape, lambda g, i: (g,) + zeros)

    def states(array):
        return [
            (array, (hg * 64, 2 * feats), lambda g, i: (g, 0)),
            (array, (16, 2 * feats), lambda g, i: (heads * 4, 0)),
        ]

    ins = [
        (qf,) + back_rows(hg * 2 * feats),
        (kf,) + back_rows(hg * 2 * feats),
        (v,) + back_rows(hg * size),
        (uq,) + back_rows(hg * size),
        (uk,) + back_rows(hg * size),
        (rq,) + back_rows(hg * size),
        (rk,) + back_rows(hg * size),
        (a,) + back_rows(hg * LANES),
        (gcol,) + back_rows(LANES, False),
        (grow, (3 * heads, span * C), lambda g, i: (0, blocks - 1 - i)),
        (before, (span, hg, LANES, 2 * feats), lambda g, i: (blocks - 1 - i, g, 0, 0)),
    ]
    ins += states(entry) + states(after)
    ins += [
        per_group(projections, hg, size, feats),
        hbm(x),
        hbm(mg),
        hbm(ml),
        hbm(query_weight),
        hbm(key_weight),
        hbm(value_weight),
        const(gate_rows),
        const(mixer_gain),
    ]
    w_shape, small_shape = (groups, width, 3 * hg * size), (16, width)

    def sums(shape, dtype):
        return result(shape, dtype) if comm else keep(shape, dtype)

    outs = [keep((tokens, width), F32), sums(w_shape, BF16), sums(small_shape, F32)]
    scratch = [
        vmem(hg, LANES, 2 * feats, dtype=F32),
        vmem(groups, tokens, 3 * hg * size),
        vmem(groups, 8, tokens, dtype=F32),
        vmem(tokens, width),
        vmem(tokens, width, dtype=F32),
        vmem(tokens, width),
        vmem(width, width),
        vmem(width, width),
        vmem(width, width),
        pltpu.SemaphoreType.DMA((12,)),
        vmem(hg // 2, LANES, 2 * feats),
    ]
    if comm:
        ins += [hbm(part) for part in (*u_late, out_state, flat)]
        summed = [
            ((len(u_late), 2 * width, hb), BF16),
            (out_state.shape, BF16),
            (flat.shape, F32),
        ]
        outs += [result(*part) for part in summed]
        scratch += [vmem(*part.shape) for part in u_late]
        scratch += [
            vmem(*out_state.shape),
            vmem(*flat.shape, dtype=F32),
            vmem(*w_shape),
            vmem(*small_shape, dtype=F32),
        ]
        scratch += [vmem(*shape, dtype=dtype) for shape, dtype in summed]
        scratch += [vmem(*w_shape), vmem(*small_shape, dtype=F32)]
        plans = back_plans(out_state.shape, flat.shape, w_shape, small_shape)
        first_names = ("w_last",) * W_PIECES + ("w",) * (groups - 1)
        plans = (
            [plans[name] for name in first_names]
            + late_plans(hb)
            + [plans[name] for name in ("os", "f", "small")]
        )
        scratch += [pltpu.SemaphoreType.DMA((len(plans),))]
        for plan in plans:
            scratch += plan.scratch()
    found = call(
        partial(back_kernel, heads, hg, span, blocks, comm),
        (groups, blocks),
        ins,
        outs,
        scratch,
        "back",
        3 if comm else None,
    )
    dx, sum_w, small = found[:3]
    if comm:
        sum_late, out_state, flat = found[3:]
        results = finish(heads, sum_late, sum_w, out_state, flat, small)
        sum_up, sum_down, sum_q, sum_k, sum_v, sum_o, sum_state = results[:7]
        mixer_two, sum_feed = results[7:9], results[9:12]
        sum_upb, sum_norm, sum_gate, gate_bias_sum = results[12:]
        gate_bias_sum = gate_bias_sum.reshape(-1)
    else:
        own = lax.psum_scatter(
            jnp.stack([up_grad, down_grad]), "seq", scatter_dimension=1, tiled=True
        )
        upb_own = lax.psum_scatter(upb_grad, "seq", scatter_dimension=0, tiled=True)
        (sum_up, sum_down), sum_upb = lax.psum((own[:, 0], upb_own.reshape(-1)), "dp")
        sum_w, sum_o, sum_state, small, sum_norm, sum_feed = lax.psum(
            (sum_w, output_grad, state_grad, small, norm_grad, feed_three), ("dp", "seq")
        )
        mixer_two = (small[heads + 1], small[heads + 2])
        sum_gate, gate_bias_sum = small[:heads], small[heads, :heads]
        sum_w = sum_w.reshape(groups, width, 3, hg * size).transpose(2, 1, 0, 3)
        sum_q, sum_k, sum_v = sum_w.reshape(3, width, width).astype(F32)
        sum_state = sum_state.reshape(heads, size, 2 * feats).astype(F32)
    return (
        out.reshape(inputs.shape),
        dx.reshape(inputs.shape),
        mixer_two[0].reshape(-1),
        mixer_two[1].reshape(-1),
        sum_q,
        sum_k,
        sum_v,
        sum_gate.T,
        gate_bias_sum,
        sum_o.astype(F32),
        sum_state.transpose(0, 2, 1),
        sum_norm,
        sum_feed[0].reshape(-1),
        sum_feed[1].reshape(-1),
        sum_up.astype(F32),
        sum_upb.reshape(-1),
        sum_down.astype(F32),
        sum_feed[2].reshape(-1),
    )


def solution(mesh):
    tokens = P("dp", "seq", None)
    columns = P(None, "seq")
    return jax.shard_map(
        local,
        mesh=mesh,
        in_specs=(tokens, tokens) + (P(),) * 13 + (columns, P("seq"), columns, P()),
        out_specs=(tokens, tokens) + (P(),) * 12 + (columns, P("seq"), columns, P()),
        check_vma=False,
    )
```
